32 devices in a mesh: ctx: 8 (over z, core), fsdp: 4 (over y, x).
Axes of the slice: x: 2, y: 2, z: 4, core: 2. Of those that a mesh axis runs over, the one named last changes fastest.
Arguments:
- tokens: bfloat16 [4, 2048, 2048], P('fsdp', 'ctx'), may hold values from -6 to 6
- positions: int32 [4, 2048], P('fsdp', 'ctx'), may hold values from 0 to 2047, as said below
- expert_ids: int32 [4, 2048, 8], P('fsdp', 'ctx'), may hold values from 0 to 31, all different within a row; in each aligned block of 256 rows (0 to 255, 256 to 511, ..., all dimensions but the last counted through in order) at most 96 rows name the same one
- attn_gain: float32 [2048], replicated, may hold values from 0.5 to 1.5
- query_key_value_weight: bfloat16 [2048, 5120], P('fsdp'), may hold values from -0.125 to 0.125
- q_gain: float32 [128], replicated, may hold values from 0.5 to 1.5
- k_gain: float32 [128], replicated, may hold values from 0.5 to 1.5
- output_weight: bfloat16 [4096, 2048], P('fsdp'), may hold values from -1 to 1
- ffn_gain: float32 [2048], replicated, may hold values from 0.5 to 1.5
- router_weight: bfloat16 [2048, 32], P('fsdp'), may hold values from -0.0625 to 0.0625
- w_gate: bfloat16 [32, 2048, 768], P(('ctx', 'fsdp')), may hold values from -0.125 to 0.125
- w_up: bfloat16 [32, 2048, 768], P(('ctx', 'fsdp')), may hold values from -0.125 to 0.125
- w_down: bfloat16 [32, 768, 2048], P(('ctx', 'fsdp')), may hold values from -0.21875 to 0.21875
- cotangent: bfloat16 [4, 2048, 2048], P('fsdp', 'ctx'), may hold values from -6 to 6
Outputs:
- output: bfloat16 [4, 2048, 2048], P('fsdp', 'ctx')
- grad_tokens: float32 [4, 2048, 2048], P('fsdp', 'ctx')
- grad_attn_gain: float32 [2048], replicated
- grad_w_qkv: float32 [2048, 5120], P(('ctx', 'fsdp'))
- grad_q_gain: float32 [128], replicated
- grad_k_gain: float32 [128], replicated
- grad_w_out: float32 [4096, 2048], P(('ctx', 'fsdp'))
- grad_ffn_gain: float32 [2048], replicated
- grad_w_router: float32 [2048, 32], P(('ctx', 'fsdp'))
- grad_w_gate: float32 [32, 2048, 768], P(('ctx', 'fsdp'))
- grad_w_up: float32 [32, 2048, 768], P(('ctx', 'fsdp'))
- grad_w_down: float32 [32, 768, 2048], P(('ctx', 'fsdp'))
The draws below stay inside these ranges and needn't reach their ends.
Inputs may be any that keep to these rules, and one draw needn't show every extreme that they name: In each sequence every position below 2048 occurs once. The sequence is cut into 16 blocks of 128 consecutive positions; the tokens of one device along ctx are block b in rising order and then block 15 - b in rising order, with b below 8 and different for each device of the sequence. `expert_ids`: each row names 8 different experts. Among the 256 rows of one device (aligned blocks of rows in order) no expert is named more than 96 times, and in some device's rows some expert is named exactly 96 times.
All inputs are finite; a program needn't handle non-finite values.
Results may differ from the reference program's by a relative error of at most 0.019.
Values may be sent and summed in bfloat16 or wider, within the bound.
A program may use at most 320 MiB of HBM per device.

```python
import math
import jax
import jax.numpy as jnp
import numpy as np
from jax import lax

D = 2048
HQ = 32
HK = 4
HD = 128
F = 768
TOP = 8
TOK_DEV = 256
SEQ = 2048
SEQS = 4
EXPERTS = 32
CAP = 96
N_CTX = 8
N_FSDP = 4


def draw_positions(key, part):
    key = jax.random.fold_in(key, 7)
    ctx_count = SEQ // TOK_DEV
    half_len = TOK_DEV // 2
    subkeys = jax.random.split(key, SEQS)
    ranking = jax.vmap(lambda subkey: jax.random.permutation(subkey, ctx_count))(subkeys).astype(jnp.int32)
    offsets = jnp.arange(TOK_DEV, dtype=jnp.int32)[None, None, :]
    first_run = ranking[:, :, None] * half_len + offsets
    second_run = (2 * ctx_count - 1 - ranking[:, :, None]) * half_len + offsets - half_len
    result = jnp.where(offsets < half_len, first_run, second_run)
    return result.reshape(SEQS, SEQ).astype(jnp.int32)


def levels(rng, dims, shards, least, high):
    level, own = 1.0, jax.random.fold_in(rng, 6)
    for axis_at, parts in shards:
        heights = jnp.exp(jax.random.uniform(jax.random.fold_in(own, axis_at), (parts,), jnp.float32, least / len(shards), high / len(shards)))
        level = level * jnp.repeat(heights, dims[axis_at] // parts).reshape([-1 if axis == axis_at else 1 for axis in range(len(dims))])
    return level


def shared_out(own_key, own, number, rows, number_of, top, bound, lean):
    sequence = jax.random.permutation(own_key, number_of)
    heavy_load, usual = load_shares(number_of, rows * top, bound, lean, True), load_shares(number_of, rows * top, bound, lean, False)
    places = jnp.arange(number_of)

    def named(tallies, rotation):
        used = int((tallies > 0).sum())
        fixed = max(1, used // 4)
        moved = fixed + (places - fixed + rotation * (used - fixed)) % max(1, number_of - fixed)
        return jnp.zeros((number_of,), jnp.int32).at[sequence[jnp.where(places < fixed, places, moved)]].set(jnp.asarray(tallies, jnp.int32))

    tallies = jnp.where(number % 4 == 0, named(heavy_load, number // 4), named(usual, number - number // 4 - 1))
    mixed = jax.random.permutation(jax.random.fold_in(own, 3), number_of)
    giver, taker = mixed[0:number_of // 2 * 2:2], mixed[1:number_of // 2 * 2:2]
    room = jnp.minimum(tallies[giver] - 1, bound - tallies[taker]) // 2
    room = jnp.where((giver == sequence[0]) | (taker == sequence[0]) | (tallies[taker] == 0), 0, jnp.maximum(room, 0))
    moved = jax.random.randint(jax.random.fold_in(own, 4), (number_of // 2,), 0, 1 << 20) % (room + 1)
    tallies = tallies.at[giver].add(-moved).at[taker].add(moved)
    items = jnp.searchsorted(jnp.cumsum(tallies), jnp.arange(rows * top), side="right").astype(jnp.int32)
    listing = items.reshape(top, rows).T
    listing = listing[jax.random.permutation(jax.random.fold_in(own, 1), rows)]
    rotation = jax.random.randint(jax.random.fold_in(own, 2), (rows, 1), 0, top)
    return jnp.take_along_axis(listing, (jnp.arange(top)[None, :] + rotation) % top, axis=1)


def load_shares(count, total, limit, skew, full):
    weights = [(1 << 20) // math.isqrt(standing ** skew) + 1 for standing in range(1, count + 1)]
    largest = limit if full else min(limit, max(-(-total // count), total * weights[0] // sum(weights)))
    least = 1 if total - largest >= count - 1 else 0
    given, rest = [largest] + [least] * (count - 1), total - largest - least * (count - 1)
    while rest > 0:
        candidates = [i for i in range(1, count) if given[i] < largest] or [i for i in range(1, count) if given[i] < limit]
        mass, budget = sum([weights[i] for i in candidates]), rest
        for i in candidates:
            extra = min(limit - given[i], max(1, budget * weights[i] // mass), rest)
            given[i] = given[i] + extra
            rest = rest - extra
    return np.array(given)


def gaussian(key, extent, width, limit, cuts=(), kind=jnp.bfloat16):
    loudness = levels(key, extent, cuts, -0.22, 0.18) if cuts else 1.0
    values = jax.random.normal(key, extent, jnp.float32) * width * loudness
    return jnp.minimum(jnp.maximum(values, -limit), limit).astype(kind)


def setup_inputs(seed: int = 0) -> dict:
    splits = jax.random.split(jax.random.key(seed), 15)
    tokens = gaussian(splits[0], (SEQS, SEQ, D), 1.0, 6.0, ((0, 4), (1, 8)))
    positions = draw_positions(jax.random.fold_in(splits[14], 71), 0)
    expert_ids_keys = jax.random.split(jax.random.fold_in(splits[2], 1), SEQS * SEQ // TOK_DEV)
    expert_ids_turns = jax.random.permutation(jax.random.fold_in(splits[2], 3), SEQS * SEQ // TOK_DEV)
    expert_ids = jax.vmap(lambda own, number: shared_out(jax.random.fold_in(splits[2], 2), own, number, TOK_DEV, EXPERTS, TOP, CAP, 1))(expert_ids_keys, expert_ids_turns).reshape((SEQS, SEQ, TOP))
    attn_gain = jnp.clip(1.0 + 0.1 * jax.random.normal(splits[3], (D,), jnp.float32), 0.5, 1.5)
    query_key_value_weight = gaussian(splits[4], (D, (HQ + 2 * HK) * HD), D ** -0.5, 0.125, ((0, 4),))
    q_gain = jnp.clip(1.0 + 0.1 * jax.random.normal(splits[5], (HD,), jnp.float32), 0.5, 1.5)
    k_gain = jnp.clip(1.0 + 0.1 * jax.random.normal(splits[6], (HD,), jnp.float32), 0.5, 1.5)
    output_weight = gaussian(splits[7], (HQ * HD, D), (HQ * HD * 16 // SEQ) ** -0.5, 1.0, ((0, 4),))
    ffn_gain = jnp.clip(1.0 + 0.1 * jax.random.normal(splits[8], (D,), jnp.float32), 0.5, 1.5)
    router_weight = gaussian(splits[9], (D, EXPERTS), (4 * D) ** -0.5, 0.0625, ((0, 4),))
    w_gate = gaussian(splits[10], (EXPERTS, D, F), D ** -0.5, 0.125, ((0, 32),))
    w_up = gaussian(splits[11], (EXPERTS, D, F), D ** -0.5, 0.125, ((0, 32),))
    w_down = gaussian(splits[12], (EXPERTS, F, D), F ** -0.5, 0.21875, ((0, 32),))
    cotangent = gaussian(splits[13], (SEQS, SEQ, D), 1.0, 6.0, ((0, 4), (1, 8)))
    return {"tokens": tokens, "positions": positions, "expert_ids": expert_ids, "attn_gain": attn_gain, "query_key_value_weight": query_key_value_weight, "q_gain": q_gain, "k_gain": k_gain, "output_weight": output_weight, "ffn_gain": ffn_gain, "router_weight": router_weight, "w_gate": w_gate, "w_up": w_up, "w_down": w_down, "cotangent": cotangent}


eps_norm = 1e-06
rope_base = 1000000.0
masked_value = -1e+30
highest_precision = lax.Precision.HIGHEST

@jax.custom_vjp
def low(v):
    return lax.optimization_barrier(v.astype(jnp.bfloat16)).astype(jnp.float32)

@jax.custom_vjp
def reduced_backward(v):
    return v

def low_keep(v):
    return (low(v), None)

def low_pass(kept, grad):
    return (grad,)

def back_keep(v):
    return (v, None)

def back_low(kept, grad):
    return (low(grad),)
low.defvjp(low_keep, low_pass)
reduced_backward.defvjp(back_keep, back_low)

def rms_scale(values, gain):
    mean_sq = lax.optimization_barrier(jnp.mean(values * values, axis=-1, keepdims=True))
    return values * lax.rsqrt(mean_sq + eps_norm) * gain

def frequencies(head_dim):
    return 1.0 / rope_base ** (jnp.arange(0, head_dim, 2).astype(jnp.float32) / head_dim)

def rotate(values, angles):
    half_dim = values.shape[-1] // 2
    cosine = jnp.cos(angles)
    sine_val = jnp.sin(angles)
    first_half = values[..., :half_dim]
    second_half = values[..., half_dim:]
    return jnp.concatenate([first_half * cosine - second_half * sine_val, second_half * cosine + first_half * sine_val], axis=-1)

def head_prep(projected, gain_q, gain_k, angles, heads_q, heads_kv):
    head_dim = gain_q.shape[0]
    row_count = projected.shape[0]
    q_width = heads_q * head_dim
    kv_width = heads_kv * head_dim
    queries = projected[:, :q_width].reshape(row_count, heads_q, head_dim)
    key_heads = projected[:, q_width:q_width + kv_width].reshape(row_count, heads_kv, head_dim)
    value_heads = projected[:, q_width + kv_width:].reshape(row_count, heads_kv, head_dim)
    queries = rotate(rms_scale(queries, gain_q), angles)
    key_heads = rotate(rms_scale(key_heads, gain_k), angles)
    return (queries, key_heads, value_heads)

def attend_block(query_blk, place_blk, key_low, value_low, key_places):
    heads_kv = key_low.shape[1]
    head_dim = key_low.shape[2]
    block_rows = query_blk.shape[0]
    group_size = query_blk.shape[1] // heads_kv
    grouped = query_blk.reshape(block_rows, heads_kv, group_size, head_dim)
    scores = jnp.einsum('qhgd,khd->hgqk', grouped, key_low, precision=highest_precision) * (1.0 / math.sqrt(head_dim))
    scores = reduced_backward(scores)
    visible = key_places[None, :] <= place_blk[:, None]
    prob_vals = jax.nn.softmax(jnp.where(visible, scores, masked_value), axis=-1)
    mixed_out = jnp.einsum('hgqk,khd->qhgd', low(prob_vals), value_low, precision=highest_precision)
    return mixed_out.reshape(block_rows, -1)

def attend_sequence(query_low, key_low, value_low, places):
    seq_len = query_low.shape[0]
    block_rows = min(512, seq_len)
    block_count = seq_len // block_rows
    query_blocks = query_low.reshape(block_count, block_rows, query_low.shape[1], query_low.shape[2])
    place_blocks = places.reshape(block_count, block_rows)
    block_step = jax.checkpoint(lambda query_blk, place_blk: attend_block(query_blk, place_blk, key_low, value_low, places))
    mixed_out = lax.map(lambda blocks_in: block_step(blocks_in[0], blocks_in[1]), (query_blocks, place_blocks))
    return mixed_out.reshape(seq_len, -1)

def forward(params, positions, expert_ids, slot_rows, slot_live):
    tokens, attn_gain, query_key_value_weight, q_gain, k_gain, output_weight, ffn_gain, router_weight, w_gate, w_up, w_down = params
    seq_count, seq_len, model_width = tokens.shape
    head_dim = q_gain.shape[0]
    heads_q = output_weight.shape[0] // head_dim
    heads_kv = (query_key_value_weight.shape[1] - output_weight.shape[0]) // (2 * head_dim)
    top_count = expert_ids.shape[2]
    first_activations = low(rms_scale(tokens, attn_gain))
    query_key_value_projected = reduced_backward(jnp.einsum('act,th->ach', first_activations, query_key_value_weight, precision=highest_precision))
    angles = positions.astype(jnp.float32)[..., None, None] * frequencies(head_dim)
    queries, key_heads, value_heads = head_prep(query_key_value_projected.reshape(seq_count * seq_len, -1), q_gain, k_gain, angles.reshape(seq_count * seq_len, 1, -1), heads_q, heads_kv)
    shape_q = (seq_count, seq_len, heads_q, head_dim)
    shape_kv = (seq_count, seq_len, heads_kv, head_dim)
    stacked = (low(queries).reshape(shape_q), low(key_heads).reshape(shape_kv), low(value_heads).reshape(shape_kv), positions)
    mixed_out = lax.map(lambda item_set: attend_sequence(item_set[0], item_set[1], item_set[2], item_set[3]), stacked)
    heads_reduced_precision = reduced_backward(low(mixed_out))
    residual_stream = tokens + reduced_backward(jnp.einsum('xib,by->xiy', heads_reduced_precision, output_weight, precision=highest_precision))
    second_activations = low(rms_scale(residual_stream, ffn_gain))
    router_logits = reduced_backward(jnp.einsum('act,th->ach', second_activations, router_weight, precision=highest_precision))
    gate_vals = jax.nn.softmax(jnp.take_along_axis(router_logits, expert_ids, axis=-1), axis=-1)
    flat_acts = second_activations.reshape(seq_count * seq_len, model_width)
    flat_gates = gate_vals.reshape(-1)

    def expert_rows(item_set):
        rows_here, live_mask, gate_w, up_w, down_w = item_set
        arrived = reduced_backward(flat_acts[rows_here // top_count]) * live_mask[:, None]
        gate_pre = reduced_backward(jnp.dot(arrived, gate_w, precision=highest_precision))
        up_pre = reduced_backward(jnp.dot(arrived, up_w, precision=highest_precision))
        hidden = low(jax.nn.silu(gate_pre) * up_pre)
        return reduced_backward(low(jnp.dot(hidden, down_w, precision=highest_precision)))
    produced = lax.map(jax.checkpoint(expert_rows), (slot_rows, slot_live, w_gate, w_up, w_down))
    scaled = (flat_gates[slot_rows] * slot_live)[..., None] * produced
    moe_sum = jnp.zeros((seq_count * seq_len, model_width), jnp.float32).at[(slot_rows // top_count).reshape(-1)].add(scaled.reshape(-1, model_width))
    return residual_stream + moe_sum.reshape(seq_count, seq_len, model_width)

def reference(tokens, positions, expert_ids, attn_gain, query_key_value_weight, q_gain, k_gain, output_weight, ffn_gain, router_weight, w_gate, w_up, w_down, cotangent):
    flat_ids = expert_ids.reshape(-1)
    row_span = min(flat_ids.shape[0], N_CTX * N_FSDP * CAP)

    def slot_table(expert):
        ranking = jnp.argsort((flat_ids != expert).astype(jnp.int32), stable=True)[:row_span].astype(jnp.int32)
        return (ranking, (flat_ids[ranking] == expert).astype(jnp.float32))
    slot_rows, slot_live = jax.vmap(slot_table)(jnp.arange(w_gate.shape[0], dtype=jnp.int32))
    primals = (tokens.astype(jnp.float32), attn_gain, query_key_value_weight.astype(jnp.float32), q_gain, k_gain, output_weight.astype(jnp.float32), ffn_gain, router_weight.astype(jnp.float32), w_gate.astype(jnp.float32), w_up.astype(jnp.float32), w_down.astype(jnp.float32))

    def layer_fn(params):
        return forward(params, positions, expert_ids, slot_rows, slot_live)
    result, pullback = jax.vjp(layer_fn, primals)
    gradients = pullback(cotangent.astype(jnp.float32))[0]
    return (result.astype(jnp.bfloat16), gradients[0], gradients[1], gradients[2], gradients[3], gradients[4], gradients[5], gradients[6], gradients[7], gradients[8], gradients[9], gradients[10])
```

```python
import functools
import math

import jax
import jax.numpy as jnp
from jax import lax
from jax.experimental import pallas as pl
from jax.experimental.pallas import tpu as pltpu
from jax.sharding import PartitionSpec as P

eps_norm = 1e-06
rope_base = 1000000.0
masked_value = -1e30
run_rows = 128
bf16 = jnp.bfloat16
f32 = jnp.float32


def rms_scale(values, gain):
    mean_sq = jnp.mean(values * values, axis=-1, keepdims=True)
    return values * lax.rsqrt(mean_sq + eps_norm) * gain


def frequencies(head_dim):
    return 1.0 / rope_base ** (jnp.arange(0, head_dim, 2).astype(jnp.float32) / head_dim)


def rotate(values, angles):
    half_dim = values.shape[-1] // 2
    cosine = jnp.cos(angles)
    sine_val = jnp.sin(angles)
    first_half = values[..., :half_dim]
    second_half = values[..., half_dim:]
    return jnp.concatenate(
        [
            first_half * cosine - second_half * sine_val,
            second_half * cosine + first_half * sine_val,
        ],
        axis=-1,
    )


def head_prep(projected, gain_q, gain_k, angles, heads_q, heads_kv):
    head_dim = gain_q.shape[0]
    row_count = projected.shape[0]
    q_width = heads_q * head_dim
    kv_width = heads_kv * head_dim
    queries = projected[:, :q_width].reshape(row_count, heads_q, head_dim)
    key_heads = projected[:, q_width : q_width + kv_width].reshape(row_count, heads_kv, head_dim)
    value_heads = projected[:, q_width + kv_width :].reshape(row_count, heads_kv, head_dim)
    queries = rotate(rms_scale(queries, gain_q), angles)
    key_heads = rotate(rms_scale(key_heads, gain_k), angles)
    return (queries, key_heads, value_heads)


def general_body(
    tokens,
    positions,
    expert_ids,
    attn_gain,
    query_key_value_weight,
    q_gain,
    k_gain,
    output_weight,
    ffn_gain,
    router_weight,
    w_gate,
    w_up,
    w_down,
    cotangent,
):
    row_count = tokens.shape[1]
    model_width = tokens.shape[2]
    head_dim = q_gain.shape[0]
    inputs = tokens.reshape(row_count, model_width).astype(jnp.float32)
    places = positions.reshape(row_count)
    chosen = expert_ids.reshape(row_count, -1)
    top_count = chosen.shape[1]
    full_qkv, full_out, full_router = (
        lax.all_gather(query_key_value_weight, "fsdp", axis=0, tiled=True),
        lax.all_gather(output_weight, "fsdp", axis=0, tiled=True),
        lax.all_gather(router_weight, "fsdp", axis=0, tiled=True),
    )
    heads_q = full_out.shape[0] // head_dim
    heads_kv = (full_qkv.shape[1] - full_out.shape[0]) // (2 * head_dim)
    group_size = heads_q // heads_kv
    expert_count = full_router.shape[1]
    capacity = row_count * top_count * 3 // (2 * expert_count)
    local_experts = w_gate.shape[0]
    score_scale = 1.0 / math.sqrt(head_dim)
    normed, norm_back = jax.vjp(rms_scale, inputs, attn_gain)
    first_activations = normed.astype(jnp.bfloat16)
    query_key_value_projected = jnp.dot(
        first_activations, full_qkv, preferred_element_type=jnp.float32
    )
    angles = places.astype(jnp.float32)[:, None, None] * frequencies(head_dim)[None, None, :]

    def prepare(proj_in, gain_q, gain_k):
        return head_prep(proj_in, gain_q, gain_k, angles, heads_q, heads_kv)

    (queries, key_heads, value_heads), prep_back = jax.vjp(
        prepare, query_key_value_projected, q_gain, k_gain
    )
    query_low = queries.astype(jnp.bfloat16).reshape(row_count, heads_kv, group_size, head_dim)
    key_low = key_heads.astype(jnp.bfloat16)
    value_low = value_heads.astype(jnp.bfloat16)
    all_keys, all_values = (
        lax.all_gather(key_low, "ctx", axis=0, tiled=True),
        lax.all_gather(value_low, "ctx", axis=0, tiled=True),
    )
    key_places = lax.all_gather(places, "ctx", axis=0, tiled=True)
    seq_len = all_keys.shape[0]
    sorted_keys = jnp.zeros_like(all_keys).at[key_places].set(all_keys)
    sorted_values = jnp.zeros_like(all_values).at[key_places].set(all_values)
    block_len = min(512, seq_len)
    run_len = row_count // 2

    def block_scores(query_run, place_run, block_index):
        start = block_index * block_len
        key_blk = lax.dynamic_slice_in_dim(sorted_keys, start, block_len, 0)
        value_blk = lax.dynamic_slice_in_dim(sorted_values, start, block_len, 0)
        raw_scores = (
            jnp.einsum("qhgd,khd->hgqk", query_run, key_blk, preferred_element_type=jnp.float32)
            * score_scale
        )
        key_pos = start + jnp.arange(block_len, dtype=jnp.int32)
        visible = key_pos[None, :] <= place_run[:, None]
        return (jnp.where(visible, raw_scores, masked_value), visible, key_blk, value_blk)

    run_info = []
    mixed_runs = []
    for run_index in range(2):
        query_run = query_low[run_index * run_len : (run_index + 1) * run_len]
        place_run = places[run_index * run_len : (run_index + 1) * run_len]
        block_total = jnp.max(place_run) // block_len + 1

        def stats_step(block_index, carried):
            run_max, run_sum = carried
            scores, visible, key_blk, value_blk = block_scores(query_run, place_run, block_index)
            new_max = jnp.maximum(run_max, jnp.max(scores, axis=-1))
            weights = jnp.where(visible, jnp.exp(scores - new_max[..., None]), 0.0)
            run_sum = run_sum * jnp.exp(run_max - new_max) + jnp.sum(weights, axis=-1)
            return (new_max, run_sum)

        stat_shape = (heads_kv, group_size, run_len)
        initial = (
            jnp.full(stat_shape, masked_value, jnp.float32),
            jnp.zeros(stat_shape, jnp.float32),
        )
        run_max, run_sum = lax.fori_loop(0, block_total, stats_step, initial)
        log_total = run_max + jnp.log(run_sum)

        def output_step(block_index, running):
            scores, visible, key_blk, value_blk = block_scores(query_run, place_run, block_index)
            prob_vals = jnp.exp(scores - log_total[..., None])
            return running + jnp.einsum(
                "hgqk,khd->qhgd",
                prob_vals.astype(jnp.bfloat16),
                value_blk,
                preferred_element_type=jnp.float32,
            )

        mixed_run = lax.fori_loop(
            0,
            block_total,
            output_step,
            jnp.zeros((run_len, heads_kv, group_size, head_dim), jnp.float32),
        )
        mixed_runs.append(mixed_run)
        run_info.append((query_run, place_run, block_total, log_total))
    heads_out = jnp.concatenate(mixed_runs, axis=0)
    heads_reduced_precision = heads_out.reshape(row_count, heads_q * head_dim).astype(jnp.bfloat16)
    residual_stream = inputs + jnp.dot(
        heads_reduced_precision, full_out, preferred_element_type=jnp.float32
    )
    normed_two, norm_two_back = jax.vjp(rms_scale, residual_stream, ffn_gain)
    second_activations = normed_two.astype(jnp.bfloat16)
    router_logits = jnp.dot(second_activations, full_router, preferred_element_type=jnp.float32)
    pick_table = (chosen[:, :, None] == jnp.arange(expert_count)[None, None, :]).astype(jnp.float32)
    picked = jnp.sum(router_logits[:, None, :] * pick_table, axis=-1)
    gate_vals, gate_back = jax.vjp(lambda values: jax.nn.softmax(values, axis=-1), picked)
    flat_choice = chosen.reshape(-1)
    slot_hot = (flat_choice[:, None] == jnp.arange(expert_count)[None, :]).astype(jnp.int32)
    slot_rank = jnp.sum((jnp.cumsum(slot_hot, axis=0) - slot_hot) * slot_hot, axis=1)
    targets = flat_choice * capacity + slot_rank
    source_rows = jnp.repeat(second_activations, top_count, axis=0)
    outgoing = (
        jnp.zeros((expert_count * capacity, model_width), jnp.bfloat16).at[targets].set(source_rows)
    )
    outgoing = outgoing.reshape(expert_count, capacity, model_width)
    arrived = lax.all_to_all(outgoing, ("ctx", "fsdp"), split_axis=0, concat_axis=0, tiled=True)
    sources = arrived.shape[0] // local_experts
    slot_count = arrived.shape[1]
    grouped = arrived.reshape(sources, local_experts, slot_count, model_width)
    gate_pre = jnp.einsum("secd,edf->secf", grouped, w_gate, preferred_element_type=jnp.float32)
    up_pre = jnp.einsum("secd,edf->secf", grouped, w_up, preferred_element_type=jnp.float32)
    hidden = (jax.nn.silu(gate_pre) * up_pre).astype(jnp.bfloat16)
    produced = jnp.einsum("secf,efd->secd", hidden, w_down, preferred_element_type=jnp.float32)
    produced = produced.astype(jnp.bfloat16).reshape(arrived.shape)
    flat_shape = (arrived.shape[0], slot_count, gate_pre.shape[3])
    expert_results = (produced, arrived, gate_pre.reshape(flat_shape), up_pre.reshape(flat_shape))
    produced = expert_results[0]
    arrived = expert_results[1]
    returned = lax.all_to_all(produced, ("ctx", "fsdp"), split_axis=0, concat_axis=0, tiled=True)
    expert_rows = returned.reshape(expert_count * capacity, model_width)[targets].reshape(
        row_count, top_count, model_width
    )
    expert_vals = expert_rows.astype(jnp.float32)
    result = residual_stream + jnp.sum(gate_vals[:, :, None] * expert_vals, axis=1)
    output = result.astype(jnp.bfloat16).reshape(tokens.shape)
    grad_res = cotangent.reshape(row_count, model_width).astype(jnp.float32)
    gate_grad = jnp.sum(grad_res[:, None, :] * expert_vals, axis=-1)
    out_grad = (gate_vals[:, :, None] * grad_res[:, None, :]).astype(jnp.bfloat16)
    back_out = (
        jnp.zeros((expert_count * capacity, model_width), jnp.bfloat16)
        .at[targets]
        .set(out_grad.reshape(-1, model_width))
    )
    back_out = back_out.reshape(expert_count, capacity, model_width)
    (picked_grad,) = gate_back(gate_grad)
    logit_grad = jnp.sum(picked_grad[:, :, None] * pick_table, axis=1).astype(jnp.bfloat16)
    full_qkv, full_out, full_router = (
        lax.all_gather(query_key_value_weight, "fsdp", axis=0, tiled=True),
        lax.all_gather(output_weight, "fsdp", axis=0, tiled=True),
        lax.all_gather(router_weight, "fsdp", axis=0, tiled=True),
    )
    arrived_grad = lax.all_to_all(
        back_out, ("ctx", "fsdp"), split_axis=0, concat_axis=0, tiled=True
    )
    sources = arrived.shape[0] // local_experts
    grouped = arrived.reshape(sources, local_experts, capacity, model_width)
    grad_grouped = arrived_grad.reshape(sources, local_experts, capacity, model_width)
    gate_pre = expert_results[2].reshape(sources, local_experts, capacity, -1)
    up_pre = expert_results[3].reshape(sources, local_experts, capacity, -1)
    hidden, hidden_back = jax.vjp(
        lambda gate_in, up_in: jax.nn.silu(gate_in) * up_in, gate_pre, up_pre
    )
    hidden_low = hidden.astype(jnp.bfloat16)
    hidden_grad = jnp.einsum(
        "secd,efd->secf", grad_grouped, w_down, preferred_element_type=jnp.float32
    )
    gate_pre_grad, up_pre_grad = hidden_back(hidden_grad)
    gate_low = gate_pre_grad.astype(jnp.bfloat16)
    up_low = up_pre_grad.astype(jnp.bfloat16)
    grad_w_down = jnp.einsum(
        "secf,secd->efd", hidden_low, grad_grouped, preferred_element_type=jnp.float32
    )
    grad_w_gate = jnp.einsum(
        "secd,secf->edf", grouped, gate_low, preferred_element_type=jnp.float32
    )
    grad_w_up = jnp.einsum("secd,secf->edf", grouped, up_low, preferred_element_type=jnp.float32)
    row_grad = jnp.einsum(
        "secf,edf->secd", gate_low, w_gate, preferred_element_type=jnp.float32
    ) + jnp.einsum("secf,edf->secd", up_low, w_up, preferred_element_type=jnp.float32)
    row_grad = row_grad.astype(jnp.bfloat16).reshape(arrived.shape)
    row_back = lax.all_to_all(row_grad, ("ctx", "fsdp"), split_axis=0, concat_axis=0, tiled=True)
    token_rows = row_back.reshape(expert_count * capacity, model_width)[targets].reshape(
        row_count, top_count, model_width
    )
    acts_two_grad = jnp.sum(token_rows.astype(jnp.float32), axis=1) + jnp.dot(
        logit_grad, full_router.T, preferred_element_type=jnp.float32
    )
    grad_w_router = jnp.dot(second_activations.T, logit_grad, preferred_element_type=jnp.float32)
    resid_extra, grad_ffn_gain = norm_two_back(acts_two_grad)
    resid_grad = grad_res + resid_extra
    attn_grad = resid_grad.astype(jnp.bfloat16)
    grad_w_out = jnp.dot(heads_reduced_precision.T, attn_grad, preferred_element_type=jnp.float32)
    heads_grad = jnp.dot(attn_grad, full_out.T, preferred_element_type=jnp.float32).astype(
        jnp.bfloat16
    )
    heads_grad = heads_grad.reshape(row_count, heads_kv, group_size, head_dim)
    row_delta = jnp.moveaxis(jnp.sum(heads_grad.astype(jnp.float32) * heads_out, axis=-1), 0, 2)
    key_grad_sorted = jnp.zeros((seq_len, heads_kv, head_dim), jnp.float32)
    value_grad_sorted = jnp.zeros((seq_len, heads_kv, head_dim), jnp.float32)
    query_grad_runs = []
    for run_index in range(2):
        query_run, place_run, block_total, log_total = run_info[run_index]
        grad_run = heads_grad[run_index * run_len : (run_index + 1) * run_len]
        delta_run = row_delta[:, :, run_index * run_len : (run_index + 1) * run_len]

        def back_step(block_index, carried):
            query_grad, key_acc, value_acc = carried
            scores, visible, key_blk, value_blk = block_scores(query_run, place_run, block_index)
            prob_vals = jnp.exp(scores - log_total[..., None])
            value_grad = jnp.einsum(
                "hgqk,qhgd->khd",
                prob_vals.astype(jnp.bfloat16),
                grad_run,
                preferred_element_type=jnp.float32,
            )
            prob_grad = jnp.einsum(
                "qhgd,khd->hgqk", grad_run, value_blk, preferred_element_type=jnp.float32
            )
            score_grad = (prob_vals * (prob_grad - delta_run[..., None])).astype(jnp.bfloat16)
            query_grad = (
                query_grad
                + jnp.einsum(
                    "hgqk,khd->qhgd", score_grad, key_blk, preferred_element_type=jnp.float32
                )
                * score_scale
            )
            key_grad = (
                jnp.einsum(
                    "hgqk,qhgd->khd", score_grad, query_run, preferred_element_type=jnp.float32
                )
                * score_scale
            )
            start = block_index * block_len
            key_acc = lax.dynamic_update_slice_in_dim(
                key_acc, lax.dynamic_slice_in_dim(key_acc, start, block_len, 0) + key_grad, start, 0
            )
            value_acc = lax.dynamic_update_slice_in_dim(
                value_acc,
                lax.dynamic_slice_in_dim(value_acc, start, block_len, 0) + value_grad,
                start,
                0,
            )
            return (query_grad, key_acc, value_acc)

        start_state = (
            jnp.zeros((run_len, heads_kv, group_size, head_dim), jnp.float32),
            key_grad_sorted,
            value_grad_sorted,
        )
        query_grad_run, key_grad_sorted, value_grad_sorted = lax.fori_loop(
            0, block_total, back_step, start_state
        )
        query_grad_runs.append(query_grad_run)
    query_grad = jnp.concatenate(query_grad_runs, axis=0)
    key_grads = key_grad_sorted[key_places]
    value_grads = value_grad_sorted[key_places]
    key_grad_own, value_grad_own = (
        lax.psum_scatter(
            key_grads.astype(jnp.bfloat16), "ctx", scatter_dimension=0, tiled=True
        ).astype(jnp.float32),
        lax.psum_scatter(
            value_grads.astype(jnp.bfloat16), "ctx", scatter_dimension=0, tiled=True
        ).astype(jnp.float32),
    )
    proj_grad, grad_q_gain, grad_k_gain = prep_back(
        (query_grad.reshape(row_count, heads_q, head_dim), key_grad_own, value_grad_own)
    )
    proj_low = proj_grad.astype(jnp.bfloat16)
    grad_w_qkv = jnp.dot(first_activations.T, proj_low, preferred_element_type=jnp.float32)
    acts_grad = jnp.dot(proj_low, full_qkv.T, preferred_element_type=jnp.float32)
    inputs_extra, grad_attn_gain = norm_back(acts_grad)
    grad_tokens = (resid_grad + inputs_extra).reshape(tokens.shape)
    grad_w_qkv, grad_w_out, grad_w_router = (
        lax.psum_scatter(grad_w_qkv, ("ctx", "fsdp"), scatter_dimension=0, tiled=True),
        lax.psum_scatter(grad_w_out, ("ctx", "fsdp"), scatter_dimension=0, tiled=True),
        lax.psum_scatter(grad_w_router, ("ctx", "fsdp"), scatter_dimension=0, tiled=True),
    )
    grad_attn_gain, grad_q_gain, grad_k_gain, grad_ffn_gain = lax.psum(
        (grad_attn_gain, grad_q_gain, grad_k_gain, grad_ffn_gain), ("ctx", "fsdp")
    )
    return (
        output,
        grad_tokens,
        grad_attn_gain,
        grad_w_qkv,
        grad_q_gain,
        grad_k_gain,
        grad_w_out,
        grad_ffn_gain,
        grad_w_router,
        grad_w_gate,
        grad_w_up,
        grad_w_down,
    )


def swap(values, axis, count, bit):
    return lax.ppermute(values, axis, [(i, i ^ bit) for i in range(count)])


def plane_gather(values):
    half = values.shape[0] // 2
    near_x = swap(values, "fsdp", 4, 1)
    near_y = swap(values, "fsdp", 4, 2)
    far_low = swap(near_x[:half], "fsdp", 4, 2)
    far_high = swap(near_y[half:], "fsdp", 4, 1)
    return jnp.concatenate([values, near_x, near_y, far_low, far_high], axis=0)


def plane_scatter(parts):
    half = parts.shape[1] // 2
    from_x = swap(parts[3, :half], "fsdp", 4, 1)
    from_y = swap(parts[3, half:], "fsdp", 4, 2)
    for_y = jnp.concatenate(
        [(parts[2, :half].astype(f32) + from_x.astype(f32)).astype(bf16), parts[2, half:]], axis=0
    )
    for_x = jnp.concatenate(
        [parts[1, :half], (parts[1, half:].astype(f32) + from_y.astype(f32)).astype(bf16)], axis=0
    )
    got_x = swap(for_x, "fsdp", 4, 1)
    got_y = swap(for_y, "fsdp", 4, 2)
    return parts[0].astype(f32) + got_x.astype(f32) + got_y.astype(f32)


def pick(values, index):
    return lax.dynamic_index_in_dim(values, index, 0, keepdims=False)


def exchange_small(table, n_ctx):
    count, width = table.shape
    bit = 1
    while bit < count:
        split = table.reshape(count // (2 * bit), 2, bit, width)
        moved = split[:, 1]
        if bit < 4:
            moved = swap(moved, "fsdp", 4, bit)
        else:
            moved = swap(moved, "ctx", n_ctx, bit // 4)
        table = jnp.stack([split[:, 0], moved], axis=1).reshape(count, width)
        bit *= 2
    return table


def sum_everywhere(values, n_ctx):
    bit = 1
    while bit < 4:
        values = values + swap(values, "fsdp", 4, bit)
        bit *= 2
    bit = 1
    while bit < n_ctx:
        values = values + swap(values, "ctx", n_ctx, bit)
        bit *= 2
    return values


def ctx_scatter(parts, n_ctx, ctx_at, low):
    bit = 1
    held = parts
    while bit < n_ctx:
        mine = (ctx_at // bit) % 2
        split = held.reshape((held.shape[0] // 2, 2) + held.shape[1:])
        keep = lax.dynamic_index_in_dim(split, mine, 1, keepdims=False)
        away = lax.dynamic_index_in_dim(split, 1 - mine, 1, keepdims=False)
        got = swap(away, "ctx", n_ctx, bit)
        held = keep.astype(f32) + got.astype(f32)
        bit *= 2
        if low and bit < n_ctx:
            held = held.astype(bf16)
    return held.reshape(parts.shape[1:])


def attend_kernel(place_ref, source_ref, q_ref, kv_ref, o_ref, lse_ref, keys, vals_t, q_t, acc, total):
    seq = pl.program_id(0)
    rows = run_rows
    heads = q_ref.shape[2] // rows
    blocks = keys.shape[0] // rows
    scale = math.log2(math.e) / math.sqrt(rows)
    for p in range(blocks):
        at = source_ref[seq * blocks + p]
        block = kv_ref[at // 2, 0, pl.ds(pl.multiple_of((at % 2) * rows, rows), rows), :]
        keys[p * rows : (p + 1) * rows, :] = block[:, :rows]
        vals_t[:, p * rows : (p + 1) * rows] = block[:, rows:].T
    key_iota = lax.broadcasted_iota(jnp.int32, (2 * rows, 2 * rows), 0)
    query_iota = lax.broadcasted_iota(jnp.int32, (2 * rows, 2 * rows), 1) % rows
    for run in range(2):
        place = place_ref[seq * 2 + run]
        for h in range(heads):
            q_t[:, h * rows : (h + 1) * rows] = q_ref[
                0, run * rows : (run + 1) * rows, h * rows : (h + 1) * rows
            ].T
        acc[...] = jnp.zeros_like(acc)
        total[...] = jnp.zeros_like(total)

        def step(j, masked):
            start = pl.multiple_of(j * 2 * rows, 2 * rows)
            key_blk = keys[pl.ds(start, 2 * rows), :]
            val_blk = vals_t[:, pl.ds(start, 2 * rows)]
            for pair in range(heads // 2):
                cols = slice(pair * 2 * rows, (pair + 1) * 2 * rows)
                scores = jnp.dot(key_blk, q_t[:, cols], preferred_element_type=f32)
                weights = jnp.exp2(scores * scale)
                if masked:
                    seen = start + key_iota <= place * rows + query_iota
                    weights = jnp.where(seen, weights, 0.0)
                total[:, cols] += jnp.sum(weights.reshape(2 * rows // 8, 8, 2 * rows), axis=0)
                acc[:, cols] += jnp.dot(val_blk, weights.astype(bf16), preferred_element_type=f32)

        lax.fori_loop(0, place // 2, lambda j, c: (step(j, False), c)[1], 0)
        step(place // 2, True)
        norm = jnp.sum(total[...], axis=0, keepdims=True)
        lse_ref[0, run : run + 1, :] = jnp.log2(norm)
        mixed = acc[...] / norm
        for h in range(heads):
            o_ref[0, run * rows : (run + 1) * rows, h * rows : (h + 1) * rows] = (
                mixed[:, h * rows : (h + 1) * rows].T.astype(bf16)
            )


def attend_back_kernel(
    place_ref,
    source_ref,
    q_ref,
    kv_ref,
    o_ref,
    do_ref,
    lse_ref,
    dq_ref,
    dkv_ref,
    keys,
    keys_t,
    vals,
    q_n,
    q_t,
    do_n,
    do_t,
    delta,
    dq_acc,
    dk_acc,
    dv_acc,
):
    seq = pl.program_id(0)
    rows = run_rows
    heads = q_ref.shape[2] // rows
    blocks = keys.shape[0] // rows
    scale = math.log2(math.e) / math.sqrt(rows)
    plain_scale = 1.0 / math.sqrt(rows)
    for p in range(blocks):
        at = source_ref[seq * blocks + p]
        block = kv_ref[at // 2, 0, pl.ds(pl.multiple_of((at % 2) * rows, rows), rows), :]
        keys[p * rows : (p + 1) * rows, :] = block[:, :rows]
        keys_t[:, p * rows : (p + 1) * rows] = block[:, :rows].T
        vals[p * rows : (p + 1) * rows, :] = block[:, rows:]
    dk_acc[...] = jnp.zeros_like(dk_acc)
    dv_acc[...] = jnp.zeros_like(dv_acc)
    key_iota = lax.broadcasted_iota(jnp.int32, (2 * rows, 2 * rows), 0)
    query_iota = lax.broadcasted_iota(jnp.int32, (2 * rows, 2 * rows), 1) % rows
    for run in range(2):
        place = place_ref[seq * 2 + run]
        here = slice(run * rows, (run + 1) * rows)
        for h in range(heads):
            cols = slice(h * rows, (h + 1) * rows)
            q_h = q_ref[0, here, cols]
            q_n[cols, :] = q_h
            q_t[:, cols] = q_h.T
            do_h = do_ref[0, here, cols]
            do_n[cols, :] = do_h
            do_ht = do_h.T
            do_t[:, cols] = do_ht
            o_ht = o_ref[0, here, cols].T
            delta[:, cols] = jnp.sum(do_ht.astype(f32) * o_ht.astype(f32), axis=0, keepdims=True)
        dq_acc[...] = jnp.zeros_like(dq_acc)

        def step(j, masked):
            start = pl.multiple_of(j * 2 * rows, 2 * rows)
            key_blk = keys[pl.ds(start, 2 * rows), :]
            key_t_blk = keys_t[:, pl.ds(start, 2 * rows)]
            val_blk = vals[pl.ds(start, 2 * rows), :]
            dk_sum = jnp.zeros((2 * rows, rows), f32)
            dv_sum = jnp.zeros((2 * rows, rows), f32)
            for pair in range(heads // 2):
                cols = slice(pair * 2 * rows, (pair + 1) * 2 * rows)
                scores = jnp.dot(key_blk, q_t[:, cols], preferred_element_type=f32)
                probs = jnp.exp2(scores * scale - lse_ref[0, run : run + 1, cols])
                if masked:
                    seen = start + key_iota <= place * rows + query_iota
                    probs = jnp.where(seen, probs, 0.0)
                prob_grad = jnp.dot(val_blk, do_t[:, cols], preferred_element_type=f32)
                score_grad = (probs * (prob_grad - delta[:, cols])).astype(bf16)
                dv_sum += jnp.dot(probs.astype(bf16), do_n[cols, :], preferred_element_type=f32)
                dk_sum += jnp.dot(score_grad, q_n[cols, :], preferred_element_type=f32)
                dq_acc[:, cols] += jnp.dot(key_t_blk, score_grad, preferred_element_type=f32)
            dk_acc[pl.ds(start, 2 * rows), :] += dk_sum
            dv_acc[pl.ds(start, 2 * rows), :] += dv_sum

        lax.fori_loop(0, place // 2, lambda j, c: (step(j, False), c)[1], 0)
        step(place // 2, True)
        for h in range(heads):
            cols = slice(h * rows, (h + 1) * rows)
            dq_ref[0, here, cols] = dq_acc[:, cols].T * plain_scale
    for p in range(blocks):
        at = source_ref[seq * blocks + p]
        span = slice(p * rows, (p + 1) * rows)
        there = pl.ds(pl.multiple_of((at % 2) * rows, rows), rows)
        dkv_ref[at // 2, 0, there, :rows] = (dk_acc[span, :] * plain_scale).astype(bf16)
        dkv_ref[at // 2, 0, there, rows:] = dv_acc[span, :].astype(bf16)


def attend(places, sources, queries, kv):
    seqs, rows, width = queries.shape
    slots, _, _, pair_width = kv.shape
    head_dim = pair_width // 2
    seq_len = slots * rows
    return pl.pallas_call(
        attend_kernel,
        out_shape=(
            jax.ShapeDtypeStruct(queries.shape, bf16),
            jax.ShapeDtypeStruct((seqs, 2, width), f32),
        ),
        grid_spec=pltpu.PrefetchScalarGridSpec(
            num_scalar_prefetch=2,
            grid=(seqs,),
            in_specs=[
                pl.BlockSpec((1, rows, width), lambda s, *_: (s, 0, 0)),
                pl.BlockSpec((slots, 1, rows, pair_width), lambda s, *_: (0, s, 0, 0)),
            ],
            out_specs=[
                pl.BlockSpec((1, rows, width), lambda s, *_: (s, 0, 0)),
                pl.BlockSpec((1, 2, width), lambda s, *_: (s, 0, 0)),
            ],
            scratch_shapes=[
                pltpu.VMEM((seq_len, head_dim), bf16),
                pltpu.VMEM((head_dim, seq_len), bf16),
                pltpu.VMEM((head_dim, width), bf16),
                pltpu.VMEM((head_dim, width), f32),
                pltpu.VMEM((8, width), f32),
            ],
        ),
        compiler_params=pltpu.CompilerParams(vmem_limit_bytes=32 * 2**20),
        cost_estimate=pl.CostEstimate(
            flops=seqs * rows * width * seq_len * 2,
            bytes_accessed=2 * (2 * queries.size + kv.size),
            transcendentals=seqs * rows * width * slots,
        ),
        name="attend",
    )(places, sources, queries, kv)


def attend_back(places, sources, queries, kv, mixed, mixed_grad, lse):
    seqs, rows, width = queries.shape
    slots, _, _, pair_width = kv.shape
    head_dim = pair_width // 2
    seq_len = slots * rows
    block = pl.BlockSpec((1, rows, width), lambda s, *_: (s, 0, 0))
    kv_block = pl.BlockSpec((slots, 1, rows, pair_width), lambda s, *_: (0, s, 0, 0))
    return pl.pallas_call(
        attend_back_kernel,
        out_shape=(
            jax.ShapeDtypeStruct(queries.shape, f32),
            jax.ShapeDtypeStruct(kv.shape, bf16),
        ),
        grid_spec=pltpu.PrefetchScalarGridSpec(
            num_scalar_prefetch=2,
            grid=(seqs,),
            in_specs=[
                block,
                kv_block,
                block,
                block,
                pl.BlockSpec((1, 2, width), lambda s, *_: (s, 0, 0)),
            ],
            out_specs=[block, kv_block],
            scratch_shapes=[
                pltpu.VMEM((seq_len, head_dim), bf16),
                pltpu.VMEM((head_dim, seq_len), bf16),
                pltpu.VMEM((seq_len, head_dim), bf16),
                pltpu.VMEM((width, head_dim), bf16),
                pltpu.VMEM((head_dim, width), bf16),
                pltpu.VMEM((width, head_dim), bf16),
                pltpu.VMEM((head_dim, width), bf16),
                pltpu.VMEM((1, width), f32),
                pltpu.VMEM((head_dim, width), f32),
                pltpu.VMEM((seq_len, head_dim), f32),
                pltpu.VMEM((seq_len, head_dim), f32),
            ],
        ),
        compiler_params=pltpu.CompilerParams(vmem_limit_bytes=40 * 2**20),
        cost_estimate=pl.CostEstimate(
            flops=seqs * rows * width * seq_len * 5,
            bytes_accessed=2 * (5 * queries.size + 2 * kv.size),
            transcendentals=seqs * rows * width * slots,
        ),
        name="attend_back",
    )(places, sources, queries, kv, mixed, mixed_grad, lse)


def fast_body(
    n_ctx,
    tokens,
    positions,
    expert_ids,
    attn_gain,
    query_key_value_weight,
    q_gain,
    k_gain,
    output_weight,
    ffn_gain,
    router_weight,
    w_gate,
    w_up,
    w_down,
    cotangent,
):
    n_fsdp = 4
    n_all = n_ctx * n_fsdp
    ctx_at = lax.axis_index("ctx")
    fsdp_at = lax.axis_index("fsdp")
    core_at = ctx_at % 2
    own_at = ctx_at * n_fsdp + fsdp_at
    row_count = tokens.shape[1]
    model_width = tokens.shape[2]
    head_dim = q_gain.shape[0]
    shard_rows = query_key_value_weight.shape[0]
    heads = output_weight.shape[0] // head_dim
    q_width = heads * head_dim
    all_q = q_width * n_fsdp
    kv_heads = (query_key_value_weight.shape[1] - all_q) // (2 * head_dim)
    own_width = q_width + 2 * head_dim
    expert_count = n_all
    top_count = expert_ids.shape[2]
    capacity = row_count * top_count * 3 // (2 * expert_count)
    z_count = n_ctx // 2
    chunk_rows = 2 * n_fsdp * capacity

    inputs = tokens.reshape(row_count, model_width).astype(f32)
    places = positions.reshape(row_count)
    chosen = expert_ids.reshape(row_count, top_count)
    grad_res_low = cotangent.reshape(row_count, model_width)
    grad_res = grad_res_low.astype(f32)

    relative = jnp.bitwise_xor(own_at, jnp.arange(n_all, dtype=jnp.int32))
    chosen_rel = (chosen[:, :, None] == relative[None, None, :]).astype(f32)
    named = jnp.sum(chosen_rel, axis=1).T
    first_block = jnp.broadcast_to((places[0] // run_rows).astype(f32), (n_all, 128))
    small = exchange_small(jnp.concatenate([named, first_block], axis=1), n_ctx)
    named_here = small[:, :row_count]
    block_table = small[:, row_count].astype(jnp.int32).reshape(n_ctx, n_fsdp)

    rms_one = lax.rsqrt(jnp.mean(inputs * inputs, axis=-1, keepdims=True) + eps_norm)
    acts = (inputs * rms_one * attn_gain).astype(bf16)
    acts_group = plane_gather(acts)

    def columns_of(weight_rows, group):
        return jnp.concatenate(
            [
                lax.dynamic_slice_in_dim(weight_rows, group * q_width, q_width, 1),
                lax.dynamic_slice_in_dim(weight_rows, all_q + group * head_dim, head_dim, 1),
                lax.dynamic_slice_in_dim(
                    weight_rows, all_q + (kv_heads + group) * head_dim, head_dim, 1
                ),
            ],
            axis=1,
        )

    half_shard = shard_rows // 2
    half_weight = lax.dynamic_slice_in_dim(
        query_key_value_weight, core_at * half_shard, half_shard, 0
    )
    got_weight = [
        swap(columns_of(half_weight, fsdp_at ^ k), "fsdp", n_fsdp, k) for k in range(1, n_fsdp)
    ]
    sibling_weight = [swap(piece, "ctx", n_ctx, 1) for piece in got_weight]
    weight_qkv = jnp.zeros((n_fsdp * shard_rows, own_width), bf16)
    weight_qkv = lax.dynamic_update_slice_in_dim(
        weight_qkv, columns_of(query_key_value_weight, fsdp_at), fsdp_at * shard_rows, 0
    )
    for k in range(1, n_fsdp):
        base = (fsdp_at ^ k) * shard_rows
        weight_qkv = lax.dynamic_update_slice_in_dim(
            weight_qkv, got_weight[k - 1], base + core_at * half_shard, 0
        )
        weight_qkv = lax.dynamic_update_slice_in_dim(
            weight_qkv, sibling_weight[k - 1], base + (1 - core_at) * half_shard, 0
        )
    router_got = [router_weight] + [
        swap(router_weight, "fsdp", n_fsdp, k) for k in range(1, n_fsdp)
    ]
    full_router = jnp.zeros((n_fsdp * shard_rows, expert_count), bf16)
    for k in range(n_fsdp):
        full_router = lax.dynamic_update_slice_in_dim(
            full_router, router_got[k], (fsdp_at ^ k) * shard_rows, 0
        )

    projected = jnp.dot(acts_group, weight_qkv, preferred_element_type=f32)
    group_rows = n_fsdp * row_count

    blocks_total = 2 * n_ctx
    own_blocks = block_table[0]
    run_blocks = jnp.stack([own_blocks, blocks_total - 1 - own_blocks], axis=1)
    row_places = (
        run_blocks[:, :, None] * run_rows + jnp.arange(run_rows, dtype=jnp.int32)[None, None, :]
    ).reshape(group_rows)
    angles = row_places.astype(f32)[:, None, None] * frequencies(head_dim)[None, None, :]
    block_index = jnp.arange(blocks_total, dtype=jnp.int32)
    slot_index = jnp.arange(n_ctx, dtype=jnp.int32)[:, None, None]
    source_table = jnp.sum(
        jnp.where(block_table[:, :, None] == block_index, 2 * slot_index, 0)
        + jnp.where(blocks_total - 1 - block_table[:, :, None] == block_index, 2 * slot_index + 1, 0),
        axis=0,
    )
    place_list = run_blocks.reshape(-1)
    source_list = source_table.reshape(-1)

    def prepare(proj_in, gain_q, gain_k):
        return head_prep(proj_in, gain_q, gain_k, angles, heads, 1)

    (queries, key_heads, value_heads), prep_back = jax.vjp(prepare, projected, q_gain, k_gain)
    query_low = queries.astype(bf16).reshape(n_fsdp, row_count, q_width)
    kv_own = jnp.concatenate([key_heads, value_heads], axis=-1).astype(bf16)
    kv_own = kv_own.reshape(n_fsdp, row_count, 2 * head_dim)
    kv_slots = [kv_own] + [swap(kv_own, "ctx", n_ctx, 2 * k) for k in range(1, z_count)]
    kv_slots = jnp.stack(kv_slots)
    kv_all = jnp.stack([kv_slots, swap(kv_slots, "ctx", n_ctx, 1)], axis=1)
    kv_all = kv_all.reshape(n_ctx, n_fsdp, row_count, 2 * head_dim)

    mixed, lse = attend(place_list, source_list, query_low, kv_all)
    heads_low = mixed.reshape(group_rows, q_width)

    resid_parts = jnp.dot(heads_low, output_weight, preferred_element_type=f32).astype(bf16)
    resid = inputs + plane_scatter(resid_parts.reshape(n_fsdp, row_count, model_width))
    rms_two = lax.rsqrt(jnp.mean(resid * resid, axis=-1, keepdims=True) + eps_norm)
    acts_two = (resid * rms_two * ffn_gain).astype(bf16)

    logits = jnp.dot(acts_two, full_router, preferred_element_type=f32)
    pick_table = (chosen[:, :, None] == jnp.arange(expert_count)[None, None, :]).astype(f32)
    picked = jnp.sum(logits[:, None, :] * pick_table, axis=-1)
    gate_vals, gate_back = jax.vjp(lambda values: jax.nn.softmax(values, axis=-1), picked)
    gates_rel = jnp.sum(chosen_rel * gate_vals[:, :, None], axis=1).T
    gates_here = exchange_small(gates_rel, n_ctx)

    upper = jnp.triu(jnp.ones((row_count, row_count), bf16), 1)
    rank = jnp.dot(named_here.astype(bf16), upper, preferred_element_type=f32)
    slot_of = jnp.where(named_here > 0.5, rank, -1.0)
    hot = slot_of[:, None, :] == jnp.arange(capacity, dtype=jnp.int32).astype(f32)[None, :, None]
    dispatch = hot.astype(bf16).reshape(z_count, 2 * n_fsdp, capacity, row_count)
    gate_rows = jnp.sum(jnp.where(hot, gates_here[:, None, :], 0.0), axis=-1)
    gate_rows = gate_rows.reshape(z_count, chunk_rows, 1)

    def gather_chunk(slot):
        plane = plane_gather(slot)
        return jnp.stack([plane, swap(plane, "ctx", n_ctx, 1)]).reshape(
            2 * n_fsdp, row_count, model_width
        )

    def dispatch_rows(k, chunk):
        return jnp.einsum("sit,std->sid", dispatch[k], chunk, preferred_element_type=f32).astype(
            bf16
        ).reshape(chunk_rows, model_width)

    def combine(k, rows_in):
        return jnp.einsum(
            "sit,sid->std",
            dispatch[k],
            rows_in.reshape(2 * n_fsdp, capacity, model_width),
            preferred_element_type=f32,
        ).astype(bf16)

    def reduce_chunk(k, parts):
        parts = parts.reshape(2, n_fsdp, row_count, model_width)
        got = swap(parts[1], "ctx", n_ctx, 1)
        parts = (parts[0].astype(f32) + got.astype(f32)).astype(bf16)
        own = plane_scatter(parts)
        if k:
            own = swap(own.astype(bf16), "ctx", n_ctx, 2 * k).astype(f32)
        return own

    gate_w = w_gate[0]
    up_w = w_up[0]
    down_w = w_down[0]

    grad_slots = [grad_res_low] + [
        swap(grad_res_low, "ctx", n_ctx, 2 * k) for k in range(1, z_count)
    ]
    grad_rows = []
    down_back = []
    for k in range(z_count):
        rows_k = dispatch_rows(k, gather_chunk(grad_slots[k]))
        grad_rows.append(rows_k)
        down_back.append(
            jnp.einsum("rd,fd->rf", rows_k, down_w, preferred_element_type=f32)
        )

    act_slots = [acts_two] + [swap(acts_two, "ctx", n_ctx, 2 * k) for k in range(1, z_count)]
    act_rows, hidden_rows, gate_lows, up_lows, gate_grads = [], [], [], [], []
    acts_two_grad = None
    for k in range(z_count):
        rows_k = dispatch_rows(k, gather_chunk(act_slots[k]))
        gate_pre = jnp.dot(rows_k, gate_w, preferred_element_type=f32)
        up_pre = jnp.dot(rows_k, up_w, preferred_element_type=f32)
        sig = 1.0 / (1.0 + jnp.exp(-gate_pre))
        silu = gate_pre * sig
        hidden = (silu * up_pre).astype(bf16)
        back = down_back[k]
        gate_grads.append(jnp.sum(hidden.astype(f32) * back, axis=-1))
        hidden_grad = gate_rows[k] * back
        gate_low = (hidden_grad * up_pre * sig * (1.0 + gate_pre * (1.0 - sig))).astype(bf16)
        up_low = (hidden_grad * silu).astype(bf16)
        row_grad = (
            jnp.einsum("rf,df->rd", gate_low, gate_w, preferred_element_type=f32)
            + jnp.einsum("rf,df->rd", up_low, up_w, preferred_element_type=f32)
        ).astype(bf16)
        part = reduce_chunk(k, combine(k, row_grad))
        acts_two_grad = part if acts_two_grad is None else acts_two_grad + part
        act_rows.append(rows_k)
        hidden_rows.append(hidden)
        gate_lows.append(gate_low)
        up_lows.append(up_low)

    gate_grad_here = jnp.stack(gate_grads).reshape(n_all, capacity, 1)
    gate_grad_here = jnp.sum(
        jnp.where(hot, gate_grad_here, 0.0), axis=1
    )
    gate_grad_rel = exchange_small(gate_grad_here, n_ctx)
    gate_grad = jnp.sum(chosen_rel * gate_grad_rel.T[:, None, :], axis=-1)
    (picked_grad,) = gate_back(gate_grad)
    logit_grad = jnp.sum(picked_grad[:, :, None] * pick_table, axis=1).astype(bf16)
    acts_two_grad = acts_two_grad + jnp.dot(
        logit_grad, full_router.T, preferred_element_type=f32
    )

    scaled = ffn_gain * acts_two_grad
    grad_ffn_gain = jnp.sum(acts_two_grad * resid * rms_two, axis=0)
    resid_grad = (
        grad_res
        + rms_two * scaled
        - resid * (rms_two**3 * jnp.mean(scaled * resid, axis=-1, keepdims=True))
    )
    attn_grad = resid_grad.astype(bf16)
    attn_grad_group = plane_gather(attn_grad)
    heads_grad = jnp.einsum(
        "td,cd->tc", attn_grad_group, output_weight, preferred_element_type=f32
    ).astype(bf16)
    dq, dkv = attend_back(
        place_list,
        source_list,
        query_low,
        kv_all,
        mixed,
        heads_grad.reshape(n_fsdp, row_count, q_width),
        lse,
    )

    held = dkv.reshape(z_count, 2, n_fsdp, row_count, 2 * head_dim)
    held = (held[:, 0].astype(f32) + swap(held[:, 1], "ctx", n_ctx, 1).astype(f32)).astype(bf16)
    dkv_own = held[0].astype(f32)
    for k in range(1, z_count):
        dkv_own = dkv_own + swap(held[k], "ctx", n_ctx, 2 * k).astype(f32)
    dkv_own = dkv_own.reshape(group_rows, 1, 2 * head_dim)
    proj_grad, grad_q_gain, grad_k_gain = prep_back(
        (
            dq.reshape(group_rows, heads, head_dim),
            dkv_own[:, :, :head_dim],
            dkv_own[:, :, head_dim:],
        )
    )
    proj_low = proj_grad.astype(bf16)
    acts_parts = jnp.einsum("tc,dc->td", proj_low, weight_qkv, preferred_element_type=f32)
    acts_grad = plane_scatter(
        acts_parts.astype(bf16).reshape(n_fsdp, row_count, model_width)
    )
    scaled = attn_gain * acts_grad
    grad_attn_gain = jnp.sum(acts_grad * inputs * rms_one, axis=0)
    grad_tokens = (
        resid_grad
        + rms_one * scaled
        - inputs * (rms_one**3 * jnp.mean(scaled * inputs, axis=-1, keepdims=True))
    ).reshape(tokens.shape)

    grad_w_qkv = jnp.einsum(
        "td,tc->dc", acts_group, proj_low, preferred_element_type=f32
    ).astype(bf16)
    own_rows = ctx_scatter(
        grad_w_qkv.reshape(n_ctx, n_fsdp, -1, own_width), n_ctx, ctx_at, True
    )
    pieces = jnp.zeros((n_fsdp,) + own_rows.shape[1:], f32)
    pieces = lax.dynamic_update_index_in_dim(pieces, pick(own_rows, fsdp_at), fsdp_at, 0)
    for k in range(1, n_fsdp):
        got = swap(pick(own_rows, fsdp_at ^ k), "fsdp", n_fsdp, k)
        pieces = lax.dynamic_update_index_in_dim(pieces, got, fsdp_at ^ k, 0)
    pieces = jnp.swapaxes(pieces, 0, 1)
    out_rows = pieces.shape[0]
    grad_w_qkv = jnp.concatenate(
        [
            pieces[:, :, :q_width].reshape(out_rows, -1),
            pieces[:, :, q_width : q_width + head_dim].reshape(out_rows, -1),
            pieces[:, :, q_width + head_dim :].reshape(out_rows, -1),
        ],
        axis=1,
    )

    grad_w_out = jnp.einsum(
        "tc,td->cd", heads_low, attn_grad_group, preferred_element_type=f32
    ).astype(bf16)
    per_ctx = grad_w_out.shape[0] // n_ctx
    grad_w_out = ctx_scatter(
        grad_w_out.reshape(n_ctx, per_ctx, model_width), n_ctx, ctx_at, True
    ).astype(bf16)
    grad_w_out = lax.ppermute(
        grad_w_out,
        ("ctx", "fsdp"),
        [(c * n_fsdp + f, f * n_ctx + c) for c in range(n_ctx) for f in range(n_fsdp)],
    ).astype(f32)

    grad_w_router = jnp.einsum("td,te->de", acts_two, logit_grad, preferred_element_type=f32)
    grad_w_router = ctx_scatter(
        grad_w_router.reshape(n_ctx, n_fsdp, -1, expert_count), n_ctx, ctx_at, False
    )
    bit = 1
    while bit < n_fsdp:
        mine = (fsdp_at // bit) % 2
        split = grad_w_router.reshape((-1, 2) + grad_w_router.shape[1:])
        keep = lax.dynamic_index_in_dim(split, mine, 1, keepdims=False)
        away = lax.dynamic_index_in_dim(split, 1 - mine, 1, keepdims=False)
        grad_w_router = keep + swap(away, "fsdp", n_fsdp, bit)
        bit *= 2
    grad_w_router = grad_w_router[0]

    result = resid
    for k in range(z_count):
        produced = jnp.dot(hidden_rows[k], down_w, preferred_element_type=f32).astype(bf16)
        weighted = (produced.astype(f32) * gate_rows[k]).astype(bf16)
        result = result + reduce_chunk(k, combine(k, weighted))
    output = result.astype(bf16).reshape(tokens.shape)
    act_all = jnp.concatenate(act_rows)
    out_grad = (jnp.concatenate(grad_rows).astype(f32) * gate_rows.reshape(-1, 1)).astype(bf16)
    grad_w_down = jnp.einsum(
        "rf,rd->fd", jnp.concatenate(hidden_rows), out_grad, preferred_element_type=f32
    )[None]
    grad_w_gate = jnp.einsum(
        "rd,rf->df", act_all, jnp.concatenate(gate_lows), preferred_element_type=f32
    )[None]
    grad_w_up = jnp.einsum(
        "rd,rf->df", act_all, jnp.concatenate(up_lows), preferred_element_type=f32
    )[None]

    gains = sum_everywhere(
        jnp.concatenate([grad_attn_gain, grad_ffn_gain, grad_q_gain, grad_k_gain]), n_ctx
    )
    grad_attn_gain = gains[:model_width]
    grad_ffn_gain = gains[model_width : 2 * model_width]
    grad_q_gain = gains[2 * model_width : 2 * model_width + head_dim]
    grad_k_gain = gains[2 * model_width + head_dim :]
    return (
        output,
        grad_tokens,
        grad_attn_gain,
        grad_w_qkv,
        grad_q_gain,
        grad_k_gain,
        grad_w_out,
        grad_ffn_gain,
        grad_w_router,
        grad_w_gate,
        grad_w_up,
        grad_w_down,
    )


def solution(mesh):
    n_ctx, n_fsdp = mesh.shape["ctx"], mesh.shape["fsdp"]

    def body(*arrays):
        heads_kv = (arrays[4].shape[1] - arrays[7].shape[0] * n_fsdp) // (2 * arrays[5].shape[0])
        if n_fsdp == 4 and heads_kv == n_fsdp and n_ctx & (n_ctx - 1) == 0:
            return fast_body(n_ctx, *arrays)
        return general_body(*arrays)

    whole = P(("ctx", "fsdp"), None, None)
    rows = P(("ctx", "fsdp"), None)
    split = P("fsdp", "ctx", None)
    return jax.shard_map(
        body,
        mesh=mesh,
        in_specs=(
            split,
            P("fsdp", "ctx"),
            split,
            P(),
            P("fsdp", None),
            P(),
            P(),
            P("fsdp", None),
            P(),
            P("fsdp", None),
            whole,
            whole,
            whole,
            split,
        ),
        out_specs=(split, split, P(), rows, P(), P(), rows, P(), rows, whole, whole, whole),
        check_vma=False,
    )
```

```python
import functools
import math

import jax
import jax.numpy as jnp
from jax import lax
from jax.experimental import pallas as pl
from jax.experimental.pallas import tpu as pltpu
from jax.sharding import PartitionSpec as P

eps_norm = 1e-06
rope_base = 1000000.0
masked_value = -1e30
run_rows = 128
bf16 = jnp.bfloat16
f32 = jnp.float32


def rms_scale(values, gain):
    mean_sq = jnp.mean(values * values, axis=-1, keepdims=True)
    return values * lax.rsqrt(mean_sq + eps_norm) * gain


def frequencies(head_dim):
    return 1.0 / rope_base ** (jnp.arange(0, head_dim, 2).astype(jnp.float32) / head_dim)


def rotate(values, angles):
    half_dim = values.shape[-1] // 2
    cosine = jnp.cos(angles)
    sine_val = jnp.sin(angles)
    first_half = values[..., :half_dim]
    second_half = values[..., half_dim:]
    return jnp.concatenate(
        [
            first_half * cosine - second_half * sine_val,
            second_half * cosine + first_half * sine_val,
        ],
        axis=-1,
    )


def head_prep(projected, gain_q, gain_k, angles, heads_q, heads_kv):
    head_dim = gain_q.shape[0]
    row_count = projected.shape[0]
    q_width = heads_q * head_dim
    kv_width = heads_kv * head_dim
    queries = projected[:, :q_width].reshape(row_count, heads_q, head_dim)
    key_heads = projected[:, q_width : q_width + kv_width].reshape(row_count, heads_kv, head_dim)
    value_heads = projected[:, q_width + kv_width :].reshape(row_count, heads_kv, head_dim)
    queries = rotate(rms_scale(queries, gain_q), angles)
    key_heads = rotate(rms_scale(key_heads, gain_k), angles)
    return (queries, key_heads, value_heads)


def general_body(
    tokens,
    positions,
    expert_ids,
    attn_gain,
    query_key_value_weight,
    q_gain,
    k_gain,
    output_weight,
    ffn_gain,
    router_weight,
    w_gate,
    w_up,
    w_down,
    cotangent,
):
    row_count = tokens.shape[1]
    model_width = tokens.shape[2]
    head_dim = q_gain.shape[0]
    inputs = tokens.reshape(row_count, model_width).astype(jnp.float32)
    places = positions.reshape(row_count)
    chosen = expert_ids.reshape(row_count, -1)
    top_count = chosen.shape[1]
    full_qkv, full_out, full_router = (
        lax.all_gather(query_key_value_weight, "fsdp", axis=0, tiled=True),
        lax.all_gather(output_weight, "fsdp", axis=0, tiled=True),
        lax.all_gather(router_weight, "fsdp", axis=0, tiled=True),
    )
    heads_q = full_out.shape[0] // head_dim
    heads_kv = (full_qkv.shape[1] - full_out.shape[0]) // (2 * head_dim)
    group_size = heads_q // heads_kv
    expert_count = full_router.shape[1]
    capacity = row_count * top_count * 3 // (2 * expert_count)
    local_experts = w_gate.shape[0]
    score_scale = 1.0 / math.sqrt(head_dim)
    normed, norm_back = jax.vjp(rms_scale, inputs, attn_gain)
    first_activations = normed.astype(jnp.bfloat16)
    query_key_value_projected = jnp.dot(
        first_activations, full_qkv, preferred_element_type=jnp.float32
    )
    angles = places.astype(jnp.float32)[:, None, None] * frequencies(head_dim)[None, None, :]

    def prepare(proj_in, gain_q, gain_k):
        return head_prep(proj_in, gain_q, gain_k, angles, heads_q, heads_kv)

    (queries, key_heads, value_heads), prep_back = jax.vjp(
        prepare, query_key_value_projected, q_gain, k_gain
    )
    query_low = queries.astype(jnp.bfloat16).reshape(row_count, heads_kv, group_size, head_dim)
    key_low = key_heads.astype(jnp.bfloat16)
    value_low = value_heads.astype(jnp.bfloat16)
    all_keys, all_values = (
        lax.all_gather(key_low, "ctx", axis=0, tiled=True),
        lax.all_gather(value_low, "ctx", axis=0, tiled=True),
    )
    key_places = lax.all_gather(places, "ctx", axis=0, tiled=True)
    seq_len = all_keys.shape[0]
    sorted_keys = jnp.zeros_like(all_keys).at[key_places].set(all_keys)
    sorted_values = jnp.zeros_like(all_values).at[key_places].set(all_values)
    block_len = min(512, seq_len)
    run_len = row_count // 2

    def block_scores(query_run, place_run, block_index):
        start = block_index * block_len
        key_blk = lax.dynamic_slice_in_dim(sorted_keys, start, block_len, 0)
        value_blk = lax.dynamic_slice_in_dim(sorted_values, start, block_len, 0)
        raw_scores = (
            jnp.einsum("qhgd,khd->hgqk", query_run, key_blk, preferred_element_type=jnp.float32)
            * score_scale
        )
        key_pos = start + jnp.arange(block_len, dtype=jnp.int32)
        visible = key_pos[None, :] <= place_run[:, None]
        return (jnp.where(visible, raw_scores, masked_value), visible, key_blk, value_blk)

    run_info = []
    mixed_runs = []
    for run_index in range(2):
        query_run = query_low[run_index * run_len : (run_index + 1) * run_len]
        place_run = places[run_index * run_len : (run_index + 1) * run_len]
        block_total = jnp.max(place_run) // block_len + 1

        def stats_step(block_index, carried):
            run_max, run_sum = carried
            scores, visible, key_blk, value_blk = block_scores(query_run, place_run, block_index)
            new_max = jnp.maximum(run_max, jnp.max(scores, axis=-1))
            weights = jnp.where(visible, jnp.exp(scores - new_max[..., None]), 0.0)
            run_sum = run_sum * jnp.exp(run_max - new_max) + jnp.sum(weights, axis=-1)
            return (new_max, run_sum)

        stat_shape = (heads_kv, group_size, run_len)
        initial = (
            jnp.full(stat_shape, masked_value, jnp.float32),
            jnp.zeros(stat_shape, jnp.float32),
        )
        run_max, run_sum = lax.fori_loop(0, block_total, stats_step, initial)
        log_total = run_max + jnp.log(run_sum)

        def output_step(block_index, running):
            scores, visible, key_blk, value_blk = block_scores(query_run, place_run, block_index)
            prob_vals = jnp.exp(scores - log_total[..., None])
            return running + jnp.einsum(
                "hgqk,khd->qhgd",
                prob_vals.astype(jnp.bfloat16),
                value_blk,
                preferred_element_type=jnp.float32,
            )

        mixed_run = lax.fori_loop(
            0,
            block_total,
            output_step,
            jnp.zeros((run_len, heads_kv, group_size, head_dim), jnp.float32),
        )
        mixed_runs.append(mixed_run)
        run_info.append((query_run, place_run, block_total, log_total))
    heads_out = jnp.concatenate(mixed_runs, axis=0)
    heads_reduced_precision = heads_out.reshape(row_count, heads_q * head_dim).astype(jnp.bfloat16)
    residual_stream = inputs + jnp.dot(
        heads_reduced_precision, full_out, preferred_element_type=jnp.float32
    )
    normed_two, norm_two_back = jax.vjp(rms_scale, residual_stream, ffn_gain)
    second_activations = normed_two.astype(jnp.bfloat16)
    router_logits = jnp.dot(second_activations, full_router, preferred_element_type=jnp.float32)
    pick_table = (chosen[:, :, None] == jnp.arange(expert_count)[None, None, :]).astype(jnp.float32)
    picked = jnp.sum(router_logits[:, None, :] * pick_table, axis=-1)
    gate_vals, gate_back = jax.vjp(lambda values: jax.nn.softmax(values, axis=-1), picked)
    flat_choice = chosen.reshape(-1)
    slot_hot = (flat_choice[:, None] == jnp.arange(expert_count)[None, :]).astype(jnp.int32)
    slot_rank = jnp.sum((jnp.cumsum(slot_hot, axis=0) - slot_hot) * slot_hot, axis=1)
    targets = flat_choice * capacity + slot_rank
    source_rows = jnp.repeat(second_activations, top_count, axis=0)
    outgoing = (
        jnp.zeros((expert_count * capacity, model_width), jnp.bfloat16).at[targets].set(source_rows)
    )
    outgoing = outgoing.reshape(expert_count, capacity, model_width)
    arrived = lax.all_to_all(outgoing, ("ctx", "fsdp"), split_axis=0, concat_axis=0, tiled=True)
    sources = arrived.shape[0] // local_experts
    slot_count = arrived.shape[1]
    grouped = arrived.reshape(sources, local_experts, slot_count, model_width)
    gate_pre = jnp.einsum("secd,edf->secf", grouped, w_gate, preferred_element_type=jnp.float32)
    up_pre = jnp.einsum("secd,edf->secf", grouped, w_up, preferred_element_type=jnp.float32)
    hidden = (jax.nn.silu(gate_pre) * up_pre).astype(jnp.bfloat16)
    produced = jnp.einsum("secf,efd->secd", hidden, w_down, preferred_element_type=jnp.float32)
    produced = produced.astype(jnp.bfloat16).reshape(arrived.shape)
    flat_shape = (arrived.shape[0], slot_count, gate_pre.shape[3])
    expert_results = (produced, arrived, gate_pre.reshape(flat_shape), up_pre.reshape(flat_shape))
    produced = expert_results[0]
    arrived = expert_results[1]
    returned = lax.all_to_all(produced, ("ctx", "fsdp"), split_axis=0, concat_axis=0, tiled=True)
    expert_rows = returned.reshape(expert_count * capacity, model_width)[targets].reshape(
        row_count, top_count, model_width
    )
    expert_vals = expert_rows.astype(jnp.float32)
    result = residual_stream + jnp.sum(gate_vals[:, :, None] * expert_vals, axis=1)
    output = result.astype(jnp.bfloat16).reshape(tokens.shape)
    grad_res = cotangent.reshape(row_count, model_width).astype(jnp.float32)
    gate_grad = jnp.sum(grad_res[:, None, :] * expert_vals, axis=-1)
    out_grad = (gate_vals[:, :, None] * grad_res[:, None, :]).astype(jnp.bfloat16)
    back_out = (
        jnp.zeros((expert_count * capacity, model_width), jnp.bfloat16)
        .at[targets]
        .set(out_grad.reshape(-1, model_width))
    )
    back_out = back_out.reshape(expert_count, capacity, model_width)
    (picked_grad,) = gate_back(gate_grad)
    logit_grad = jnp.sum(picked_grad[:, :, None] * pick_table, axis=1).astype(jnp.bfloat16)
    full_qkv, full_out, full_router = (
        lax.all_gather(query_key_value_weight, "fsdp", axis=0, tiled=True),
        lax.all_gather(output_weight, "fsdp", axis=0, tiled=True),
        lax.all_gather(router_weight, "fsdp", axis=0, tiled=True),
    )
    arrived_grad = lax.all_to_all(
        back_out, ("ctx", "fsdp"), split_axis=0, concat_axis=0, tiled=True
    )
    sources = arrived.shape[0] // local_experts
    grouped = arrived.reshape(sources, local_experts, capacity, model_width)
    grad_grouped = arrived_grad.reshape(sources, local_experts, capacity, model_width)
    gate_pre = expert_results[2].reshape(sources, local_experts, capacity, -1)
    up_pre = expert_results[3].reshape(sources, local_experts, capacity, -1)
    hidden, hidden_back = jax.vjp(
        lambda gate_in, up_in: jax.nn.silu(gate_in) * up_in, gate_pre, up_pre
    )
    hidden_low = hidden.astype(jnp.bfloat16)
    hidden_grad = jnp.einsum(
        "secd,efd->secf", grad_grouped, w_down, preferred_element_type=jnp.float32
    )
    gate_pre_grad, up_pre_grad = hidden_back(hidden_grad)
    gate_low = gate_pre_grad.astype(jnp.bfloat16)
    up_low = up_pre_grad.astype(jnp.bfloat16)
    grad_w_down = jnp.einsum(
        "secf,secd->efd", hidden_low, grad_grouped, preferred_element_type=jnp.float32
    )
    grad_w_gate = jnp.einsum(
        "secd,secf->edf", grouped, gate_low, preferred_element_type=jnp.float32
    )
    grad_w_up = jnp.einsum("secd,secf->edf", grouped, up_low, preferred_element_type=jnp.float32)
    row_grad = jnp.einsum(
        "secf,edf->secd", gate_low, w_gate, preferred_element_type=jnp.float32
    ) + jnp.einsum("secf,edf->secd", up_low, w_up, preferred_element_type=jnp.float32)
    row_grad = row_grad.astype(jnp.bfloat16).reshape(arrived.shape)
    row_back = lax.all_to_all(row_grad, ("ctx", "fsdp"), split_axis=0, concat_axis=0, tiled=True)
    token_rows = row_back.reshape(expert_count * capacity, model_width)[targets].reshape(
        row_count, top_count, model_width
    )
    acts_two_grad = jnp.sum(token_rows.astype(jnp.float32), axis=1) + jnp.dot(
        logit_grad, full_router.T, preferred_element_type=jnp.float32
    )
    grad_w_router = jnp.dot(second_activations.T, logit_grad, preferred_element_type=jnp.float32)
    resid_extra, grad_ffn_gain = norm_two_back(acts_two_grad)
    resid_grad = grad_res + resid_extra
    attn_grad = resid_grad.astype(jnp.bfloat16)
    grad_w_out = jnp.dot(heads_reduced_precision.T, attn_grad, preferred_element_type=jnp.float32)
    heads_grad = jnp.dot(attn_grad, full_out.T, preferred_element_type=jnp.float32).astype(
        jnp.bfloat16
    )
    heads_grad = heads_grad.reshape(row_count, heads_kv, group_size, head_dim)
    row_delta = jnp.moveaxis(jnp.sum(heads_grad.astype(jnp.float32) * heads_out, axis=-1), 0, 2)
    key_grad_sorted = jnp.zeros((seq_len, heads_kv, head_dim), jnp.float32)
    value_grad_sorted = jnp.zeros((seq_len, heads_kv, head_dim), jnp.float32)
    query_grad_runs = []
    for run_index in range(2):
        query_run, place_run, block_total, log_total = run_info[run_index]
        grad_run = heads_grad[run_index * run_len : (run_index + 1) * run_len]
        delta_run = row_delta[:, :, run_index * run_len : (run_index + 1) * run_len]

        def back_step(block_index, carried):
            query_grad, key_acc, value_acc = carried
            scores, visible, key_blk, value_blk = block_scores(query_run, place_run, block_index)
            prob_vals = jnp.exp(scores - log_total[..., None])
            value_grad = jnp.einsum(
                "hgqk,qhgd->khd",
                prob_vals.astype(jnp.bfloat16),
                grad_run,
                preferred_element_type=jnp.float32,
            )
            prob_grad = jnp.einsum(
                "qhgd,khd->hgqk", grad_run, value_blk, preferred_element_type=jnp.float32
            )
            score_grad = (prob_vals * (prob_grad - delta_run[..., None])).astype(jnp.bfloat16)
            query_grad = (
                query_grad
                + jnp.einsum(
                    "hgqk,khd->qhgd", score_grad, key_blk, preferred_element_type=jnp.float32
                )
                * score_scale
            )
            key_grad = (
                jnp.einsum(
                    "hgqk,qhgd->khd", score_grad, query_run, preferred_element_type=jnp.float32
                )
                * score_scale
            )
            start = block_index * block_len
            key_acc = lax.dynamic_update_slice_in_dim(
                key_acc, lax.dynamic_slice_in_dim(key_acc, start, block_len, 0) + key_grad, start, 0
            )
            value_acc = lax.dynamic_update_slice_in_dim(
                value_acc,
                lax.dynamic_slice_in_dim(value_acc, start, block_len, 0) + value_grad,
                start,
                0,
            )
            return (query_grad, key_acc, value_acc)

        start_state = (
            jnp.zeros((run_len, heads_kv, group_size, head_dim), jnp.float32),
            key_grad_sorted,
            value_grad_sorted,
        )
        query_grad_run, key_grad_sorted, value_grad_sorted = lax.fori_loop(
            0, block_total, back_step, start_state
        )
        query_grad_runs.append(query_grad_run)
    query_grad = jnp.concatenate(query_grad_runs, axis=0)
    key_grads = key_grad_sorted[key_places]
    value_grads = value_grad_sorted[key_places]
    key_grad_own, value_grad_own = (
        lax.psum_scatter(
            key_grads.astype(jnp.bfloat16), "ctx", scatter_dimension=0, tiled=True
        ).astype(jnp.float32),
        lax.psum_scatter(
            value_grads.astype(jnp.bfloat16), "ctx", scatter_dimension=0, tiled=True
        ).astype(jnp.float32),
    )
    proj_grad, grad_q_gain, grad_k_gain = prep_back(
        (query_grad.reshape(row_count, heads_q, head_dim), key_grad_own, value_grad_own)
    )
    proj_low = proj_grad.astype(jnp.bfloat16)
    grad_w_qkv = jnp.dot(first_activations.T, proj_low, preferred_element_type=jnp.float32)
    acts_grad = jnp.dot(proj_low, full_qkv.T, preferred_element_type=jnp.float32)
    inputs_extra, grad_attn_gain = norm_back(acts_grad)
    grad_tokens = (resid_grad + inputs_extra).reshape(tokens.shape)
    grad_w_qkv, grad_w_out, grad_w_router = (
        lax.psum_scatter(grad_w_qkv, ("ctx", "fsdp"), scatter_dimension=0, tiled=True),
        lax.psum_scatter(grad_w_out, ("ctx", "fsdp"), scatter_dimension=0, tiled=True),
        lax.psum_scatter(grad_w_router, ("ctx", "fsdp"), scatter_dimension=0, tiled=True),
    )
    grad_attn_gain, grad_q_gain, grad_k_gain, grad_ffn_gain = lax.psum(
        (grad_attn_gain, grad_q_gain, grad_k_gain, grad_ffn_gain), ("ctx", "fsdp")
    )
    return (
        output,
        grad_tokens,
        grad_attn_gain,
        grad_w_qkv,
        grad_q_gain,
        grad_k_gain,
        grad_w_out,
        grad_ffn_gain,
        grad_w_router,
        grad_w_gate,
        grad_w_up,
        grad_w_down,
    )


def swap(values, axis, count, bit):
    return lax.ppermute(values, axis, [(i, i ^ bit) for i in range(count)])


def after(values, earlier):
    return lax.optimization_barrier((values, earlier))[0]


def pick(values, index):
    return lax.dynamic_index_in_dim(values, index, 0, keepdims=False)


def by_fsdp(pieces, fsdp_at):
    stacked = jnp.stack(pieces)
    stacked = jnp.where(fsdp_at % 2 == 1, jnp.stack([pieces[k ^ 1] for k in range(4)]), stacked)
    turned = jnp.stack([stacked[k ^ 2] for k in range(4)])
    return jnp.where(fsdp_at // 2 == 1, turned, stacked)


def plane_gather(values):
    half = values.shape[-2] // 2
    near_x = swap(values, "fsdp", 4, 1)
    near_y = swap(values, "fsdp", 4, 2)
    far_low = swap(near_x[..., :half, :], "fsdp", 4, 2)
    far_high = swap(near_y[..., half:, :], "fsdp", 4, 1)
    return [values, near_x, near_y, far_low, far_high]


def plane_scatter(own, x_low, x_high, y_low, y_high, far_low, far_high):
    from_x = swap(far_low, "fsdp", 4, 1)
    from_y = swap(far_high, "fsdp", 4, 2)
    got_x_low = swap(x_low, "fsdp", 4, 1)
    got_y_high = swap(y_high, "fsdp", 4, 2)
    got_y_low = swap((y_low.astype(f32) + from_x.astype(f32)).astype(bf16), "fsdp", 4, 2)
    got_x_high = swap((x_high.astype(f32) + from_y.astype(f32)).astype(bf16), "fsdp", 4, 1)
    added = jnp.concatenate(
        [
            got_x_low.astype(f32) + got_y_low.astype(f32),
            got_x_high.astype(f32) + got_y_high.astype(f32),
        ],
        axis=-2,
    )
    return own.astype(f32) + added


def scatter_parts(parts):
    half = parts.shape[1] // 2
    return plane_scatter(
        parts[0],
        parts[1, :half],
        parts[1, half:],
        parts[2, :half],
        parts[2, half:],
        parts[3, :half],
        parts[3, half:],
    )


def exchange_small(table, n_ctx):
    count, width = table.shape
    bit = 1
    while bit < count:
        split = table.reshape(count // (2 * bit), 2, bit, width)
        moved = split[:, 1]
        if bit < 4:
            moved = swap(moved, "fsdp", 4, bit)
        else:
            moved = swap(moved, "ctx", n_ctx, bit // 4)
        table = jnp.stack([split[:, 0], moved], axis=1).reshape(count, width)
        bit *= 2
    return table


def sum_everywhere(values, n_ctx):
    bit = 1
    while bit < 4:
        values = values + swap(values, "fsdp", 4, bit)
        bit *= 2
    bit = 1
    while bit < n_ctx:
        values = values + swap(values, "ctx", n_ctx, bit)
        bit *= 2
    return values


def ctx_scatter(parts, n_ctx, ctx_at, low):
    bit = 1
    held = parts
    while bit < n_ctx:
        mine = (ctx_at // bit) % 2
        split = held.reshape((held.shape[0] // 2, 2) + held.shape[1:])
        keep = lax.dynamic_index_in_dim(split, mine, 1, keepdims=False)
        away = lax.dynamic_index_in_dim(split, 1 - mine, 1, keepdims=False)
        got = swap(away, "ctx", n_ctx, bit)
        held = keep.astype(f32) + got.astype(f32)
        bit *= 2
        if low and bit < n_ctx:
            held = held.astype(bf16)
    return held.reshape(parts.shape[1:])


def attend_kernel(place_ref, source_ref, q_ref, kv_ref, o_ref, lse_ref, keys, vals_t, q_t, acc, total):
    seq = pl.program_id(0)
    rows = run_rows
    heads = q_ref.shape[2] // rows
    blocks = keys.shape[0] // rows
    scale = math.log2(math.e) / math.sqrt(rows)
    for p in range(blocks):
        at = source_ref[seq * blocks + p]
        block = kv_ref[at // 2, 0, pl.ds(pl.multiple_of((at % 2) * rows, rows), rows), :]
        keys[p * rows : (p + 1) * rows, :] = block[:, :rows]
        vals_t[:, p * rows : (p + 1) * rows] = block[:, rows:].T
    key_iota = lax.broadcasted_iota(jnp.int32, (2 * rows, 2 * rows), 0)
    query_iota = lax.broadcasted_iota(jnp.int32, (2 * rows, 2 * rows), 1) % rows
    for run in range(2):
        place = place_ref[seq * 2 + run]
        for h in range(heads):
            q_t[:, h * rows : (h + 1) * rows] = q_ref[
                0, run * rows : (run + 1) * rows, h * rows : (h + 1) * rows
            ].T
        acc[...] = jnp.zeros_like(acc)
        total[...] = jnp.zeros_like(total)

        def step(j, masked):
            start = pl.multiple_of(j * 2 * rows, 2 * rows)
            key_blk = keys[pl.ds(start, 2 * rows), :]
            val_blk = vals_t[:, pl.ds(start, 2 * rows)]
            for pair in range(heads // 2):
                cols = slice(pair * 2 * rows, (pair + 1) * 2 * rows)
                scores = jnp.dot(key_blk, q_t[:, cols], preferred_element_type=f32)
                weights = jnp.exp2(scores * scale)
                if masked:
                    seen = start + key_iota <= place * rows + query_iota
                    weights = jnp.where(seen, weights, 0.0)
                total[:, cols] += jnp.sum(weights.reshape(2 * rows // 8, 8, 2 * rows), axis=0)
                acc[:, cols] += jnp.dot(val_blk, weights.astype(bf16), preferred_element_type=f32)

        lax.fori_loop(0, place // 2, lambda j, c: (step(j, False), c)[1], 0)
        step(place // 2, True)
        norm = jnp.sum(total[...], axis=0, keepdims=True)
        lse_ref[0, run : run + 1, :] = jnp.log2(norm)
        mixed = acc[...] / norm
        for h in range(heads):
            o_ref[0, run * rows : (run + 1) * rows, h * rows : (h + 1) * rows] = (
                mixed[:, h * rows : (h + 1) * rows].T.astype(bf16)
            )


def head_back(turned, vector, cosine, sine, gain):
    grad = turned * cosine - pltpu.roll(turned, turned.shape[1] // 2, 1) * sine
    scale = lax.rsqrt(jnp.mean(vector * vector, axis=-1, keepdims=True) + eps_norm)
    unit = vector * scale
    scaled = grad * gain
    back = scale * (scaled - unit * jnp.mean(scaled * unit, axis=-1, keepdims=True))
    return back, grad * unit


def project_kernel(heads, acts_ref, weight_ref, cos_ref, sin_ref, gain_q_ref, gain_k_ref, proj_ref, q_ref, kv_ref):
    width = cos_ref.shape[2]
    proj_ref[0] = jnp.dot(acts_ref[0], weight_ref[...], preferred_element_type=f32)
    for h in range(heads + 1):
        vector = proj_ref[0, :, h * width : (h + 1) * width]
        gain = gain_q_ref[...] if h < heads else gain_k_ref[...]
        scale = lax.rsqrt(jnp.mean(vector * vector, axis=-1, keepdims=True) + eps_norm)
        normed = vector * scale * gain
        turned = normed * cos_ref[0] + pltpu.roll(normed, width // 2, 1) * sin_ref[0]
        if h < heads:
            q_ref[0, :, h * width : (h + 1) * width] = turned.astype(bf16)
        else:
            kv_ref[0, :, :width] = turned.astype(bf16)
    kv_ref[0, :, width:] = proj_ref[0, :, (heads + 1) * width :].astype(bf16)


def key_back_kernel(a_ref, b_ref, c_ref, d_ref, proj_ref, cos_ref, sin_ref, gain_ref, dkv_ref, dgain_ref):
    width = cos_ref.shape[2]
    total = (
        a_ref[0].astype(f32) + b_ref[0].astype(f32) + c_ref[0].astype(f32) + d_ref[0].astype(f32)
    )
    back, share = head_back(
        total[:, :width], proj_ref[0, :, :width], cos_ref[0], sin_ref[0], gain_ref[...]
    )
    dkv_ref[0, :, :width] = back.astype(bf16)
    dkv_ref[0, :, width:] = total[:, width:].astype(bf16)

    @pl.when(pl.program_id(0) == 0)
    def _():
        dgain_ref[...] = jnp.zeros_like(dgain_ref)

    dgain_ref[...] += jnp.sum(share.reshape(-1, 8, width), axis=0)


def attend_back_kernel(
    place_ref,
    source_ref,
    q_ref,
    kv_ref,
    o_ref,
    do_ref,
    lse_ref,
    proj_ref,
    cos_ref,
    sin_ref,
    gain_ref,
    dq_ref,
    dkv_ref,
    dgain_ref,
    keys,
    keys_t,
    vals,
    q_n,
    q_t,
    do_n,
    do_t,
    delta,
    dq_acc,
    dk_acc,
    dv_acc,
):
    seq = pl.program_id(0)
    rows = run_rows
    heads = q_ref.shape[2] // rows
    blocks = keys.shape[0] // rows
    scale = math.log2(math.e) / math.sqrt(rows)
    plain_scale = 1.0 / math.sqrt(rows)
    for p in range(blocks):
        at = source_ref[seq * blocks + p]
        block = kv_ref[at // 2, 0, pl.ds(pl.multiple_of((at % 2) * rows, rows), rows), :]
        keys[p * rows : (p + 1) * rows, :] = block[:, :rows]
        keys_t[:, p * rows : (p + 1) * rows] = block[:, :rows].T
        vals[p * rows : (p + 1) * rows, :] = block[:, rows:]
    dk_acc[...] = jnp.zeros_like(dk_acc)
    dv_acc[...] = jnp.zeros_like(dv_acc)

    @pl.when(seq == 0)
    def _():
        dgain_ref[...] = jnp.zeros_like(dgain_ref)

    key_iota = lax.broadcasted_iota(jnp.int32, (2 * rows, 2 * rows), 0)
    query_iota = lax.broadcasted_iota(jnp.int32, (2 * rows, 2 * rows), 1) % rows
    for run in range(2):
        place = place_ref[seq * 2 + run]
        here = slice(run * rows, (run + 1) * rows)
        for h in range(heads):
            cols = slice(h * rows, (h + 1) * rows)
            q_h = q_ref[0, here, cols]
            q_n[cols, :] = q_h
            q_t[:, cols] = q_h.T
            do_h = do_ref[0, here, cols]
            do_n[cols, :] = do_h
            do_ht = do_h.T
            do_t[:, cols] = do_ht
            o_ht = o_ref[0, here, cols].T
            delta[:, cols] = jnp.sum(do_ht.astype(f32) * o_ht.astype(f32), axis=0, keepdims=True)
        dq_acc[...] = jnp.zeros_like(dq_acc)

        def step(j, masked):
            start = pl.multiple_of(j * 2 * rows, 2 * rows)
            key_blk = keys[pl.ds(start, 2 * rows), :]
            key_t_blk = keys_t[:, pl.ds(start, 2 * rows)]
            val_blk = vals[pl.ds(start, 2 * rows), :]
            dk_sum = jnp.zeros((2 * rows, rows), f32)
            dv_sum = jnp.zeros((2 * rows, rows), f32)
            for pair in range(heads // 2):
                cols = slice(pair * 2 * rows, (pair + 1) * 2 * rows)
                scores = jnp.dot(key_blk, q_t[:, cols], preferred_element_type=f32)
                probs = jnp.exp2(scores * scale - lse_ref[0, run : run + 1, cols])
                if masked:
                    seen = start + key_iota <= place * rows + query_iota
                    probs = jnp.where(seen, probs, 0.0)
                prob_grad = jnp.dot(val_blk, do_t[:, cols], preferred_element_type=f32)
                score_grad = (probs * (prob_grad - delta[:, cols])).astype(bf16)
                dv_sum += jnp.dot(probs.astype(bf16), do_n[cols, :], preferred_element_type=f32)
                dk_sum += jnp.dot(score_grad, q_n[cols, :], preferred_element_type=f32)
                dq_acc[:, cols] += jnp.dot(key_t_blk, score_grad, preferred_element_type=f32)
            dk_acc[pl.ds(start, 2 * rows), :] += dk_sum
            dv_acc[pl.ds(start, 2 * rows), :] += dv_sum

        lax.fori_loop(0, place // 2, lambda j, c: (step(j, False), c)[1], 0)
        step(place // 2, True)
        for h in range(heads):
            cols = slice(h * rows, (h + 1) * rows)
            turned = dq_acc[:, cols].T * plain_scale
            back, share = head_back(
                turned, proj_ref[0, here, cols], cos_ref[0, here, :], sin_ref[0, here, :], gain_ref[...]
            )
            dq_ref[0, here, cols] = back.astype(bf16)
            dgain_ref[...] += jnp.sum(share.reshape(rows // 8, 8, rows), axis=0)
    for p in range(blocks):
        at = source_ref[seq * blocks + p]
        span = slice(p * rows, (p + 1) * rows)
        there = pl.ds(pl.multiple_of((at % 2) * rows, rows), rows)
        dkv_ref[at // 2, 0, there, :rows] = (dk_acc[span, :] * plain_scale).astype(bf16)
        dkv_ref[at // 2, 0, there, rows:] = dv_acc[span, :].astype(bf16)


def attend(places, sources, queries, kv):
    seqs, rows, width = queries.shape
    slots, _, _, pair_width = kv.shape
    head_dim = pair_width // 2
    seq_len = slots * rows
    return pl.pallas_call(
        attend_kernel,
        out_shape=(
            jax.ShapeDtypeStruct(queries.shape, bf16),
            jax.ShapeDtypeStruct((seqs, 2, width), f32),
        ),
        grid_spec=pltpu.PrefetchScalarGridSpec(
            num_scalar_prefetch=2,
            grid=(seqs,),
            in_specs=[
                pl.BlockSpec((1, rows, width), lambda s, *_: (s, 0, 0)),
                pl.BlockSpec((slots, 1, rows, pair_width), lambda s, *_: (0, s, 0, 0)),
            ],
            out_specs=[
                pl.BlockSpec((1, rows, width), lambda s, *_: (s, 0, 0)),
                pl.BlockSpec((1, 2, width), lambda s, *_: (s, 0, 0)),
            ],
            scratch_shapes=[
                pltpu.VMEM((seq_len, head_dim), bf16),
                pltpu.VMEM((head_dim, seq_len), bf16),
                pltpu.VMEM((head_dim, width), bf16),
                pltpu.VMEM((head_dim, width), f32),
                pltpu.VMEM((8, width), f32),
            ],
        ),
        compiler_params=pltpu.CompilerParams(vmem_limit_bytes=32 * 2**20),
        cost_estimate=pl.CostEstimate(
            flops=seqs * rows * width * seq_len * 2,
            bytes_accessed=2 * (2 * queries.size + kv.size),
            transcendentals=seqs * rows * width * slots,
        ),
        name="attend",
    )(places, sources, queries, kv)


def attend_back(places, sources, queries, kv, mixed, mixed_grad, lse, projected, cosine, sine, gain):
    seqs, rows, width = queries.shape
    slots, _, _, pair_width = kv.shape
    head_dim = pair_width // 2
    seq_len = slots * rows
    block = pl.BlockSpec((1, rows, width), lambda s, *_: (s, 0, 0))
    angle_block = pl.BlockSpec((1, rows, head_dim), lambda s, *_: (s, 0, 0))
    kv_block = pl.BlockSpec((slots, 1, rows, pair_width), lambda s, *_: (0, s, 0, 0))
    return pl.pallas_call(
        attend_back_kernel,
        out_shape=(
            jax.ShapeDtypeStruct(queries.shape, bf16),
            jax.ShapeDtypeStruct(kv.shape, bf16),
            jax.ShapeDtypeStruct((8, head_dim), f32),
        ),
        grid_spec=pltpu.PrefetchScalarGridSpec(
            num_scalar_prefetch=2,
            grid=(seqs,),
            in_specs=[
                block,
                kv_block,
                block,
                block,
                pl.BlockSpec((1, 2, width), lambda s, *_: (s, 0, 0)),
                block,
                angle_block,
                angle_block,
                pl.BlockSpec((1, head_dim), lambda s, *_: (0, 0)),
            ],
            out_specs=[block, kv_block, pl.BlockSpec((8, head_dim), lambda s, *_: (0, 0))],
            scratch_shapes=[
                pltpu.VMEM((seq_len, head_dim), bf16),
                pltpu.VMEM((head_dim, seq_len), bf16),
                pltpu.VMEM((seq_len, head_dim), bf16),
                pltpu.VMEM((width, head_dim), bf16),
                pltpu.VMEM((head_dim, width), bf16),
                pltpu.VMEM((width, head_dim), bf16),
                pltpu.VMEM((head_dim, width), bf16),
                pltpu.VMEM((1, width), f32),
                pltpu.VMEM((head_dim, width), f32),
                pltpu.VMEM((seq_len, head_dim), f32),
                pltpu.VMEM((seq_len, head_dim), f32),
            ],
        ),
        compiler_params=pltpu.CompilerParams(vmem_limit_bytes=40 * 2**20),
        cost_estimate=pl.CostEstimate(
            flops=seqs * rows * width * seq_len * 5,
            bytes_accessed=2 * (6 * queries.size + 2 * kv.size),
            transcendentals=seqs * rows * width * slots,
        ),
        name="attend_back",
    )(places, sources, queries, kv, mixed, mixed_grad, lse, projected, cosine, sine, gain)


def project(acts, weight, cosine, sine, gain_q, gain_k, heads):
    seqs, rows, depth = acts.shape
    head_dim = cosine.shape[2]
    width = weight.shape[1]
    angle_block = pl.BlockSpec((1, rows, head_dim), lambda s: (s, 0, 0))
    gain_block = pl.BlockSpec((1, head_dim), lambda s: (0, 0))

    def block(columns):
        return pl.BlockSpec((1, rows, columns), lambda s: (s, 0, 0))

    return pl.pallas_call(
        functools.partial(project_kernel, heads),
        out_shape=(
            jax.ShapeDtypeStruct((seqs, rows, width), f32),
            jax.ShapeDtypeStruct((seqs, rows, heads * head_dim), bf16),
            jax.ShapeDtypeStruct((seqs, rows, 2 * head_dim), bf16),
        ),
        grid=(seqs,),
        in_specs=[
            block(depth),
            pl.BlockSpec((depth, width), lambda s: (0, 0)),
            angle_block,
            angle_block,
            gain_block,
            gain_block,
        ],
        out_specs=[block(width), block(heads * head_dim), block(2 * head_dim)],
        compiler_params=pltpu.CompilerParams(vmem_limit_bytes=40 * 2**20),
        cost_estimate=pl.CostEstimate(
            flops=2 * seqs * rows * depth * width,
            bytes_accessed=2 * (acts.size + weight.size) + 6 * seqs * rows * width,
            transcendentals=0,
        ),
        name="project",
    )(acts, weight, cosine, sine, gain_q, gain_k)


def key_back(held, projected, cosine, sine, gain):
    seqs, rows, pair_width = held[0].shape
    head_dim = pair_width // 2
    pairs_before = projected.shape[2] // pair_width - 1
    block = pl.BlockSpec((1, rows, pair_width), lambda s: (s, 0, 0))
    angle_block = pl.BlockSpec((1, rows, head_dim), lambda s: (s, 0, 0))
    return pl.pallas_call(
        key_back_kernel,
        out_shape=(
            jax.ShapeDtypeStruct(held[0].shape, bf16),
            jax.ShapeDtypeStruct((8, head_dim), f32),
        ),
        grid=(seqs,),
        in_specs=[
            block,
            block,
            block,
            block,
            pl.BlockSpec((1, rows, pair_width), lambda s: (s, 0, pairs_before)),
            angle_block,
            angle_block,
            pl.BlockSpec((1, head_dim), lambda s: (0, 0)),
        ],
        out_specs=[block, pl.BlockSpec((8, head_dim), lambda s: (0, 0))],
        name="key_back",
    )(*held, projected, cosine, sine, gain)


def hot_rows(slot_row, capacity):
    count = slot_row.shape[1]
    return slot_row == lax.broadcasted_iota(jnp.int32, (capacity, count), 0).astype(f32)


def hot_columns(slot_column, capacity):
    count = slot_column.shape[0]
    return (slot_column == lax.broadcasted_iota(jnp.int32, (count, capacity), 1).astype(f32)).astype(bf16)


def select_rows(capacity, slot_ref, pieces, store):
    for core in range(2):
        near = pieces[5 * core : 5 * core + 3]
        low, high = pieces[5 * core + 3], pieces[5 * core + 4]
        for k in range(4):
            source = 4 * core + k
            hot = hot_rows(slot_ref[0, source : source + 1, :], capacity).astype(bf16)
            if k < 3:
                rows = jnp.dot(hot, near[k][0], preferred_element_type=f32)
            else:
                half = low.shape[1]
                rows = jnp.dot(hot[:, :half], low[0], preferred_element_type=f32)
                rows += jnp.dot(hot[:, half:], high[0], preferred_element_type=f32)
            store(source, rows.astype(bf16))


def gate_column(capacity, slot_ref, gates_ref, source):
    hot = hot_rows(slot_ref[0, source : source + 1, :], capacity)
    weighted = jnp.where(hot, gates_ref[0, source : source + 1, :], 0.0)
    return jnp.sum(weighted, axis=1, keepdims=True)


def grad_rows_kernel(capacity, *refs):
    slot_ref, pieces, down_ref, rows_ref, back_ref = refs[0], refs[1:11], refs[11], refs[12], refs[13]

    def store(source, rows):
        rows_ref[0, source * capacity : (source + 1) * capacity, :] = rows

    select_rows(capacity, slot_ref, pieces, store)
    part = lax.dot_general(
        rows_ref[0], down_ref[...], (((1,), (1,)), ((), ())), preferred_element_type=f32
    )

    @pl.when(pl.program_id(1) == 0)
    def _():
        back_ref[0] = part

    @pl.when(pl.program_id(1) > 0)
    def _():
        back_ref[0] += part


def outputs_kernel(capacity, slot_ref, column_ref, gates_ref, hidden_ref, down_ref, rows_ref, given_ref, kept_ref, out_grad_ref):
    produced = jnp.dot(hidden_ref[0], down_ref[...], preferred_element_type=f32).astype(bf16)
    for source in range(8):
        span = slice(source * capacity, (source + 1) * capacity)
        gate_val = gate_column(capacity, slot_ref, gates_ref, source)
        out_grad_ref[0, span, :] = (rows_ref[0, span, :].astype(f32) * gate_val).astype(bf16)
        weighted = (produced[span].astype(f32) * gate_val).astype(bf16)
        if source < 4:
            kept_ref[0, span, :] = weighted
        else:
            hot = hot_columns(column_ref[0, :, source : source + 1], capacity)
            given_ref[0, source - 4] = jnp.dot(hot, weighted, preferred_element_type=f32).astype(bf16)


def combine_kernel(capacity, column_ref, kept_ref, got_ref, own_ref, *half_refs):
    for k in range(4):
        hot = hot_columns(column_ref[0, :, k : k + 1], capacity)
        total = jnp.dot(hot, kept_ref[0, k * capacity : (k + 1) * capacity, :], preferred_element_type=f32)
        total = (total + got_ref[0, k].astype(f32)).astype(bf16)
        if k == 0:
            own_ref[0] = total
        else:
            half = total.shape[0] // 2
            half_refs[2 * k - 2][0] = total[:half]
            half_refs[2 * k - 1][0] = total[half:]


def piece_specs(rows, tile, at):
    whole = pl.BlockSpec((1, rows, tile), at)
    half = pl.BlockSpec((1, rows // 2, tile), at)
    return [whole, whole, whole, half, half] * 2


def select_grad_rows(slots, pieces, down_w, capacity):
    chunks, sources, rows = slots.shape
    hidden, width = down_w.shape
    tile = width // 4
    return pl.pallas_call(
        functools.partial(grad_rows_kernel, capacity),
        out_shape=(
            jax.ShapeDtypeStruct((chunks, sources * capacity, width), bf16),
            jax.ShapeDtypeStruct((chunks, sources * capacity, hidden), f32),
        ),
        grid=(chunks, 4),
        in_specs=[pl.BlockSpec((1, sources, rows), lambda k, d: (k, 0, 0))]
        + piece_specs(rows, tile, lambda k, d: (k, 0, d))
        + [pl.BlockSpec((hidden, tile), lambda k, d: (0, d))],
        out_specs=[
            pl.BlockSpec((1, sources * capacity, tile), lambda k, d: (k, 0, d)),
            pl.BlockSpec((1, sources * capacity, hidden), lambda k, d: (k, 0, 0)),
        ],
        compiler_params=pltpu.CompilerParams(vmem_limit_bytes=48 * 2**20),
        cost_estimate=pl.CostEstimate(
            flops=2 * chunks * sources * capacity * width * (hidden + rows),
            bytes_accessed=chunks * 2 * width * (sources * (rows + capacity) + hidden),
            transcendentals=0,
        ),
        name="select_grad_rows",
    )(slots, *pieces, down_w)


def expert_outputs(slots, columns, gates, hidden_rows, down_w, grad_rows, capacity):
    chunks, sources, rows = slots.shape
    hidden, width = down_w.shape
    tile = width // 4
    group = sources * capacity

    def whole(*shape):
        return pl.BlockSpec((1,) + shape, lambda k, d: (k,) + (0,) * len(shape))

    row_tile = pl.BlockSpec((1, group, tile), lambda k, d: (k, 0, d))
    return pl.pallas_call(
        functools.partial(outputs_kernel, capacity),
        out_shape=(
            jax.ShapeDtypeStruct((chunks, 4, rows, width), bf16),
            jax.ShapeDtypeStruct((chunks, 4 * capacity, width), bf16),
            jax.ShapeDtypeStruct((chunks, group, width), bf16),
        ),
        grid=(chunks, 4),
        in_specs=[
            whole(sources, rows),
            whole(rows, sources),
            whole(sources, rows),
            whole(group, hidden),
            pl.BlockSpec((hidden, tile), lambda k, d: (0, d)),
            row_tile,
        ],
        out_specs=[
            pl.BlockSpec((1, 4, rows, tile), lambda k, d: (k, 0, 0, d)),
            pl.BlockSpec((1, 4 * capacity, tile), lambda k, d: (k, 0, d)),
            row_tile,
        ],
        compiler_params=pltpu.CompilerParams(vmem_limit_bytes=48 * 2**20),
        cost_estimate=pl.CostEstimate(
            flops=2 * chunks * group * width * (hidden + rows // 2),
            bytes_accessed=chunks * 2 * width * (3 * group + 4 * rows + hidden),
            transcendentals=0,
        ),
        name="expert_outputs",
    )(slots, columns, gates, hidden_rows, down_w, grad_rows)


def combine_rows(columns, kept, got, capacity):
    chunks, rows, _ = columns.shape
    width = kept.shape[2]
    tile = width // 4
    at = lambda k, d: (k, 0, d)
    half = pl.BlockSpec((1, rows // 2, tile), at)
    return pl.pallas_call(
        functools.partial(combine_kernel, capacity),
        out_shape=[jax.ShapeDtypeStruct((chunks, rows, width), bf16)]
        + [jax.ShapeDtypeStruct((chunks, rows // 2, width), bf16)] * 6,
        grid=(chunks, 4),
        in_specs=[
            pl.BlockSpec((1, rows, columns.shape[2]), lambda k, d: (k, 0, 0)),
            pl.BlockSpec((1, 4 * capacity, tile), at),
            pl.BlockSpec((1, 4, rows, tile), lambda k, d: (k, 0, 0, d)),
        ],
        out_specs=[pl.BlockSpec((1, rows, tile), at)] + [half] * 6,
        cost_estimate=pl.CostEstimate(
            flops=2 * chunks * rows * 4 * capacity * width,
            bytes_accessed=chunks * 2 * width * (8 * rows + 4 * capacity),
            transcendentals=0,
        ),
        name="combine_rows",
    )(columns, kept, got)


def flip(index, bit):
    return index + bit - 2 * bit * ((index // bit) % 2)


def neighbours():
    ctx, fsdp = lax.axis_index("ctx"), lax.axis_index("fsdp")
    return dict(
        core=(flip(ctx, 1), fsdp),
        x=(ctx, flip(fsdp, 1)),
        y=(ctx, flip(fsdp, 2)),
        z=[None, (flip(ctx, 2), fsdp), (flip(ctx, 4), fsdp), (flip(flip(ctx, 2), 4), fsdp)],
    )


def greet(partners):
    barrier = pltpu.get_barrier_semaphore()
    for partner in partners:
        pl.semaphore_signal(barrier, inc=1, device_id=partner, device_id_type=pl.DeviceIdType.MESH)
    pl.semaphore_wait(barrier, len(partners))


def send(source, target, sent, received, partner):
    return pltpu.make_async_remote_copy(
        src_ref=source,
        dst_ref=target,
        send_sem=sent,
        recv_sem=received,
        device_id=partner,
        device_id_type=pl.DeviceIdType.MESH,
    )


def gather_experts_kernel(
    capacity,
    steps,
    acts_ref,
    slot_ref,
    column_ref,
    gates_ref,
    back_ref,
    gate_ref,
    up_ref,
    rows_ref,
    hidden_ref,
    gate_low_ref,
    up_low_ref,
    kept_ref,
    got_ref,
    scalar_ref,
    buffer_ref,
    given_ref,
    gate_acc,
    up_acc,
    back_now,
    hidden_now,
    gate_low_now,
    up_low_now,
    z_sent,
    z_got,
    near_sent,
    near_got,
    far_sent,
    far_got,
    core_sent,
    core_got,
    given_sent,
    given_got,
    local,
):
    near = neighbours()
    chunks = slot_ref.shape[0]
    half = acts_ref.shape[0] // 2
    width = acts_ref.shape[1]
    tile = width // steps
    hidden_width = gate_ref.shape[1]
    group = 8 * capacity
    greet([near["core"], near["x"], near["y"]] + near["z"][1:])

    def along_z(s):
        return send(acts_ref, buffer_ref.at[s, 0, 0], z_sent.at[s - 1], z_got.at[s - 1], near["z"][s])

    def own(s):
        return acts_ref if s == 0 else buffer_ref.at[s, 0, 0]

    def to_near(s, k):
        return send(
            own(s), buffer_ref.at[s, 0, 1 + k], near_sent.at[s, k], near_got.at[s, k], near["xy"[k]]
        )

    def to_far(s, k):
        span = pl.ds(k * half, half)
        return send(
            buffer_ref.at[s, 0, 1 + k, span],
            buffer_ref.at[s, 0, 3, span],
            far_sent.at[s, k],
            far_got.at[s, k],
            near["yx"[k]],
        )

    def to_core(s, j):
        if j == 0:
            source, target = own(s), buffer_ref.at[s, 1, 0]
        elif j < 3:
            source, target = buffer_ref.at[s, 0, j], buffer_ref.at[s, 1, j]
        else:
            span = pl.ds((j - 3) * half, half)
            source, target = buffer_ref.at[s, 0, 3, span], buffer_ref.at[s, 1, 3, span]
        return send(source, target, core_sent.at[s, j], core_got.at[s, j], near["core"])

    def to_sibling(s):
        return send(given_ref.at[s], got_ref.at[s], given_sent.at[s], given_got.at[s], near["core"])

    def experts_step(s, buffer_blk, gate_blk, up_blk, rows_blk, given_blk, kept_blk):
        step = pl.program_id(0)

        @pl.when(step == 0)
        def _():
            gate_acc[...] = jnp.zeros_like(gate_acc)
            up_acc[...] = jnp.zeros_like(up_acc)

        @pl.when(step < steps)
        def _():
            for source in range(8):
                hot = hot_rows(slot_ref[s, source : source + 1, :], capacity).astype(bf16)
                rows_blk[source * capacity : (source + 1) * capacity, :] = jnp.dot(
                    hot, buffer_blk[source // 4, source % 4], preferred_element_type=f32
                ).astype(bf16)
            gate_acc[...] += jnp.dot(rows_blk[...], gate_blk[...], preferred_element_type=f32)
            up_acc[...] += jnp.dot(rows_blk[...], up_blk[...], preferred_element_type=f32)

        @pl.when(step == steps - 1)
        def _():
            for source in range(8):
                span = slice(source * capacity, (source + 1) * capacity)
                hot = hot_rows(slot_ref[s, source : source + 1, :], capacity)
                weighted = jnp.where(hot, gates_ref[s, source : source + 1, :], 0.0)
                gate_val = jnp.sum(weighted, axis=1, keepdims=True)
                gate_pre, up_pre, back = gate_acc[span, :], up_acc[span, :], back_now[span, :]
                sig = 1.0 / (1.0 + jnp.exp(-gate_pre))
                silu = gate_pre * sig
                hidden = (silu * up_pre).astype(bf16)
                hidden_now[span, :] = hidden
                scalar = jnp.sum(hidden.astype(f32) * back, axis=1, keepdims=True)
                scalar_ref[s, source : source + 1, :] = jnp.sum(
                    jnp.where(hot, scalar, 0.0), axis=0, keepdims=True
                )
                hidden_grad = gate_val * back
                gate_low_now[span, :] = (
                    hidden_grad * up_pre * sig * (1.0 + gate_pre * (1.0 - sig))
                ).astype(bf16)
                up_low_now[span, :] = (hidden_grad * silu).astype(bf16)

        @pl.when(step >= steps)
        def _():
            last = (((1,), (1,)), ((), ()))
            row_grad = lax.dot_general(
                gate_low_now[...], gate_blk[...], last, preferred_element_type=f32
            )
            row_grad += lax.dot_general(
                up_low_now[...], up_blk[...], last, preferred_element_type=f32
            )
            row_grad = row_grad.astype(bf16)
            kept_blk[...] = row_grad[: 4 * capacity]
            for k in range(4):
                hot = hot_columns(column_ref[s, :, 4 + k : 5 + k], capacity)
                given_blk[k] = jnp.dot(
                    hot, row_grad[(4 + k) * capacity : (5 + k) * capacity], preferred_element_type=f32
                ).astype(bf16)

    def compute(s):
        fetch = pltpu.make_async_copy(back_ref.at[s], back_now, local.at[0])
        fetch.start()
        fetch.wait()
        weight = pl.BlockSpec((tile, hidden_width), lambda d: (d % steps, 0))
        pltpu.emit_pipeline(
            functools.partial(experts_step, s),
            grid=(2 * steps,),
            in_specs=[
                pl.BlockSpec((2, 4, 2 * half, tile), lambda d: (0, 0, 0, jnp.minimum(d, steps - 1))),
                weight,
                weight,
            ],
            out_specs=[
                pl.BlockSpec((group, tile), lambda d: (0, jnp.minimum(d, steps - 1))),
                pl.BlockSpec((4, 2 * half, tile), lambda d: (0, 0, jnp.maximum(d - steps, 0))),
                pl.BlockSpec((4 * capacity, tile), lambda d: (0, jnp.maximum(d - steps, 0))),
            ],
        )(
            buffer_ref.at[s],
            gate_ref,
            up_ref,
            rows_ref.at[s],
            given_ref.at[s],
            kept_ref.at[s],
        )
        stores = [
            pltpu.make_async_copy(now, whole.at[s], local.at[1 + i])
            for i, (now, whole) in enumerate(
                ((hidden_now, hidden_ref), (gate_low_now, gate_low_ref), (up_low_now, up_low_ref))
            )
        ]
        for store in stores:
            store.start()
        for store in stores:
            store.wait()

    along_z(1).start()
    to_near(0, 0).start()
    to_near(0, 1).start()
    to_core(0, 0).start()
    keep = pltpu.make_async_copy(acts_ref, buffer_ref.at[0, 0, 0], local.at[0])
    keep.start()
    keep.wait()
    for s in range(chunks):
        for k in range(2):
            to_near(s, k).wait_recv()
            to_far(s, k).start()
            to_core(s, 1 + k).start()
        if s + 1 < chunks:
            along_z(s + 1).wait_recv()
            if s + 2 < chunks:
                along_z(s + 2).start()
            to_near(s + 1, 0).start()
            to_near(s + 1, 1).start()
            to_core(s + 1, 0).start()
        for k in range(2):
            to_far(s, k).wait_recv()
            to_core(s, 3 + k).start()
        for j in range(5):
            to_core(s, j).wait_recv()
        compute(s)
        to_sibling(s).start()
    for s in range(chunks):
        if s:
            along_z(s).wait_send()
        for k in range(2):
            to_near(s, k).wait_send()
            to_far(s, k).wait_send()
        for j in range(5):
            to_core(s, j).wait_send()
        to_sibling(s).wait()


def gather_experts(acts, slots, columns, gates, back, gate_w, up_w, capacity):
    chunks, sources, rows = slots.shape
    width, hidden = gate_w.shape
    group = sources * capacity
    steps = 4
    anywhere = pl.BlockSpec(memory_space=pl.ANY)
    held = pl.BlockSpec(memory_space=pltpu.VMEM)
    dma = pltpu.SemaphoreType.DMA
    return pl.pallas_call(
        functools.partial(gather_experts_kernel, capacity, steps),
        out_shape=(
            jax.ShapeDtypeStruct((chunks, group, width), bf16),
            jax.ShapeDtypeStruct((chunks, group, hidden), bf16),
            jax.ShapeDtypeStruct((chunks, group, hidden), bf16),
            jax.ShapeDtypeStruct((chunks, group, hidden), bf16),
            jax.ShapeDtypeStruct((chunks, 4 * capacity, width), bf16),
            jax.ShapeDtypeStruct((chunks, 4, rows, width), bf16),
            jax.ShapeDtypeStruct((chunks, sources, rows), f32),
            jax.ShapeDtypeStruct((chunks, 2, 4, rows, width), bf16),
            jax.ShapeDtypeStruct((chunks, 4, rows, width), bf16),
        ),
        in_specs=[held, held, held, held, anywhere, anywhere, anywhere],
        out_specs=[anywhere] * 6 + [held, anywhere, anywhere],
        scratch_shapes=[
            pltpu.VMEM((group, hidden), f32),
            pltpu.VMEM((group, hidden), f32),
            pltpu.VMEM((group, hidden), f32),
            pltpu.VMEM((group, hidden), bf16),
            pltpu.VMEM((group, hidden), bf16),
            pltpu.VMEM((group, hidden), bf16),
            dma((chunks - 1,)),
            dma((chunks - 1,)),
            dma((chunks, 2)),
            dma((chunks, 2)),
            dma((chunks, 2)),
            dma((chunks, 2)),
            dma((chunks, 5)),
            dma((chunks, 5)),
            dma((chunks,)),
            dma((chunks,)),
            dma((4,)),
        ],
        compiler_params=pltpu.CompilerParams(
            collective_id=1, has_side_effects=True, vmem_limit_bytes=56 * 2**20
        ),
        cost_estimate=pl.CostEstimate(
            flops=2 * chunks * group * width * (4 * hidden + rows + rows // 2),
            bytes_accessed=chunks * 2 * (width * (4 * sources * rows + 4 * hidden) + 6 * group * hidden),
            transcendentals=chunks * group * hidden,
        ),
        name="gather_experts",
    )(acts, slots, columns, gates, back, gate_w, up_w)


def return_rows_kernel(
    capacity,
    column_ref,
    kept_ref,
    got_ref,
    out_ref,
    kept_now,
    sums,
    relay,
    from_x,
    from_y,
    own,
    from_z,
    kept_sem,
    got_sem,
    first_sent,
    first_got,
    second_sent,
    second_got,
    z_sent,
    z_got,
):
    near = neighbours()
    chunks, rows = sums.shape[0], sums.shape[2]
    half = rows // 2
    low, high = pl.ds(0, half), pl.ds(half, half)
    greet([near["x"], near["y"]] + near["z"][1:])
    order = list(range(chunks))[::-1]

    def fetch(s):
        return (
            pltpu.make_async_copy(kept_ref.at[s], kept_now.at[s], kept_sem.at[s]),
            pltpu.make_async_copy(got_ref.at[s], sums.at[s], got_sem.at[s]),
        )

    def first(s, i):
        source, target, partner = (
            (sums.at[s, 3, low], relay.at[s, 0], near["x"]),
            (sums.at[s, 3, high], relay.at[s, 1], near["y"]),
            (sums.at[s, 1, low], from_x.at[s, low], near["x"]),
            (sums.at[s, 2, high], from_y.at[s, high], near["y"]),
        )[i]
        return send(source, target, first_sent.at[s, i], first_got.at[s, i], partner)

    def second(s, i):
        source, target, partner = (
            (sums.at[s, 2, low], from_y.at[s, low], near["y"]),
            (sums.at[s, 1, high], from_x.at[s, high], near["x"]),
        )[i]
        return send(source, target, second_sent.at[s, i], second_got.at[s, i], partner)

    def along_z(s):
        return send(own.at[s], from_z.at[s - 1], z_sent.at[s - 1], z_got.at[s - 1], near["z"][s])

    for s in order:
        for copy in fetch(s):
            copy.start()
    tile = 256
    for s in order:
        for copy in fetch(s):
            copy.wait()

        def combine(d, carry):
            cols = pl.ds(pl.multiple_of(d * tile, tile), tile)
            for k in range(4):
                hot = hot_columns(column_ref[s, :, k : k + 1], capacity)
                part = jnp.dot(
                    hot,
                    kept_now[s, k * capacity : (k + 1) * capacity, cols],
                    preferred_element_type=f32,
                )
                sums[s, k, :, cols] = (part + sums[s, k, :, cols].astype(f32)).astype(bf16)
            return carry

        lax.fori_loop(0, sums.shape[3] // tile, combine, 0)
        for i in range(4):
            first(s, i).start()
    for s in order:
        for i in range(2):
            first(s, i).wait_recv()
        sums[s, 2, :half] = (sums[s, 2, :half].astype(f32) + relay[s, 0].astype(f32)).astype(bf16)
        sums[s, 1, half:] = (sums[s, 1, half:].astype(f32) + relay[s, 1].astype(f32)).astype(bf16)
        for i in range(2):
            second(s, i).start()
    for s in order:
        for i in range(2):
            first(s, 2 + i).wait_recv()
            second(s, i).wait_recv()
        total = sums[s, 0].astype(f32) + from_x[s].astype(f32) + from_y[s].astype(f32)
        if s:
            own[s] = total.astype(bf16)
            along_z(s).start()
        else:
            out_ref[...] = total
    for s in order[:-1]:
        along_z(s).wait_recv()
        out_ref[...] += from_z[s - 1].astype(f32)
    for s in order:
        for i in range(4):
            first(s, i).wait_send()
        for i in range(2):
            second(s, i).wait_send()
        if s:
            along_z(s).wait_send()


def return_rows(columns, kept, got, capacity):
    chunks, rows, _ = columns.shape
    width = kept.shape[2]
    held = pl.BlockSpec(memory_space=pltpu.VMEM)
    anywhere = pl.BlockSpec(memory_space=pl.ANY)
    dma = pltpu.SemaphoreType.DMA
    return pl.pallas_call(
        functools.partial(return_rows_kernel, capacity),
        out_shape=jax.ShapeDtypeStruct((rows, width), f32),
        in_specs=[held, anywhere, anywhere],
        out_specs=held,
        scratch_shapes=[
            pltpu.VMEM((chunks, 4 * capacity, width), bf16),
            pltpu.VMEM((chunks, 4, rows, width), bf16),
            pltpu.VMEM((chunks, 2, rows // 2, width), bf16),
            pltpu.VMEM((chunks, rows, width), bf16),
            pltpu.VMEM((chunks, rows, width), bf16),
            pltpu.VMEM((chunks, rows, width), bf16),
            pltpu.VMEM((chunks - 1, rows, width), bf16),
            dma((chunks,)),
            dma((chunks,)),
            dma((chunks, 4)),
            dma((chunks, 4)),
            dma((chunks, 2)),
            dma((chunks, 2)),
            dma((chunks - 1,)),
            dma((chunks - 1,)),
        ],
        compiler_params=pltpu.CompilerParams(
            collective_id=2, has_side_effects=True, vmem_limit_bytes=60 * 2**20
        ),
        cost_estimate=pl.CostEstimate(
            flops=2 * chunks * rows * 4 * capacity * width,
            bytes_accessed=chunks * 2 * width * (8 * rows + 4 * capacity),
            transcendentals=0,
        ),
        name="return_rows",
    )(columns, kept, got)


def fast_body(
    n_ctx,
    tokens,
    positions,
    expert_ids,
    attn_gain,
    query_key_value_weight,
    q_gain,
    k_gain,
    output_weight,
    ffn_gain,
    router_weight,
    w_gate,
    w_up,
    w_down,
    cotangent,
):
    n_fsdp = 4
    n_all = n_ctx * n_fsdp
    ctx_at = lax.axis_index("ctx")
    fsdp_at = lax.axis_index("fsdp")
    core_at = ctx_at % 2
    own_at = ctx_at * n_fsdp + fsdp_at
    row_count = tokens.shape[1]
    model_width = tokens.shape[2]
    head_dim = q_gain.shape[0]
    shard_rows = query_key_value_weight.shape[0]
    heads = output_weight.shape[0] // head_dim
    q_width = heads * head_dim
    all_q = q_width * n_fsdp
    kv_heads = (query_key_value_weight.shape[1] - all_q) // (2 * head_dim)
    own_width = q_width + 2 * head_dim
    expert_count = n_all
    top_count = expert_ids.shape[2]
    capacity = row_count * top_count * 3 // (2 * expert_count)
    z_count = n_ctx // 2
    chunk_rows = 2 * n_fsdp * capacity

    inputs = tokens.reshape(row_count, model_width).astype(f32)
    places = positions.reshape(row_count)
    chosen = expert_ids.reshape(row_count, top_count)
    grad_res_low = cotangent.reshape(row_count, model_width)
    grad_res = grad_res_low.astype(f32)

    relative = jnp.bitwise_xor(own_at, jnp.arange(n_all, dtype=jnp.int32))
    chosen_rel = (chosen[:, :, None] == relative[None, None, :]).astype(f32)
    named = jnp.sum(chosen_rel, axis=1).T
    first_block = jnp.broadcast_to((places[0] // run_rows).astype(f32), (n_all, 128))
    small = exchange_small(jnp.concatenate([named, first_block], axis=1), n_ctx)
    named_here = small[:, :row_count]
    block_table = small[:, row_count].astype(jnp.int32).reshape(n_ctx, n_fsdp)

    rms_one = lax.rsqrt(jnp.mean(inputs * inputs, axis=-1, keepdims=True) + eps_norm)
    acts = (inputs * rms_one * attn_gain).astype(bf16)
    acts_group = jnp.concatenate(plane_gather(acts), axis=0)

    def columns_of(weight_rows, group):
        return jnp.concatenate(
            [
                lax.dynamic_slice_in_dim(weight_rows, group * q_width, q_width, 1),
                lax.dynamic_slice_in_dim(weight_rows, all_q + group * head_dim, head_dim, 1),
                lax.dynamic_slice_in_dim(
                    weight_rows, all_q + (kv_heads + group) * head_dim, head_dim, 1
                ),
            ],
            axis=1,
        )

    half_shard = shard_rows // 2
    half_weight = lax.dynamic_slice_in_dim(
        query_key_value_weight, core_at * half_shard, half_shard, 0
    )
    weight_pieces = [columns_of(query_key_value_weight, fsdp_at)]
    for k in range(1, n_fsdp):
        got = swap(columns_of(half_weight, fsdp_at ^ k), "fsdp", n_fsdp, k)
        other = swap(got, "ctx", n_ctx, 1)
        weight_pieces.append(
            jnp.where(
                core_at == 0,
                jnp.concatenate([got, other], axis=0),
                jnp.concatenate([other, got], axis=0),
            )
        )
    weight_qkv = by_fsdp(weight_pieces, fsdp_at).reshape(n_fsdp * shard_rows, own_width)

    group_rows = n_fsdp * row_count
    blocks_total = 2 * n_ctx
    own_blocks = block_table[0]
    run_blocks = jnp.stack([own_blocks, blocks_total - 1 - own_blocks], axis=1)
    row_places = (
        run_blocks[:, :, None] * run_rows + jnp.arange(run_rows, dtype=jnp.int32)[None, None, :]
    ).reshape(n_fsdp, row_count, 1)
    angles = row_places.astype(f32) * frequencies(head_dim)
    cosine, sine = jnp.cos(angles), jnp.sin(angles)
    cosine = jnp.concatenate([cosine, cosine], axis=-1)
    sine = jnp.concatenate([-sine, sine], axis=-1)
    block_index = jnp.arange(blocks_total, dtype=jnp.int32)
    slot_index = jnp.arange(n_ctx, dtype=jnp.int32)[:, None, None]
    source_table = jnp.sum(
        jnp.where(block_table[:, :, None] == block_index, 2 * slot_index, 0)
        + jnp.where(blocks_total - 1 - block_table[:, :, None] == block_index, 2 * slot_index + 1, 0),
        axis=0,
    )
    place_list = run_blocks.reshape(-1)
    source_list = source_table.reshape(-1)

    projected, query_low, kv_own = project(
        acts_group.reshape(n_fsdp, row_count, model_width),
        weight_qkv,
        cosine,
        sine,
        q_gain[None],
        k_gain[None],
        heads,
    )

    grad_slots = jnp.stack(
        [grad_res_low] + [swap(grad_res_low, "ctx", n_ctx, 2 * k) for k in range(1, z_count)]
    )
    grad_slots = after(grad_slots, projected)
    half_rows = row_count // 2
    grad_x = swap(grad_slots, "fsdp", n_fsdp, 1)
    grad_y = swap(grad_slots, "fsdp", n_fsdp, 2)

    kv_slots = [kv_own] + [swap(kv_own, "ctx", n_ctx, 2 * k) for k in range(1, z_count)]
    kv_slots = jnp.stack(kv_slots)
    kv_all = jnp.stack([kv_slots, swap(kv_slots, "ctx", n_ctx, 1)], axis=1)
    kv_all = kv_all.reshape(n_ctx, n_fsdp, row_count, 2 * head_dim)

    mixed, lse = attend(place_list, source_list, query_low, kv_all)
    heads_low = mixed.reshape(group_rows, q_width)
    grad_x, grad_y = after((grad_x, grad_y), mixed)
    grad_pieces = [
        grad_slots,
        grad_x,
        grad_y,
        swap(grad_x[:, :half_rows], "fsdp", n_fsdp, 2),
        swap(grad_y[:, half_rows:], "fsdp", n_fsdp, 1),
    ]

    resid_parts = jnp.dot(heads_low, output_weight, preferred_element_type=f32).astype(bf16)
    resid = inputs + scatter_parts(resid_parts.reshape(n_fsdp, row_count, model_width))
    rms_two = lax.rsqrt(jnp.mean(resid * resid, axis=-1, keepdims=True) + eps_norm)
    acts_two = (resid * rms_two * ffn_gain).astype(bf16)

    full_router = by_fsdp(
        [router_weight] + [swap(router_weight, "fsdp", n_fsdp, k) for k in range(1, n_fsdp)], fsdp_at
    ).reshape(n_fsdp * shard_rows, expert_count)
    logits = jnp.dot(acts_two, full_router, preferred_element_type=f32)
    pick_table = (chosen[:, :, None] == jnp.arange(expert_count)[None, None, :]).astype(f32)
    picked = jnp.sum(logits[:, None, :] * pick_table, axis=-1)
    gate_vals, gate_back = jax.vjp(lambda values: jax.nn.softmax(values, axis=-1), picked)
    gates_rel = jnp.sum(chosen_rel * gate_vals[:, :, None], axis=1).T
    gates_here = exchange_small(gates_rel, n_ctx)

    upper = jnp.triu(jnp.ones((row_count, row_count), bf16), 1)
    rank = jnp.dot(named_here.astype(bf16), upper, preferred_element_type=f32)
    slots = jnp.where(named_here > 0.5, rank, -1.0).reshape(z_count, 2 * n_fsdp, row_count)
    columns = jnp.swapaxes(slots, 1, 2)
    gates = gates_here.reshape(z_count, 2 * n_fsdp, row_count)
    gate_w = w_gate[0]
    up_w = w_up[0]
    down_w = w_down[0]

    grad_pieces = after(grad_pieces, acts_two)
    grad_pieces = grad_pieces + [swap(piece, "ctx", n_ctx, 1) for piece in grad_pieces]
    grad_rows, down_back = select_grad_rows(slots, grad_pieces, down_w, capacity)

    def reduce_plane(first, count, given, kept):
        got = swap(given, "ctx", n_ctx, 1)
        return plane_scatter(*combine_rows(columns[first : first + count], kept, got, capacity))

    def reduce_along_z(first, reduced):
        total = None
        for i in range(reduced.shape[0]):
            own = reduced[i]
            if first + i:
                own = swap(own.astype(bf16), "ctx", n_ctx, 2 * (first + i)).astype(f32)
            total = own if total is None else total + own
        return total

    act_rows, hidden_rows, gate_lows, up_lows, kept, got, scalars, _, _ = gather_experts(
        acts_two, slots, columns, gates, down_back, gate_w, up_w, capacity
    )
    gate_grad_here = scalars.reshape(n_all, row_count)
    acts_two_grad = return_rows(columns, kept, got, capacity)
    experts_done = acts_two_grad

    gate_grad_rel = exchange_small(gate_grad_here, n_ctx)
    gate_grad = jnp.sum(chosen_rel * gate_grad_rel.T[:, None, :], axis=-1)
    (picked_grad,) = gate_back(gate_grad)
    logit_grad = jnp.sum(picked_grad[:, :, None] * pick_table, axis=1).astype(bf16)
    acts_two_grad = acts_two_grad + jnp.dot(
        logit_grad, full_router.T, preferred_element_type=f32
    )

    scaled = ffn_gain * acts_two_grad
    grad_ffn_gain = jnp.sum(acts_two_grad * resid * rms_two, axis=0)
    resid_grad = (
        grad_res
        + rms_two * scaled
        - resid * (rms_two**3 * jnp.mean(scaled * resid, axis=-1, keepdims=True))
    )
    attn_grad = resid_grad.astype(bf16)
    attn_grad_group = jnp.concatenate(plane_gather(attn_grad), axis=0)
    heads_grad = jnp.einsum(
        "td,cd->tc", attn_grad_group, output_weight, preferred_element_type=f32
    ).astype(bf16)
    grad_w_out = jnp.einsum(
        "tc,td->cd", heads_low, attn_grad_group, preferred_element_type=f32
    ).astype(bf16)
    dq, dkv, dq_gain = attend_back(
        place_list,
        source_list,
        query_low,
        kv_all,
        mixed,
        heads_grad.reshape(n_fsdp, row_count, q_width),
        lse,
        projected,
        cosine,
        sine,
        q_gain[None],
    )
    proj_low_q = dq.reshape(group_rows, q_width)

    held = dkv.reshape(z_count, 2, n_fsdp, row_count, 2 * head_dim)
    held = (held[:, 0].astype(f32) + swap(held[:, 1], "ctx", n_ctx, 1).astype(f32)).astype(bf16)
    held = [held[0]] + [swap(held[k], "ctx", n_ctx, 2 * k) for k in range(1, z_count)]
    dkv_own, dk_gain = key_back(held, projected, cosine, sine, k_gain[None])
    proj_low_kv = dkv_own.reshape(group_rows, 2 * head_dim)
    grad_q_gain = jnp.sum(dq_gain, axis=0)
    grad_k_gain = jnp.sum(dk_gain, axis=0)
    acts_parts = jnp.einsum(
        "tc,dc->td", proj_low_q, weight_qkv[:, :q_width], preferred_element_type=f32
    ) + jnp.einsum("tc,dc->td", proj_low_kv, weight_qkv[:, q_width:], preferred_element_type=f32)
    acts_grad = scatter_parts(
        acts_parts.astype(bf16).reshape(n_fsdp, row_count, model_width)
    )
    scaled = attn_gain * acts_grad
    grad_attn_gain = jnp.sum(acts_grad * inputs * rms_one, axis=0)
    grad_tokens = (
        resid_grad
        + rms_one * scaled
        - inputs * (rms_one**3 * jnp.mean(scaled * inputs, axis=-1, keepdims=True))
    ).reshape(tokens.shape)

    def own_qkv_rows(proj_low):
        grad = jnp.einsum("td,tc->dc", acts_group, proj_low, preferred_element_type=f32)
        rows = ctx_scatter(
            grad.astype(bf16).reshape(n_ctx, n_fsdp, -1, proj_low.shape[1]), n_ctx, ctx_at, True
        )
        pieces = [pick(rows, fsdp_at)] + [
            swap(pick(rows, fsdp_at ^ k), "fsdp", n_fsdp, k) for k in range(1, n_fsdp)
        ]
        return by_fsdp(pieces, fsdp_at)

    q_rows = own_qkv_rows(after(proj_low_q, dkv_own))
    kv_rows = own_qkv_rows(proj_low_kv)
    out_rows = q_rows.shape[1]

    def side_by_side(pieces):
        return jnp.swapaxes(pieces, 0, 1).reshape(out_rows, -1)

    grad_w_qkv = jnp.concatenate(
        [
            side_by_side(q_rows),
            side_by_side(kv_rows[:, :, :head_dim]),
            side_by_side(kv_rows[:, :, head_dim:]),
        ],
        axis=1,
    )

    per_ctx = grad_w_out.shape[0] // n_ctx
    grad_w_out = ctx_scatter(
        grad_w_out.reshape(n_ctx, per_ctx, model_width), n_ctx, ctx_at, True
    ).astype(bf16)
    grad_w_out = lax.ppermute(
        grad_w_out,
        ("ctx", "fsdp"),
        [(c * n_fsdp + f, f * n_ctx + c) for c in range(n_ctx) for f in range(n_fsdp)],
    ).astype(f32)

    router_acts = after(acts_two, attn_grad_group)
    grad_w_router = jnp.einsum("td,te->de", router_acts, logit_grad, preferred_element_type=f32)
    grad_w_router = ctx_scatter(
        grad_w_router.reshape(n_ctx, n_fsdp, -1, expert_count), n_ctx, ctx_at, False
    )
    bit = 1
    while bit < n_fsdp:
        mine = (fsdp_at // bit) % 2
        split = grad_w_router.reshape((-1, 2) + grad_w_router.shape[1:])
        keep = lax.dynamic_index_in_dim(split, mine, 1, keepdims=False)
        away = lax.dynamic_index_in_dim(split, 1 - mine, 1, keepdims=False)
        grad_w_router = keep + swap(away, "fsdp", n_fsdp, bit)
        bit *= 2
    grad_w_router = grad_w_router[0]

    given, kept, out_grad = expert_outputs(
        after(slots, experts_done), columns, gates, hidden_rows, down_w, grad_rows, capacity
    )
    given = after(given, attn_grad_group)
    result = resid + reduce_along_z(0, reduce_plane(0, z_count, given, kept))
    output = result.astype(bf16).reshape(tokens.shape)
    row_total = z_count * chunk_rows

    def weight_grad(left, right):
        return jnp.einsum(
            "rd,rf->df",
            left.reshape(row_total, -1),
            right.reshape(row_total, -1),
            preferred_element_type=f32,
        )[None]

    grad_w_down = weight_grad(hidden_rows, out_grad)
    grad_w_gate = weight_grad(act_rows, gate_lows)
    grad_w_up = weight_grad(act_rows, up_lows)

    gains = sum_everywhere(
        jnp.concatenate([grad_attn_gain, grad_ffn_gain, grad_q_gain, grad_k_gain]), n_ctx
    )
    grad_attn_gain = gains[:model_width]
    grad_ffn_gain = gains[model_width : 2 * model_width]
    grad_q_gain = gains[2 * model_width : 2 * model_width + head_dim]
    grad_k_gain = gains[2 * model_width + head_dim :]
    return (
        output,
        grad_tokens,
        grad_attn_gain,
        grad_w_qkv,
        grad_q_gain,
        grad_k_gain,
        grad_w_out,
        grad_ffn_gain,
        grad_w_router,
        grad_w_gate,
        grad_w_up,
        grad_w_down,
    )


def solution(mesh):
    n_ctx, n_fsdp = mesh.shape["ctx"], mesh.shape["fsdp"]

    def body(*arrays):
        heads_kv = (arrays[4].shape[1] - arrays[7].shape[0] * n_fsdp) // (2 * arrays[5].shape[0])
        if n_fsdp == 4 and heads_kv == n_fsdp and n_ctx == 8:
            return fast_body(n_ctx, *arrays)
        return general_body(*arrays)

    whole = P(("ctx", "fsdp"), None, None)
    rows = P(("ctx", "fsdp"), None)
    split = P("fsdp", "ctx", None)
    return jax.shard_map(
        body,
        mesh=mesh,
        in_specs=(
            split,
            P("fsdp", "ctx"),
            split,
            P(),
            P("fsdp", None),
            P(),
            P(),
            P("fsdp", None),
            P(),
            P("fsdp", None),
            whole,
            whole,
            whole,
            split,
        ),
        out_specs=(split, split, P(), rows, P(), P(), rows, P(), rows, whole, whole, whole),
        check_vma=False,
    )
```

```python
import functools
import math

import jax
import jax.numpy as jnp
from jax import lax
from jax.experimental import pallas as pl
from jax.experimental.pallas import tpu as pltpu
from jax.sharding import PartitionSpec as P

eps_norm = 1e-06
rope_base = 1000000.0
masked_value = -1e30
run_rows = 128
bf16 = jnp.bfloat16
f32 = jnp.float32


def rms_scale(values, gain):
    mean_sq = jnp.mean(values * values, axis=-1, keepdims=True)
    return values * lax.rsqrt(mean_sq + eps_norm) * gain


def frequencies(head_dim):
    return 1.0 / rope_base ** (jnp.arange(0, head_dim, 2).astype(jnp.float32) / head_dim)


def rotate(values, angles):
    half_dim = values.shape[-1] // 2
    cosine = jnp.cos(angles)
    sine_val = jnp.sin(angles)
    first_half = values[..., :half_dim]
    second_half = values[..., half_dim:]
    return jnp.concatenate(
        [
            first_half * cosine - second_half * sine_val,
            second_half * cosine + first_half * sine_val,
        ],
        axis=-1,
    )


def head_prep(projected, gain_q, gain_k, angles, heads_q, heads_kv):
    head_dim = gain_q.shape[0]
    row_count = projected.shape[0]
    q_width = heads_q * head_dim
    kv_width = heads_kv * head_dim
    queries = projected[:, :q_width].reshape(row_count, heads_q, head_dim)
    key_heads = projected[:, q_width : q_width + kv_width].reshape(row_count, heads_kv, head_dim)
    value_heads = projected[:, q_width + kv_width :].reshape(row_count, heads_kv, head_dim)
    queries = rotate(rms_scale(queries, gain_q), angles)
    key_heads = rotate(rms_scale(key_heads, gain_k), angles)
    return (queries, key_heads, value_heads)


def general_body(
    tokens,
    positions,
    expert_ids,
    attn_gain,
    query_key_value_weight,
    q_gain,
    k_gain,
    output_weight,
    ffn_gain,
    router_weight,
    w_gate,
    w_up,
    w_down,
    cotangent,
):
    row_count = tokens.shape[1]
    model_width = tokens.shape[2]
    head_dim = q_gain.shape[0]
    inputs = tokens.reshape(row_count, model_width).astype(jnp.float32)
    places = positions.reshape(row_count)
    chosen = expert_ids.reshape(row_count, -1)
    top_count = chosen.shape[1]
    full_qkv, full_out, full_router = (
        lax.all_gather(query_key_value_weight, "fsdp", axis=0, tiled=True),
        lax.all_gather(output_weight, "fsdp", axis=0, tiled=True),
        lax.all_gather(router_weight, "fsdp", axis=0, tiled=True),
    )
    heads_q = full_out.shape[0] // head_dim
    heads_kv = (full_qkv.shape[1] - full_out.shape[0]) // (2 * head_dim)
    group_size = heads_q // heads_kv
    expert_count = full_router.shape[1]
    capacity = row_count * top_count * 3 // (2 * expert_count)
    local_experts = w_gate.shape[0]
    score_scale = 1.0 / math.sqrt(head_dim)
    normed, norm_back = jax.vjp(rms_scale, inputs, attn_gain)
    first_activations = normed.astype(jnp.bfloat16)
    query_key_value_projected = jnp.dot(
        first_activations, full_qkv, preferred_element_type=jnp.float32
    )
    angles = places.astype(jnp.float32)[:, None, None] * frequencies(head_dim)[None, None, :]

    def prepare(proj_in, gain_q, gain_k):
        return head_prep(proj_in, gain_q, gain_k, angles, heads_q, heads_kv)

    (queries, key_heads, value_heads), prep_back = jax.vjp(
        prepare, query_key_value_projected, q_gain, k_gain
    )
    query_low = queries.astype(jnp.bfloat16).reshape(row_count, heads_kv, group_size, head_dim)
    key_low = key_heads.astype(jnp.bfloat16)
    value_low = value_heads.astype(jnp.bfloat16)
    all_keys, all_values = (
        lax.all_gather(key_low, "ctx", axis=0, tiled=True),
        lax.all_gather(value_low, "ctx", axis=0, tiled=True),
    )
    key_places = lax.all_gather(places, "ctx", axis=0, tiled=True)
    seq_len = all_keys.shape[0]
    sorted_keys = jnp.zeros_like(all_keys).at[key_places].set(all_keys)
    sorted_values = jnp.zeros_like(all_values).at[key_places].set(all_values)
    block_len = min(512, seq_len)
    run_len = row_count // 2

    def block_scores(query_run, place_run, block_index):
        start = block_index * block_len
        key_blk = lax.dynamic_slice_in_dim(sorted_keys, start, block_len, 0)
        value_blk = lax.dynamic_slice_in_dim(sorted_values, start, block_len, 0)
        raw_scores = (
            jnp.einsum("qhgd,khd->hgqk", query_run, key_blk, preferred_element_type=jnp.float32)
            * score_scale
        )
        key_pos = start + jnp.arange(block_len, dtype=jnp.int32)
        visible = key_pos[None, :] <= place_run[:, None]
        return (jnp.where(visible, raw_scores, masked_value), visible, key_blk, value_blk)

    run_info = []
    mixed_runs = []
    for run_index in range(2):
        query_run = query_low[run_index * run_len : (run_index + 1) * run_len]
        place_run = places[run_index * run_len : (run_index + 1) * run_len]
        block_total = jnp.max(place_run) // block_len + 1

        def stats_step(block_index, carried):
            run_max, run_sum = carried
            scores, visible, key_blk, value_blk = block_scores(query_run, place_run, block_index)
            new_max = jnp.maximum(run_max, jnp.max(scores, axis=-1))
            weights = jnp.where(visible, jnp.exp(scores - new_max[..., None]), 0.0)
            run_sum = run_sum * jnp.exp(run_max - new_max) + jnp.sum(weights, axis=-1)
            return (new_max, run_sum)

        stat_shape = (heads_kv, group_size, run_len)
        initial = (
            jnp.full(stat_shape, masked_value, jnp.float32),
            jnp.zeros(stat_shape, jnp.float32),
        )
        run_max, run_sum = lax.fori_loop(0, block_total, stats_step, initial)
        log_total = run_max + jnp.log(run_sum)

        def output_step(block_index, running):
            scores, visible, key_blk, value_blk = block_scores(query_run, place_run, block_index)
            prob_vals = jnp.exp(scores - log_total[..., None])
            return running + jnp.einsum(
                "hgqk,khd->qhgd",
                prob_vals.astype(jnp.bfloat16),
                value_blk,
                preferred_element_type=jnp.float32,
            )

        mixed_run = lax.fori_loop(
            0,
            block_total,
            output_step,
            jnp.zeros((run_len, heads_kv, group_size, head_dim), jnp.float32),
        )
        mixed_runs.append(mixed_run)
        run_info.append((query_run, place_run, block_total, log_total))
    heads_out = jnp.concatenate(mixed_runs, axis=0)
    heads_reduced_precision = heads_out.reshape(row_count, heads_q * head_dim).astype(jnp.bfloat16)
    residual_stream = inputs + jnp.dot(
        heads_reduced_precision, full_out, preferred_element_type=jnp.float32
    )
    normed_two, norm_two_back = jax.vjp(rms_scale, residual_stream, ffn_gain)
    second_activations = normed_two.astype(jnp.bfloat16)
    router_logits = jnp.dot(second_activations, full_router, preferred_element_type=jnp.float32)
    pick_table = (chosen[:, :, None] == jnp.arange(expert_count)[None, None, :]).astype(jnp.float32)
    picked = jnp.sum(router_logits[:, None, :] * pick_table, axis=-1)
    gate_vals, gate_back = jax.vjp(lambda values: jax.nn.softmax(values, axis=-1), picked)
    flat_choice = chosen.reshape(-1)
    slot_hot = (flat_choice[:, None] == jnp.arange(expert_count)[None, :]).astype(jnp.int32)
    slot_rank = jnp.sum((jnp.cumsum(slot_hot, axis=0) - slot_hot) * slot_hot, axis=1)
    targets = flat_choice * capacity + slot_rank
    source_rows = jnp.repeat(second_activations, top_count, axis=0)
    outgoing = (
        jnp.zeros((expert_count * capacity, model_width), jnp.bfloat16).at[targets].set(source_rows)
    )
    outgoing = outgoing.reshape(expert_count, capacity, model_width)
    arrived = lax.all_to_all(outgoing, ("ctx", "fsdp"), split_axis=0, concat_axis=0, tiled=True)
    sources = arrived.shape[0] // local_experts
    slot_count = arrived.shape[1]
    grouped = arrived.reshape(sources, local_experts, slot_count, model_width)
    gate_pre = jnp.einsum("secd,edf->secf", grouped, w_gate, preferred_element_type=jnp.float32)
    up_pre = jnp.einsum("secd,edf->secf", grouped, w_up, preferred_element_type=jnp.float32)
    hidden = (jax.nn.silu(gate_pre) * up_pre).astype(jnp.bfloat16)
    produced = jnp.einsum("secf,efd->secd", hidden, w_down, preferred_element_type=jnp.float32)
    produced = produced.astype(jnp.bfloat16).reshape(arrived.shape)
    flat_shape = (arrived.shape[0], slot_count, gate_pre.shape[3])
    expert_results = (produced, arrived, gate_pre.reshape(flat_shape), up_pre.reshape(flat_shape))
    produced = expert_results[0]
    arrived = expert_results[1]
    returned = lax.all_to_all(produced, ("ctx", "fsdp"), split_axis=0, concat_axis=0, tiled=True)
    expert_rows = returned.reshape(expert_count * capacity, model_width)[targets].reshape(
        row_count, top_count, model_width
    )
    expert_vals = expert_rows.astype(jnp.float32)
    result = residual_stream + jnp.sum(gate_vals[:, :, None] * expert_vals, axis=1)
    output = result.astype(jnp.bfloat16).reshape(tokens.shape)
    grad_res = cotangent.reshape(row_count, model_width).astype(jnp.float32)
    gate_grad = jnp.sum(grad_res[:, None, :] * expert_vals, axis=-1)
    out_grad = (gate_vals[:, :, None] * grad_res[:, None, :]).astype(jnp.bfloat16)
    back_out = (
        jnp.zeros((expert_count * capacity, model_width), jnp.bfloat16)
        .at[targets]
        .set(out_grad.reshape(-1, model_width))
    )
    back_out = back_out.reshape(expert_count, capacity, model_width)
    (picked_grad,) = gate_back(gate_grad)
    logit_grad = jnp.sum(picked_grad[:, :, None] * pick_table, axis=1).astype(jnp.bfloat16)
    full_qkv, full_out, full_router = (
        lax.all_gather(query_key_value_weight, "fsdp", axis=0, tiled=True),
        lax.all_gather(output_weight, "fsdp", axis=0, tiled=True),
        lax.all_gather(router_weight, "fsdp", axis=0, tiled=True),
    )
    arrived_grad = lax.all_to_all(
        back_out, ("ctx", "fsdp"), split_axis=0, concat_axis=0, tiled=True
    )
    sources = arrived.shape[0] // local_experts
    grouped = arrived.reshape(sources, local_experts, capacity, model_width)
    grad_grouped = arrived_grad.reshape(sources, local_experts, capacity, model_width)
    gate_pre = expert_results[2].reshape(sources, local_experts, capacity, -1)
    up_pre = expert_results[3].reshape(sources, local_experts, capacity, -1)
    hidden, hidden_back = jax.vjp(
        lambda gate_in, up_in: jax.nn.silu(gate_in) * up_in, gate_pre, up_pre
    )
    hidden_low = hidden.astype(jnp.bfloat16)
    hidden_grad = jnp.einsum(
        "secd,efd->secf", grad_grouped, w_down, preferred_element_type=jnp.float32
    )
    gate_pre_grad, up_pre_grad = hidden_back(hidden_grad)
    gate_low = gate_pre_grad.astype(jnp.bfloat16)
    up_low = up_pre_grad.astype(jnp.bfloat16)
    grad_w_down = jnp.einsum(
        "secf,secd->efd", hidden_low, grad_grouped, preferred_element_type=jnp.float32
    )
    grad_w_gate = jnp.einsum(
        "secd,secf->edf", grouped, gate_low, preferred_element_type=jnp.float32
    )
    grad_w_up = jnp.einsum("secd,secf->edf", grouped, up_low, preferred_element_type=jnp.float32)
    row_grad = jnp.einsum(
        "secf,edf->secd", gate_low, w_gate, preferred_element_type=jnp.float32
    ) + jnp.einsum("secf,edf->secd", up_low, w_up, preferred_element_type=jnp.float32)
    row_grad = row_grad.astype(jnp.bfloat16).reshape(arrived.shape)
    row_back = lax.all_to_all(row_grad, ("ctx", "fsdp"), split_axis=0, concat_axis=0, tiled=True)
    token_rows = row_back.reshape(expert_count * capacity, model_width)[targets].reshape(
        row_count, top_count, model_width
    )
    acts_two_grad = jnp.sum(token_rows.astype(jnp.float32), axis=1) + jnp.dot(
        logit_grad, full_router.T, preferred_element_type=jnp.float32
    )
    grad_w_router = jnp.dot(second_activations.T, logit_grad, preferred_element_type=jnp.float32)
    resid_extra, grad_ffn_gain = norm_two_back(acts_two_grad)
    resid_grad = grad_res + resid_extra
    attn_grad = resid_grad.astype(jnp.bfloat16)
    grad_w_out = jnp.dot(heads_reduced_precision.T, attn_grad, preferred_element_type=jnp.float32)
    heads_grad = jnp.dot(attn_grad, full_out.T, preferred_element_type=jnp.float32).astype(
        jnp.bfloat16
    )
    heads_grad = heads_grad.reshape(row_count, heads_kv, group_size, head_dim)
    row_delta = jnp.moveaxis(jnp.sum(heads_grad.astype(jnp.float32) * heads_out, axis=-1), 0, 2)
    key_grad_sorted = jnp.zeros((seq_len, heads_kv, head_dim), jnp.float32)
    value_grad_sorted = jnp.zeros((seq_len, heads_kv, head_dim), jnp.float32)
    query_grad_runs = []
    for run_index in range(2):
        query_run, place_run, block_total, log_total = run_info[run_index]
        grad_run = heads_grad[run_index * run_len : (run_index + 1) * run_len]
        delta_run = row_delta[:, :, run_index * run_len : (run_index + 1) * run_len]

        def back_step(block_index, carried):
            query_grad, key_acc, value_acc = carried
            scores, visible, key_blk, value_blk = block_scores(query_run, place_run, block_index)
            prob_vals = jnp.exp(scores - log_total[..., None])
            value_grad = jnp.einsum(
                "hgqk,qhgd->khd",
                prob_vals.astype(jnp.bfloat16),
                grad_run,
                preferred_element_type=jnp.float32,
            )
            prob_grad = jnp.einsum(
                "qhgd,khd->hgqk", grad_run, value_blk, preferred_element_type=jnp.float32
            )
            score_grad = (prob_vals * (prob_grad - delta_run[..., None])).astype(jnp.bfloat16)
            query_grad = (
                query_grad
                + jnp.einsum(
                    "hgqk,khd->qhgd", score_grad, key_blk, preferred_element_type=jnp.float32
                )
                * score_scale
            )
            key_grad = (
                jnp.einsum(
                    "hgqk,qhgd->khd", score_grad, query_run, preferred_element_type=jnp.float32
                )
                * score_scale
            )
            start = block_index * block_len
            key_acc = lax.dynamic_update_slice_in_dim(
                key_acc, lax.dynamic_slice_in_dim(key_acc, start, block_len, 0) + key_grad, start, 0
            )
            value_acc = lax.dynamic_update_slice_in_dim(
                value_acc,
                lax.dynamic_slice_in_dim(value_acc, start, block_len, 0) + value_grad,
                start,
                0,
            )
            return (query_grad, key_acc, value_acc)

        start_state = (
            jnp.zeros((run_len, heads_kv, group_size, head_dim), jnp.float32),
            key_grad_sorted,
            value_grad_sorted,
        )
        query_grad_run, key_grad_sorted, value_grad_sorted = lax.fori_loop(
            0, block_total, back_step, start_state
        )
        query_grad_runs.append(query_grad_run)
    query_grad = jnp.concatenate(query_grad_runs, axis=0)
    key_grads = key_grad_sorted[key_places]
    value_grads = value_grad_sorted[key_places]
    key_grad_own, value_grad_own = (
        lax.psum_scatter(
            key_grads.astype(jnp.bfloat16), "ctx", scatter_dimension=0, tiled=True
        ).astype(jnp.float32),
        lax.psum_scatter(
            value_grads.astype(jnp.bfloat16), "ctx", scatter_dimension=0, tiled=True
        ).astype(jnp.float32),
    )
    proj_grad, grad_q_gain, grad_k_gain = prep_back(
        (query_grad.reshape(row_count, heads_q, head_dim), key_grad_own, value_grad_own)
    )
    proj_low = proj_grad.astype(jnp.bfloat16)
    grad_w_qkv = jnp.dot(first_activations.T, proj_low, preferred_element_type=jnp.float32)
    acts_grad = jnp.dot(proj_low, full_qkv.T, preferred_element_type=jnp.float32)
    inputs_extra, grad_attn_gain = norm_back(acts_grad)
    grad_tokens = (resid_grad + inputs_extra).reshape(tokens.shape)
    grad_w_qkv, grad_w_out, grad_w_router = (
        lax.psum_scatter(grad_w_qkv, ("ctx", "fsdp"), scatter_dimension=0, tiled=True),
        lax.psum_scatter(grad_w_out, ("ctx", "fsdp"), scatter_dimension=0, tiled=True),
        lax.psum_scatter(grad_w_router, ("ctx", "fsdp"), scatter_dimension=0, tiled=True),
    )
    grad_attn_gain, grad_q_gain, grad_k_gain, grad_ffn_gain = lax.psum(
        (grad_attn_gain, grad_q_gain, grad_k_gain, grad_ffn_gain), ("ctx", "fsdp")
    )
    return (
        output,
        grad_tokens,
        grad_attn_gain,
        grad_w_qkv,
        grad_q_gain,
        grad_k_gain,
        grad_w_out,
        grad_ffn_gain,
        grad_w_router,
        grad_w_gate,
        grad_w_up,
        grad_w_down,
    )


def swap(values, axis, count, bit):
    return lax.ppermute(values, axis, [(i, i ^ bit) for i in range(count)])


def after(values, earlier, both=False):
    values, earlier = lax.optimization_barrier((values, earlier))
    return (*values, *earlier) if both else values


def pick(values, index):
    return lax.dynamic_index_in_dim(values, index, 0, keepdims=False)


def by_fsdp(pieces, fsdp_at):
    stacked = jnp.stack(pieces)
    stacked = jnp.where(fsdp_at % 2 == 1, jnp.stack([pieces[k ^ 1] for k in range(4)]), stacked)
    turned = jnp.stack([stacked[k ^ 2] for k in range(4)])
    return jnp.where(fsdp_at // 2 == 1, turned, stacked)


def plane_gather(values):
    half = values.shape[-2] // 2
    near_x = swap(values, "fsdp", 4, 1)
    near_y = swap(values, "fsdp", 4, 2)
    far_low = swap(near_x[..., :half, :], "fsdp", 4, 2)
    far_high = swap(near_y[..., half:, :], "fsdp", 4, 1)
    return [values, near_x, near_y, far_low, far_high]


def plane_scatter(own, x_low, x_high, y_low, y_high, far_low, far_high):
    from_x = swap(far_low, "fsdp", 4, 1)
    from_y = swap(far_high, "fsdp", 4, 2)
    got_x_low = swap(x_low, "fsdp", 4, 1)
    got_y_high = swap(y_high, "fsdp", 4, 2)
    got_y_low = swap((y_low.astype(f32) + from_x.astype(f32)).astype(bf16), "fsdp", 4, 2)
    got_x_high = swap((x_high.astype(f32) + from_y.astype(f32)).astype(bf16), "fsdp", 4, 1)
    added = jnp.concatenate(
        [
            got_x_low.astype(f32) + got_y_low.astype(f32),
            got_x_high.astype(f32) + got_y_high.astype(f32),
        ],
        axis=-2,
    )
    return own.astype(f32) + added


def scatter_parts(parts):
    half = parts.shape[1] // 2
    return plane_scatter(
        parts[0],
        parts[1, :half],
        parts[1, half:],
        parts[2, :half],
        parts[2, half:],
        parts[3, :half],
        parts[3, half:],
    )


def ctx_scatter(parts, n_ctx, ctx_at, low):
    bit = 1
    held = parts
    while bit < n_ctx:
        mine = (ctx_at // bit) % 2
        split = held.reshape((held.shape[0] // 2, 2) + held.shape[1:])
        keep = lax.dynamic_index_in_dim(split, mine, 1, keepdims=False)
        away = lax.dynamic_index_in_dim(split, 1 - mine, 1, keepdims=False)
        got = swap(away, "ctx", n_ctx, bit)
        held = keep.astype(f32) + got.astype(f32)
        bit *= 2
        if low and bit < n_ctx:
            held = held.astype(bf16)
    return held.reshape(parts.shape[1:])


def attend_kernel(place_ref, source_ref, q_ref, kv_ref, o_ref, lse_ref, keys, vals_t, q_t, acc, total):
    seq = pl.program_id(0)
    rows = run_rows
    heads = q_ref.shape[2] // rows
    blocks = keys.shape[0] // rows
    scale = math.log2(math.e) / math.sqrt(rows)
    for p in range(blocks):
        at = source_ref[seq * blocks + p]
        block = kv_ref[at // 2, 0, pl.ds(pl.multiple_of((at % 2) * rows, rows), rows), :]
        keys[p * rows : (p + 1) * rows, :] = block[:, :rows]
        vals_t[:, p * rows : (p + 1) * rows] = block[:, rows:].T
    key_iota = lax.broadcasted_iota(jnp.int32, (2 * rows, 2 * rows), 0)
    query_iota = lax.broadcasted_iota(jnp.int32, (2 * rows, 2 * rows), 1) % rows
    for run in range(2):
        place = place_ref[seq * 2 + run]
        for h in range(heads):
            q_t[:, h * rows : (h + 1) * rows] = q_ref[
                0, run * rows : (run + 1) * rows, h * rows : (h + 1) * rows
            ].T
        acc[...] = jnp.zeros_like(acc)
        total[...] = jnp.zeros_like(total)

        def step(j, masked):
            start = pl.multiple_of(j * 2 * rows, 2 * rows)
            key_blk = keys[pl.ds(start, 2 * rows), :]
            val_blk = vals_t[:, pl.ds(start, 2 * rows)]
            for pair in range(heads // 2):
                cols = slice(pair * 2 * rows, (pair + 1) * 2 * rows)
                scores = jnp.dot(key_blk, q_t[:, cols], preferred_element_type=f32)
                weights = jnp.exp2(scores * scale)
                if masked:
                    seen = start + key_iota <= place * rows + query_iota
                    weights = jnp.where(seen, weights, 0.0)
                total[:, cols] += jnp.sum(weights.reshape(2 * rows // 8, 8, 2 * rows), axis=0)
                acc[:, cols] += jnp.dot(val_blk, weights.astype(bf16), preferred_element_type=f32)

        lax.fori_loop(0, place // 2, lambda j, c: (step(j, False), c)[1], 0)
        step(place // 2, True)
        norm = jnp.sum(total[...], axis=0, keepdims=True)
        lse_ref[0, run : run + 1, :] = jnp.log2(norm)
        mixed = acc[...] / norm
        for h in range(heads):
            o_ref[0, run * rows : (run + 1) * rows, h * rows : (h + 1) * rows] = (
                mixed[:, h * rows : (h + 1) * rows].T.astype(bf16)
            )


def head_back(turned, vector, cosine, sine, gain):
    grad = turned * cosine - pltpu.roll(turned, turned.shape[1] // 2, 1) * sine
    scale = lax.rsqrt(jnp.mean(vector * vector, axis=-1, keepdims=True) + eps_norm)
    unit = vector * scale
    scaled = grad * gain
    back = scale * (scaled - unit * jnp.mean(scaled * unit, axis=-1, keepdims=True))
    return back, grad * unit


def project_kernel(heads, acts_ref, weight_ref, cos_ref, sin_ref, gain_q_ref, gain_k_ref, proj_ref, q_ref, kv_ref):
    width = cos_ref.shape[2]
    proj_ref[0] = jnp.dot(acts_ref[0], weight_ref[...], preferred_element_type=f32)
    for h in range(heads + 1):
        vector = proj_ref[0, :, h * width : (h + 1) * width]
        gain = gain_q_ref[...] if h < heads else gain_k_ref[...]
        scale = lax.rsqrt(jnp.mean(vector * vector, axis=-1, keepdims=True) + eps_norm)
        normed = vector * scale * gain
        turned = normed * cos_ref[0] + pltpu.roll(normed, width // 2, 1) * sin_ref[0]
        if h < heads:
            q_ref[0, :, h * width : (h + 1) * width] = turned.astype(bf16)
        else:
            kv_ref[0, :, :width] = turned.astype(bf16)
    kv_ref[0, :, width:] = proj_ref[0, :, (heads + 1) * width :].astype(bf16)


def key_back_kernel(a_ref, b_ref, c_ref, d_ref, proj_ref, cos_ref, sin_ref, gain_ref, dkv_ref, dgain_ref):
    width = cos_ref.shape[2]
    total = (
        a_ref[0].astype(f32) + b_ref[0].astype(f32) + c_ref[0].astype(f32) + d_ref[0].astype(f32)
    )
    back, share = head_back(
        total[:, :width], proj_ref[0, :, :width], cos_ref[0], sin_ref[0], gain_ref[...]
    )
    dkv_ref[0, :, :width] = back.astype(bf16)
    dkv_ref[0, :, width:] = total[:, width:].astype(bf16)

    @pl.when(pl.program_id(0) == 0)
    def _():
        dgain_ref[...] = jnp.zeros_like(dgain_ref)

    dgain_ref[...] += jnp.sum(share.reshape(-1, 8, width), axis=0)


def attend_back_kernel(
    place_ref,
    source_ref,
    q_ref,
    kv_ref,
    o_ref,
    do_ref,
    lse_ref,
    proj_ref,
    cos_ref,
    sin_ref,
    gain_ref,
    dq_ref,
    dkv_ref,
    dgain_ref,
    keys,
    keys_t,
    vals,
    q_n,
    q_t,
    do_n,
    do_t,
    delta,
    dq_acc,
    dk_acc,
    dv_acc,
):
    seq = pl.program_id(0)
    rows = run_rows
    heads = q_ref.shape[2] // rows
    blocks = keys.shape[0] // rows
    scale = math.log2(math.e) / math.sqrt(rows)
    plain_scale = 1.0 / math.sqrt(rows)
    for p in range(blocks):
        at = source_ref[seq * blocks + p]
        block = kv_ref[at // 2, 0, pl.ds(pl.multiple_of((at % 2) * rows, rows), rows), :]
        keys[p * rows : (p + 1) * rows, :] = block[:, :rows]
        keys_t[:, p * rows : (p + 1) * rows] = block[:, :rows].T
        vals[p * rows : (p + 1) * rows, :] = block[:, rows:]
    dk_acc[...] = jnp.zeros_like(dk_acc)
    dv_acc[...] = jnp.zeros_like(dv_acc)

    @pl.when(seq == 0)
    def _():
        dgain_ref[...] = jnp.zeros_like(dgain_ref)

    key_iota = lax.broadcasted_iota(jnp.int32, (2 * rows, 2 * rows), 0)
    query_iota = lax.broadcasted_iota(jnp.int32, (2 * rows, 2 * rows), 1) % rows
    for run in range(2):
        place = place_ref[seq * 2 + run]
        here = slice(run * rows, (run + 1) * rows)
        for h in range(heads):
            cols = slice(h * rows, (h + 1) * rows)
            q_h = q_ref[0, here, cols]
            q_n[cols, :] = q_h
            q_t[:, cols] = q_h.T
            do_h = do_ref[0, here, cols]
            do_n[cols, :] = do_h
            do_ht = do_h.T
            do_t[:, cols] = do_ht
            o_ht = o_ref[0, here, cols].T
            delta[:, cols] = jnp.sum(do_ht.astype(f32) * o_ht.astype(f32), axis=0, keepdims=True)
        dq_acc[...] = jnp.zeros_like(dq_acc)

        def step(j, masked):
            start = pl.multiple_of(j * 2 * rows, 2 * rows)
            key_blk = keys[pl.ds(start, 2 * rows), :]
            key_t_blk = keys_t[:, pl.ds(start, 2 * rows)]
            val_blk = vals[pl.ds(start, 2 * rows), :]
            dk_sum = jnp.zeros((2 * rows, rows), f32)
            dv_sum = jnp.zeros((2 * rows, rows), f32)
            for pair in range(heads // 2):
                cols = slice(pair * 2 * rows, (pair + 1) * 2 * rows)
                scores = jnp.dot(key_blk, q_t[:, cols], preferred_element_type=f32)
                probs = jnp.exp2(scores * scale - lse_ref[0, run : run + 1, cols])
                if masked:
                    seen = start + key_iota <= place * rows + query_iota
                    probs = jnp.where(seen, probs, 0.0)
                prob_grad = jnp.dot(val_blk, do_t[:, cols], preferred_element_type=f32)
                score_grad = (probs * (prob_grad - delta[:, cols])).astype(bf16)
                dv_sum += jnp.dot(probs.astype(bf16), do_n[cols, :], preferred_element_type=f32)
                dk_sum += jnp.dot(score_grad, q_n[cols, :], preferred_element_type=f32)
                dq_acc[:, cols] += jnp.dot(key_t_blk, score_grad, preferred_element_type=f32)
            dk_acc[pl.ds(start, 2 * rows), :] += dk_sum
            dv_acc[pl.ds(start, 2 * rows), :] += dv_sum

        lax.fori_loop(0, place // 2, lambda j, c: (step(j, False), c)[1], 0)
        step(place // 2, True)
        for h in range(heads):
            cols = slice(h * rows, (h + 1) * rows)
            turned = dq_acc[:, cols].T * plain_scale
            back, share = head_back(
                turned, proj_ref[0, here, cols], cos_ref[0, here, :], sin_ref[0, here, :], gain_ref[...]
            )
            dq_ref[0, here, cols] = back.astype(bf16)
            dgain_ref[...] += jnp.sum(share.reshape(rows // 8, 8, rows), axis=0)
    for p in range(blocks):
        at = source_ref[seq * blocks + p]
        span = slice(p * rows, (p + 1) * rows)
        there = pl.ds(pl.multiple_of((at % 2) * rows, rows), rows)
        dkv_ref[at // 2, 0, there, :rows] = (dk_acc[span, :] * plain_scale).astype(bf16)
        dkv_ref[at // 2, 0, there, rows:] = dv_acc[span, :].astype(bf16)


def attend(places, sources, queries, kv):
    seqs, rows, width = queries.shape
    slots, _, _, pair_width = kv.shape
    head_dim = pair_width // 2
    seq_len = slots * rows
    return pl.pallas_call(
        attend_kernel,
        out_shape=(
            jax.ShapeDtypeStruct(queries.shape, bf16),
            jax.ShapeDtypeStruct((seqs, 2, width), f32),
        ),
        grid_spec=pltpu.PrefetchScalarGridSpec(
            num_scalar_prefetch=2,
            grid=(seqs,),
            in_specs=[
                pl.BlockSpec((1, rows, width), lambda s, *_: (s, 0, 0)),
                pl.BlockSpec((slots, 1, rows, pair_width), lambda s, *_: (0, s, 0, 0)),
            ],
            out_specs=[
                pl.BlockSpec((1, rows, width), lambda s, *_: (s, 0, 0)),
                pl.BlockSpec((1, 2, width), lambda s, *_: (s, 0, 0)),
            ],
            scratch_shapes=[
                pltpu.VMEM((seq_len, head_dim), bf16),
                pltpu.VMEM((head_dim, seq_len), bf16),
                pltpu.VMEM((head_dim, width), bf16),
                pltpu.VMEM((head_dim, width), f32),
                pltpu.VMEM((8, width), f32),
            ],
        ),
        compiler_params=pltpu.CompilerParams(vmem_limit_bytes=32 * 2**20),
        cost_estimate=pl.CostEstimate(flops=1000, bytes_accessed=1000, transcendentals=0),
        name="attend",
    )(places, sources, queries, kv)


def attend_back(places, sources, queries, kv, mixed, mixed_grad, lse, projected, cosine, sine, gain):
    seqs, rows, width = queries.shape
    slots, _, _, pair_width = kv.shape
    head_dim = pair_width // 2
    seq_len = slots * rows
    block = pl.BlockSpec((1, rows, width), lambda s, *_: (s, 0, 0))
    angle_block = pl.BlockSpec((1, rows, head_dim), lambda s, *_: (s, 0, 0))
    kv_block = pl.BlockSpec((slots, 1, rows, pair_width), lambda s, *_: (0, s, 0, 0))
    return pl.pallas_call(
        attend_back_kernel,
        out_shape=(
            jax.ShapeDtypeStruct(queries.shape, bf16),
            jax.ShapeDtypeStruct(kv.shape, bf16),
            jax.ShapeDtypeStruct((8, head_dim), f32),
        ),
        grid_spec=pltpu.PrefetchScalarGridSpec(
            num_scalar_prefetch=2,
            grid=(seqs,),
            in_specs=[
                block,
                kv_block,
                block,
                block,
                pl.BlockSpec((1, 2, width), lambda s, *_: (s, 0, 0)),
                block,
                angle_block,
                angle_block,
                pl.BlockSpec((1, head_dim), lambda s, *_: (0, 0)),
            ],
            out_specs=[block, kv_block, pl.BlockSpec((8, head_dim), lambda s, *_: (0, 0))],
            scratch_shapes=[
                pltpu.VMEM((seq_len, head_dim), bf16),
                pltpu.VMEM((head_dim, seq_len), bf16),
                pltpu.VMEM((seq_len, head_dim), bf16),
                pltpu.VMEM((width, head_dim), bf16),
                pltpu.VMEM((head_dim, width), bf16),
                pltpu.VMEM((width, head_dim), bf16),
                pltpu.VMEM((head_dim, width), bf16),
                pltpu.VMEM((1, width), f32),
                pltpu.VMEM((head_dim, width), f32),
                pltpu.VMEM((seq_len, head_dim), f32),
                pltpu.VMEM((seq_len, head_dim), f32),
            ],
        ),
        compiler_params=pltpu.CompilerParams(vmem_limit_bytes=40 * 2**20),
        cost_estimate=pl.CostEstimate(flops=1000, bytes_accessed=1000, transcendentals=0),
        name="attend_back",
    )(places, sources, queries, kv, mixed, mixed_grad, lse, projected, cosine, sine, gain)


def project(acts, weight, cosine, sine, gain_q, gain_k, heads):
    seqs, rows, depth = acts.shape
    head_dim = cosine.shape[2]
    width = weight.shape[1]
    angle_block = pl.BlockSpec((1, rows, head_dim), lambda s: (s, 0, 0))
    gain_block = pl.BlockSpec((1, head_dim), lambda s: (0, 0))

    def block(columns):
        return pl.BlockSpec((1, rows, columns), lambda s: (s, 0, 0))

    return pl.pallas_call(
        functools.partial(project_kernel, heads),
        out_shape=(
            jax.ShapeDtypeStruct((seqs, rows, width), f32),
            jax.ShapeDtypeStruct((seqs, rows, heads * head_dim), bf16),
            jax.ShapeDtypeStruct((seqs, rows, 2 * head_dim), bf16),
        ),
        grid=(seqs,),
        in_specs=[
            block(depth),
            pl.BlockSpec((depth, width), lambda s: (0, 0)),
            angle_block,
            angle_block,
            gain_block,
            gain_block,
        ],
        out_specs=[block(width), block(heads * head_dim), block(2 * head_dim)],
        compiler_params=pltpu.CompilerParams(vmem_limit_bytes=40 * 2**20),
        cost_estimate=pl.CostEstimate(flops=1000, bytes_accessed=1000, transcendentals=0),
        name="project",
    )(acts, weight, cosine, sine, gain_q, gain_k)


def key_back(held, projected, cosine, sine, gain):
    seqs, rows, pair_width = held[0].shape
    head_dim = pair_width // 2
    pairs_before = projected.shape[2] // pair_width - 1
    block = pl.BlockSpec((1, rows, pair_width), lambda s: (s, 0, 0))
    angle_block = pl.BlockSpec((1, rows, head_dim), lambda s: (s, 0, 0))
    return pl.pallas_call(
        key_back_kernel,
        out_shape=(
            jax.ShapeDtypeStruct(held[0].shape, bf16),
            jax.ShapeDtypeStruct((8, head_dim), f32),
        ),
        grid=(seqs,),
        in_specs=[
            block,
            block,
            block,
            block,
            pl.BlockSpec((1, rows, pair_width), lambda s: (s, 0, pairs_before)),
            angle_block,
            angle_block,
            pl.BlockSpec((1, head_dim), lambda s: (0, 0)),
        ],
        out_specs=[block, pl.BlockSpec((8, head_dim), lambda s: (0, 0))],
        name="key_back",
    )(*held, projected, cosine, sine, gain)


def hot_rows(slot_row, capacity):
    count = slot_row.shape[1]
    return slot_row == lax.broadcasted_iota(jnp.int32, (capacity, count), 0).astype(f32)


def hot_columns(slot_column, capacity):
    count = slot_column.shape[0]
    return (slot_column == lax.broadcasted_iota(jnp.int32, (count, capacity), 1).astype(f32)).astype(bf16)


def select_rows(capacity, slot_ref, s, pieces, store):
    for core in range(2):
        near = pieces[5 * core : 5 * core + 3]
        low, high = pieces[5 * core + 3], pieces[5 * core + 4]
        for k in range(4):
            source = 4 * core + k
            hot = hot_rows(slot_ref[s, source : source + 1, :], capacity).astype(bf16)
            if k < 3:
                rows = jnp.dot(hot, near[k][...], preferred_element_type=f32)
            else:
                half = low.shape[0]
                rows = jnp.dot(hot[:, :half], low[...], preferred_element_type=f32)
                rows += jnp.dot(hot[:, half:], high[...], preferred_element_type=f32)
            store(source, rows.astype(bf16))


def combine_kernel(capacity, column_ref, kept_ref, got_ref, own_ref, x_ref, y_ref, low_ref, high_ref):
    for k in range(4):
        hot = hot_columns(column_ref[0, :, k : k + 1], capacity)
        total = jnp.dot(hot, kept_ref[0, k * capacity : (k + 1) * capacity, :], preferred_element_type=f32)
        total = (total + got_ref[0, k].astype(f32)).astype(bf16)
        if k < 3:
            (own_ref, x_ref, y_ref)[k][0] = total
        else:
            half = total.shape[0] // 2
            low_ref[0] = total[:half]
            high_ref[0] = total[half:]


def combine_rows(columns, kept, got, capacity):
    chunks, rows, sources = columns.shape
    width = kept.shape[2]
    tile = width // 4
    at = lambda k, d: (k, 0, d)
    whole = pl.BlockSpec((1, rows, tile), at)
    half = pl.BlockSpec((1, rows // 2, tile), at)
    return pl.pallas_call(
        functools.partial(combine_kernel, capacity),
        out_shape=[jax.ShapeDtypeStruct((chunks, rows, width), bf16)] * 3
        + [jax.ShapeDtypeStruct((chunks, rows // 2, width), bf16)] * 2,
        grid=(chunks, 4),
        in_specs=[
            pl.BlockSpec((1, rows, sources), lambda k, d: (k, 0, 0)),
            pl.BlockSpec((1, 4 * capacity, tile), at),
            pl.BlockSpec((1, 4, rows, tile), lambda k, d: (k, 0, 0, d)),
        ],
        out_specs=[whole] * 3 + [half] * 2,
        cost_estimate=pl.CostEstimate(flops=1000, bytes_accessed=1000, transcendentals=0),
        name="combine_rows",
    )(columns, kept, got)


def flip(index, bit):
    return index + bit - 2 * bit * ((index // bit) % 2)


def neighbours():
    ctx, fsdp = lax.axis_index("ctx"), lax.axis_index("fsdp")
    return dict(
        core=(flip(ctx, 1), fsdp),
        x=(ctx, flip(fsdp, 1)),
        y=(ctx, flip(fsdp, 2)),
        z=[None, (flip(ctx, 2), fsdp), (flip(ctx, 4), fsdp), (flip(flip(ctx, 2), 4), fsdp)],
    )


def greet(partners):
    barrier = pltpu.get_barrier_semaphore()
    for partner in partners:
        pl.semaphore_signal(barrier, inc=1, device_id=partner, device_id_type=pl.DeviceIdType.MESH)
    pl.semaphore_wait(barrier, len(partners))


def send(source, target, sent, received, partner):
    return pltpu.make_async_remote_copy(
        src_ref=source,
        dst_ref=target,
        send_sem=sent,
        recv_sem=received,
        device_id=partner,
        device_id_type=pl.DeviceIdType.MESH,
    )


class Exchange:
    def __init__(self, near, table, outgoing, landing, sent, got):
        self.partners = [near["x"], near["y"], near["core"], near["z"][1], near["z"][2]]
        self.table, self.outgoing, self.landing = table, outgoing, landing
        self.sent, self.got = sent, got
        self.rows = [[r for r in range(32) if (r >> bit) % 2] for bit in range(5)]

    def copy(self, bit):
        return send(
            self.outgoing.at[bit],
            self.landing.at[bit],
            self.sent.at[bit],
            self.got.at[bit],
            self.partners[bit],
        )

    def start(self, bit):
        for i, r in enumerate(self.rows[bit]):
            self.outgoing[bit, i] = self.table[r]
        self.copy(bit).start()

    def end(self, bit):
        self.copy(bit).wait_recv()
        for i, r in enumerate(self.rows[bit]):
            self.table[r] = self.landing[bit, i]

    def finish(self):
        for bit in range(5):
            self.copy(bit).wait_send()


def exchange_scratch(width):
    return [
        pltpu.VMEM((5, 16, 1, width), f32),
        pltpu.VMEM((5, 16, 1, width), f32),
        pltpu.SemaphoreType.DMA((5,)),
        pltpu.SemaphoreType.DMA((5,)),
    ]


class Chain:
    def __init__(self, near, own, place, sent, got):
        self.near, self.own, self.place, self.sent, self.got = near, own, place, sent, got
        z = lax.axis_index("ctx") // 2
        self.inner = (z == 1) | (z == 2)
        self.outer = (z == 0) | (z == 3)

    def copy(self, source, slot, number, partner):
        return send(
            source, self.place(slot), self.sent.at[number], self.got.at[slot - 1], self.near["z"][partner]
        )

    def first(self):
        return self.copy(self.own, 1, 0, 1)

    def inner_copies(self, stage):
        if stage == 0:
            return [(self.own, 3, 1, 3)]
        if stage == 1:
            return [(self.place(1), 2, 2, 3), (self.place(3), 2, 3, 1)]
        return [(self.place(2), 3, 4, 1)]

    def start(self):
        self.first().start()
        self.start_inner(0)

    def start_inner(self, stage):
        @pl.when(self.inner)
        def _():
            for copy in self.inner_copies(stage):
                self.copy(*copy).start()

    def wait(self, slot):
        if slot < 3:
            self.copy(self.own, slot, 0, 1).wait_recv()
        else:
            @pl.when(self.outer)
            def _():
                self.copy(self.own, 3, 0, 1).wait_recv()

    def wait_inner_last(self):
        @pl.when(self.inner)
        def _():
            self.copy(self.own, 3, 0, 1).wait_recv()

    def step(self, slot):
        if slot == 1:
            self.wait(1)
            self.wait_inner_last()
            self.start_inner(1)
        elif slot == 2:
            self.wait(2)
            self.start_inner(2)
        else:
            self.wait(3)

    def finish(self):
        self.first().wait_send()

        @pl.when(self.inner)
        def _():
            for stage in range(3):
                for copy in self.inner_copies(stage):
                    self.copy(*copy).wait_send()


def gather_experts_kernel(
    capacity,
    steps,
    acts_ref,
    slot_ref,
    column_ref,
    gates_ref,
    gate_ref,
    up_ref,
    down_ref,
    grad_ref,
    grad_x_ref,
    grad_y_ref,
    *refs,
):
    (
        rows_ref,
        grad_rows_ref,
        hidden_ref,
        gate_low_ref,
        up_low_ref,
        kept_ref,
        got_ref,
        given_ref,
        out_kept_ref,
        out_got_ref,
        out_given_ref,
        scalar_ref,
        buffer_ref,
        grad_far_ref,
        grad_core_ref,
        gate_acc,
        up_acc,
        back_acc,
        hidden_now,
        gate_low_now,
        up_low_now,
        z_sent,
        z_got,
        near_sent,
        near_got,
        far_sent,
        far_got,
        core_sent,
        core_got,
        given_sent,
        given_got,
        grad_far_sent,
        grad_far_got,
        grad_core_sent,
        grad_core_got,
        local,
        gate_table,
        *exchange_refs,
    ) = refs
    near = neighbours()
    chunks = slot_ref.shape[0]
    half = acts_ref.shape[0] // 2
    width = acts_ref.shape[1]
    tile = width // steps
    hidden_width = gate_ref.shape[1]
    group = 8 * capacity
    greet([near["core"], near["x"], near["y"]] + near["z"][1:])
    chain = Chain(near, acts_ref, lambda s: buffer_ref.at[s, 0, 0], z_sent, z_got)
    exchange = Exchange(near, gate_table, *exchange_refs)

    def own(s):
        return acts_ref if s == 0 else buffer_ref.at[s, 0, 0]

    def to_near(s, k):
        return send(
            own(s), buffer_ref.at[s, 0, 1 + k], near_sent.at[s, k], near_got.at[s, k], near["xy"[k]]
        )

    def to_far(s, k):
        span = pl.ds(k * half, half)
        return send(
            buffer_ref.at[s, 0, 1 + k, span],
            buffer_ref.at[s, 0, 3, span],
            far_sent.at[s, k],
            far_got.at[s, k],
            near["yx"[k]],
        )

    def to_core(s, j):
        if j == 0:
            source, target = own(s), buffer_ref.at[s, 1, 0]
        elif j < 3:
            source, target = buffer_ref.at[s, 0, j], buffer_ref.at[s, 1, j]
        else:
            span = pl.ds((j - 3) * half, half)
            source, target = buffer_ref.at[s, 0, 3, span], buffer_ref.at[s, 1, 3, span]
        return send(source, target, core_sent.at[s, j], core_got.at[s, j], near["core"])

    def to_sibling(s, i):
        source, target = ((given_ref, got_ref), (out_given_ref, out_got_ref))[i]
        return send(
            source.at[s], target.at[s], given_sent.at[s, i], given_got.at[s, i], near["core"]
        )

    def grad_to_far(s, k):
        span = pl.ds(k * half, half)
        return send(
            (grad_x_ref, grad_y_ref)[k].at[s, span],
            grad_far_ref.at[s, span],
            grad_far_sent.at[s, k],
            grad_far_got.at[s, k],
            near["yx"[k]],
        )

    def grad_to_core(s, j):
        source = (grad_ref, grad_x_ref, grad_y_ref, grad_far_ref)[j].at[s]
        return send(
            source,
            grad_core_ref.at[s, j],
            grad_core_sent.at[s, j],
            grad_core_got.at[s, j],
            near["core"],
        )

    def grad_step(s, own_blk, x_blk, y_blk, far_blk, core_blk, down_blk, rows_blk):
        @pl.when(pl.program_id(0) == 0)
        def _():
            back_acc[...] = jnp.zeros_like(back_acc)

        for source in range(8):
            hot = hot_rows(slot_ref[s, source : source + 1, :], capacity).astype(bf16)
            block = (own_blk, x_blk, y_blk, far_blk)[source][...] if source < 4 else core_blk[source - 4]
            rows_blk[source * capacity : (source + 1) * capacity, :] = jnp.dot(
                hot, block, preferred_element_type=f32
            ).astype(bf16)
        back_acc[...] += lax.dot_general(
            rows_blk[...], down_blk[...], (((1,), (1,)), ((), ())), preferred_element_type=f32
        )

    def compute_grad(s):
        whole = pl.BlockSpec((2 * half, tile), lambda d: (0, d))
        pltpu.emit_pipeline(
            functools.partial(grad_step, s),
            grid=(steps,),
            in_specs=[whole] * 4
            + [
                pl.BlockSpec((4, 2 * half, tile), lambda d: (0, 0, d)),
                pl.BlockSpec((hidden_width, tile), lambda d: (0, d)),
            ],
            out_specs=[pl.BlockSpec((group, tile), lambda d: (0, d))],
        )(
            grad_ref.at[s],
            grad_x_ref.at[s],
            grad_y_ref.at[s],
            grad_far_ref.at[s],
            grad_core_ref.at[s],
            down_ref,
            grad_rows_ref.at[s],
        )

    def experts_step(
        s, buffer_blk, gate_blk, up_blk, down_blk, rows_blk, given_blk, kept_blk, out_given_blk, out_kept_blk
    ):
        step = pl.program_id(0)

        @pl.when(step == 0)
        def _():
            gate_acc[...] = jnp.zeros_like(gate_acc)
            up_acc[...] = jnp.zeros_like(up_acc)

        @pl.when(step < steps)
        def _():
            for source in range(8):
                hot = hot_rows(slot_ref[s, source : source + 1, :], capacity).astype(bf16)
                rows_blk[source * capacity : (source + 1) * capacity, :] = jnp.dot(
                    hot, buffer_blk[source // 4, source % 4], preferred_element_type=f32
                ).astype(bf16)
            gate_acc[...] += jnp.dot(rows_blk[...], gate_blk[...], preferred_element_type=f32)
            up_acc[...] += jnp.dot(rows_blk[...], up_blk[...], preferred_element_type=f32)

        @pl.when(step == steps - 1)
        def _():
            for source in range(8):
                span = slice(source * capacity, (source + 1) * capacity)
                hot = hot_rows(slot_ref[s, source : source + 1, :], capacity)
                weighted = jnp.where(hot, gate_table[8 * s + source], 0.0)
                gate_val = jnp.sum(weighted, axis=1, keepdims=True)
                gate_pre, up_pre, back = gate_acc[span, :], up_acc[span, :], back_acc[span, :]
                sig = 1.0 / (1.0 + jnp.exp(-gate_pre))
                silu = gate_pre * sig
                hidden = (silu * up_pre).astype(bf16).astype(f32)
                hidden_now[span, :] = (hidden * gate_val).astype(bf16)
                scalar = jnp.sum(hidden * back, axis=1, keepdims=True)
                scalar_ref[s, source : source + 1, :] = jnp.sum(
                    jnp.where(hot, scalar, 0.0), axis=0, keepdims=True
                )
                hidden_grad = gate_val * back
                gate_low_now[span, :] = (
                    hidden_grad * up_pre * sig * (1.0 + gate_pre * (1.0 - sig))
                ).astype(bf16)
                up_low_now[span, :] = (hidden_grad * silu).astype(bf16)

        if s + 1 < chunks:

            @pl.when(step == steps)
            def _():
                near_done(s + 1)
                if s + 2 < chunks:
                    next_slot(s + 2)

        @pl.when(step >= steps)
        def _():
            last = (((1,), (1,)), ((), ()))
            row_grad = lax.dot_general(
                gate_low_now[...], gate_blk[...], last, preferred_element_type=f32
            )
            row_grad += lax.dot_general(
                up_low_now[...], up_blk[...], last, preferred_element_type=f32
            )
            row_grad = row_grad.astype(bf16)
            kept_blk[...] = row_grad[: 4 * capacity]
            weighted = jnp.dot(
                hidden_now[...], down_blk[...], preferred_element_type=f32
            ).astype(bf16)
            out_kept_blk[...] = weighted[: 4 * capacity]
            for k in range(4):
                hot = hot_columns(column_ref[s, :, 4 + k : 5 + k], capacity)
                span = slice((4 + k) * capacity, (5 + k) * capacity)
                given_blk[k] = jnp.dot(hot, row_grad[span], preferred_element_type=f32).astype(bf16)
                out_given_blk[k] = jnp.dot(
                    hot, weighted[span], preferred_element_type=f32
                ).astype(bf16)

    def compute(s):
        weight = pl.BlockSpec((tile, hidden_width), lambda d: (d % steps, 0))
        late = lambda d: jnp.maximum(d - steps, 0)
        given = pl.BlockSpec((4, 2 * half, tile), lambda d: (0, 0, late(d)))
        kept = pl.BlockSpec((4 * capacity, tile), lambda d: (0, late(d)))
        pltpu.emit_pipeline(
            functools.partial(experts_step, s),
            grid=(2 * steps,),
            in_specs=[
                pl.BlockSpec((2, 4, 2 * half, tile), lambda d: (0, 0, 0, jnp.minimum(d, steps - 1))),
                weight,
                weight,
                pl.BlockSpec((hidden_width, tile), lambda d: (0, late(d))),
            ],
            out_specs=[
                pl.BlockSpec((group, tile), lambda d: (0, jnp.minimum(d, steps - 1))),
                given,
                kept,
                given,
                kept,
            ],
        )(
            buffer_ref.at[s],
            gate_ref,
            up_ref,
            down_ref,
            rows_ref.at[s],
            given_ref.at[s],
            kept_ref.at[s],
            out_given_ref.at[s],
            out_kept_ref.at[s],
        )
        stores = [
            pltpu.make_async_copy(now, whole.at[s], local.at[1 + i])
            for i, (now, whole) in enumerate(
                ((hidden_now, hidden_ref), (gate_low_now, gate_low_ref), (up_low_now, up_low_ref))
            )
        ]
        for store in stores:
            store.start()
        for store in stores:
            store.wait()

    def near_done(s):
        for k in range(2):
            to_near(s, k).wait_recv()
            to_far(s, k).start()
            to_core(s, 1 + k).start()

    def far_done(s):
        for k in range(2):
            to_far(s, k).wait_recv()
            to_core(s, 3 + k).start()

    def next_slot(s):
        chain.step(s)
        to_near(s, 0).start()
        to_near(s, 1).start()
        to_core(s, 0).start()
        for k in range(2):
            grad_to_far(s, k).start()

    gate_table[...] = gates_ref[...]
    exchange.start(0)
    chain.start()
    to_near(0, 0).start()
    to_core(0, 0).start()
    exchange.end(0)
    exchange.start(1)
    to_near(0, 1).start()
    exchange.end(1)
    keep = pltpu.make_async_copy(acts_ref, buffer_ref.at[0, 0, 0], local.at[0])
    keep.start()
    for k in range(2):
        grad_to_far(0, k).start()
    for s in range(chunks):
        for j in range(3):
            grad_to_core(s, j).start()
    for bit in range(2, 5):
        exchange.start(bit)
        exchange.end(bit)
    keep.wait()
    near_done(0)
    next_slot(1)
    for s in range(chunks):
        for k in range(2):
            grad_to_far(s, k).wait_recv()
        grad_to_core(s, 3).start()
        for j in range(4):
            grad_to_core(s, j).wait_recv()
        compute_grad(s)
        far_done(s)
        for j in range(5):
            to_core(s, j).wait_recv()
        compute(s)
        if s + 1 < chunks:
            to_sibling(s, 0).start()
            to_sibling(s, 1).start()
    chain.finish()
    exchange.finish()
    for s in range(chunks):
        for k in range(2):
            to_near(s, k).wait_send()
            to_far(s, k).wait_send()
            grad_to_far(s, k).wait_send()
        for j in range(5):
            to_core(s, j).wait_send()
        for j in range(4):
            grad_to_core(s, j).wait_send()
        if s + 1 < chunks:
            to_sibling(s, 0).wait()
            to_sibling(s, 1).wait()


def gather_experts(acts, slots, columns, gates, gate_w, up_w, down_w, pieces, capacity):
    chunks, sources, rows = slots.shape
    width, hidden = gate_w.shape
    group = sources * capacity
    steps = 4
    anywhere = pl.BlockSpec(memory_space=pl.ANY)
    held = pl.BlockSpec(memory_space=pltpu.VMEM)
    dma = pltpu.SemaphoreType.DMA
    kept = jax.ShapeDtypeStruct((chunks, 4 * capacity, width), bf16)
    given = jax.ShapeDtypeStruct((chunks, 4, rows, width), bf16)
    return pl.pallas_call(
        functools.partial(gather_experts_kernel, capacity, steps),
        out_shape=(
            jax.ShapeDtypeStruct((chunks, group, width), bf16),
            jax.ShapeDtypeStruct((chunks, group, width), bf16),
            jax.ShapeDtypeStruct((chunks, group, hidden), bf16),
            jax.ShapeDtypeStruct((chunks, group, hidden), bf16),
            jax.ShapeDtypeStruct((chunks, group, hidden), bf16),
            kept,
            given,
            given,
            kept,
            given,
            given,
            jax.ShapeDtypeStruct((chunks, sources, rows), f32),
            jax.ShapeDtypeStruct((chunks, 2, 4, rows, width), bf16),
            jax.ShapeDtypeStruct((chunks, rows, width), bf16),
            given,
        ),
        in_specs=[held] * 4 + [anywhere] * 6,
        out_specs=[anywhere] * 11 + [held] + [anywhere] * 3,
        scratch_shapes=[
            pltpu.VMEM((group, hidden), f32),
            pltpu.VMEM((group, hidden), f32),
            pltpu.VMEM((group, hidden), f32),
            pltpu.VMEM((group, hidden), bf16),
            pltpu.VMEM((group, hidden), bf16),
            pltpu.VMEM((group, hidden), bf16),
            dma((5,)),
            dma((3,)),
            dma((chunks, 2)),
            dma((chunks, 2)),
            dma((chunks, 2)),
            dma((chunks, 2)),
            dma((chunks, 5)),
            dma((chunks, 5)),
            dma((chunks, 2)),
            dma((chunks, 2)),
            dma((chunks, 2)),
            dma((chunks, 2)),
            dma((chunks, 4)),
            dma((chunks, 4)),
            dma((4,)),
            pltpu.VMEM(gates.shape, f32),
        ]
        + exchange_scratch(rows),
        compiler_params=pltpu.CompilerParams(
            collective_id=1, has_side_effects=True, vmem_limit_bytes=60 * 2**20
        ),
        cost_estimate=pl.CostEstimate(flops=1000, bytes_accessed=1000, transcendentals=0),
        name="gather_experts",
    )(acts, slots, columns, gates, gate_w, up_w, down_w, *pieces)


def return_rows_kernel(
    capacity,
    column_ref,
    kept_ref,
    got_ref,
    given_ref,
    out_given_ref,
    out_got_in_ref,
    scalar_ref,
    out_ref,
    out_got_ref,
    table_ref,
    kept_now,
    sums,
    relay,
    from_x,
    from_y,
    own,
    from_z,
    kept_sem,
    got_sem,
    first_sent,
    first_got,
    second_sent,
    second_got,
    z_sent,
    z_got,
    core_sent,
    core_got,
    *exchange_refs,
):
    near = neighbours()
    exchange = Exchange(near, table_ref, *exchange_refs)
    chunks, rows = sums.shape[0], sums.shape[2]
    final = chunks - 1
    half = rows // 2
    low, high = pl.ds(0, half), pl.ds(half, half)
    greet([near["core"], near["x"], near["y"]] + near["z"][1:])
    order = [2, 3, 1, 0]

    def fetch_kept(s):
        return pltpu.make_async_copy(kept_ref.at[s], kept_now.at[s], kept_sem.at[s])

    def fetch_got(s):
        if s == final:
            return send(
                given_ref.at[s], sums.at[s], core_sent.at[0], core_got.at[0], near["core"]
            )
        return pltpu.make_async_copy(got_ref.at[s], sums.at[s], got_sem.at[s])

    def to_sibling():
        return send(
            out_given_ref.at[final], out_got_ref.at[final], core_sent.at[1], core_got.at[1], near["core"]
        )

    def first(s, i):
        source, target, partner = (
            (sums.at[s, 3, low], relay.at[s, 0], near["x"]),
            (sums.at[s, 3, high], relay.at[s, 1], near["y"]),
            (sums.at[s, 1, low], from_x.at[s, low], near["x"]),
            (sums.at[s, 2, high], from_y.at[s, high], near["y"]),
        )[i]
        return send(source, target, first_sent.at[s, i], first_got.at[s, i], partner)

    def second(s, i):
        source, target, partner = (
            (sums.at[s, 2, low], from_y.at[s, low], near["y"]),
            (sums.at[s, 1, high], from_x.at[s, high], near["x"]),
        )[i]
        return send(source, target, second_sent.at[s, i], second_got.at[s, i], partner)

    def along_z(s):
        return send(own.at[s], from_z.at[s - 1], z_sent.at[s - 1], z_got.at[s - 1], near["z"][s])

    tile = 256

    def combine(s):
        fetch_kept(s).wait()
        if s == final:
            fetch_got(s).wait_recv()
        else:
            fetch_got(s).wait()

        def columns_step(d, carry):
            cols = pl.ds(pl.multiple_of(d * tile, tile), tile)
            for k in range(4):
                hot = hot_columns(column_ref[s, :, k : k + 1], capacity)
                part = jnp.dot(
                    hot,
                    kept_now[s, k * capacity : (k + 1) * capacity, cols],
                    preferred_element_type=f32,
                )
                sums[s, k, :, cols] = (part + sums[s, k, :, cols].astype(f32)).astype(bf16)
            return carry

        lax.fori_loop(0, sums.shape[3] // tile, columns_step, 0)
        for i in range(4):
            first(s, i).start()

    def pass_on(s):
        for i in range(2):
            first(s, i).wait_recv()
        sums[s, 2, :half] = (sums[s, 2, :half].astype(f32) + relay[s, 0].astype(f32)).astype(bf16)
        sums[s, 1, half:] = (sums[s, 1, half:].astype(f32) + relay[s, 1].astype(f32)).astype(bf16)
        for i in range(2):
            second(s, i).start()

    def finish(s):
        for i in range(2):
            first(s, 2 + i).wait_recv()
            second(s, i).wait_recv()
        total = sums[s, 0].astype(f32) + from_x[s].astype(f32) + from_y[s].astype(f32)
        if s:
            own[s] = total.astype(bf16)
            along_z(s).start()
        else:
            out_ref[...] = total

    fetch_got(final).start()
    for s in order:
        fetch_kept(s).start()
        if s != final:
            fetch_got(s).start()
    table_ref[...] = scalar_ref[...]
    for bit in range(2):
        exchange.start(bit)
        exchange.end(bit)
    for i, s in enumerate(order):
        combine(s)
        if i < 3:
            exchange.start(2 + i)
            exchange.end(2 + i)
        if i == 0:
            to_sibling().start()
        if i >= 1:
            pass_on(order[i - 1])
        if i >= 2:
            finish(order[i - 2])
    pass_on(order[-1])
    finish(order[-2])
    finish(order[-1])
    for s in order[:-1]:
        along_z(s).wait_recv()
        out_ref[...] += from_z[s - 1].astype(f32)
    to_sibling().wait()
    exchange.finish()
    fetch_got(final).wait_send()
    for s in order:
        for i in range(4):
            first(s, i).wait_send()
        for i in range(2):
            second(s, i).wait_send()
        if s:
            along_z(s).wait_send()


def return_rows(columns, kept, got, given, out_given, out_got, scalars, capacity):
    chunks, rows, _ = columns.shape
    width = kept.shape[2]
    held = pl.BlockSpec(memory_space=pltpu.VMEM)
    anywhere = pl.BlockSpec(memory_space=pl.ANY)
    dma = pltpu.SemaphoreType.DMA
    return pl.pallas_call(
        functools.partial(return_rows_kernel, capacity),
        out_shape=(
            jax.ShapeDtypeStruct((rows, width), f32),
            jax.ShapeDtypeStruct(out_got.shape, out_got.dtype),
            jax.ShapeDtypeStruct(scalars.shape, f32),
        ),
        in_specs=[held] + [anywhere] * 5 + [held],
        out_specs=[held, anywhere, held],
        input_output_aliases={5: 1},
        scratch_shapes=[
            pltpu.VMEM((chunks, 4 * capacity, width), bf16),
            pltpu.VMEM((chunks, 4, rows, width), bf16),
            pltpu.VMEM((chunks, 2, rows // 2, width), bf16),
            pltpu.VMEM((chunks, rows, width), bf16),
            pltpu.VMEM((chunks, rows, width), bf16),
            pltpu.VMEM((chunks, rows, width), bf16),
            pltpu.VMEM((chunks - 1, rows, width), bf16),
            dma((chunks,)),
            dma((chunks,)),
            dma((chunks, 4)),
            dma((chunks, 4)),
            dma((chunks, 2)),
            dma((chunks, 2)),
            dma((chunks - 1,)),
            dma((chunks - 1,)),
            dma((2,)),
            dma((2,)),
        ]
        + exchange_scratch(scalars.shape[2]),
        compiler_params=pltpu.CompilerParams(
            collective_id=2, has_side_effects=True, vmem_limit_bytes=60 * 2**20
        ),
        cost_estimate=pl.CostEstimate(flops=1000, bytes_accessed=1000, transcendentals=0),
        name="return_rows",
    )(columns, kept, got, given, out_given, out_got, scalars)


def gather_first_kernel(
    q_width,
    kv_heads,
    acts_ref,
    grad_ref,
    weight_ref,
    named_ref,
    acts_out,
    grad_out,
    weight_out,
    table_ref,
    own_weight,
    near_sent,
    near_got,
    far_sent,
    far_got,
    weight_sent,
    weight_got,
    core_sent,
    core_got,
    z_sent,
    z_got,
    local,
    *exchange_refs,
):
    near = neighbours()
    exchange = Exchange(near, table_ref, *exchange_refs)
    ctx, fsdp = lax.axis_index("ctx"), lax.axis_index("fsdp")
    far = (ctx, flip(flip(fsdp, 1), 2))
    partners = [near["x"], near["y"], far]
    groups = [flip(fsdp, 1), flip(fsdp, 2), flip(flip(fsdp, 1), 2)]
    greet([near["core"]] + partners + near["z"][1:])
    rows = acts_ref.shape[0]
    half = rows // 2
    shard_rows = weight_ref.shape[0]
    half_shard = shard_rows // 2
    own_width = weight_out.shape[1]
    head_dim = (own_width - q_width) // 2
    all_q = weight_ref.shape[1] - 2 * kv_heads * head_dim
    core = lax.rem(ctx, 2)
    chain = Chain(near, grad_ref, lambda s: grad_out.at[s], z_sent, z_got)

    def to_near(k):
        return send(acts_ref, acts_out.at[1 + k], near_sent.at[k], near_got.at[k], partners[k])

    def to_far(k):
        span = pl.ds(k * half, half)
        return send(
            acts_out.at[1 + k, span], acts_out.at[3, span], far_sent.at[k], far_got.at[k], partners[1 - k]
        )

    def spans(group):
        return (
            (pl.ds(pl.multiple_of(group * q_width, 128), q_width), pl.ds(0, q_width)),
            (pl.ds(pl.multiple_of(all_q + group * head_dim, 128), head_dim), pl.ds(q_width, head_dim)),
            (
                pl.ds(pl.multiple_of(all_q + (kv_heads + group) * head_dim, 128), head_dim),
                pl.ds(q_width + head_dim, head_dim),
            ),
        )

    def weight_to(k, i):
        there, here = spans(groups[k])[i]
        from_row = pl.multiple_of(core * half_shard, 16)
        to_row = pl.multiple_of(fsdp * shard_rows + core * half_shard, 16)
        return send(
            weight_ref.at[pl.ds(from_row, half_shard), there],
            weight_out.at[pl.ds(to_row, half_shard), here],
            weight_sent.at[k, i],
            weight_got.at[k, i],
            partners[k],
        )

    def weight_on(k):
        row = pl.multiple_of(groups[k] * shard_rows + core * half_shard, 16)
        part = weight_out.at[pl.ds(row, half_shard)]
        return send(part, part, core_sent.at[k], core_got.at[k], near["core"])

    table_ref[...] = named_ref[...]
    exchange.start(0)
    to_near(0).start()
    chain.start()
    exchange.end(0)
    exchange.start(1)
    to_near(1).start()
    exchange.end(1)
    for k in (2, 0, 1):
        for i in range(3):
            weight_to(k, i).start()
    exchange.start(2)
    exchange.end(2)
    own_parts = [
        pltpu.make_async_copy(weight_ref.at[:, there], own_weight.at[:, here], local.at[i])
        for i, (there, here) in enumerate(spans(fsdp))
    ]
    keeps = [
        pltpu.make_async_copy(acts_ref, acts_out.at[0], local.at[3]),
        pltpu.make_async_copy(grad_ref, grad_out.at[0], local.at[4]),
    ]
    for copy in own_parts + keeps:
        copy.start()
    for copy in own_parts:
        copy.wait()
    place = pltpu.make_async_copy(
        own_weight,
        weight_out.at[pl.ds(pl.multiple_of(fsdp * shard_rows, 16), shard_rows)],
        local.at[5],
    )
    place.start()
    for k in range(2):
        to_near(k).wait_recv()
        to_far(k).start()
    chain.wait(1)
    chain.wait_inner_last()
    for bit in (3, 4):
        exchange.start(bit)
        exchange.end(bit)
    chain.start_inner(1)
    for k in (2, 0, 1):
        for i in range(3):
            weight_to(k, i).wait_recv()
        weight_on(k).start()
    chain.step(2)
    for k in range(2):
        to_far(k).wait_recv()
    for k in range(3):
        weight_on(k).wait_recv()
    chain.step(3)
    for copy in keeps + [place]:
        copy.wait()
    chain.finish()
    exchange.finish()
    for k in range(2):
        to_near(k).wait_send()
        to_far(k).wait_send()
    for k in range(3):
        for i in range(3):
            weight_to(k, i).wait_send()
        weight_on(k).wait_send()


def gather_first(acts, grad, weight, named, n_fsdp, z_count, q_width, kv_heads, head_dim):
    rows, width = acts.shape
    own_width = q_width + 2 * head_dim
    held = pl.BlockSpec(memory_space=pltpu.VMEM)
    anywhere = pl.BlockSpec(memory_space=pl.ANY)
    dma = pltpu.SemaphoreType.DMA
    return pl.pallas_call(
        functools.partial(gather_first_kernel, q_width, kv_heads),
        out_shape=(
            jax.ShapeDtypeStruct((n_fsdp, rows, width), bf16),
            jax.ShapeDtypeStruct((z_count, rows, width), bf16),
            jax.ShapeDtypeStruct((n_fsdp * weight.shape[0], own_width), bf16),
            jax.ShapeDtypeStruct(named.shape, f32),
        ),
        in_specs=[held, held, anywhere, held],
        out_specs=[anywhere] * 3 + [held],
        scratch_shapes=[
            pltpu.VMEM((weight.shape[0], own_width), bf16),
            dma((2,)),
            dma((2,)),
            dma((2,)),
            dma((2,)),
            dma((3, 3)),
            dma((3, 3)),
            dma((3,)),
            dma((3,)),
            dma((5,)),
            dma((3,)),
            dma((6,)),
        ]
        + exchange_scratch(named.shape[2]),
        compiler_params=pltpu.CompilerParams(
            collective_id=3, has_side_effects=True, vmem_limit_bytes=32 * 2**20
        ),
        cost_estimate=pl.CostEstimate(flops=1000, bytes_accessed=1000, transcendentals=0),
        name="gather_first",
    )(acts, grad, weight, named)


def finish_kernel(
    kv_heads,
    parts_ref,
    tokens_ref,
    resid_grad_ref,
    gain_ref,
    shares_ref,
    q_ref,
    kv_ref,
    router_ref,
    later_ref,
    own_ref,
    for_x_ref,
    for_y_ref,
    resid_ref,
    grad_ref,
    gains_ref,
    weight_ref,
    router_out_ref,
    output_ref,
    rows_x,
    rows_y,
    rows_z,
    rows_own,
    relay,
    from_x,
    from_y,
    q_core,
    kv_core,
    router_core,
    q_sum,
    kv_sum,
    router_sum,
    q_z,
    kv_z,
    router_z,
    q_total,
    kv_total,
    router_total,
    router_got,
    gain_got,
    first_sent,
    first_got,
    second_sent,
    second_got,
    core_sent,
    core_got,
    z_sent,
    z_got,
    row_sent,
    row_got,
    gain_sent,
    gain_in,
    rows_sent,
    rows_got,
    local,
):
    near = neighbours()
    ctx, fsdp = lax.axis_index("ctx"), lax.axis_index("fsdp")
    groups = [fsdp, flip(fsdp, 1), flip(fsdp, 2), flip(flip(fsdp, 1), 2)]
    partners = [None] + [(ctx, group) for group in groups[1:]]
    greet([near["core"]] + partners[1:] + near["z"][1:])
    rows = tokens_ref.shape[0]
    half = rows // 2
    low, high = pl.ds(0, half), pl.ds(half, half)
    own_ctx = [ctx] + [partner[0] for partner in near["z"][1:]]
    chunks = len(own_ctx)
    streams = (
        (q_ref, q_core, q_sum, q_z, q_total),
        (kv_ref, kv_core, kv_sum, kv_z, kv_total),
        (router_ref, router_core, router_sum, router_z, router_total),
    )
    out_rows = weight_ref.shape[0]
    q_width = q_ref.shape[2]
    head_dim = kv_ref.shape[2] // 2
    all_q = weight_ref.shape[1] - 2 * kv_heads * head_dim

    def first(i):
        source, target, partner = (
            (parts_ref.at[3, low], relay.at[0], near["x"]),
            (parts_ref.at[3, high], relay.at[1], near["y"]),
            (parts_ref.at[1, low], from_x.at[low], near["x"]),
            (parts_ref.at[2, high], from_y.at[high], near["y"]),
        )[i]
        return send(source, target, first_sent.at[i], first_got.at[i], partner)

    def second(i):
        source, target, partner = (
            (relay.at[0], from_y.at[low], near["y"]),
            (relay.at[1], from_x.at[high], near["x"]),
        )[i]
        return send(source, target, second_sent.at[i], second_got.at[i], partner)

    def to_core(i, s):
        source, landing = streams[i][:2]
        return send(
            source.at[flip(own_ctx[s], 1)],
            landing.at[s],
            core_sent.at[i, s],
            core_got.at[i, s],
            near["core"],
        )

    def along_z(i, s):
        return send(
            streams[i][2].at[s],
            streams[i][3].at[s - 1],
            z_sent.at[i, s - 1],
            z_got.at[i, s - 1],
            near["z"][s],
        )

    def row_parts(k):
        span = pl.ds(pl.multiple_of(groups[k] * out_rows, 8), out_rows)

        def at(start, width):
            return pl.ds(pl.multiple_of(start, 128), width)

        return (
            (q_total.at[span], weight_ref.at[:, at(fsdp * q_width, q_width)]),
            (
                kv_total.at[span, pl.ds(0, head_dim)],
                weight_ref.at[:, at(all_q + fsdp * head_dim, head_dim)],
            ),
            (
                kv_total.at[span, pl.ds(head_dim, head_dim)],
                weight_ref.at[:, at(all_q + (kv_heads + fsdp) * head_dim, head_dim)],
            ),
            (router_total.at[span], router_got.at[k]),
        )

    def to_row(k, i):
        source, target = row_parts(k)[i]
        return send(source, target, row_sent.at[k - 1, i], row_got.at[k - 1, i], partners[k])

    def keep_row(i):
        source, target = row_parts(0)[i]
        return pltpu.make_async_copy(source, target, local.at[i])

    gain_partners = [near["core"], near["x"], near["y"], near["z"][1], near["z"][2]]

    def share(i):
        return send(
            gains_ref, gain_got.at[i], gain_sent.at[i], gain_in.at[i], gain_partners[i]
        )

    def rows_copy(i):
        source, target, partner = (
            (later_ref.at[1], rows_z.at[0], near["z"][1]),
            (for_x_ref, rows_x, near["x"]),
            (for_y_ref, rows_y, near["y"]),
            (rows_own.at[0], rows_z.at[1], near["z"][2]),
            (rows_own.at[1], rows_z.at[2], near["z"][1]),
        )[i]
        return send(source, target, rows_sent.at[i], rows_got.at[i], partner)

    rows_copy(0).start()
    for i in range(4):
        first(i).start()
    for s in (2, 3, 1, 0):
        for i in range(3):
            to_core(i, s).start()
    for s in (2, 3, 1, 0):
        for i in range(3):
            source, landing, total, _, _ = streams[i]
            to_core(i, s).wait_recv()
            total[s] = (source[own_ctx[s]].astype(f32) + landing[s].astype(f32)).astype(bf16)
            if s:
                along_z(i, s).start()
    for i in range(2):
        first(i).wait_recv()
    relay[0] = (relay[0].astype(f32) + parts_ref[2, :half].astype(f32)).astype(bf16)
    relay[1] = (relay[1].astype(f32) + parts_ref[1, half:].astype(f32)).astype(bf16)
    for i in range(2):
        second(i).start()
    rows_copy(1).start()
    rows_copy(2).start()
    rows_copy(0).wait_recv()
    rows_own[0] = (later_ref[0].astype(f32) + rows_z[0].astype(f32)).astype(bf16)
    rows_copy(3).start()
    for i in range(2):
        first(2 + i).wait_recv()
        second(i).wait_recv()
    gains_ref[...] = shares_ref[...]
    block = 32

    def back_step(b, carry):
        span = pl.ds(pl.multiple_of(b * block, block), block)
        grad = (
            parts_ref[0, span, :].astype(f32)
            + from_x[span, :].astype(f32)
            + from_y[span, :].astype(f32)
        )
        values = tokens_ref[span, :].astype(f32)
        scale = lax.rsqrt(jnp.mean(values * values, axis=-1, keepdims=True) + eps_norm)
        unit = values * scale
        scaled = grad * gain_ref[...]
        back = scale * (scaled - unit * jnp.mean(scaled * unit, axis=-1, keepdims=True))
        grad_ref[span, :] = resid_grad_ref[span, :] + back
        gains_ref[0] += jnp.sum(grad * unit, axis=0, keepdims=True)
        return carry

    lax.fori_loop(0, rows // block, back_step, 0)
    share(0).start()
    for i in range(3):
        _, _, held, landing, total = streams[i]
        for s in range(1, chunks):
            along_z(i, s).wait_recv()
        added = held[0].astype(f32)
        for s in range(1, chunks):
            added += landing[s - 1].astype(f32)
        total[...] = added
    for k in range(1, 4):
        for i in range(4):
            to_row(k, i).start()
    for i in range(3):
        keep_row(i).start()
    rows_copy(1).wait_recv()
    rows_copy(2).wait_recv()
    rows_own[1] = (own_ref[1].astype(f32) + rows_x[1].astype(f32) + rows_y[1].astype(f32)).astype(bf16)
    rows_copy(4).start()
    for i in range(len(gain_partners)):
        if i:
            share(i).start()
        share(i).wait()
        gains_ref[...] += gain_got[i]
    own = pl.ds(pl.multiple_of(fsdp * out_rows, 8), out_rows)
    router_all = router_total[own, :]
    for k in range(1, 4):
        for i in range(4):
            to_row(k, i).wait()
        router_all += router_got[k]
    router_out_ref[...] = router_all
    for i in range(3):
        keep_row(i).wait()
    rows_copy(3).wait_recv()
    rows_copy(4).wait_recv()

    def output_step(b, carry):
        span = pl.ds(pl.multiple_of(b * block, block), block)
        total = resid_ref[span, :] + own_ref[0, span, :].astype(f32)
        for part in (rows_x[0, span, :], rows_y[0, span, :], rows_z[1, span, :], rows_z[2, span, :]):
            total += part.astype(f32)
        output_ref[span, :] = total.astype(bf16)
        return carry

    lax.fori_loop(0, rows // block, output_step, 0)
    for i in range(5):
        rows_copy(i).wait_send()
    for i in range(4):
        first(i).wait_send()
    for i in range(2):
        second(i).wait_send()
    for i in range(3):
        for s in range(chunks):
            to_core(i, s).wait_send()
            if s:
                along_z(i, s).wait_send()


def finish(parts, tokens, resid_grad, gain, shares, grad_q, grad_kv, grad_router, expert_rows, resid, kv_heads):
    rows, width = tokens.shape
    n_ctx, share_rows, q_width = grad_q.shape
    pair_width, router_width = grad_kv.shape[2], grad_router.shape[2]
    chunks = n_ctx // 2
    out_rows = share_rows // 4
    all_width = 4 * q_width + kv_heads * pair_width
    held = pl.BlockSpec(memory_space=pltpu.VMEM)
    dma = pltpu.SemaphoreType.DMA
    widths = (q_width, pair_width, router_width)
    return pl.pallas_call(
        functools.partial(finish_kernel, kv_heads),
        out_shape=(
            jax.ShapeDtypeStruct((rows, width), f32),
            jax.ShapeDtypeStruct(shares.shape, f32),
            jax.ShapeDtypeStruct((out_rows, all_width), f32),
            jax.ShapeDtypeStruct((out_rows, router_width), f32),
            jax.ShapeDtypeStruct((rows, width), bf16),
        ),
        in_specs=[held] * 13,
        out_specs=[held] * 5,
        scratch_shapes=[
            pltpu.VMEM((2, rows, width), bf16),
            pltpu.VMEM((2, rows, width), bf16),
            pltpu.VMEM((3, rows, width), bf16),
            pltpu.VMEM((2, rows, width), bf16),
            pltpu.VMEM((2, rows // 2, width), bf16),
            pltpu.VMEM((rows, width), bf16),
            pltpu.VMEM((rows, width), bf16),
        ]
        + [pltpu.VMEM((chunks, share_rows, columns), bf16) for columns in widths]
        + [pltpu.VMEM((chunks, share_rows, columns), bf16) for columns in widths]
        + [pltpu.VMEM((chunks - 1, share_rows, columns), bf16) for columns in widths]
        + [pltpu.VMEM((share_rows, columns), f32) for columns in widths]
        + [
            pltpu.VMEM((4, out_rows, router_width), f32),
            pltpu.VMEM((5,) + shares.shape, f32),
            dma((4,)),
            dma((4,)),
            dma((2,)),
            dma((2,)),
            dma((3, chunks)),
            dma((3, chunks)),
            dma((3, chunks - 1)),
            dma((3, chunks - 1)),
            dma((3, 4)),
            dma((3, 4)),
            dma((5,)),
            dma((5,)),
            dma((5,)),
            dma((5,)),
            dma((3,)),
        ],
        compiler_params=pltpu.CompilerParams(
            collective_id=4, has_side_effects=True, vmem_limit_bytes=62 * 2**20
        ),
        cost_estimate=pl.CostEstimate(flops=1000, bytes_accessed=1000, transcendentals=0),
        name="finish",
    )(parts, tokens, resid_grad, gain, shares, grad_q, grad_kv, grad_router, *expert_rows, resid)


def fast_body(
    n_ctx,
    tokens,
    positions,
    expert_ids,
    attn_gain,
    query_key_value_weight,
    q_gain,
    k_gain,
    output_weight,
    ffn_gain,
    router_weight,
    w_gate,
    w_up,
    w_down,
    cotangent,
):
    n_fsdp = 4
    n_all = n_ctx * n_fsdp
    ctx_at = lax.axis_index("ctx")
    fsdp_at = lax.axis_index("fsdp")
    core_at = ctx_at % 2
    own_at = ctx_at * n_fsdp + fsdp_at
    row_count = tokens.shape[1]
    model_width = tokens.shape[2]
    head_dim = q_gain.shape[0]
    shard_rows = query_key_value_weight.shape[0]
    heads = output_weight.shape[0] // head_dim
    q_width = heads * head_dim
    all_q = q_width * n_fsdp
    kv_heads = (query_key_value_weight.shape[1] - all_q) // (2 * head_dim)
    own_width = q_width + 2 * head_dim
    expert_count = n_all
    top_count = expert_ids.shape[2]
    capacity = row_count * top_count * 3 // (2 * expert_count)
    z_count = n_ctx // 2
    chunk_rows = 2 * n_fsdp * capacity

    inputs = tokens.reshape(row_count, model_width).astype(f32)
    places = positions.reshape(row_count)
    chosen = expert_ids.reshape(row_count, top_count)
    grad_res_low = cotangent.reshape(row_count, model_width)
    grad_res = grad_res_low.astype(f32)

    relative = jnp.bitwise_xor(own_at, jnp.arange(n_all, dtype=jnp.int32))
    chosen_rel = (chosen[:, :, None] == relative[None, None, :]).astype(f32)
    named = jnp.sum(chosen_rel, axis=1).T
    first_block = jnp.broadcast_to((places[0] // run_rows).astype(f32), (n_all, 128))
    named = jnp.concatenate([named, first_block], axis=1)[:, None, :]

    rms_one = lax.rsqrt(jnp.mean(inputs * inputs, axis=-1, keepdims=True) + eps_norm)
    acts = (inputs * rms_one * attn_gain).astype(bf16)
    acts_group, grad_slots, weight_qkv, small = gather_first(
        acts, grad_res_low, query_key_value_weight, named, n_fsdp, z_count, q_width, kv_heads, head_dim
    )
    named_here = small[:, 0, :row_count]
    block_table = small[:, 0, row_count].astype(jnp.int32).reshape(n_ctx, n_fsdp)
    acts_group = acts_group.reshape(n_fsdp * row_count, model_width)

    group_rows = n_fsdp * row_count
    blocks_total = 2 * n_ctx
    own_blocks = block_table[0]
    run_blocks = jnp.stack([own_blocks, blocks_total - 1 - own_blocks], axis=1)
    row_places = (
        run_blocks[:, :, None] * run_rows + jnp.arange(run_rows, dtype=jnp.int32)[None, None, :]
    ).reshape(n_fsdp, row_count, 1)
    angles = row_places.astype(f32) * frequencies(head_dim)
    cosine, sine = jnp.cos(angles), jnp.sin(angles)
    cosine = jnp.concatenate([cosine, cosine], axis=-1)
    sine = jnp.concatenate([-sine, sine], axis=-1)
    block_index = jnp.arange(blocks_total, dtype=jnp.int32)
    slot_index = jnp.arange(n_ctx, dtype=jnp.int32)[:, None, None]
    source_table = jnp.sum(
        jnp.where(block_table[:, :, None] == block_index, 2 * slot_index, 0)
        + jnp.where(blocks_total - 1 - block_table[:, :, None] == block_index, 2 * slot_index + 1, 0),
        axis=0,
    )
    place_list = run_blocks.reshape(-1)
    source_list = source_table.reshape(-1)

    projected, query_low, kv_own = project(
        acts_group.reshape(n_fsdp, row_count, model_width),
        weight_qkv,
        cosine,
        sine,
        q_gain[None],
        k_gain[None],
        heads,
    )

    grad_x = swap(grad_slots, "fsdp", n_fsdp, 1)
    grad_y = swap(grad_slots, "fsdp", n_fsdp, 2)

    kv_slots = [kv_own] + [swap(kv_own, "ctx", n_ctx, 2 * k) for k in range(1, z_count)]
    kv_slots = jnp.stack(kv_slots)
    kv_all = jnp.stack([kv_slots, swap(kv_slots, "ctx", n_ctx, 1)], axis=1)
    kv_all = kv_all.reshape(n_ctx, n_fsdp, row_count, 2 * head_dim)

    mixed, lse = attend(place_list, source_list, query_low, kv_all)
    heads_low = mixed.reshape(group_rows, q_width)
    heads_low = after(heads_low, (grad_x, grad_y))

    resid_parts = jnp.dot(heads_low, output_weight, preferred_element_type=f32).astype(bf16)
    resid = inputs + scatter_parts(resid_parts.reshape(n_fsdp, row_count, model_width))
    rms_two = lax.rsqrt(jnp.mean(resid * resid, axis=-1, keepdims=True) + eps_norm)
    acts_two = (resid * rms_two * ffn_gain).astype(bf16)

    full_router = by_fsdp(
        [router_weight] + [swap(router_weight, "fsdp", n_fsdp, k) for k in range(1, n_fsdp)], fsdp_at
    ).reshape(n_fsdp * shard_rows, expert_count)
    logits = jnp.dot(acts_two, full_router, preferred_element_type=f32)
    pick_table = (chosen[:, :, None] == jnp.arange(expert_count)[None, None, :]).astype(f32)
    picked = jnp.sum(logits[:, None, :] * pick_table, axis=-1)
    gate_vals, gate_back = jax.vjp(lambda values: jax.nn.softmax(values, axis=-1), picked)
    gates_rel = jnp.sum(chosen_rel * gate_vals[:, :, None], axis=1).T

    upper = jnp.triu(jnp.ones((row_count, row_count), bf16), 1)
    rank = jnp.dot(named_here.astype(bf16), upper, preferred_element_type=f32)
    slots = jnp.where(named_here > 0.5, rank, -1.0).reshape(z_count, 2 * n_fsdp, row_count)
    columns = jnp.swapaxes(slots, 1, 2)
    gates = gates_rel[:, None, :]
    gate_w = w_gate[0]
    up_w = w_up[0]
    down_w = w_down[0]


    (
        act_rows,
        grad_rows,
        hidden_rows,
        gate_lows,
        up_lows,
        kept,
        got,
        given,
        out_kept,
        out_got,
        out_given,
        scalars,
        *_,
    ) = gather_experts(
        acts_two,
        slots,
        columns,
        gates,
        gate_w,
        up_w,
        down_w,
        [grad_slots, grad_x, grad_y],
        capacity,
    )
    acts_two_grad, out_got, gate_grad_rel = return_rows(
        columns, kept, got, given, out_given, out_got, scalars.reshape(n_all, 1, row_count), capacity
    )
    gate_grad = jnp.sum(chosen_rel * gate_grad_rel[:, 0].T[:, None, :], axis=-1)
    (picked_grad,) = gate_back(gate_grad)
    logit_grad = jnp.sum(picked_grad[:, :, None] * pick_table, axis=1).astype(bf16)
    acts_two_grad = acts_two_grad + jnp.dot(
        logit_grad, full_router.T, preferred_element_type=f32
    )

    scaled = ffn_gain * acts_two_grad
    grad_ffn_gain = jnp.sum(acts_two_grad * resid * rms_two, axis=0)
    resid_grad = (
        grad_res
        + rms_two * scaled
        - resid * (rms_two**3 * jnp.mean(scaled * resid, axis=-1, keepdims=True))
    )
    attn_grad = resid_grad.astype(bf16)
    row_total = z_count * chunk_rows

    def weight_grad(left, right, earlier):
        left = after(left, earlier)
        return jnp.einsum(
            "rd,rf->df",
            left.reshape(row_total, -1),
            right.reshape(row_total, -1),
            preferred_element_type=f32,
        )[None]

    grad_w_down = weight_grad(hidden_rows, grad_rows, attn_grad)
    combined = combine_rows(after(columns, attn_grad), out_kept, out_got, capacity)
    half_rows = row_count // 2
    near_x = swap(attn_grad, "fsdp", n_fsdp, 1)
    near_y = swap(attn_grad, "fsdp", n_fsdp, 2)
    near_x, near_y, *combined = after((near_x, near_y), combined, True)
    out_own, out_x, out_y, out_low, out_high = combined
    far_low = swap(near_x[:half_rows], "fsdp", n_fsdp, 2)
    far_high = swap(near_y[half_rows:], "fsdp", n_fsdp, 1)
    far_low, far_high, grad_w_down = after((far_low, far_high), (grad_w_down,), True)
    attn_grad_group = jnp.concatenate([attn_grad, near_x, near_y, far_low, far_high], axis=0)
    heads_grad = jnp.einsum(
        "td,cd->tc", attn_grad_group, output_weight, preferred_element_type=f32
    ).astype(bf16)
    grad_w_out = jnp.einsum(
        "tc,td->cd", heads_low, attn_grad_group, preferred_element_type=f32
    ).astype(bf16)
    heads_grad = heads_grad.reshape(n_fsdp, row_count, q_width)
    per_ctx = grad_w_out.shape[0] // n_ctx
    out_split = grad_w_out.reshape(z_count, 2, per_ctx, model_width)
    out_keep = lax.dynamic_index_in_dim(out_split, core_at, 1, keepdims=False)
    out_away = lax.dynamic_index_in_dim(out_split, 1 - core_at, 1, keepdims=False)
    out_sum = (out_keep.astype(f32) + swap(out_away, "ctx", n_ctx, 1).astype(f32)).astype(bf16)
    z_at = ctx_at // 2
    heads_grad = after(heads_grad, out_sum)
    out_terms = [
        swap(pick(out_sum, z_at ^ k), "ctx", n_ctx, 2 * k) for k in range(1, z_count)
    ]
    dq, dkv, dq_gain = attend_back(
        place_list,
        source_list,
        query_low,
        kv_all,
        mixed,
        heads_grad,
        lse,
        projected,
        cosine,
        sine,
        q_gain[None],
    )

    half_slots = z_count // 2
    out_low, out_high = after((out_low, out_high), attn_grad_group)
    from_x = swap(out_low, "fsdp", n_fsdp, 1)
    from_y = swap(out_high, "fsdp", n_fsdp, 2)
    dq, dkv, dq_gain, from_x, from_y, *out_terms = after(
        (dq, dkv, dq_gain), (from_x, from_y, *out_terms), True
    )

    def added(parts, term, low, span):
        term = term[span].astype(f32)
        parts = parts[span].astype(f32)
        pad = ((0, 0), (0, half_rows), (0, 0)) if low else ((0, 0), (half_rows, 0), (0, 0))
        return (parts + jnp.pad(term, pad)).astype(bf16)

    near_span, far_span = slice(0, half_slots), slice(half_slots, z_count)
    later_x = swap(added(out_x, from_y, False, far_span), "fsdp", n_fsdp, 1)
    later_y = swap(added(out_y, from_x, True, far_span), "fsdp", n_fsdp, 2)
    sooner_x = added(out_x, from_y, False, near_span)
    sooner_y = added(out_y, from_x, True, near_span)
    proj_low_q = dq.reshape(group_rows, q_width)

    held = dkv.reshape(z_count, 2, n_fsdp, row_count, 2 * head_dim)
    held = (held[:, 0].astype(f32) + swap(held[:, 1], "ctx", n_ctx, 1).astype(f32)).astype(bf16)
    held_core = held
    held = [held[0]] + [swap(held[k], "ctx", n_ctx, 2 * k) for k in range(1, z_count)]
    held = after(held, (later_x, later_y))
    dkv_own, dk_gain = key_back(held, projected, cosine, sine, k_gain[None])
    proj_low_kv = dkv_own.reshape(group_rows, 2 * head_dim)
    acts_parts = (
        jnp.einsum("tc,dc->td", proj_low_q, weight_qkv[:, :q_width], preferred_element_type=f32)
        + jnp.einsum("tc,dc->td", proj_low_kv, weight_qkv[:, q_width:], preferred_element_type=f32)
    ).astype(bf16)

    def token_sum(left, right):
        return jnp.einsum("td,tc->dc", left, right, preferred_element_type=f32).astype(bf16)

    share_rows = model_width // n_ctx
    grad_q = token_sum(acts_group, proj_low_q).reshape(n_ctx, share_rows, q_width)
    grad_kv = token_sum(acts_group, proj_low_kv).reshape(n_ctx, share_rows, 2 * head_dim)
    padded = jnp.pad(logit_grad, ((0, 0), (0, -expert_count % 128)))
    grad_router = token_sum(after(acts_two, attn_grad_group), padded)
    grad_router = grad_router.reshape(n_ctx, share_rows, -1)
    small_gains = jnp.concatenate([jnp.sum(dq_gain, axis=0), jnp.sum(dk_gain, axis=0)])
    shares = jnp.stack(
        [
            jnp.zeros_like(grad_ffn_gain),
            grad_ffn_gain,
            jnp.pad(small_gains, (0, model_width - small_gains.shape[0])),
        ]
    )[:, None, :]
    out_later = (
        out_own[far_span].astype(f32) + later_x.astype(f32) + later_y.astype(f32)
    ).astype(bf16)
    grad_tokens, gains, grad_w_qkv, grad_w_router, output = finish(
        acts_parts.reshape(n_fsdp, row_count, model_width),
        tokens.reshape(row_count, model_width),
        resid_grad,
        attn_gain[None],
        shares,
        grad_q,
        grad_kv,
        grad_router,
        (out_later, out_own[near_span], sooner_x, sooner_y),
        resid,
        kv_heads,
    )
    output = output.reshape(tokens.shape)
    grad_tokens = grad_tokens.reshape(tokens.shape)
    grad_w_router = grad_w_router[:, :expert_count]
    grad_attn_gain = gains[0, 0]
    grad_ffn_gain = gains[1, 0]
    grad_q_gain = gains[2, 0, :head_dim]
    grad_k_gain = gains[2, 0, head_dim : 2 * head_dim]

    grad_w_out = pick(out_sum, z_at).astype(f32)
    for term in out_terms:
        grad_w_out = grad_w_out + term.astype(f32)
    grad_w_out = lax.ppermute(
        grad_w_out.astype(bf16),
        ("ctx", "fsdp"),
        [(c * n_fsdp + f, f * n_ctx + c) for c in range(n_ctx) for f in range(n_fsdp)],
    ).astype(f32)

    grad_w_gate = weight_grad(act_rows, gate_lows, held_core)
    grad_w_up = weight_grad(act_rows, up_lows, held_core)

    return (
        output,
        grad_tokens,
        grad_attn_gain,
        grad_w_qkv,
        grad_q_gain,
        grad_k_gain,
        grad_w_out,
        grad_ffn_gain,
        grad_w_router,
        grad_w_gate,
        grad_w_up,
        grad_w_down,
    )


def solution(mesh):
    n_ctx, n_fsdp = mesh.shape["ctx"], mesh.shape["fsdp"]

    def body(*arrays):
        heads_kv = (arrays[4].shape[1] - arrays[7].shape[0] * n_fsdp) // (2 * arrays[5].shape[0])
        if n_fsdp == 4 and heads_kv == n_fsdp and n_ctx == 8:
            return fast_body(n_ctx, *arrays)
        return general_body(*arrays)

    whole = P(("ctx", "fsdp"), None, None)
    rows = P(("ctx", "fsdp"), None)
    split = P("fsdp", "ctx", None)
    return jax.shard_map(
        body,
        mesh=mesh,
        in_specs=(
            split,
            P("fsdp", "ctx"),
            split,
            P(),
            P("fsdp", None),
            P(),
            P(),
            P("fsdp", None),
            P(),
            P("fsdp", None),
            whole,
            whole,
            whole,
            split,
        ),
        out_specs=(split, split, P(), rows, P(), P(), rows, P(), rows, whole, whole, whole),
        check_vma=False,
    )
```

```python
import functools
import math

import jax
import jax.numpy as jnp
from jax import lax
from jax.experimental import pallas as pl
from jax.experimental.pallas import tpu as pltpu
from jax.sharding import PartitionSpec as P

eps_norm = 1e-06
rope_base = 1000000.0
masked_value = -1e30
run_rows = 128
bf16 = jnp.bfloat16
f32 = jnp.float32


def rms_scale(values, gain):
    mean_sq = jnp.mean(values * values, axis=-1, keepdims=True)
    return values * lax.rsqrt(mean_sq + eps_norm) * gain


def frequencies(head_dim):
    return 1.0 / rope_base ** (jnp.arange(0, head_dim, 2).astype(jnp.float32) / head_dim)


def rotate(values, angles):
    half_dim = values.shape[-1] // 2
    cosine = jnp.cos(angles)
    sine_val = jnp.sin(angles)
    first_half = values[..., :half_dim]
    second_half = values[..., half_dim:]
    return jnp.concatenate(
        [
            first_half * cosine - second_half * sine_val,
            second_half * cosine + first_half * sine_val,
        ],
        axis=-1,
    )


def head_prep(projected, gain_q, gain_k, angles, heads_q, heads_kv):
    head_dim = gain_q.shape[0]
    row_count = projected.shape[0]
    q_width = heads_q * head_dim
    kv_width = heads_kv * head_dim
    queries = projected[:, :q_width].reshape(row_count, heads_q, head_dim)
    key_heads = projected[:, q_width : q_width + kv_width].reshape(row_count, heads_kv, head_dim)
    value_heads = projected[:, q_width + kv_width :].reshape(row_count, heads_kv, head_dim)
    queries = rotate(rms_scale(queries, gain_q), angles)
    key_heads = rotate(rms_scale(key_heads, gain_k), angles)
    return (queries, key_heads, value_heads)


def general_body(
    tokens,
    positions,
    expert_ids,
    attn_gain,
    query_key_value_weight,
    q_gain,
    k_gain,
    output_weight,
    ffn_gain,
    router_weight,
    w_gate,
    w_up,
    w_down,
    cotangent,
):
    row_count = tokens.shape[1]
    model_width = tokens.shape[2]
    head_dim = q_gain.shape[0]
    inputs = tokens.reshape(row_count, model_width).astype(jnp.float32)
    places = positions.reshape(row_count)
    chosen = expert_ids.reshape(row_count, -1)
    top_count = chosen.shape[1]
    full_qkv, full_out, full_router = (
        lax.all_gather(query_key_value_weight, "fsdp", axis=0, tiled=True),
        lax.all_gather(output_weight, "fsdp", axis=0, tiled=True),
        lax.all_gather(router_weight, "fsdp", axis=0, tiled=True),
    )
    heads_q = full_out.shape[0] // head_dim
    heads_kv = (full_qkv.shape[1] - full_out.shape[0]) // (2 * head_dim)
    group_size = heads_q // heads_kv
    expert_count = full_router.shape[1]
    capacity = row_count * top_count * 3 // (2 * expert_count)
    local_experts = w_gate.shape[0]
    score_scale = 1.0 / math.sqrt(head_dim)
    normed, norm_back = jax.vjp(rms_scale, inputs, attn_gain)
    first_activations = normed.astype(jnp.bfloat16)
    query_key_value_projected = jnp.dot(
        first_activations, full_qkv, preferred_element_type=jnp.float32
    )
    angles = places.astype(jnp.float32)[:, None, None] * frequencies(head_dim)[None, None, :]

    def prepare(proj_in, gain_q, gain_k):
        return head_prep(proj_in, gain_q, gain_k, angles, heads_q, heads_kv)

    (queries, key_heads, value_heads), prep_back = jax.vjp(
        prepare, query_key_value_projected, q_gain, k_gain
    )
    query_low = queries.astype(jnp.bfloat16).reshape(row_count, heads_kv, group_size, head_dim)
    key_low = key_heads.astype(jnp.bfloat16)
    value_low = value_heads.astype(jnp.bfloat16)
    all_keys, all_values = (
        lax.all_gather(key_low, "ctx", axis=0, tiled=True),
        lax.all_gather(value_low, "ctx", axis=0, tiled=True),
    )
    key_places = lax.all_gather(places, "ctx", axis=0, tiled=True)
    seq_len = all_keys.shape[0]
    sorted_keys = jnp.zeros_like(all_keys).at[key_places].set(all_keys)
    sorted_values = jnp.zeros_like(all_values).at[key_places].set(all_values)
    block_len = min(512, seq_len)
    run_len = row_count // 2

    def block_scores(query_run, place_run, block_index):
        start = block_index * block_len
        key_blk = lax.dynamic_slice_in_dim(sorted_keys, start, block_len, 0)
        value_blk = lax.dynamic_slice_in_dim(sorted_values, start, block_len, 0)
        raw_scores = (
            jnp.einsum("qhgd,khd->hgqk", query_run, key_blk, preferred_element_type=jnp.float32)
            * score_scale
        )
        key_pos = start + jnp.arange(block_len, dtype=jnp.int32)
        visible = key_pos[None, :] <= place_run[:, None]
        return (jnp.where(visible, raw_scores, masked_value), visible, key_blk, value_blk)

    run_info = []
    mixed_runs = []
    for run_index in range(2):
        query_run = query_low[run_index * run_len : (run_index + 1) * run_len]
        place_run = places[run_index * run_len : (run_index + 1) * run_len]
        block_total = jnp.max(place_run) // block_len + 1

        def stats_step(block_index, carried):
            run_max, run_sum = carried
            scores, visible, key_blk, value_blk = block_scores(query_run, place_run, block_index)
            new_max = jnp.maximum(run_max, jnp.max(scores, axis=-1))
            weights = jnp.where(visible, jnp.exp(scores - new_max[..., None]), 0.0)
            run_sum = run_sum * jnp.exp(run_max - new_max) + jnp.sum(weights, axis=-1)
            return (new_max, run_sum)

        stat_shape = (heads_kv, group_size, run_len)
        initial = (
            jnp.full(stat_shape, masked_value, jnp.float32),
            jnp.zeros(stat_shape, jnp.float32),
        )
        run_max, run_sum = lax.fori_loop(0, block_total, stats_step, initial)
        log_total = run_max + jnp.log(run_sum)

        def output_step(block_index, running):
            scores, visible, key_blk, value_blk = block_scores(query_run, place_run, block_index)
            prob_vals = jnp.exp(scores - log_total[..., None])
            return running + jnp.einsum(
                "hgqk,khd->qhgd",
                prob_vals.astype(jnp.bfloat16),
                value_blk,
                preferred_element_type=jnp.float32,
            )

        mixed_run = lax.fori_loop(
            0,
            block_total,
            output_step,
            jnp.zeros((run_len, heads_kv, group_size, head_dim), jnp.float32),
        )
        mixed_runs.append(mixed_run)
        run_info.append((query_run, place_run, block_total, log_total))
    heads_out = jnp.concatenate(mixed_runs, axis=0)
    heads_reduced_precision = heads_out.reshape(row_count, heads_q * head_dim).astype(jnp.bfloat16)
    residual_stream = inputs + jnp.dot(
        heads_reduced_precision, full_out, preferred_element_type=jnp.float32
    )
    normed_two, norm_two_back = jax.vjp(rms_scale, residual_stream, ffn_gain)
    second_activations = normed_two.astype(jnp.bfloat16)
    router_logits = jnp.dot(second_activations, full_router, preferred_element_type=jnp.float32)
    pick_table = (chosen[:, :, None] == jnp.arange(expert_count)[None, None, :]).astype(jnp.float32)
    picked = jnp.sum(router_logits[:, None, :] * pick_table, axis=-1)
    gate_vals, gate_back = jax.vjp(lambda values: jax.nn.softmax(values, axis=-1), picked)
    flat_choice = chosen.reshape(-1)
    slot_hot = (flat_choice[:, None] == jnp.arange(expert_count)[None, :]).astype(jnp.int32)
    slot_rank = jnp.sum((jnp.cumsum(slot_hot, axis=0) - slot_hot) * slot_hot, axis=1)
    targets = flat_choice * capacity + slot_rank
    source_rows = jnp.repeat(second_activations, top_count, axis=0)
    outgoing = (
        jnp.zeros((expert_count * capacity, model_width), jnp.bfloat16).at[targets].set(source_rows)
    )
    outgoing = outgoing.reshape(expert_count, capacity, model_width)
    arrived = lax.all_to_all(outgoing, ("ctx", "fsdp"), split_axis=0, concat_axis=0, tiled=True)
    sources = arrived.shape[0] // local_experts
    slot_count = arrived.shape[1]
    grouped = arrived.reshape(sources, local_experts, slot_count, model_width)
    gate_pre = jnp.einsum("secd,edf->secf", grouped, w_gate, preferred_element_type=jnp.float32)
    up_pre = jnp.einsum("secd,edf->secf", grouped, w_up, preferred_element_type=jnp.float32)
    hidden = (jax.nn.silu(gate_pre) * up_pre).astype(jnp.bfloat16)
    produced = jnp.einsum("secf,efd->secd", hidden, w_down, preferred_element_type=jnp.float32)
    produced = produced.astype(jnp.bfloat16).reshape(arrived.shape)
    flat_shape = (arrived.shape[0], slot_count, gate_pre.shape[3])
    expert_results = (produced, arrived, gate_pre.reshape(flat_shape), up_pre.reshape(flat_shape))
    produced = expert_results[0]
    arrived = expert_results[1]
    returned = lax.all_to_all(produced, ("ctx", "fsdp"), split_axis=0, concat_axis=0, tiled=True)
    expert_rows = returned.reshape(expert_count * capacity, model_width)[targets].reshape(
        row_count, top_count, model_width
    )
    expert_vals = expert_rows.astype(jnp.float32)
    result = residual_stream + jnp.sum(gate_vals[:, :, None] * expert_vals, axis=1)
    output = result.astype(jnp.bfloat16).reshape(tokens.shape)
    grad_res = cotangent.reshape(row_count, model_width).astype(jnp.float32)
    gate_grad = jnp.sum(grad_res[:, None, :] * expert_vals, axis=-1)
    out_grad = (gate_vals[:, :, None] * grad_res[:, None, :]).astype(jnp.bfloat16)
    back_out = (
        jnp.zeros((expert_count * capacity, model_width), jnp.bfloat16)
        .at[targets]
        .set(out_grad.reshape(-1, model_width))
    )
    back_out = back_out.reshape(expert_count, capacity, model_width)
    (picked_grad,) = gate_back(gate_grad)
    logit_grad = jnp.sum(picked_grad[:, :, None] * pick_table, axis=1).astype(jnp.bfloat16)
    full_qkv, full_out, full_router = (
        lax.all_gather(query_key_value_weight, "fsdp", axis=0, tiled=True),
        lax.all_gather(output_weight, "fsdp", axis=0, tiled=True),
        lax.all_gather(router_weight, "fsdp", axis=0, tiled=True),
    )
    arrived_grad = lax.all_to_all(
        back_out, ("ctx", "fsdp"), split_axis=0, concat_axis=0, tiled=True
    )
    sources = arrived.shape[0] // local_experts
    grouped = arrived.reshape(sources, local_experts, capacity, model_width)
    grad_grouped = arrived_grad.reshape(sources, local_experts, capacity, model_width)
    gate_pre = expert_results[2].reshape(sources, local_experts, capacity, -1)
    up_pre = expert_results[3].reshape(sources, local_experts, capacity, -1)
    hidden, hidden_back = jax.vjp(
        lambda gate_in, up_in: jax.nn.silu(gate_in) * up_in, gate_pre, up_pre
    )
    hidden_low = hidden.astype(jnp.bfloat16)
    hidden_grad = jnp.einsum(
        "secd,efd->secf", grad_grouped, w_down, preferred_element_type=jnp.float32
    )
    gate_pre_grad, up_pre_grad = hidden_back(hidden_grad)
    gate_low = gate_pre_grad.astype(jnp.bfloat16)
    up_low = up_pre_grad.astype(jnp.bfloat16)
    grad_w_down = jnp.einsum(
        "secf,secd->efd", hidden_low, grad_grouped, preferred_element_type=jnp.float32
    )
    grad_w_gate = jnp.einsum(
        "secd,secf->edf", grouped, gate_low, preferred_element_type=jnp.float32
    )
    grad_w_up = jnp.einsum("secd,secf->edf", grouped, up_low, preferred_element_type=jnp.float32)
    row_grad = jnp.einsum(
        "secf,edf->secd", gate_low, w_gate, preferred_element_type=jnp.float32
    ) + jnp.einsum("secf,edf->secd", up_low, w_up, preferred_element_type=jnp.float32)
    row_grad = row_grad.astype(jnp.bfloat16).reshape(arrived.shape)
    row_back = lax.all_to_all(row_grad, ("ctx", "fsdp"), split_axis=0, concat_axis=0, tiled=True)
    token_rows = row_back.reshape(expert_count * capacity, model_width)[targets].reshape(
        row_count, top_count, model_width
    )
    acts_two_grad = jnp.sum(token_rows.astype(jnp.float32), axis=1) + jnp.dot(
        logit_grad, full_router.T, preferred_element_type=jnp.float32
    )
    grad_w_router = jnp.dot(second_activations.T, logit_grad, preferred_element_type=jnp.float32)
    resid_extra, grad_ffn_gain = norm_two_back(acts_two_grad)
    resid_grad = grad_res + resid_extra
    attn_grad = resid_grad.astype(jnp.bfloat16)
    grad_w_out = jnp.dot(heads_reduced_precision.T, attn_grad, preferred_element_type=jnp.float32)
    heads_grad = jnp.dot(attn_grad, full_out.T, preferred_element_type=jnp.float32).astype(
        jnp.bfloat16
    )
    heads_grad = heads_grad.reshape(row_count, heads_kv, group_size, head_dim)
    row_delta = jnp.moveaxis(jnp.sum(heads_grad.astype(jnp.float32) * heads_out, axis=-1), 0, 2)
    key_grad_sorted = jnp.zeros((seq_len, heads_kv, head_dim), jnp.float32)
    value_grad_sorted = jnp.zeros((seq_len, heads_kv, head_dim), jnp.float32)
    query_grad_runs = []
    for run_index in range(2):
        query_run, place_run, block_total, log_total = run_info[run_index]
        grad_run = heads_grad[run_index * run_len : (run_index + 1) * run_len]
        delta_run = row_delta[:, :, run_index * run_len : (run_index + 1) * run_len]

        def back_step(block_index, carried):
            query_grad, key_acc, value_acc = carried
            scores, visible, key_blk, value_blk = block_scores(query_run, place_run, block_index)
            prob_vals = jnp.exp(scores - log_total[..., None])
            value_grad = jnp.einsum(
                "hgqk,qhgd->khd",
                prob_vals.astype(jnp.bfloat16),
                grad_run,
                preferred_element_type=jnp.float32,
            )
            prob_grad = jnp.einsum(
                "qhgd,khd->hgqk", grad_run, value_blk, preferred_element_type=jnp.float32
            )
            score_grad = (prob_vals * (prob_grad - delta_run[..., None])).astype(jnp.bfloat16)
            query_grad = (
                query_grad
                + jnp.einsum(
                    "hgqk,khd->qhgd", score_grad, key_blk, preferred_element_type=jnp.float32
                )
                * score_scale
            )
            key_grad = (
                jnp.einsum(
                    "hgqk,qhgd->khd", score_grad, query_run, preferred_element_type=jnp.float32
                )
                * score_scale
            )
            start = block_index * block_len
            key_acc = lax.dynamic_update_slice_in_dim(
                key_acc, lax.dynamic_slice_in_dim(key_acc, start, block_len, 0) + key_grad, start, 0
            )
            value_acc = lax.dynamic_update_slice_in_dim(
                value_acc,
                lax.dynamic_slice_in_dim(value_acc, start, block_len, 0) + value_grad,
                start,
                0,
            )
            return (query_grad, key_acc, value_acc)

        start_state = (
            jnp.zeros((run_len, heads_kv, group_size, head_dim), jnp.float32),
            key_grad_sorted,
            value_grad_sorted,
        )
        query_grad_run, key_grad_sorted, value_grad_sorted = lax.fori_loop(
            0, block_total, back_step, start_state
        )
        query_grad_runs.append(query_grad_run)
    query_grad = jnp.concatenate(query_grad_runs, axis=0)
    key_grads = key_grad_sorted[key_places]
    value_grads = value_grad_sorted[key_places]
    key_grad_own, value_grad_own = (
        lax.psum_scatter(
            key_grads.astype(jnp.bfloat16), "ctx", scatter_dimension=0, tiled=True
        ).astype(jnp.float32),
        lax.psum_scatter(
            value_grads.astype(jnp.bfloat16), "ctx", scatter_dimension=0, tiled=True
        ).astype(jnp.float32),
    )
    proj_grad, grad_q_gain, grad_k_gain = prep_back(
        (query_grad.reshape(row_count, heads_q, head_dim), key_grad_own, value_grad_own)
    )
    proj_low = proj_grad.astype(jnp.bfloat16)
    grad_w_qkv = jnp.dot(first_activations.T, proj_low, preferred_element_type=jnp.float32)
    acts_grad = jnp.dot(proj_low, full_qkv.T, preferred_element_type=jnp.float32)
    inputs_extra, grad_attn_gain = norm_back(acts_grad)
    grad_tokens = (resid_grad + inputs_extra).reshape(tokens.shape)
    grad_w_qkv, grad_w_out, grad_w_router = (
        lax.psum_scatter(grad_w_qkv, ("ctx", "fsdp"), scatter_dimension=0, tiled=True),
        lax.psum_scatter(grad_w_out, ("ctx", "fsdp"), scatter_dimension=0, tiled=True),
        lax.psum_scatter(grad_w_router, ("ctx", "fsdp"), scatter_dimension=0, tiled=True),
    )
    grad_attn_gain, grad_q_gain, grad_k_gain, grad_ffn_gain = lax.psum(
        (grad_attn_gain, grad_q_gain, grad_k_gain, grad_ffn_gain), ("ctx", "fsdp")
    )
    return (
        output,
        grad_tokens,
        grad_attn_gain,
        grad_w_qkv,
        grad_q_gain,
        grad_k_gain,
        grad_w_out,
        grad_ffn_gain,
        grad_w_router,
        grad_w_gate,
        grad_w_up,
        grad_w_down,
    )


def swap(values, axis, count, bit):
    return lax.ppermute(values, axis, [(i, i ^ bit) for i in range(count)])


def after(values, earlier, both=False):
    values, earlier = lax.optimization_barrier((values, earlier))
    return (*values, *earlier) if both else values


def pick(values, index):
    return lax.dynamic_index_in_dim(values, index, 0, keepdims=False)


def by_fsdp(pieces, fsdp_at):
    stacked = jnp.stack(pieces)
    stacked = jnp.where(fsdp_at % 2 == 1, jnp.stack([pieces[k ^ 1] for k in range(4)]), stacked)
    turned = jnp.stack([stacked[k ^ 2] for k in range(4)])
    return jnp.where(fsdp_at // 2 == 1, turned, stacked)


def plane_gather(values):
    half = values.shape[-2] // 2
    near_x = swap(values, "fsdp", 4, 1)
    near_y = swap(values, "fsdp", 4, 2)
    far_low = swap(near_x[..., :half, :], "fsdp", 4, 2)
    far_high = swap(near_y[..., half:, :], "fsdp", 4, 1)
    return [values, near_x, near_y, far_low, far_high]


def plane_scatter(own, x_low, x_high, y_low, y_high, far_low, far_high):
    from_x = swap(far_low, "fsdp", 4, 1)
    from_y = swap(far_high, "fsdp", 4, 2)
    got_x_low = swap(x_low, "fsdp", 4, 1)
    got_y_high = swap(y_high, "fsdp", 4, 2)
    got_y_low = swap((y_low.astype(f32) + from_x.astype(f32)).astype(bf16), "fsdp", 4, 2)
    got_x_high = swap((x_high.astype(f32) + from_y.astype(f32)).astype(bf16), "fsdp", 4, 1)
    added = jnp.concatenate(
        [
            got_x_low.astype(f32) + got_y_low.astype(f32),
            got_x_high.astype(f32) + got_y_high.astype(f32),
        ],
        axis=-2,
    )
    return own.astype(f32) + added


def scatter_parts(parts):
    half = parts.shape[1] // 2
    return plane_scatter(
        parts[0],
        parts[1, :half],
        parts[1, half:],
        parts[2, :half],
        parts[2, half:],
        parts[3, :half],
        parts[3, half:],
    )


def ctx_scatter(parts, n_ctx, ctx_at, low):
    bit = 1
    held = parts
    while bit < n_ctx:
        mine = (ctx_at // bit) % 2
        split = held.reshape((held.shape[0] // 2, 2) + held.shape[1:])
        keep = lax.dynamic_index_in_dim(split, mine, 1, keepdims=False)
        away = lax.dynamic_index_in_dim(split, 1 - mine, 1, keepdims=False)
        got = swap(away, "ctx", n_ctx, bit)
        held = keep.astype(f32) + got.astype(f32)
        bit *= 2
        if low and bit < n_ctx:
            held = held.astype(bf16)
    return held.reshape(parts.shape[1:])


def attend_kernel(place_ref, source_ref, q_ref, kv_ref, o_ref, lse_ref, keys, vals_t, q_t, acc, total):
    seq = pl.program_id(0)
    rows = run_rows
    heads = q_ref.shape[2] // rows
    blocks = keys.shape[0] // rows
    scale = math.log2(math.e) / math.sqrt(rows)
    for p in range(blocks):
        at = source_ref[seq * blocks + p]
        block = kv_ref[at // 2, 0, pl.ds(pl.multiple_of((at % 2) * rows, rows), rows), :]
        keys[p * rows : (p + 1) * rows, :] = block[:, :rows]
        vals_t[:, p * rows : (p + 1) * rows] = block[:, rows:].T
    key_iota = lax.broadcasted_iota(jnp.int32, (2 * rows, 2 * rows), 0)
    query_iota = lax.broadcasted_iota(jnp.int32, (2 * rows, 2 * rows), 1) % rows
    for run in range(2):
        place = place_ref[seq * 2 + run]
        for h in range(heads):
            q_t[:, h * rows : (h + 1) * rows] = q_ref[
                0, run * rows : (run + 1) * rows, h * rows : (h + 1) * rows
            ].T
        acc[...] = jnp.zeros_like(acc)
        total[...] = jnp.zeros_like(total)

        def step(j, masked):
            start = pl.multiple_of(j * 2 * rows, 2 * rows)
            key_blk = keys[pl.ds(start, 2 * rows), :]
            val_blk = vals_t[:, pl.ds(start, 2 * rows)]
            for pair in range(heads // 2):
                cols = slice(pair * 2 * rows, (pair + 1) * 2 * rows)
                scores = jnp.dot(key_blk, q_t[:, cols], preferred_element_type=f32)
                weights = jnp.exp2(scores * scale)
                if masked:
                    seen = start + key_iota <= place * rows + query_iota
                    weights = jnp.where(seen, weights, 0.0)
                total[:, cols] += jnp.sum(weights.reshape(2 * rows // 8, 8, 2 * rows), axis=0)
                acc[:, cols] += jnp.dot(val_blk, weights.astype(bf16), preferred_element_type=f32)

        lax.fori_loop(0, place // 2, lambda j, c: (step(j, False), c)[1], 0)
        step(place // 2, True)
        norm = jnp.sum(total[...], axis=0, keepdims=True)
        lse_ref[0, run : run + 1, :] = jnp.log2(norm)
        mixed = acc[...] / norm
        for h in range(heads):
            o_ref[0, run * rows : (run + 1) * rows, h * rows : (h + 1) * rows] = (
                mixed[:, h * rows : (h + 1) * rows].T.astype(bf16)
            )


def head_back(turned, vector, cosine, sine, gain):
    grad = turned * cosine - pltpu.roll(turned, turned.shape[1] // 2, 1) * sine
    scale = lax.rsqrt(jnp.mean(vector * vector, axis=-1, keepdims=True) + eps_norm)
    unit = vector * scale
    scaled = grad * gain
    back = scale * (scaled - unit * jnp.mean(scaled * unit, axis=-1, keepdims=True))
    return back, grad * unit


def project_kernel(heads, acts_ref, weight_ref, cos_ref, sin_ref, gain_q_ref, gain_k_ref, proj_ref, q_ref, kv_ref):
    width = cos_ref.shape[2]
    proj_ref[0] = jnp.dot(acts_ref[0], weight_ref[...], preferred_element_type=f32)
    for h in range(heads + 1):
        vector = proj_ref[0, :, h * width : (h + 1) * width]
        gain = gain_q_ref[...] if h < heads else gain_k_ref[...]
        scale = lax.rsqrt(jnp.mean(vector * vector, axis=-1, keepdims=True) + eps_norm)
        normed = vector * scale * gain
        turned = normed * cos_ref[0] + pltpu.roll(normed, width // 2, 1) * sin_ref[0]
        if h < heads:
            q_ref[0, :, h * width : (h + 1) * width] = turned.astype(bf16)
        else:
            kv_ref[0, :, :width] = turned.astype(bf16)
    kv_ref[0, :, width:] = proj_ref[0, :, (heads + 1) * width :].astype(bf16)


def key_back_kernel(a_ref, b_ref, c_ref, d_ref, proj_ref, cos_ref, sin_ref, gain_ref, dkv_ref, dgain_ref):
    width = cos_ref.shape[2]
    total = (
        a_ref[0].astype(f32) + b_ref[0].astype(f32) + c_ref[0].astype(f32) + d_ref[0].astype(f32)
    )
    back, share = head_back(
        total[:, :width], proj_ref[0, :, :width], cos_ref[0], sin_ref[0], gain_ref[...]
    )
    dkv_ref[0, :, :width] = back.astype(bf16)
    dkv_ref[0, :, width:] = total[:, width:].astype(bf16)

    @pl.when(pl.program_id(0) == 0)
    def _():
        dgain_ref[...] = jnp.zeros_like(dgain_ref)

    dgain_ref[...] += jnp.sum(share.reshape(-1, 8, width), axis=0)


def attend_back_kernel(
    place_ref,
    source_ref,
    q_ref,
    kv_ref,
    o_ref,
    do_ref,
    lse_ref,
    proj_ref,
    cos_ref,
    sin_ref,
    gain_ref,
    dq_ref,
    dkv_ref,
    dkv_sibling_ref,
    dgain_ref,
    keys,
    keys_t,
    vals,
    q_n,
    q_t,
    do_n,
    do_t,
    delta,
    dq_acc,
    dk_acc,
    dv_acc,
):
    seq = pl.program_id(0)
    rows = run_rows
    heads = q_ref.shape[2] // rows
    blocks = keys.shape[0] // rows
    scale = math.log2(math.e) / math.sqrt(rows)
    plain_scale = 1.0 / math.sqrt(rows)
    for p in range(blocks):
        at = source_ref[seq * blocks + p]
        block = kv_ref[at // 2, 0, pl.ds(pl.multiple_of((at % 2) * rows, rows), rows), :]
        keys[p * rows : (p + 1) * rows, :] = block[:, :rows]
        keys_t[:, p * rows : (p + 1) * rows] = block[:, :rows].T
        vals[p * rows : (p + 1) * rows, :] = block[:, rows:]
    dk_acc[...] = jnp.zeros_like(dk_acc)
    dv_acc[...] = jnp.zeros_like(dv_acc)

    @pl.when(seq == 0)
    def _():
        dgain_ref[...] = jnp.zeros_like(dgain_ref)

    key_iota = lax.broadcasted_iota(jnp.int32, (2 * rows, 2 * rows), 0)
    query_iota = lax.broadcasted_iota(jnp.int32, (2 * rows, 2 * rows), 1) % rows
    for run in range(2):
        place = place_ref[seq * 2 + run]
        here = slice(run * rows, (run + 1) * rows)
        for h in range(heads):
            cols = slice(h * rows, (h + 1) * rows)
            q_h = q_ref[0, here, cols]
            q_n[cols, :] = q_h
            q_t[:, cols] = q_h.T
            do_h = do_ref[0, here, cols]
            do_n[cols, :] = do_h
            do_ht = do_h.T
            do_t[:, cols] = do_ht
            o_ht = o_ref[0, here, cols].T
            delta[:, cols] = jnp.sum(do_ht.astype(f32) * o_ht.astype(f32), axis=0, keepdims=True)
        dq_acc[...] = jnp.zeros_like(dq_acc)

        def step(j, masked):
            start = pl.multiple_of(j * 2 * rows, 2 * rows)
            key_blk = keys[pl.ds(start, 2 * rows), :]
            key_t_blk = keys_t[:, pl.ds(start, 2 * rows)]
            val_blk = vals[pl.ds(start, 2 * rows), :]
            dk_sum = jnp.zeros((2 * rows, rows), f32)
            dv_sum = jnp.zeros((2 * rows, rows), f32)
            for pair in range(heads // 2):
                cols = slice(pair * 2 * rows, (pair + 1) * 2 * rows)
                scores = jnp.dot(key_blk, q_t[:, cols], preferred_element_type=f32)
                probs = jnp.exp2(scores * scale - lse_ref[0, run : run + 1, cols])
                if masked:
                    seen = start + key_iota <= place * rows + query_iota
                    probs = jnp.where(seen, probs, 0.0)
                prob_grad = jnp.dot(val_blk, do_t[:, cols], preferred_element_type=f32)
                score_grad = (probs * (prob_grad - delta[:, cols])).astype(bf16)
                dv_sum += jnp.dot(probs.astype(bf16), do_n[cols, :], preferred_element_type=f32)
                dk_sum += jnp.dot(score_grad, q_n[cols, :], preferred_element_type=f32)
                dq_acc[:, cols] += jnp.dot(key_t_blk, score_grad, preferred_element_type=f32)
            dk_acc[pl.ds(start, 2 * rows), :] += dk_sum
            dv_acc[pl.ds(start, 2 * rows), :] += dv_sum

        lax.fori_loop(0, place // 2, lambda j, c: (step(j, False), c)[1], 0)
        step(place // 2, True)
        for h in range(heads):
            cols = slice(h * rows, (h + 1) * rows)
            turned = dq_acc[:, cols].T * plain_scale
            back, share = head_back(
                turned, proj_ref[0, here, cols], cos_ref[0, here, :], sin_ref[0, here, :], gain_ref[...]
            )
            dq_ref[0, here, cols] = back.astype(bf16)
            dgain_ref[...] += jnp.sum(share.reshape(rows // 8, 8, rows), axis=0)
    for p in range(blocks):
        at = source_ref[seq * blocks + p]
        span = slice(p * rows, (p + 1) * rows)
        there = pl.ds(pl.multiple_of((at % 2) * rows, rows), rows)
        slot = at // 2

        def put(ref):
            ref[slot // 2, 0, there, :rows] = (dk_acc[span, :] * plain_scale).astype(bf16)
            ref[slot // 2, 0, there, rows:] = dv_acc[span, :].astype(bf16)

        pl.when(slot % 2 == 0)(functools.partial(put, dkv_ref))
        pl.when(slot % 2 == 1)(functools.partial(put, dkv_sibling_ref))


def attend(places, sources, queries, kv):
    seqs, rows, width = queries.shape
    slots, _, _, pair_width = kv.shape
    head_dim = pair_width // 2
    seq_len = slots * rows
    return pl.pallas_call(
        attend_kernel,
        out_shape=(
            jax.ShapeDtypeStruct(queries.shape, bf16),
            jax.ShapeDtypeStruct((seqs, 2, width), f32),
        ),
        grid_spec=pltpu.PrefetchScalarGridSpec(
            num_scalar_prefetch=2,
            grid=(seqs,),
            in_specs=[
                pl.BlockSpec((1, rows, width), lambda s, *_: (s, 0, 0)),
                pl.BlockSpec((slots, 1, rows, pair_width), lambda s, *_: (0, s, 0, 0)),
            ],
            out_specs=[
                pl.BlockSpec((1, rows, width), lambda s, *_: (s, 0, 0)),
                pl.BlockSpec((1, 2, width), lambda s, *_: (s, 0, 0)),
            ],
            scratch_shapes=[
                pltpu.VMEM((seq_len, head_dim), bf16),
                pltpu.VMEM((head_dim, seq_len), bf16),
                pltpu.VMEM((head_dim, width), bf16),
                pltpu.VMEM((head_dim, width), f32),
                pltpu.VMEM((8, width), f32),
            ],
        ),
        compiler_params=pltpu.CompilerParams(vmem_limit_bytes=32 * 2**20),
        cost_estimate=pl.CostEstimate(flops=1000, bytes_accessed=1000, transcendentals=0),
        name="attend",
    )(places, sources, queries, kv)


def attend_back(places, sources, queries, kv, mixed, mixed_grad, lse, projected, cosine, sine, gain):
    seqs, rows, width = queries.shape
    slots, _, _, pair_width = kv.shape
    head_dim = pair_width // 2
    seq_len = slots * rows
    block = pl.BlockSpec((1, rows, width), lambda s, *_: (s, 0, 0))
    angle_block = pl.BlockSpec((1, rows, head_dim), lambda s, *_: (s, 0, 0))
    kv_block = pl.BlockSpec((slots, 1, rows, pair_width), lambda s, *_: (0, s, 0, 0))
    half_kv_block = pl.BlockSpec((slots // 2, 1, rows, pair_width), lambda s, *_: (0, s, 0, 0))
    return pl.pallas_call(
        attend_back_kernel,
        out_shape=(
            jax.ShapeDtypeStruct(queries.shape, bf16),
            jax.ShapeDtypeStruct((slots // 2,) + kv.shape[1:], bf16),
            jax.ShapeDtypeStruct((slots // 2,) + kv.shape[1:], bf16),
            jax.ShapeDtypeStruct((8, head_dim), f32),
        ),
        grid_spec=pltpu.PrefetchScalarGridSpec(
            num_scalar_prefetch=2,
            grid=(seqs,),
            in_specs=[
                block,
                kv_block,
                block,
                block,
                pl.BlockSpec((1, 2, width), lambda s, *_: (s, 0, 0)),
                block,
                angle_block,
                angle_block,
                pl.BlockSpec((1, head_dim), lambda s, *_: (0, 0)),
            ],
            out_specs=[
                block,
                half_kv_block,
                half_kv_block,
                pl.BlockSpec((8, head_dim), lambda s, *_: (0, 0)),
            ],
            scratch_shapes=[
                pltpu.VMEM((seq_len, head_dim), bf16),
                pltpu.VMEM((head_dim, seq_len), bf16),
                pltpu.VMEM((seq_len, head_dim), bf16),
                pltpu.VMEM((width, head_dim), bf16),
                pltpu.VMEM((head_dim, width), bf16),
                pltpu.VMEM((width, head_dim), bf16),
                pltpu.VMEM((head_dim, width), bf16),
                pltpu.VMEM((1, width), f32),
                pltpu.VMEM((head_dim, width), f32),
                pltpu.VMEM((seq_len, head_dim), f32),
                pltpu.VMEM((seq_len, head_dim), f32),
            ],
        ),
        compiler_params=pltpu.CompilerParams(vmem_limit_bytes=40 * 2**20),
        cost_estimate=pl.CostEstimate(flops=1000, bytes_accessed=1000, transcendentals=0),
        name="attend_back",
    )(places, sources, queries, kv, mixed, mixed_grad, lse, projected, cosine, sine, gain)


def project(acts, weight, cosine, sine, gain_q, gain_k, heads):
    seqs, rows, depth = acts.shape
    head_dim = cosine.shape[2]
    width = weight.shape[1]
    angle_block = pl.BlockSpec((1, rows, head_dim), lambda s: (s, 0, 0))
    gain_block = pl.BlockSpec((1, head_dim), lambda s: (0, 0))

    def block(columns):
        return pl.BlockSpec((1, rows, columns), lambda s: (s, 0, 0))

    return pl.pallas_call(
        functools.partial(project_kernel, heads),
        out_shape=(
            jax.ShapeDtypeStruct((seqs, rows, width), f32),
            jax.ShapeDtypeStruct((seqs, rows, heads * head_dim), bf16),
            jax.ShapeDtypeStruct((seqs, rows, 2 * head_dim), bf16),
        ),
        grid=(seqs,),
        in_specs=[
            block(depth),
            pl.BlockSpec((depth, width), lambda s: (0, 0)),
            angle_block,
            angle_block,
            gain_block,
            gain_block,
        ],
        out_specs=[block(width), block(heads * head_dim), block(2 * head_dim)],
        compiler_params=pltpu.CompilerParams(vmem_limit_bytes=40 * 2**20),
        cost_estimate=pl.CostEstimate(flops=1000, bytes_accessed=1000, transcendentals=0),
        name="project",
    )(acts, weight, cosine, sine, gain_q, gain_k)


def key_back(held, projected, cosine, sine, gain):
    seqs, rows, pair_width = held[0].shape
    head_dim = pair_width // 2
    pairs_before = projected.shape[2] // pair_width - 1
    block = pl.BlockSpec((1, rows, pair_width), lambda s: (s, 0, 0))
    angle_block = pl.BlockSpec((1, rows, head_dim), lambda s: (s, 0, 0))
    return pl.pallas_call(
        key_back_kernel,
        out_shape=(
            jax.ShapeDtypeStruct(held[0].shape, bf16),
            jax.ShapeDtypeStruct((8, head_dim), f32),
        ),
        grid=(seqs,),
        in_specs=[
            block,
            block,
            block,
            block,
            pl.BlockSpec((1, rows, pair_width), lambda s: (s, 0, pairs_before)),
            angle_block,
            angle_block,
            pl.BlockSpec((1, head_dim), lambda s: (0, 0)),
        ],
        out_specs=[block, pl.BlockSpec((8, head_dim), lambda s: (0, 0))],
        name="key_back",
    )(*held, projected, cosine, sine, gain)


def hot_rows(slot_row, capacity):
    count = slot_row.shape[1]
    return slot_row == lax.broadcasted_iota(jnp.int32, (capacity, count), 0).astype(f32)


def hot_columns(slot_column, capacity):
    count = slot_column.shape[0]
    return (slot_column == lax.broadcasted_iota(jnp.int32, (count, capacity), 1).astype(f32)).astype(bf16)


def select_rows(capacity, slot_ref, s, pieces, store):
    for core in range(2):
        near = pieces[5 * core : 5 * core + 3]
        low, high = pieces[5 * core + 3], pieces[5 * core + 4]
        for k in range(4):
            source = 4 * core + k
            hot = hot_rows(slot_ref[s, source : source + 1, :], capacity).astype(bf16)
            if k < 3:
                rows = jnp.dot(hot, near[k][...], preferred_element_type=f32)
            else:
                half = low.shape[0]
                rows = jnp.dot(hot[:, :half], low[...], preferred_element_type=f32)
                rows += jnp.dot(hot[:, half:], high[...], preferred_element_type=f32)
            store(source, rows.astype(bf16))


def combine_kernel(capacity, column_ref, kept_ref, got_ref, own_ref, x_ref, y_ref, low_ref, high_ref):
    for k in range(4):
        span = slice(k * capacity, (k + 1) * capacity)
        own_hot = hot_columns(column_ref[0, :, k : k + 1], capacity)
        sibling_hot = hot_columns(column_ref[0, :, 4 + k : 5 + k], capacity)
        total = jnp.dot(own_hot, kept_ref[0, span, :], preferred_element_type=f32)
        total += jnp.dot(sibling_hot, got_ref[0, span, :], preferred_element_type=f32)
        total = total.astype(bf16)
        if k < 3:
            (own_ref, x_ref, y_ref)[k][0] = total
        else:
            half = total.shape[0] // 2
            low_ref[0] = total[:half]
            high_ref[0] = total[half:]


def combine_rows(columns, kept, got, capacity):
    chunks, rows, sources = columns.shape
    width = kept.shape[2]
    tile = width // 4
    at = lambda k, d: (k, 0, d)
    whole = pl.BlockSpec((1, rows, tile), at)
    half = pl.BlockSpec((1, rows // 2, tile), at)
    return pl.pallas_call(
        functools.partial(combine_kernel, capacity),
        out_shape=[jax.ShapeDtypeStruct((chunks, rows, width), bf16)] * 3
        + [jax.ShapeDtypeStruct((chunks, rows // 2, width), bf16)] * 2,
        grid=(chunks, 4),
        in_specs=[
            pl.BlockSpec((1, rows, sources), lambda k, d: (k, 0, 0)),
            pl.BlockSpec((1, 4 * capacity, tile), at),
            pl.BlockSpec((1, 4 * capacity, tile), at),
        ],
        out_specs=[whole] * 3 + [half] * 2,
        cost_estimate=pl.CostEstimate(flops=1000, bytes_accessed=1000, transcendentals=0),
        name="combine_rows",
    )(columns, kept, got)


def flip(index, bit):
    return index + bit - 2 * bit * ((index // bit) % 2)


def neighbours():
    ctx, fsdp = lax.axis_index("ctx"), lax.axis_index("fsdp")
    return dict(
        core=(flip(ctx, 1), fsdp),
        x=(ctx, flip(fsdp, 1)),
        y=(ctx, flip(fsdp, 2)),
        z=[None, (flip(ctx, 2), fsdp), (flip(ctx, 4), fsdp), (flip(flip(ctx, 2), 4), fsdp)],
    )


def greet(partners):
    barrier = pltpu.get_barrier_semaphore()
    for partner in partners:
        pl.semaphore_signal(barrier, inc=1, device_id=partner, device_id_type=pl.DeviceIdType.MESH)
    pl.semaphore_wait(barrier, len(partners))


def send(source, target, sent, received, partner):
    return pltpu.make_async_remote_copy(
        src_ref=source,
        dst_ref=target,
        send_sem=sent,
        recv_sem=received,
        device_id=partner,
        device_id_type=pl.DeviceIdType.MESH,
    )


class Exchange:
    def __init__(self, near, table, outgoing, landing, sent, got):
        self.partners = [near["x"], near["y"], near["core"], near["z"][1], near["z"][2]]
        self.table, self.outgoing, self.landing = table, outgoing, landing
        self.sent, self.got = sent, got
        self.rows = [[r for r in range(32) if (r >> bit) % 2] for bit in range(5)]

    def copy(self, bit):
        return send(
            self.outgoing.at[bit],
            self.landing.at[bit],
            self.sent.at[bit],
            self.got.at[bit],
            self.partners[bit],
        )

    def start(self, bit):
        for i, r in enumerate(self.rows[bit]):
            self.outgoing[bit, i] = self.table[r]
        self.copy(bit).start()

    def end(self, bit):
        self.copy(bit).wait_recv()
        for i, r in enumerate(self.rows[bit]):
            self.table[r] = self.landing[bit, i]

    def finish(self):
        for bit in range(5):
            self.copy(bit).wait_send()


def exchange_scratch(width):
    return [
        pltpu.VMEM((5, 16, 1, width), f32),
        pltpu.VMEM((5, 16, 1, width), f32),
        pltpu.SemaphoreType.DMA((5,)),
        pltpu.SemaphoreType.DMA((5,)),
    ]


class Chain:
    def __init__(self, near, own, place, sent, got):
        self.near, self.own, self.place, self.sent, self.got = near, own, place, sent, got
        z = lax.axis_index("ctx") // 2
        self.inner = (z == 1) | (z == 2)
        self.outer = (z == 0) | (z == 3)

    def copy(self, source, slot, number, partner):
        return send(
            source, self.place(slot), self.sent.at[number], self.got.at[slot - 1], self.near["z"][partner]
        )

    def first(self):
        return self.copy(self.own, 1, 0, 1)

    def inner_copies(self, stage):
        if stage == 0:
            return [(self.own, 3, 1, 3)]
        if stage == 1:
            return [(self.place(1), 2, 2, 3), (self.place(3), 2, 3, 1)]
        return [(self.place(2), 3, 4, 1)]

    def start(self):
        self.first().start()
        self.start_inner(0)

    def start_inner(self, stage):
        @pl.when(self.inner)
        def _():
            for copy in self.inner_copies(stage):
                self.copy(*copy).start()

    def wait(self, slot):
        if slot < 3:
            self.copy(self.own, slot, 0, 1).wait_recv()
        else:
            @pl.when(self.outer)
            def _():
                self.copy(self.own, 3, 0, 1).wait_recv()

    def wait_inner_last(self):
        @pl.when(self.inner)
        def _():
            self.copy(self.own, 3, 0, 1).wait_recv()

    def step(self, slot):
        if slot == 1:
            self.wait(1)
            self.wait_inner_last()
            self.start_inner(1)
        elif slot == 2:
            self.wait(2)
            self.start_inner(2)
        else:
            self.wait(3)

    def finish(self):
        self.first().wait_send()

        @pl.when(self.inner)
        def _():
            for stage in range(3):
                for copy in self.inner_copies(stage):
                    self.copy(*copy).wait_send()


def gather_experts_kernel(
    capacity,
    steps,
    acts_ref,
    slot_ref,
    sibling_ref,
    gates_ref,
    gate_ref,
    up_ref,
    down_ref,
    grad_ref,
    grad_x_ref,
    grad_y_ref,
    rows_ref,
    grad_rows_ref,
    hidden_ref,
    gate_low_ref,
    up_low_ref,
    kept_ref,
    got_ref,
    given_ref,
    out_kept_ref,
    out_got_ref,
    out_given_ref,
    scalar_ref,
    buffer_ref,
    grad_far_ref,
    sent_ref,
    grad_sent_ref,
    gate_acc,
    up_acc,
    back_acc,
    hidden_now,
    gate_low_now,
    up_low_now,
    gate_all,
    up_all,
    down_all,
    gate_table,
    z_sent,
    z_got,
    grad_z_sent,
    grad_z_got,
    near_sent,
    near_got,
    far_sent,
    far_got,
    grad_far_sent,
    grad_far_got,
    rows_sent,
    rows_got,
    given_sent,
    given_got,
    weight_sem,
    local,
    *exchange_refs,
):
    near = neighbours()
    chunks = slot_ref.shape[0]
    half = acts_ref.shape[0] // 2
    width = acts_ref.shape[1]
    tile = width // steps
    part = 4 * capacity
    group = 2 * part
    greet([near["core"], near["x"], near["y"]] + near["z"][1:])
    chain = Chain(near, acts_ref, lambda s: buffer_ref.at[s, 0], z_sent, z_got)
    grad_chain = Chain(
        near, grad_far_ref.at[0], lambda s: grad_far_ref.at[s], grad_z_sent, grad_z_got
    )
    exchange = Exchange(near, gate_table, *exchange_refs)

    def to_near(s, k):
        source = acts_ref if s == 0 else buffer_ref.at[s, 0]
        return send(
            source, buffer_ref.at[s, 1 + k], near_sent.at[s, k], near_got.at[s, k], near["xy"[k]]
        )

    def to_far(s, k):
        span = pl.ds(k * half, half)
        return send(
            buffer_ref.at[s, 1 + k, span],
            buffer_ref.at[s, 3, span],
            far_sent.at[s, k],
            far_got.at[s, k],
            near["yx"[k]],
        )

    def grad_to_far(k):
        span = pl.ds(k * half, half)
        return send(
            (grad_x_ref, grad_y_ref)[k].at[0, span],
            grad_far_ref.at[0, span],
            grad_far_sent.at[k],
            grad_far_got.at[k],
            near["yx"[k]],
        )

    def to_sibling_rows(s, i):
        source, target = ((grad_sent_ref, grad_rows_ref), (sent_ref, rows_ref))[i]
        return send(
            source.at[s],
            target.at[s, pl.ds(part, part)],
            rows_sent.at[s, i],
            rows_got.at[s, i],
            near["core"],
        )

    def to_sibling(s, i):
        source, target = ((given_ref, got_ref), (out_given_ref, out_got_ref))[i]
        return send(
            source.at[s], target.at[s], given_sent.at[s, i], given_got.at[s, i], near["core"]
        )

    def fetch_weight(i):
        source, target = ((down_ref, down_all), (gate_ref, gate_all), (up_ref, up_all))[i]
        return pltpu.make_async_copy(source, target, weight_sem.at[i])

    def span_of(d):
        return pl.ds(pl.multiple_of(d * tile, tile), tile)

    def select_step(s, *blocks):
        tokens, (own_blk, sibling_blk) = blocks[:-2], blocks[-2:]
        for k in range(4):
            hot = jnp.concatenate(
                [
                    hot_rows(slot_ref[s, k : k + 1, :], capacity).astype(bf16),
                    hot_rows(sibling_ref[s, k : k + 1, :], capacity).astype(bf16),
                ],
                axis=0,
            )
            block = tokens[0][k] if len(tokens) == 1 else tokens[k][...]
            rows = jnp.dot(hot, block, preferred_element_type=f32).astype(bf16)
            own_blk[k * capacity : (k + 1) * capacity, :] = rows[:capacity]
            sibling_blk[k * capacity : (k + 1) * capacity, :] = rows[capacity:]

    def select(s, i):
        out = pl.BlockSpec((part, tile), lambda d: (0, d))
        if i:
            in_specs = [pl.BlockSpec((4, 2 * half, tile), lambda d: (0, 0, d))]
            tokens = [buffer_ref.at[s]]
        else:
            in_specs = [pl.BlockSpec((2 * half, tile), lambda d: (0, d))] * 4
            tokens = [ref.at[s] for ref in (grad_ref, grad_x_ref, grad_y_ref, grad_far_ref)]
        target, sent = ((grad_rows_ref, grad_sent_ref), (rows_ref, sent_ref))[i]
        pltpu.emit_pipeline(
            functools.partial(select_step, s),
            grid=(steps,),
            in_specs=in_specs,
            out_specs=[out, out],
        )(*tokens, target.at[s, pl.ds(0, part)], sent.at[s])
        to_sibling_rows(s, i).start()

    def grad_step(rows_blk):
        d = pl.program_id(0)

        @pl.when(d == 0)
        def _():
            back_acc[...] = jnp.zeros_like(back_acc)

        back_acc[...] += lax.dot_general(
            rows_blk[...],
            down_all[:, span_of(d)],
            (((1,), (1,)), ((), ())),
            preferred_element_type=f32,
        )

    def compute_grad(s):
        pltpu.emit_pipeline(
            grad_step,
            grid=(steps,),
            in_specs=[pl.BlockSpec((group, tile), lambda d: (0, d))],
        )(grad_rows_ref.at[s])

    def experts_step(s, rows_blk, given_blk, kept_blk, out_given_blk, out_kept_blk):
        step = pl.program_id(0)
        span_now = span_of(step % steps)

        @pl.when(step == 0)
        def _():
            gate_acc[...] = jnp.zeros_like(gate_acc)
            up_acc[...] = jnp.zeros_like(up_acc)

        @pl.when(step < steps)
        def _():
            gate_acc[...] += jnp.dot(
                rows_blk[...], gate_all[span_now, :], preferred_element_type=f32
            )
            up_acc[...] += jnp.dot(
                rows_blk[...], up_all[span_now, :], preferred_element_type=f32
            )

        @pl.when(step == steps - 1)
        def _():
            for source in range(8):
                span = slice(source * capacity, (source + 1) * capacity)
                hot = hot_rows(slot_ref[s, source : source + 1, :], capacity)
                weighted = jnp.where(hot, gate_table[8 * s + source], 0.0)
                gate_val = jnp.sum(weighted, axis=1, keepdims=True)
                gate_pre, up_pre, back = gate_acc[span, :], up_acc[span, :], back_acc[span, :]
                sig = 1.0 / (1.0 + jnp.exp(-gate_pre))
                silu = gate_pre * sig
                hidden = (silu * up_pre).astype(bf16).astype(f32)
                hidden_now[span, :] = (hidden * gate_val).astype(bf16)
                scalar = jnp.sum(hidden * back, axis=1, keepdims=True)
                scalar_ref[s, source : source + 1, :] = jnp.sum(
                    jnp.where(hot, scalar, 0.0), axis=0, keepdims=True
                )
                hidden_grad = gate_val * back
                gate_low_now[span, :] = (
                    hidden_grad * up_pre * sig * (1.0 + gate_pre * (1.0 - sig))
                ).astype(bf16)
                up_low_now[span, :] = (hidden_grad * silu).astype(bf16)

        if s + 1 < chunks:

            @pl.when(step == steps)
            def _():
                near_done(s + 1)
                if s + 2 < chunks:
                    next_slot(s + 2)

        @pl.when(step >= steps)
        def _():
            last = (((1,), (1,)), ((), ()))
            row_grad = lax.dot_general(
                gate_low_now[...], gate_all[span_now, :], last, preferred_element_type=f32
            )
            row_grad += lax.dot_general(
                up_low_now[...], up_all[span_now, :], last, preferred_element_type=f32
            )
            row_grad = row_grad.astype(bf16)
            kept_blk[...] = row_grad[:part]
            given_blk[...] = row_grad[part:]
            weighted = jnp.dot(
                hidden_now[...], down_all[:, span_now], preferred_element_type=f32
            ).astype(bf16)
            out_kept_blk[...] = weighted[:part]
            out_given_blk[...] = weighted[part:]

    def store(s, i):
        now, whole = (
            (hidden_now, hidden_ref),
            (gate_low_now, gate_low_ref),
            (up_low_now, up_low_ref),
        )[i]
        return pltpu.make_async_copy(now, whole.at[s], local.at[1 + i])

    def compute(s):
        if s:
            for i in range(3):
                store(s - 1, i).wait()
        late = pl.BlockSpec((part, tile), lambda d: (0, jnp.maximum(d - steps, 0)))
        pltpu.emit_pipeline(
            functools.partial(experts_step, s),
            grid=(2 * steps,),
            in_specs=[pl.BlockSpec((group, tile), lambda d: (0, jnp.minimum(d, steps - 1)))],
            out_specs=[late] * 4,
        )(
            rows_ref.at[s],
            given_ref.at[s],
            kept_ref.at[s],
            out_given_ref.at[s],
            out_kept_ref.at[s],
        )
        for i in range(3):
            store(s, i).start()

    def near_done(s):
        for k in range(2):
            to_near(s, k).wait_recv()
            to_far(s, k).start()

    def next_slot(s):
        chain.step(s)
        to_near(s, 0).start()
        to_near(s, 1).start()

    for i in range(3):
        fetch_weight(i).start()
    gate_table[...] = gates_ref[...]
    exchange.start(0)
    chain.start()
    to_near(0, 0).start()
    exchange.end(0)
    exchange.start(1)
    to_near(0, 1).start()
    exchange.end(1)
    keep = pltpu.make_async_copy(acts_ref, buffer_ref.at[0, 0], local.at[0])
    keep.start()
    for k in range(2):
        grad_to_far(k).start()
    for bit in range(2, 5):
        exchange.start(bit)
        exchange.end(bit)
    keep.wait()
    near_done(0)
    next_slot(1)
    for s in range(chunks):
        if s == 0:
            for k in range(2):
                grad_to_far(k).wait_recv()
            grad_chain.start()
        else:
            grad_chain.step(s)
        select(s, 0)
        for k in range(2):
            to_far(s, k).wait_recv()
        select(s, 1)
        if s == 0:
            for i in range(3):
                fetch_weight(i).wait()
        to_sibling_rows(s, 0).wait_recv()
        compute_grad(s)
        to_sibling_rows(s, 1).wait_recv()
        compute(s)
        if s + 1 < chunks:
            to_sibling(s, 0).start()
            to_sibling(s, 1).start()
    for i in range(3):
        store(chunks - 1, i).wait()
    chain.finish()
    grad_chain.finish()
    exchange.finish()
    for k in range(2):
        grad_to_far(k).wait_send()
    for s in range(chunks):
        for k in range(2):
            to_near(s, k).wait_send()
            to_far(s, k).wait_send()
            to_sibling_rows(s, k).wait_send()
        if s + 1 < chunks:
            to_sibling(s, 0).wait()
            to_sibling(s, 1).wait()


def gather_experts(acts, slots, sibling_slots, gates, gate_w, up_w, down_w, grads, capacity):
    chunks, sources, rows = slots.shape
    width, hidden = gate_w.shape
    group = sources * capacity
    steps = 4
    anywhere = pl.BlockSpec(memory_space=pl.ANY)
    held = pl.BlockSpec(memory_space=pltpu.VMEM)
    dma = pltpu.SemaphoreType.DMA

    def low(*shape):
        return jax.ShapeDtypeStruct((chunks,) + shape, bf16)

    return pl.pallas_call(
        functools.partial(gather_experts_kernel, capacity, steps),
        out_shape=[low(group, width)] * 2
        + [low(group, hidden)] * 3
        + [low(group // 2, width)] * 6
        + [jax.ShapeDtypeStruct((chunks, sources, rows), f32)]
        + [low(4, rows, width), low(rows, width)]
        + [low(group // 2, width)] * 2,
        in_specs=[held] * 4 + [anywhere] * 6,
        out_specs=[anywhere] * 11 + [held] + [anywhere] * 4,
        scratch_shapes=[pltpu.VMEM((group, hidden), f32)] * 3
        + [pltpu.VMEM((group, hidden), bf16)] * 3
        + [
            pltpu.VMEM(gate_w.shape, bf16),
            pltpu.VMEM(up_w.shape, bf16),
            pltpu.VMEM(down_w.shape, bf16),
            pltpu.VMEM(gates.shape, f32),
            dma((5,)),
            dma((3,)),
            dma((5,)),
            dma((3,)),
        ]
        + [dma((chunks, 2))] * 4
        + [dma((2,))] * 2
        + [dma((chunks, 2))] * 4
        + [dma((3,)), dma((4,))]
        + exchange_scratch(rows),
        compiler_params=pltpu.CompilerParams(
            collective_id=1, has_side_effects=True, vmem_limit_bytes=60 * 2**20
        ),
        cost_estimate=pl.CostEstimate(flops=1000, bytes_accessed=1000, transcendentals=0),
        name="gather_experts",
    )(acts, slots, sibling_slots, gates, gate_w, up_w, down_w, *grads)


def return_rows_kernel(
    capacity,
    column_ref,
    kept_ref,
    got_ref,
    given_ref,
    out_given_ref,
    out_got_in_ref,
    scalar_ref,
    out_ref,
    out_got_ref,
    table_ref,
    kept_now,
    got_now,
    sums,
    relay,
    from_x,
    from_y,
    own,
    from_z,
    kept_sem,
    got_sem,
    first_sent,
    first_got,
    second_sent,
    second_got,
    z_sent,
    z_got,
    core_sent,
    core_got,
    *exchange_refs,
):
    near = neighbours()
    exchange = Exchange(near, table_ref, *exchange_refs)
    chunks, rows = sums.shape[0], sums.shape[2]
    final = chunks - 1
    half = rows // 2
    low, high = pl.ds(0, half), pl.ds(half, half)
    greet([near["core"], near["x"], near["y"]] + near["z"][1:])
    order = [2, 3, 1, 0]

    def fetch_kept(s):
        return pltpu.make_async_copy(kept_ref.at[s], kept_now.at[s], kept_sem.at[s])

    def fetch_got(s):
        if s == final:
            return send(
                given_ref.at[s], got_now.at[s], core_sent.at[0], core_got.at[0], near["core"]
            )
        return pltpu.make_async_copy(got_ref.at[s], got_now.at[s], got_sem.at[s])

    def to_sibling():
        return send(
            out_given_ref.at[final], out_got_ref.at[final], core_sent.at[1], core_got.at[1], near["core"]
        )

    def first(s, i):
        source, target, partner = (
            (sums.at[s, 3, low], relay.at[s, 0], near["x"]),
            (sums.at[s, 3, high], relay.at[s, 1], near["y"]),
            (sums.at[s, 1, low], from_x.at[s, low], near["x"]),
            (sums.at[s, 2, high], from_y.at[s, high], near["y"]),
        )[i]
        return send(source, target, first_sent.at[s, i], first_got.at[s, i], partner)

    def second(s, i):
        source, target, partner = (
            (sums.at[s, 2, low], from_y.at[s, low], near["y"]),
            (sums.at[s, 1, high], from_x.at[s, high], near["x"]),
        )[i]
        return send(source, target, second_sent.at[s, i], second_got.at[s, i], partner)

    def along_z(s):
        return send(own.at[s], from_z.at[s - 1], z_sent.at[s - 1], z_got.at[s - 1], near["z"][s])

    tile = 256

    def combine(s):
        fetch_kept(s).wait()
        if s == final:
            fetch_got(s).wait_recv()
        else:
            fetch_got(s).wait()

        def columns_step(d, carry):
            cols = pl.ds(pl.multiple_of(d * tile, tile), tile)
            for k in range(4):
                span = slice(k * capacity, (k + 1) * capacity)
                own_hot = hot_columns(column_ref[s, :, k : k + 1], capacity)
                sibling_hot = hot_columns(column_ref[s, :, 4 + k : 5 + k], capacity)
                total = jnp.dot(own_hot, kept_now[s, span, cols], preferred_element_type=f32)
                total += jnp.dot(sibling_hot, got_now[s, span, cols], preferred_element_type=f32)
                sums[s, k, :, cols] = total.astype(bf16)
            return carry

        lax.fori_loop(0, sums.shape[3] // tile, columns_step, 0)
        for i in range(4):
            first(s, i).start()

    def pass_on(s):
        for i in range(2):
            first(s, i).wait_recv()
        sums[s, 2, :half] = (sums[s, 2, :half].astype(f32) + relay[s, 0].astype(f32)).astype(bf16)
        sums[s, 1, half:] = (sums[s, 1, half:].astype(f32) + relay[s, 1].astype(f32)).astype(bf16)
        for i in range(2):
            second(s, i).start()

    def finish(s):
        for i in range(2):
            first(s, 2 + i).wait_recv()
            second(s, i).wait_recv()
        total = sums[s, 0].astype(f32) + from_x[s].astype(f32) + from_y[s].astype(f32)
        if s:
            own[s] = total.astype(bf16)
            along_z(s).start()
        else:
            out_ref[...] = total

    fetch_got(final).start()
    for s in order:
        fetch_kept(s).start()
        if s != final:
            fetch_got(s).start()
    table_ref[...] = scalar_ref[...]
    for bit in range(2):
        exchange.start(bit)
        exchange.end(bit)
    for i, s in enumerate(order):
        combine(s)
        if i < 3:
            exchange.start(2 + i)
            exchange.end(2 + i)
        if i == 0:
            to_sibling().start()
        if i >= 1:
            pass_on(order[i - 1])
        if i >= 2:
            finish(order[i - 2])
    pass_on(order[-1])
    finish(order[-2])
    finish(order[-1])
    for s in order[:-1]:
        along_z(s).wait_recv()
        out_ref[...] += from_z[s - 1].astype(f32)
    to_sibling().wait()
    exchange.finish()
    fetch_got(final).wait_send()
    for s in order:
        for i in range(4):
            first(s, i).wait_send()
        for i in range(2):
            second(s, i).wait_send()
        if s:
            along_z(s).wait_send()


def return_rows(columns, kept, got, given, out_given, out_got, scalars, capacity):
    chunks, rows, _ = columns.shape
    width = kept.shape[2]
    held = pl.BlockSpec(memory_space=pltpu.VMEM)
    anywhere = pl.BlockSpec(memory_space=pl.ANY)
    dma = pltpu.SemaphoreType.DMA
    return pl.pallas_call(
        functools.partial(return_rows_kernel, capacity),
        out_shape=(
            jax.ShapeDtypeStruct((rows, width), f32),
            jax.ShapeDtypeStruct(out_got.shape, out_got.dtype),
            jax.ShapeDtypeStruct(scalars.shape, f32),
        ),
        in_specs=[held] + [anywhere] * 5 + [held],
        out_specs=[held, anywhere, held],
        input_output_aliases={5: 1},
        scratch_shapes=[
            pltpu.VMEM((chunks, 4 * capacity, width), bf16),
            pltpu.VMEM((chunks, 4 * capacity, width), bf16),
            pltpu.VMEM((chunks, 4, rows, width), bf16),
            pltpu.VMEM((chunks, 2, rows // 2, width), bf16),
            pltpu.VMEM((chunks, rows, width), bf16),
            pltpu.VMEM((chunks, rows, width), bf16),
            pltpu.VMEM((chunks, rows, width), bf16),
            pltpu.VMEM((chunks - 1, rows, width), bf16),
            dma((chunks,)),
            dma((chunks,)),
            dma((chunks, 4)),
            dma((chunks, 4)),
            dma((chunks, 2)),
            dma((chunks, 2)),
            dma((chunks - 1,)),
            dma((chunks - 1,)),
            dma((2,)),
            dma((2,)),
        ]
        + exchange_scratch(scalars.shape[2]),
        compiler_params=pltpu.CompilerParams(
            collective_id=2, has_side_effects=True, vmem_limit_bytes=60 * 2**20
        ),
        cost_estimate=pl.CostEstimate(flops=1000, bytes_accessed=1000, transcendentals=0),
        name="return_rows",
    )(columns, kept, got, given, out_given, out_got, scalars)


def gather_first_kernel(
    q_width,
    kv_heads,
    acts_ref,
    grad_ref,
    weight_ref,
    named_ref,
    acts_out,
    grad_out,
    weight_out,
    table_ref,
    own_weight,
    near_sent,
    near_got,
    far_sent,
    far_got,
    weight_sent,
    weight_got,
    core_sent,
    core_got,
    z_sent,
    z_got,
    local,
    *exchange_refs,
):
    near = neighbours()
    exchange = Exchange(near, table_ref, *exchange_refs)
    ctx, fsdp = lax.axis_index("ctx"), lax.axis_index("fsdp")
    far = (ctx, flip(flip(fsdp, 1), 2))
    partners = [near["x"], near["y"], far]
    groups = [flip(fsdp, 1), flip(fsdp, 2), flip(flip(fsdp, 1), 2)]
    greet([near["core"]] + partners + near["z"][1:])
    rows = acts_ref.shape[0]
    half = rows // 2
    shard_rows = weight_ref.shape[0]
    half_shard = shard_rows // 2
    own_width = weight_out.shape[1]
    head_dim = (own_width - q_width) // 2
    all_q = weight_ref.shape[1] - 2 * kv_heads * head_dim
    core = lax.rem(ctx, 2)
    chain = Chain(near, grad_ref, lambda s: grad_out.at[s], z_sent, z_got)

    def to_near(k):
        return send(acts_ref, acts_out.at[1 + k], near_sent.at[k], near_got.at[k], partners[k])

    def to_far(k):
        span = pl.ds(k * half, half)
        return send(
            acts_out.at[1 + k, span], acts_out.at[3, span], far_sent.at[k], far_got.at[k], partners[1 - k]
        )

    def spans(group):
        return (
            (pl.ds(pl.multiple_of(group * q_width, 128), q_width), pl.ds(0, q_width)),
            (pl.ds(pl.multiple_of(all_q + group * head_dim, 128), head_dim), pl.ds(q_width, head_dim)),
            (
                pl.ds(pl.multiple_of(all_q + (kv_heads + group) * head_dim, 128), head_dim),
                pl.ds(q_width + head_dim, head_dim),
            ),
        )

    def weight_to(k, i):
        there, here = spans(groups[k])[i]
        from_row = pl.multiple_of(core * half_shard, 16)
        to_row = pl.multiple_of(fsdp * shard_rows + core * half_shard, 16)
        return send(
            weight_ref.at[pl.ds(from_row, half_shard), there],
            weight_out.at[pl.ds(to_row, half_shard), here],
            weight_sent.at[k, i],
            weight_got.at[k, i],
            partners[k],
        )

    def weight_on(k):
        row = pl.multiple_of(groups[k] * shard_rows + core * half_shard, 16)
        part = weight_out.at[pl.ds(row, half_shard)]
        return send(part, part, core_sent.at[k], core_got.at[k], near["core"])

    table_ref[...] = named_ref[...]
    exchange.start(0)
    to_near(0).start()
    chain.start()
    exchange.end(0)
    exchange.start(1)
    to_near(1).start()
    exchange.end(1)
    for k in (2, 0, 1):
        for i in range(3):
            weight_to(k, i).start()
    exchange.start(2)
    exchange.end(2)
    own_parts = [
        pltpu.make_async_copy(weight_ref.at[:, there], own_weight.at[:, here], local.at[i])
        for i, (there, here) in enumerate(spans(fsdp))
    ]
    keeps = [
        pltpu.make_async_copy(acts_ref, acts_out.at[0], local.at[3]),
        pltpu.make_async_copy(grad_ref, grad_out.at[0], local.at[4]),
    ]
    for copy in own_parts + keeps:
        copy.start()
    for copy in own_parts:
        copy.wait()
    place = pltpu.make_async_copy(
        own_weight,
        weight_out.at[pl.ds(pl.multiple_of(fsdp * shard_rows, 16), shard_rows)],
        local.at[5],
    )
    place.start()
    for k in range(2):
        to_near(k).wait_recv()
        to_far(k).start()
    chain.wait(1)
    chain.wait_inner_last()
    for bit in (3, 4):
        exchange.start(bit)
        exchange.end(bit)
    chain.start_inner(1)
    for k in (2, 0, 1):
        for i in range(3):
            weight_to(k, i).wait_recv()
        weight_on(k).start()
    chain.step(2)
    for k in range(2):
        to_far(k).wait_recv()
    for k in range(3):
        weight_on(k).wait_recv()
    chain.step(3)
    for copy in keeps + [place]:
        copy.wait()
    chain.finish()
    exchange.finish()
    for k in range(2):
        to_near(k).wait_send()
        to_far(k).wait_send()
    for k in range(3):
        for i in range(3):
            weight_to(k, i).wait_send()
        weight_on(k).wait_send()


def gather_first(acts, grad, weight, named, n_fsdp, z_count, q_width, kv_heads, head_dim):
    rows, width = acts.shape
    own_width = q_width + 2 * head_dim
    held = pl.BlockSpec(memory_space=pltpu.VMEM)
    anywhere = pl.BlockSpec(memory_space=pl.ANY)
    dma = pltpu.SemaphoreType.DMA
    return pl.pallas_call(
        functools.partial(gather_first_kernel, q_width, kv_heads),
        out_shape=(
            jax.ShapeDtypeStruct((n_fsdp, rows, width), bf16),
            jax.ShapeDtypeStruct((z_count, rows, width), bf16),
            jax.ShapeDtypeStruct((n_fsdp * weight.shape[0], own_width), bf16),
            jax.ShapeDtypeStruct(named.shape, f32),
        ),
        in_specs=[held, held, anywhere, held],
        out_specs=[anywhere] * 3 + [held],
        scratch_shapes=[
            pltpu.VMEM((weight.shape[0], own_width), bf16),
            dma((2,)),
            dma((2,)),
            dma((2,)),
            dma((2,)),
            dma((3, 3)),
            dma((3, 3)),
            dma((3,)),
            dma((3,)),
            dma((5,)),
            dma((3,)),
            dma((6,)),
        ]
        + exchange_scratch(named.shape[2]),
        compiler_params=pltpu.CompilerParams(
            collective_id=3, has_side_effects=True, vmem_limit_bytes=32 * 2**20
        ),
        cost_estimate=pl.CostEstimate(flops=1000, bytes_accessed=1000, transcendentals=0),
        name="gather_first",
    )(acts, grad, weight, named)


def finish_kernel(
    kv_heads,
    parts_ref,
    tokens_ref,
    resid_grad_ref,
    gain_ref,
    shares_ref,
    q_ref,
    kv_ref,
    router_ref,
    later_ref,
    got_ref,
    own_ref,
    for_x_ref,
    for_y_ref,
    resid_ref,
    out_weight_ref,
    grad_ref,
    gains_ref,
    weight_ref,
    router_out_ref,
    output_ref,
    out_weight_out,
    out_weight_got,
    owner_sent,
    owner_got,
    parts_now,
    resid_grad_now,
    resid_now,
    own_now,
    q_now,
    kv_now,
    router_now,
    fetched,
    stream_fetched,
    rows_x,
    rows_y,
    rows_z,
    rows_own,
    relay,
    from_x,
    from_y,
    q_core,
    kv_core,
    router_core,
    q_sum,
    kv_sum,
    router_sum,
    q_z,
    kv_z,
    router_z,
    q_total,
    kv_total,
    router_total,
    router_got,
    gain_got,
    first_sent,
    first_got,
    second_sent,
    second_got,
    core_sent,
    core_got,
    z_sent,
    z_got,
    row_sent,
    row_got,
    gain_sent,
    gain_in,
    rows_sent,
    rows_got,
    local,
):
    near = neighbours()
    ctx, fsdp = lax.axis_index("ctx"), lax.axis_index("fsdp")
    groups = [fsdp, flip(fsdp, 1), flip(fsdp, 2), flip(flip(fsdp, 1), 2)]
    partners = [None] + [(ctx, group) for group in groups[1:]]
    moves = fsdp != 0
    stays = fsdp == 0
    owner = (
        ctx
        + 2 * (fsdp % 2) * (1 - 2 * ((ctx // 2) % 2))
        + 4 * (fsdp // 2) * (1 - 2 * ((ctx // 4) % 2)),
        fsdp,
    )
    greet([near["core"]] + partners[1:] + near["z"][1:])
    to_owner = lambda: send(out_weight_ref, out_weight_got, owner_sent, owner_got, owner)
    keep_owned = lambda: pltpu.make_async_copy(out_weight_ref, out_weight_got, owner_got)

    @pl.when(moves)
    def _():
        to_owner().start()

    @pl.when(stays)
    def _():
        keep_owned().start()

    rows = tokens_ref.shape[0]
    half = rows // 2
    low, high = pl.ds(0, half), pl.ds(half, half)
    own_ctx = [ctx] + [partner[0] for partner in near["z"][1:]]
    chunks = len(own_ctx)
    streams = (
        (q_ref, q_core, q_sum, q_z, q_total, q_now),
        (kv_ref, kv_core, kv_sum, kv_z, kv_total, kv_now),
        (router_ref, router_core, router_sum, router_z, router_total, router_now),
    )
    out_rows = weight_ref.shape[0]
    q_width = q_ref.shape[2]
    head_dim = kv_ref.shape[2] // 2
    all_q = weight_ref.shape[1] - 2 * kv_heads * head_dim

    def first(i):
        source, target, partner = (
            (parts_ref.at[3, low], relay.at[0], near["x"]),
            (parts_ref.at[3, high], relay.at[1], near["y"]),
            (parts_ref.at[1, low], from_x.at[low], near["x"]),
            (parts_ref.at[2, high], from_y.at[high], near["y"]),
        )[i]
        return send(source, target, first_sent.at[i], first_got.at[i], partner)

    def second(i):
        source, target, partner = (
            (relay.at[0], from_y.at[low], near["y"]),
            (relay.at[1], from_x.at[high], near["x"]),
        )[i]
        return send(source, target, second_sent.at[i], second_got.at[i], partner)

    def to_core(i, s):
        source, landing = streams[i][:2]
        return send(
            source.at[flip(own_ctx[s], 1)],
            landing.at[s],
            core_sent.at[i, s],
            core_got.at[i, s],
            near["core"],
        )

    def along_z(i, s):
        return send(
            streams[i][2].at[s],
            streams[i][3].at[s - 1],
            z_sent.at[i, s - 1],
            z_got.at[i, s - 1],
            near["z"][1 + (s == 2)],
        )

    def row_parts(k):
        span = pl.ds(pl.multiple_of(groups[k] * out_rows, 8), out_rows)

        def at(start, width):
            return pl.ds(pl.multiple_of(start, 128), width)

        return (
            (q_total.at[span], weight_ref.at[:, at(fsdp * q_width, q_width)]),
            (
                kv_total.at[span, pl.ds(0, head_dim)],
                weight_ref.at[:, at(all_q + fsdp * head_dim, head_dim)],
            ),
            (
                kv_total.at[span, pl.ds(head_dim, head_dim)],
                weight_ref.at[:, at(all_q + (kv_heads + fsdp) * head_dim, head_dim)],
            ),
            (router_total.at[span], router_got.at[k]),
        )

    def to_row(k, i):
        source, target = row_parts(k)[i]
        return send(source, target, row_sent.at[k - 1, i], row_got.at[k - 1, i], partners[k])

    def keep_row(i):
        source, target = row_parts(0)[i]
        return pltpu.make_async_copy(source, target, local.at[i])

    gain_partners = [near["core"], near["x"], near["y"], near["z"][1], near["z"][2]]

    def share(i):
        return send(
            gains_ref, gain_got.at[i], gain_sent.at[i], gain_in.at[i], gain_partners[i]
        )

    def fetch(i):
        source, target = (
            (parts_ref.at[0], parts_now.at[pl.ds(0, rows)]),
            (parts_ref.at[2, low], parts_now.at[pl.ds(rows, half)]),
            (parts_ref.at[1, high], parts_now.at[pl.ds(rows + half, half)]),
            (resid_grad_ref, resid_grad_now),
            (resid_ref, resid_now),
            (own_ref.at[pl.ds(0, 2)], own_now),
        )[i]
        return pltpu.make_async_copy(source, target, fetched.at[i])

    def fetch_stream(i, s):
        return pltpu.make_async_copy(
            streams[i][0].at[own_ctx[s]], streams[i][5].at[s], stream_fetched.at[i, s]
        )

    def rows_copy(i):
        source, target, partner = (
            (rows_own.at[0], rows_z.at[0], near["z"][2]),
            (for_x_ref.at[1], rows_x.at[1], near["x"]),
            (for_y_ref.at[1], rows_y.at[1], near["y"]),
            (for_x_ref.at[0], rows_x.at[0], near["x"]),
            (for_y_ref.at[0], rows_y.at[0], near["y"]),
            (rows_own.at[1], rows_z.at[1], near["z"][1]),
        )[i]
        return send(source, target, rows_sent.at[i], rows_got.at[i], partner)

    for i in range(4):
        first(i).start()
    for s in (3, 1, 2, 0):
        for i in range(3):
            to_core(i, s).start()
            fetch_stream(i, s).start()
    for i in range(6):
        fetch(i).start()
    rows_own[0] = (later_ref[...].astype(f32) + got_ref[...].astype(f32)).astype(bf16)
    rows_copy(0).start()
    for s in (3, 1, 2, 0):
        for i in range(3):
            _, landing, total, _, _, now = streams[i]
            fetch_stream(i, s).wait()
            to_core(i, s).wait_recv()
            total[s] = (now[s].astype(f32) + landing[s].astype(f32)).astype(bf16)
            if s % 2:
                along_z(i, s).start()
    for i in range(2):
        first(i).wait_recv()
    for i in range(3):
        fetch(i).wait()
    relay[0] = (relay[0].astype(f32) + parts_now[rows : rows + half].astype(f32)).astype(bf16)
    relay[1] = (relay[1].astype(f32) + parts_now[rows + half :].astype(f32)).astype(bf16)
    for i in range(2):
        second(i).start()
    for i in range(1, 5):
        rows_copy(i).start()
    for i in range(2):
        first(2 + i).wait_recv()
        second(i).wait_recv()
    gains_ref[...] = shares_ref[...]
    block = 32
    for i in range(3, 6):
        fetch(i).wait()

    def back_step(b, carry):
        span = pl.ds(pl.multiple_of(b * block, block), block)
        grad = (
            parts_now[span, :].astype(f32)
            + from_x[span, :].astype(f32)
            + from_y[span, :].astype(f32)
        )
        values = tokens_ref[span, :].astype(f32)
        scale = lax.rsqrt(jnp.mean(values * values, axis=-1, keepdims=True) + eps_norm)
        unit = values * scale
        scaled = grad * gain_ref[...]
        back = scale * (scaled - unit * jnp.mean(scaled * unit, axis=-1, keepdims=True))
        grad_ref[span, :] = resid_grad_now[span, :] + back
        gains_ref[0] += jnp.sum(grad * unit, axis=0, keepdims=True)
        return carry

    lax.fori_loop(0, rows // block, back_step, 0)
    share(0).start()
    for i in range(3):
        _, _, held, landing, _, _ = streams[i]
        along_z(i, 3).wait_recv()
        held[2] = (held[2].astype(f32) + landing[2].astype(f32)).astype(bf16)
        along_z(i, 2).start()
    for i in range(1, 3):
        rows_copy(i).wait_recv()
    rows_own[1] = (own_now[1].astype(f32) + rows_x[1].astype(f32) + rows_y[1].astype(f32)).astype(bf16)
    rows_copy(5).start()
    for i in range(len(gain_partners)):
        if i:
            share(i).start()
        share(i).wait()
        gains_ref[...] += gain_got[i]
    for i in range(3):
        _, _, held, landing, total, _ = streams[i]
        for s in range(1, 3):
            along_z(i, s).wait_recv()
        total[...] = held[0].astype(f32) + landing[0].astype(f32) + landing[1].astype(f32)
    for k in range(1, 4):
        for i in range(4):
            to_row(k, i).start()
    for i in range(3):
        keep_row(i).start()
    own = pl.ds(pl.multiple_of(fsdp * out_rows, 8), out_rows)
    router_all = router_total[own, :]
    for k in range(1, 4):
        for i in range(4):
            to_row(k, i).wait()
        router_all += router_got[k]
    router_out_ref[...] = router_all
    for i in range(3):
        keep_row(i).wait()
    for i in (0, 3, 4, 5):
        rows_copy(i).wait_recv()

    @pl.when(moves)
    def _():
        to_owner().wait()

    @pl.when(stays)
    def _():
        keep_owned().wait()

    out_weight_out[...] = out_weight_got[...].astype(f32)

    def output_step(b, carry):
        span = pl.ds(pl.multiple_of(b * block, block), block)
        total = resid_now[span, :] + own_now[0, span, :].astype(f32)
        for part in (rows_x[0, span, :], rows_y[0, span, :], rows_z[0, span, :], rows_z[1, span, :]):
            total += part.astype(f32)
        output_ref[span, :] = total.astype(bf16)
        return carry

    lax.fori_loop(0, rows // block, output_step, 0)
    for i in range(6):
        rows_copy(i).wait_send()
    for i in range(4):
        first(i).wait_send()
    for i in range(2):
        second(i).wait_send()
    for i in range(3):
        for s in range(chunks):
            to_core(i, s).wait_send()
            if s:
                along_z(i, s).wait_send()


def finish(parts, tokens, resid_grad, gain, shares, grad_q, grad_kv, grad_router, expert_rows, resid, out_weight, kv_heads):
    rows, width = tokens.shape
    n_ctx, share_rows, q_width = grad_q.shape
    pair_width, router_width = grad_kv.shape[2], grad_router.shape[2]
    chunks = n_ctx // 2
    out_rows = share_rows // 4
    all_width = 4 * q_width + kv_heads * pair_width
    held = pl.BlockSpec(memory_space=pltpu.VMEM)
    anywhere = pl.BlockSpec(memory_space=pl.ANY)
    dma = pltpu.SemaphoreType.DMA
    widths = (q_width, pair_width, router_width)
    return pl.pallas_call(
        functools.partial(finish_kernel, kv_heads),
        out_shape=(
            jax.ShapeDtypeStruct((rows, width), f32),
            jax.ShapeDtypeStruct(shares.shape, f32),
            jax.ShapeDtypeStruct((out_rows, all_width), f32),
            jax.ShapeDtypeStruct((out_rows, router_width), f32),
            jax.ShapeDtypeStruct((rows, width), bf16),
            jax.ShapeDtypeStruct(out_weight.shape, f32),
        ),
        in_specs=[anywhere, held, anywhere, held, held]
        + [anywhere] * 3
        + [held, held]
        + [anywhere] * 5,
        out_specs=[held] * 6,
        scratch_shapes=[
            pltpu.VMEM(out_weight.shape, bf16),
            dma,
            dma,
            pltpu.VMEM((2 * rows, width), bf16),
            pltpu.VMEM((rows, width), f32),
            pltpu.VMEM((rows, width), f32),
            pltpu.VMEM((2, rows, width), bf16),
        ]
        + [pltpu.VMEM((chunks, share_rows, columns), bf16) for columns in widths]
        + [
            dma((6,)),
            dma((3, chunks)),
            pltpu.VMEM((2, rows, width), bf16),
            pltpu.VMEM((2, rows, width), bf16),
            pltpu.VMEM((2, rows, width), bf16),
            pltpu.VMEM((2, rows, width), bf16),
            pltpu.VMEM((2, rows // 2, width), bf16),
            pltpu.VMEM((rows, width), bf16),
            pltpu.VMEM((rows, width), bf16),
        ]
        + [pltpu.VMEM((chunks, share_rows, columns), bf16) for columns in widths]
        + [pltpu.VMEM((chunks, share_rows, columns), bf16) for columns in widths]
        + [pltpu.VMEM((chunks - 1, share_rows, columns), bf16) for columns in widths]
        + [pltpu.VMEM((share_rows, columns), f32) for columns in widths]
        + [
            pltpu.VMEM((4, out_rows, router_width), f32),
            pltpu.VMEM((5,) + shares.shape, f32),
            dma((4,)),
            dma((4,)),
            dma((2,)),
            dma((2,)),
            dma((3, chunks)),
            dma((3, chunks)),
            dma((3, chunks - 1)),
            dma((3, chunks - 1)),
            dma((3, 4)),
            dma((3, 4)),
            dma((5,)),
            dma((5,)),
            dma((7,)),
            dma((7,)),
            dma((3,)),
        ],
        compiler_params=pltpu.CompilerParams(
            collective_id=4, has_side_effects=True, vmem_limit_bytes=62 * 2**20
        ),
        cost_estimate=pl.CostEstimate(flops=1000, bytes_accessed=1000, transcendentals=0),
        name="finish",
    )(parts, tokens, resid_grad, gain, shares, grad_q, grad_kv, grad_router, *expert_rows, resid, out_weight)


def fast_body(
    n_ctx,
    tokens,
    positions,
    expert_ids,
    attn_gain,
    query_key_value_weight,
    q_gain,
    k_gain,
    output_weight,
    ffn_gain,
    router_weight,
    w_gate,
    w_up,
    w_down,
    cotangent,
):
    n_fsdp = 4
    n_all = n_ctx * n_fsdp
    ctx_at = lax.axis_index("ctx")
    fsdp_at = lax.axis_index("fsdp")
    core_at = ctx_at % 2
    own_at = ctx_at * n_fsdp + fsdp_at
    row_count = tokens.shape[1]
    model_width = tokens.shape[2]
    head_dim = q_gain.shape[0]
    shard_rows = query_key_value_weight.shape[0]
    heads = output_weight.shape[0] // head_dim
    q_width = heads * head_dim
    all_q = q_width * n_fsdp
    kv_heads = (query_key_value_weight.shape[1] - all_q) // (2 * head_dim)
    own_width = q_width + 2 * head_dim
    expert_count = n_all
    top_count = expert_ids.shape[2]
    capacity = row_count * top_count * 3 // (2 * expert_count)
    z_count = n_ctx // 2
    chunk_rows = 2 * n_fsdp * capacity

    inputs = tokens.reshape(row_count, model_width).astype(f32)
    places = positions.reshape(row_count)
    chosen = expert_ids.reshape(row_count, top_count)
    grad_res_low = cotangent.reshape(row_count, model_width)
    grad_res = grad_res_low.astype(f32)

    relative = jnp.bitwise_xor(own_at, jnp.arange(n_all, dtype=jnp.int32))
    chosen_rel = (chosen[:, :, None] == relative[None, None, :]).astype(f32)
    named = jnp.sum(chosen_rel, axis=1).T
    first_block = jnp.broadcast_to((places[0] // run_rows).astype(f32), (n_all, 128))
    named = jnp.concatenate([named, first_block], axis=1)[:, None, :]

    rms_one = lax.rsqrt(jnp.mean(inputs * inputs, axis=-1, keepdims=True) + eps_norm)
    acts = (inputs * rms_one * attn_gain).astype(bf16)
    acts_group, grad_slots, weight_qkv, small = gather_first(
        acts, grad_res_low, query_key_value_weight, named, n_fsdp, z_count, q_width, kv_heads, head_dim
    )
    named_here = small[:, 0, :row_count]
    block_table = small[:, 0, row_count].astype(jnp.int32).reshape(n_ctx, n_fsdp)
    acts_group = acts_group.reshape(n_fsdp * row_count, model_width)

    group_rows = n_fsdp * row_count
    blocks_total = 2 * n_ctx
    own_blocks = block_table[0]
    run_blocks = jnp.stack([own_blocks, blocks_total - 1 - own_blocks], axis=1)
    row_places = (
        run_blocks[:, :, None] * run_rows + jnp.arange(run_rows, dtype=jnp.int32)[None, None, :]
    ).reshape(n_fsdp, row_count, 1)
    angles = row_places.astype(f32) * frequencies(head_dim)
    cosine, sine = jnp.cos(angles), jnp.sin(angles)
    cosine = jnp.concatenate([cosine, cosine], axis=-1)
    sine = jnp.concatenate([-sine, sine], axis=-1)
    block_index = jnp.arange(blocks_total, dtype=jnp.int32)
    slot_index = jnp.arange(n_ctx, dtype=jnp.int32)[:, None, None]
    source_table = jnp.sum(
        jnp.where(block_table[:, :, None] == block_index, 2 * slot_index, 0)
        + jnp.where(blocks_total - 1 - block_table[:, :, None] == block_index, 2 * slot_index + 1, 0),
        axis=0,
    )
    place_list = run_blocks.reshape(-1)
    source_list = source_table.reshape(-1)

    projected, query_low, kv_own = project(
        acts_group.reshape(n_fsdp, row_count, model_width),
        weight_qkv,
        cosine,
        sine,
        q_gain[None],
        k_gain[None],
        heads,
    )

    grad_x = swap(grad_slots, "fsdp", n_fsdp, 1)
    grad_y = swap(grad_slots, "fsdp", n_fsdp, 2)

    kv_slots = [kv_own] + [swap(kv_own, "ctx", n_ctx, 2 * k) for k in range(1, z_count)]
    kv_slots = jnp.stack(kv_slots)
    kv_all = jnp.stack([kv_slots, swap(kv_slots, "ctx", n_ctx, 1)], axis=1)
    kv_all = kv_all.reshape(n_ctx, n_fsdp, row_count, 2 * head_dim)

    mixed, lse = attend(place_list, source_list, query_low, kv_all)
    heads_low = mixed.reshape(group_rows, q_width)
    heads_low = after(heads_low, (grad_x, grad_y))

    resid_parts = jnp.dot(heads_low, output_weight, preferred_element_type=f32).astype(bf16)
    resid = inputs + scatter_parts(resid_parts.reshape(n_fsdp, row_count, model_width))
    rms_two = lax.rsqrt(jnp.mean(resid * resid, axis=-1, keepdims=True) + eps_norm)
    acts_two = (resid * rms_two * ffn_gain).astype(bf16)

    full_router = by_fsdp(
        [router_weight] + [swap(router_weight, "fsdp", n_fsdp, k) for k in range(1, n_fsdp)], fsdp_at
    ).reshape(n_fsdp * shard_rows, expert_count)
    logits = jnp.dot(acts_two, full_router, preferred_element_type=f32)
    pick_table = (chosen[:, :, None] == jnp.arange(expert_count)[None, None, :]).astype(f32)
    picked = jnp.sum(logits[:, None, :] * pick_table, axis=-1)
    gate_vals, gate_back = jax.vjp(lambda values: jax.nn.softmax(values, axis=-1), picked)
    gates_rel = jnp.sum(chosen_rel * gate_vals[:, :, None], axis=1).T

    upper = jnp.triu(jnp.ones((row_count, row_count), bf16), 1)
    rank = jnp.dot(named_here.astype(bf16), upper, preferred_element_type=f32)
    slots = jnp.where(named_here > 0.5, rank, -1.0).reshape(z_count, 2 * n_fsdp, row_count)
    sibling_slots = swap(slots[:, n_fsdp:], "ctx", n_ctx, 1)
    columns = jnp.swapaxes(jnp.concatenate([slots[:, :n_fsdp], sibling_slots], axis=1), 1, 2)
    gates = gates_rel[:, None, :]
    gate_w = w_gate[0]
    up_w = w_up[0]
    down_w = w_down[0]


    (
        act_rows,
        grad_rows,
        hidden_rows,
        gate_lows,
        up_lows,
        kept,
        got,
        given,
        out_kept,
        out_got,
        out_given,
        scalars,
        *_,
    ) = gather_experts(
        acts_two,
        slots,
        sibling_slots,
        gates,
        gate_w,
        up_w,
        down_w,
        [grad_slots, grad_x, grad_y],
        capacity,
    )
    acts_two_grad, out_got, gate_grad_rel = return_rows(
        columns, kept, got, given, out_given, out_got, scalars.reshape(n_all, 1, row_count), capacity
    )
    gate_grad = jnp.sum(chosen_rel * gate_grad_rel[:, 0].T[:, None, :], axis=-1)
    (picked_grad,) = gate_back(gate_grad)
    logit_grad = jnp.sum(picked_grad[:, :, None] * pick_table, axis=1).astype(bf16)
    acts_two_grad = acts_two_grad + jnp.dot(
        logit_grad, full_router.T, preferred_element_type=f32
    )

    scaled = ffn_gain * acts_two_grad
    grad_ffn_gain = jnp.sum(acts_two_grad * resid * rms_two, axis=0)
    resid_grad = (
        grad_res
        + rms_two * scaled
        - resid * (rms_two**3 * jnp.mean(scaled * resid, axis=-1, keepdims=True))
    )
    attn_grad = resid_grad.astype(bf16)
    row_total = z_count * chunk_rows

    def weight_grad(left, right, earlier):
        left = after(left, earlier)
        return jnp.einsum(
            "rd,rf->df",
            left.reshape(row_total, -1),
            right.reshape(row_total, -1),
            preferred_element_type=f32,
        )[None]

    grad_w_down = weight_grad(hidden_rows, grad_rows, attn_grad)
    combined = combine_rows(after(columns, attn_grad), out_kept, out_got, capacity)
    half_rows = row_count // 2
    near_x = swap(attn_grad, "fsdp", n_fsdp, 1)
    near_y = swap(attn_grad, "fsdp", n_fsdp, 2)
    near_x, near_y, *combined = after((near_x, near_y), combined, True)
    out_own, out_x, out_y, out_low, out_high = combined
    far_low = swap(near_x[:half_rows], "fsdp", n_fsdp, 2)
    far_high = swap(near_y[half_rows:], "fsdp", n_fsdp, 1)
    far_low, far_high, grad_w_down = after((far_low, far_high), (grad_w_down,), True)
    attn_grad_group = jnp.concatenate([attn_grad, near_x, near_y, far_low, far_high], axis=0)
    heads_grad = jnp.einsum(
        "td,cd->tc", attn_grad_group, output_weight, preferred_element_type=f32
    ).astype(bf16)
    grad_w_out = jnp.einsum(
        "tc,td->cd", heads_low, attn_grad_group, preferred_element_type=f32
    ).astype(bf16)
    heads_grad = heads_grad.reshape(n_fsdp, row_count, q_width)
    per_ctx = grad_w_out.shape[0] // n_ctx
    out_split = grad_w_out.reshape(2, z_count, per_ctx, model_width)
    out_keep = pick(out_split, core_at)
    out_away = pick(out_split, 1 - core_at)
    out_keep = after(out_keep, heads_grad)
    out_sum = (out_keep.astype(f32) + swap(out_away, "ctx", n_ctx, 1).astype(f32)).astype(bf16)
    piece_at = (ctx_at // 2) ^ fsdp_at
    heads_grad = after(heads_grad, out_sum)
    out_terms = [
        swap(pick(out_sum, piece_at ^ k), "ctx", n_ctx, 2 * k) for k in range(1, z_count)
    ]
    dq, dkv, dkv_away, dq_gain = attend_back(
        place_list,
        source_list,
        query_low,
        kv_all,
        mixed,
        heads_grad,
        lse,
        projected,
        cosine,
        sine,
        q_gain[None],
    )

    half_slots = z_count // 2
    out_low, out_high = after((out_low, out_high), attn_grad_group)
    from_x = swap(out_low, "fsdp", n_fsdp, 1)
    from_y = swap(out_high, "fsdp", n_fsdp, 2)
    dkv_got = swap(dkv_away, "ctx", n_ctx, 1)
    dq, dkv, dq_gain, from_x, from_y, *out_terms = after(
        (dq, dkv, dq_gain), (from_x, from_y, *out_terms), True
    )

    def added(parts, term, low, span):
        term = term[span].astype(f32)
        parts = parts[span].astype(f32)
        pad = ((0, 0), (0, half_rows), (0, 0)) if low else ((0, 0), (half_rows, 0), (0, 0))
        return (parts + jnp.pad(term, pad)).astype(bf16)

    near_span, far_span = slice(0, half_slots), slice(half_slots, z_count)
    later_x = swap(added(out_x, from_y, False, far_span), "fsdp", n_fsdp, 1)
    later_y = swap(added(out_y, from_x, True, far_span), "fsdp", n_fsdp, 2)
    sooner_x = added(out_x, from_y, False, near_span)
    sooner_y = added(out_y, from_x, True, near_span)
    proj_low_q = dq.reshape(group_rows, q_width)

    held = (dkv.astype(f32) + dkv_got.astype(f32)).astype(bf16)
    held_core = held
    held = [held[0]] + [swap(held[k], "ctx", n_ctx, 2 * k) for k in range(1, z_count)]
    out_later = (
        out_own[far_span].astype(f32) + later_x.astype(f32) + later_y.astype(f32)
    ).astype(bf16)
    held = after(held, out_later)
    dkv_own, dk_gain = key_back(held, projected, cosine, sine, k_gain[None])
    proj_low_kv = dkv_own.reshape(group_rows, 2 * head_dim)
    acts_parts = (
        jnp.einsum("tc,dc->td", proj_low_q, weight_qkv[:, :q_width], preferred_element_type=f32)
        + jnp.einsum("tc,dc->td", proj_low_kv, weight_qkv[:, q_width:], preferred_element_type=f32)
    ).astype(bf16)

    def token_sum(left, right):
        return jnp.einsum("td,tc->dc", left, right, preferred_element_type=f32).astype(bf16)

    share_rows = model_width // n_ctx
    grad_q = token_sum(after(acts_group, held_core), proj_low_q).reshape(n_ctx, share_rows, q_width)
    grad_kv = token_sum(acts_group, proj_low_kv).reshape(n_ctx, share_rows, 2 * head_dim)
    padded = jnp.pad(logit_grad, ((0, 0), (0, -expert_count % 128)))
    grad_router = token_sum(after(acts_two, attn_grad_group), padded)
    grad_router = grad_router.reshape(n_ctx, share_rows, -1)
    small_gains = jnp.concatenate([jnp.sum(dq_gain, axis=0), jnp.sum(dk_gain, axis=0)])
    shares = jnp.stack(
        [
            jnp.zeros_like(grad_ffn_gain),
            grad_ffn_gain,
            jnp.pad(small_gains, (0, model_width - small_gains.shape[0])),
        ]
    )[:, None, :]
    grad_w_out = pick(after(out_sum, held_core), piece_at).astype(f32)
    for term in out_terms:
        grad_w_out = grad_w_out + term.astype(f32)
    grad_w_out = lax.ppermute(
        grad_w_out.astype(bf16),
        ("ctx", "fsdp"),
        [
            (c * n_fsdp + f, c * n_fsdp + (f ^ (c // 2)))
            for c in range(n_ctx)
            for f in range(n_fsdp)
        ],
    )
    grad_tokens, gains, grad_w_qkv, grad_w_router, output, grad_w_out = finish(
        acts_parts.reshape(n_fsdp, row_count, model_width),
        tokens.reshape(row_count, model_width),
        resid_grad,
        attn_gain[None],
        shares,
        grad_q,
        grad_kv,
        grad_router,
        (out_later[0], swap(out_later[1], "ctx", n_ctx, 2), out_own, sooner_x, sooner_y),
        resid,
        grad_w_out,
        kv_heads,
    )
    output = output.reshape(tokens.shape)
    grad_tokens = grad_tokens.reshape(tokens.shape)
    grad_w_router = grad_w_router[:, :expert_count]
    grad_attn_gain = gains[0, 0]
    grad_ffn_gain = gains[1, 0]
    grad_q_gain = gains[2, 0, :head_dim]
    grad_k_gain = gains[2, 0, head_dim : 2 * head_dim]

    grad_w_gate = weight_grad(act_rows, gate_lows, held_core)
    grad_w_up = weight_grad(act_rows, up_lows, grad_q)

    return (
        output,
        grad_tokens,
        grad_attn_gain,
        grad_w_qkv,
        grad_q_gain,
        grad_k_gain,
        grad_w_out,
        grad_ffn_gain,
        grad_w_router,
        grad_w_gate,
        grad_w_up,
        grad_w_down,
    )


def solution(mesh):
    n_ctx, n_fsdp = mesh.shape["ctx"], mesh.shape["fsdp"]

    def body(*arrays):
        heads_kv = (arrays[4].shape[1] - arrays[7].shape[0] * n_fsdp) // (2 * arrays[5].shape[0])
        if n_fsdp == 4 and heads_kv == n_fsdp and n_ctx == 8:
            return fast_body(n_ctx, *arrays)
        return general_body(*arrays)

    whole = P(("ctx", "fsdp"), None, None)
    rows = P(("ctx", "fsdp"), None)
    split = P("fsdp", "ctx", None)
    return jax.shard_map(
        body,
        mesh=mesh,
        in_specs=(
            split,
            P("fsdp", "ctx"),
            split,
            P(),
            P("fsdp", None),
            P(),
            P(),
            P("fsdp", None),
            P(),
            P("fsdp", None),
            whole,
            whole,
            whole,
            split,
        ),
        out_specs=(split, split, P(), rows, P(), P(), rows, P(), rows, whole, whole, whole),
        check_vma=False,
    )
```

```python
import functools
import math

import jax
import jax.numpy as jnp
from jax import lax
from jax.experimental import pallas as pl
from jax.experimental.pallas import tpu as pltpu
from jax.sharding import PartitionSpec as P

eps_norm = 1e-06
rope_base = 1000000.0
masked_value = -1e30
run_rows = 128
bf16 = jnp.bfloat16
f32 = jnp.float32


def rms_scale(values, gain):
    mean_sq = jnp.mean(values * values, axis=-1, keepdims=True)
    return values * lax.rsqrt(mean_sq + eps_norm) * gain


def frequencies(head_dim):
    return 1.0 / rope_base ** (jnp.arange(0, head_dim, 2).astype(jnp.float32) / head_dim)


def rotate(values, angles):
    half_dim = values.shape[-1] // 2
    cosine = jnp.cos(angles)
    sine_val = jnp.sin(angles)
    first_half = values[..., :half_dim]
    second_half = values[..., half_dim:]
    return jnp.concatenate(
        [
            first_half * cosine - second_half * sine_val,
            second_half * cosine + first_half * sine_val,
        ],
        axis=-1,
    )


def head_prep(projected, gain_q, gain_k, angles, heads_q, heads_kv):
    head_dim = gain_q.shape[0]
    row_count = projected.shape[0]
    q_width = heads_q * head_dim
    kv_width = heads_kv * head_dim
    queries = projected[:, :q_width].reshape(row_count, heads_q, head_dim)
    key_heads = projected[:, q_width : q_width + kv_width].reshape(row_count, heads_kv, head_dim)
    value_heads = projected[:, q_width + kv_width :].reshape(row_count, heads_kv, head_dim)
    queries = rotate(rms_scale(queries, gain_q), angles)
    key_heads = rotate(rms_scale(key_heads, gain_k), angles)
    return (queries, key_heads, value_heads)


def general_body(
    tokens,
    positions,
    expert_ids,
    attn_gain,
    query_key_value_weight,
    q_gain,
    k_gain,
    output_weight,
    ffn_gain,
    router_weight,
    w_gate,
    w_up,
    w_down,
    cotangent,
):
    row_count = tokens.shape[1]
    model_width = tokens.shape[2]
    head_dim = q_gain.shape[0]
    inputs = tokens.reshape(row_count, model_width).astype(jnp.float32)
    places = positions.reshape(row_count)
    chosen = expert_ids.reshape(row_count, -1)
    top_count = chosen.shape[1]
    full_qkv, full_out, full_router = (
        lax.all_gather(query_key_value_weight, "fsdp", axis=0, tiled=True),
        lax.all_gather(output_weight, "fsdp", axis=0, tiled=True),
        lax.all_gather(router_weight, "fsdp", axis=0, tiled=True),
    )
    heads_q = full_out.shape[0] // head_dim
    heads_kv = (full_qkv.shape[1] - full_out.shape[0]) // (2 * head_dim)
    group_size = heads_q // heads_kv
    expert_count = full_router.shape[1]
    capacity = row_count * top_count * 3 // (2 * expert_count)
    local_experts = w_gate.shape[0]
    score_scale = 1.0 / math.sqrt(head_dim)
    normed, norm_back = jax.vjp(rms_scale, inputs, attn_gain)
    first_activations = normed.astype(jnp.bfloat16)
    query_key_value_projected = jnp.dot(
        first_activations, full_qkv, preferred_element_type=jnp.float32
    )
    angles = places.astype(jnp.float32)[:, None, None] * frequencies(head_dim)[None, None, :]

    def prepare(proj_in, gain_q, gain_k):
        return head_prep(proj_in, gain_q, gain_k, angles, heads_q, heads_kv)

    (queries, key_heads, value_heads), prep_back = jax.vjp(
        prepare, query_key_value_projected, q_gain, k_gain
    )
    query_low = queries.astype(jnp.bfloat16).reshape(row_count, heads_kv, group_size, head_dim)
    key_low = key_heads.astype(jnp.bfloat16)
    value_low = value_heads.astype(jnp.bfloat16)
    all_keys, all_values = (
        lax.all_gather(key_low, "ctx", axis=0, tiled=True),
        lax.all_gather(value_low, "ctx", axis=0, tiled=True),
    )
    key_places = lax.all_gather(places, "ctx", axis=0, tiled=True)
    seq_len = all_keys.shape[0]
    sorted_keys = jnp.zeros_like(all_keys).at[key_places].set(all_keys)
    sorted_values = jnp.zeros_like(all_values).at[key_places].set(all_values)
    block_len = min(512, seq_len)
    run_len = row_count // 2

    def block_scores(query_run, place_run, block_index):
        start = block_index * block_len
        key_blk = lax.dynamic_slice_in_dim(sorted_keys, start, block_len, 0)
        value_blk = lax.dynamic_slice_in_dim(sorted_values, start, block_len, 0)
        raw_scores = (
            jnp.einsum("qhgd,khd->hgqk", query_run, key_blk, preferred_element_type=jnp.float32)
            * score_scale
        )
        key_pos = start + jnp.arange(block_len, dtype=jnp.int32)
        visible = key_pos[None, :] <= place_run[:, None]
        return (jnp.where(visible, raw_scores, masked_value), visible, key_blk, value_blk)

    run_info = []
    mixed_runs = []
    for run_index in range(2):
        query_run = query_low[run_index * run_len : (run_index + 1) * run_len]
        place_run = places[run_index * run_len : (run_index + 1) * run_len]
        block_total = jnp.max(place_run) // block_len + 1

        def stats_step(block_index, carried):
            run_max, run_sum = carried
            scores, visible, key_blk, value_blk = block_scores(query_run, place_run, block_index)
            new_max = jnp.maximum(run_max, jnp.max(scores, axis=-1))
            weights = jnp.where(visible, jnp.exp(scores - new_max[..., None]), 0.0)
            run_sum = run_sum * jnp.exp(run_max - new_max) + jnp.sum(weights, axis=-1)
            return (new_max, run_sum)

        stat_shape = (heads_kv, group_size, run_len)
        initial = (
            jnp.full(stat_shape, masked_value, jnp.float32),
            jnp.zeros(stat_shape, jnp.float32),
        )
        run_max, run_sum = lax.fori_loop(0, block_total, stats_step, initial)
        log_total = run_max + jnp.log(run_sum)

        def output_step(block_index, running):
            scores, visible, key_blk, value_blk = block_scores(query_run, place_run, block_index)
            prob_vals = jnp.exp(scores - log_total[..., None])
            return running + jnp.einsum(
                "hgqk,khd->qhgd",
                prob_vals.astype(jnp.bfloat16),
                value_blk,
                preferred_element_type=jnp.float32,
            )

        mixed_run = lax.fori_loop(
            0,
            block_total,
            output_step,
            jnp.zeros((run_len, heads_kv, group_size, head_dim), jnp.float32),
        )
        mixed_runs.append(mixed_run)
        run_info.append((query_run, place_run, block_total, log_total))
    heads_out = jnp.concatenate(mixed_runs, axis=0)
    heads_reduced_precision = heads_out.reshape(row_count, heads_q * head_dim).astype(jnp.bfloat16)
    residual_stream = inputs + jnp.dot(
        heads_reduced_precision, full_out, preferred_element_type=jnp.float32
    )
    normed_two, norm_two_back = jax.vjp(rms_scale, residual_stream, ffn_gain)
    second_activations = normed_two.astype(jnp.bfloat16)
    router_logits = jnp.dot(second_activations, full_router, preferred_element_type=jnp.float32)
    pick_table = (chosen[:, :, None] == jnp.arange(expert_count)[None, None, :]).astype(jnp.float32)
    picked = jnp.sum(router_logits[:, None, :] * pick_table, axis=-1)
    gate_vals, gate_back = jax.vjp(lambda values: jax.nn.softmax(values, axis=-1), picked)
    flat_choice = chosen.reshape(-1)
    slot_hot = (flat_choice[:, None] == jnp.arange(expert_count)[None, :]).astype(jnp.int32)
    slot_rank = jnp.sum((jnp.cumsum(slot_hot, axis=0) - slot_hot) * slot_hot, axis=1)
    targets = flat_choice * capacity + slot_rank
    source_rows = jnp.repeat(second_activations, top_count, axis=0)
    outgoing = (
        jnp.zeros((expert_count * capacity, model_width), jnp.bfloat16).at[targets].set(source_rows)
    )
    outgoing = outgoing.reshape(expert_count, capacity, model_width)
    arrived = lax.all_to_all(outgoing, ("ctx", "fsdp"), split_axis=0, concat_axis=0, tiled=True)
    sources = arrived.shape[0] // local_experts
    slot_count = arrived.shape[1]
    grouped = arrived.reshape(sources, local_experts, slot_count, model_width)
    gate_pre = jnp.einsum("secd,edf->secf", grouped, w_gate, preferred_element_type=jnp.float32)
    up_pre = jnp.einsum("secd,edf->secf", grouped, w_up, preferred_element_type=jnp.float32)
    hidden = (jax.nn.silu(gate_pre) * up_pre).astype(jnp.bfloat16)
    produced = jnp.einsum("secf,efd->secd", hidden, w_down, preferred_element_type=jnp.float32)
    produced = produced.astype(jnp.bfloat16).reshape(arrived.shape)
    flat_shape = (arrived.shape[0], slot_count, gate_pre.shape[3])
    expert_results = (produced, arrived, gate_pre.reshape(flat_shape), up_pre.reshape(flat_shape))
    produced = expert_results[0]
    arrived = expert_results[1]
    returned = lax.all_to_all(produced, ("ctx", "fsdp"), split_axis=0, concat_axis=0, tiled=True)
    expert_rows = returned.reshape(expert_count * capacity, model_width)[targets].reshape(
        row_count, top_count, model_width
    )
    expert_vals = expert_rows.astype(jnp.float32)
    result = residual_stream + jnp.sum(gate_vals[:, :, None] * expert_vals, axis=1)
    output = result.astype(jnp.bfloat16).reshape(tokens.shape)
    grad_res = cotangent.reshape(row_count, model_width).astype(jnp.float32)
    gate_grad = jnp.sum(grad_res[:, None, :] * expert_vals, axis=-1)
    out_grad = (gate_vals[:, :, None] * grad_res[:, None, :]).astype(jnp.bfloat16)
    back_out = (
        jnp.zeros((expert_count * capacity, model_width), jnp.bfloat16)
        .at[targets]
        .set(out_grad.reshape(-1, model_width))
    )
    back_out = back_out.reshape(expert_count, capacity, model_width)
    (picked_grad,) = gate_back(gate_grad)
    logit_grad = jnp.sum(picked_grad[:, :, None] * pick_table, axis=1).astype(jnp.bfloat16)
    full_qkv, full_out, full_router = (
        lax.all_gather(query_key_value_weight, "fsdp", axis=0, tiled=True),
        lax.all_gather(output_weight, "fsdp", axis=0, tiled=True),
        lax.all_gather(router_weight, "fsdp", axis=0, tiled=True),
    )
    arrived_grad = lax.all_to_all(
        back_out, ("ctx", "fsdp"), split_axis=0, concat_axis=0, tiled=True
    )
    sources = arrived.shape[0] // local_experts
    grouped = arrived.reshape(sources, local_experts, capacity, model_width)
    grad_grouped = arrived_grad.reshape(sources, local_experts, capacity, model_width)
    gate_pre = expert_results[2].reshape(sources, local_experts, capacity, -1)
    up_pre = expert_results[3].reshape(sources, local_experts, capacity, -1)
    hidden, hidden_back = jax.vjp(
        lambda gate_in, up_in: jax.nn.silu(gate_in) * up_in, gate_pre, up_pre
    )
    hidden_low = hidden.astype(jnp.bfloat16)
    hidden_grad = jnp.einsum(
        "secd,efd->secf", grad_grouped, w_down, preferred_element_type=jnp.float32
    )
    gate_pre_grad, up_pre_grad = hidden_back(hidden_grad)
    gate_low = gate_pre_grad.astype(jnp.bfloat16)
    up_low = up_pre_grad.astype(jnp.bfloat16)
    grad_w_down = jnp.einsum(
        "secf,secd->efd", hidden_low, grad_grouped, preferred_element_type=jnp.float32
    )
    grad_w_gate = jnp.einsum(
        "secd,secf->edf", grouped, gate_low, preferred_element_type=jnp.float32
    )
    grad_w_up = jnp.einsum("secd,secf->edf", grouped, up_low, preferred_element_type=jnp.float32)
    row_grad = jnp.einsum(
        "secf,edf->secd", gate_low, w_gate, preferred_element_type=jnp.float32
    ) + jnp.einsum("secf,edf->secd", up_low, w_up, preferred_element_type=jnp.float32)
    row_grad = row_grad.astype(jnp.bfloat16).reshape(arrived.shape)
    row_back = lax.all_to_all(row_grad, ("ctx", "fsdp"), split_axis=0, concat_axis=0, tiled=True)
    token_rows = row_back.reshape(expert_count * capacity, model_width)[targets].reshape(
        row_count, top_count, model_width
    )
    acts_two_grad = jnp.sum(token_rows.astype(jnp.float32), axis=1) + jnp.dot(
        logit_grad, full_router.T, preferred_element_type=jnp.float32
    )
    grad_w_router = jnp.dot(second_activations.T, logit_grad, preferred_element_type=jnp.float32)
    resid_extra, grad_ffn_gain = norm_two_back(acts_two_grad)
    resid_grad = grad_res + resid_extra
    attn_grad = resid_grad.astype(jnp.bfloat16)
    grad_w_out = jnp.dot(heads_reduced_precision.T, attn_grad, preferred_element_type=jnp.float32)
    heads_grad = jnp.dot(attn_grad, full_out.T, preferred_element_type=jnp.float32).astype(
        jnp.bfloat16
    )
    heads_grad = heads_grad.reshape(row_count, heads_kv, group_size, head_dim)
    row_delta = jnp.moveaxis(jnp.sum(heads_grad.astype(jnp.float32) * heads_out, axis=-1), 0, 2)
    key_grad_sorted = jnp.zeros((seq_len, heads_kv, head_dim), jnp.float32)
    value_grad_sorted = jnp.zeros((seq_len, heads_kv, head_dim), jnp.float32)
    query_grad_runs = []
    for run_index in range(2):
        query_run, place_run, block_total, log_total = run_info[run_index]
        grad_run = heads_grad[run_index * run_len : (run_index + 1) * run_len]
        delta_run = row_delta[:, :, run_index * run_len : (run_index + 1) * run_len]

        def back_step(block_index, carried):
            query_grad, key_acc, value_acc = carried
            scores, visible, key_blk, value_blk = block_scores(query_run, place_run, block_index)
            prob_vals = jnp.exp(scores - log_total[..., None])
            value_grad = jnp.einsum(
                "hgqk,qhgd->khd",
                prob_vals.astype(jnp.bfloat16),
                grad_run,
                preferred_element_type=jnp.float32,
            )
            prob_grad = jnp.einsum(
                "qhgd,khd->hgqk", grad_run, value_blk, preferred_element_type=jnp.float32
            )
            score_grad = (prob_vals * (prob_grad - delta_run[..., None])).astype(jnp.bfloat16)
            query_grad = (
                query_grad
                + jnp.einsum(
                    "hgqk,khd->qhgd", score_grad, key_blk, preferred_element_type=jnp.float32
                )
                * score_scale
            )
            key_grad = (
                jnp.einsum(
                    "hgqk,qhgd->khd", score_grad, query_run, preferred_element_type=jnp.float32
                )
                * score_scale
            )
            start = block_index * block_len
            key_acc = lax.dynamic_update_slice_in_dim(
                key_acc, lax.dynamic_slice_in_dim(key_acc, start, block_len, 0) + key_grad, start, 0
            )
            value_acc = lax.dynamic_update_slice_in_dim(
                value_acc,
                lax.dynamic_slice_in_dim(value_acc, start, block_len, 0) + value_grad,
                start,
                0,
            )
            return (query_grad, key_acc, value_acc)

        start_state = (
            jnp.zeros((run_len, heads_kv, group_size, head_dim), jnp.float32),
            key_grad_sorted,
            value_grad_sorted,
        )
        query_grad_run, key_grad_sorted, value_grad_sorted = lax.fori_loop(
            0, block_total, back_step, start_state
        )
        query_grad_runs.append(query_grad_run)
    query_grad = jnp.concatenate(query_grad_runs, axis=0)
    key_grads = key_grad_sorted[key_places]
    value_grads = value_grad_sorted[key_places]
    key_grad_own, value_grad_own = (
        lax.psum_scatter(
            key_grads.astype(jnp.bfloat16), "ctx", scatter_dimension=0, tiled=True
        ).astype(jnp.float32),
        lax.psum_scatter(
            value_grads.astype(jnp.bfloat16), "ctx", scatter_dimension=0, tiled=True
        ).astype(jnp.float32),
    )
    proj_grad, grad_q_gain, grad_k_gain = prep_back(
        (query_grad.reshape(row_count, heads_q, head_dim), key_grad_own, value_grad_own)
    )
    proj_low = proj_grad.astype(jnp.bfloat16)
    grad_w_qkv = jnp.dot(first_activations.T, proj_low, preferred_element_type=jnp.float32)
    acts_grad = jnp.dot(proj_low, full_qkv.T, preferred_element_type=jnp.float32)
    inputs_extra, grad_attn_gain = norm_back(acts_grad)
    grad_tokens = (resid_grad + inputs_extra).reshape(tokens.shape)
    grad_w_qkv, grad_w_out, grad_w_router = (
        lax.psum_scatter(grad_w_qkv, ("ctx", "fsdp"), scatter_dimension=0, tiled=True),
        lax.psum_scatter(grad_w_out, ("ctx", "fsdp"), scatter_dimension=0, tiled=True),
        lax.psum_scatter(grad_w_router, ("ctx", "fsdp"), scatter_dimension=0, tiled=True),
    )
    grad_attn_gain, grad_q_gain, grad_k_gain, grad_ffn_gain = lax.psum(
        (grad_attn_gain, grad_q_gain, grad_k_gain, grad_ffn_gain), ("ctx", "fsdp")
    )
    return (
        output,
        grad_tokens,
        grad_attn_gain,
        grad_w_qkv,
        grad_q_gain,
        grad_k_gain,
        grad_w_out,
        grad_ffn_gain,
        grad_w_router,
        grad_w_gate,
        grad_w_up,
        grad_w_down,
    )


def swap(values, axis, count, bit):
    return lax.ppermute(values, axis, [(i, i ^ bit) for i in range(count)])


def after(values, earlier, both=False):
    values, earlier = lax.optimization_barrier((values, earlier))
    return (*values, *earlier) if both else values


def pick(values, index):
    return lax.dynamic_index_in_dim(values, index, 0, keepdims=False)


def by_fsdp(pieces, fsdp_at):
    stacked = jnp.stack(pieces)
    stacked = jnp.where(fsdp_at % 2 == 1, jnp.stack([pieces[k ^ 1] for k in range(4)]), stacked)
    turned = jnp.stack([stacked[k ^ 2] for k in range(4)])
    return jnp.where(fsdp_at // 2 == 1, turned, stacked)


def plane_gather(values):
    half = values.shape[-2] // 2
    near_x = swap(values, "fsdp", 4, 1)
    near_y = swap(values, "fsdp", 4, 2)
    far_low = swap(near_x[..., :half, :], "fsdp", 4, 2)
    far_high = swap(near_y[..., half:, :], "fsdp", 4, 1)
    return [values, near_x, near_y, far_low, far_high]


def plane_scatter(own, x_low, x_high, y_low, y_high, far_low, far_high):
    from_x = swap(far_low, "fsdp", 4, 1)
    from_y = swap(far_high, "fsdp", 4, 2)
    got_x_low = swap(x_low, "fsdp", 4, 1)
    got_y_high = swap(y_high, "fsdp", 4, 2)
    got_y_low = swap((y_low.astype(f32) + from_x.astype(f32)).astype(bf16), "fsdp", 4, 2)
    got_x_high = swap((x_high.astype(f32) + from_y.astype(f32)).astype(bf16), "fsdp", 4, 1)
    added = jnp.concatenate(
        [
            got_x_low.astype(f32) + got_y_low.astype(f32),
            got_x_high.astype(f32) + got_y_high.astype(f32),
        ],
        axis=-2,
    )
    return own.astype(f32) + added


def scatter_parts(parts):
    half = parts.shape[1] // 2
    return plane_scatter(
        parts[0],
        parts[1, :half],
        parts[1, half:],
        parts[2, :half],
        parts[2, half:],
        parts[3, :half],
        parts[3, half:],
    )


def ctx_scatter(parts, n_ctx, ctx_at, low):
    bit = 1
    held = parts
    while bit < n_ctx:
        mine = (ctx_at // bit) % 2
        split = held.reshape((held.shape[0] // 2, 2) + held.shape[1:])
        keep = lax.dynamic_index_in_dim(split, mine, 1, keepdims=False)
        away = lax.dynamic_index_in_dim(split, 1 - mine, 1, keepdims=False)
        got = swap(away, "ctx", n_ctx, bit)
        held = keep.astype(f32) + got.astype(f32)
        bit *= 2
        if low and bit < n_ctx:
            held = held.astype(bf16)
    return held.reshape(parts.shape[1:])


def attend_kernel(place_ref, source_ref, q_ref, kv_ref, o_ref, lse_ref, keys, vals_t, q_t, acc, total):
    seq = pl.program_id(0)
    rows = run_rows
    heads = q_ref.shape[2] // rows
    blocks = keys.shape[0] // rows
    scale = math.log2(math.e) / math.sqrt(rows)
    for p in range(blocks):
        at = source_ref[seq * blocks + p]
        block = kv_ref[at // 2, 0, pl.ds(pl.multiple_of((at % 2) * rows, rows), rows), :]
        keys[p * rows : (p + 1) * rows, :] = block[:, :rows]
        vals_t[:, p * rows : (p + 1) * rows] = block[:, rows:].T
    key_iota = lax.broadcasted_iota(jnp.int32, (2 * rows, 2 * rows), 0)
    query_iota = lax.broadcasted_iota(jnp.int32, (2 * rows, 2 * rows), 1) % rows
    for run in range(2):
        place = place_ref[seq * 2 + run]
        for h in range(heads):
            q_t[:, h * rows : (h + 1) * rows] = q_ref[
                0, run * rows : (run + 1) * rows, h * rows : (h + 1) * rows
            ].T
        acc[...] = jnp.zeros_like(acc)
        total[...] = jnp.zeros_like(total)

        def step(j, masked):
            start = pl.multiple_of(j * 2 * rows, 2 * rows)
            key_blk = keys[pl.ds(start, 2 * rows), :]
            val_blk = vals_t[:, pl.ds(start, 2 * rows)]
            for pair in range(heads // 2):
                cols = slice(pair * 2 * rows, (pair + 1) * 2 * rows)
                scores = jnp.dot(key_blk, q_t[:, cols], preferred_element_type=f32)
                weights = jnp.exp2(scores * scale)
                if masked:
                    seen = start + key_iota <= place * rows + query_iota
                    weights = jnp.where(seen, weights, 0.0)
                total[:, cols] += jnp.sum(weights.reshape(2 * rows // 8, 8, 2 * rows), axis=0)
                acc[:, cols] += jnp.dot(val_blk, weights.astype(bf16), preferred_element_type=f32)

        lax.fori_loop(0, place // 2, lambda j, c: (step(j, False), c)[1], 0)
        step(place // 2, True)
        norm = jnp.sum(total[...], axis=0, keepdims=True)
        lse_ref[0, run : run + 1, :] = jnp.log2(norm)
        mixed = acc[...] / norm
        for h in range(heads):
            o_ref[0, run * rows : (run + 1) * rows, h * rows : (h + 1) * rows] = (
                mixed[:, h * rows : (h + 1) * rows].T.astype(bf16)
            )


def head_back(turned, vector, cosine, sine, gain):
    grad = turned * cosine - pltpu.roll(turned, turned.shape[1] // 2, 1) * sine
    scale = lax.rsqrt(jnp.mean(vector * vector, axis=-1, keepdims=True) + eps_norm)
    unit = vector * scale
    scaled = grad * gain
    back = scale * (scaled - unit * jnp.mean(scaled * unit, axis=-1, keepdims=True))
    return back, grad * unit


def project_kernel(heads, acts_ref, weight_ref, cos_ref, sin_ref, gain_q_ref, gain_k_ref, proj_ref, q_ref, kv_ref):
    width = cos_ref.shape[2]
    proj_ref[0] = jnp.dot(acts_ref[0], weight_ref[...], preferred_element_type=f32)
    for h in range(heads + 1):
        vector = proj_ref[0, :, h * width : (h + 1) * width]
        gain = gain_q_ref[...] if h < heads else gain_k_ref[...]
        scale = lax.rsqrt(jnp.mean(vector * vector, axis=-1, keepdims=True) + eps_norm)
        normed = vector * scale * gain
        turned = normed * cos_ref[0] + pltpu.roll(normed, width // 2, 1) * sin_ref[0]
        if h < heads:
            q_ref[0, :, h * width : (h + 1) * width] = turned.astype(bf16)
        else:
            kv_ref[0, :, :width] = turned.astype(bf16)
    kv_ref[0, :, width:] = proj_ref[0, :, (heads + 1) * width :].astype(bf16)


def key_back_kernel(a_ref, b_ref, c_ref, d_ref, proj_ref, cos_ref, sin_ref, gain_ref, dkv_ref, dgain_ref):
    width = cos_ref.shape[2]
    total = (
        a_ref[0].astype(f32) + b_ref[0].astype(f32) + c_ref[0].astype(f32) + d_ref[0].astype(f32)
    )
    back, share = head_back(
        total[:, :width], proj_ref[0, :, :width], cos_ref[0], sin_ref[0], gain_ref[...]
    )
    dkv_ref[0, :, :width] = back.astype(bf16)
    dkv_ref[0, :, width:] = total[:, width:].astype(bf16)

    @pl.when(pl.program_id(0) == 0)
    def _():
        dgain_ref[...] = jnp.zeros_like(dgain_ref)

    dgain_ref[...] += jnp.sum(share.reshape(-1, 8, width), axis=0)


def attend_back_kernel(
    place_ref,
    source_ref,
    q_ref,
    kv_ref,
    o_ref,
    do_ref,
    lse_ref,
    proj_ref,
    cos_ref,
    sin_ref,
    gain_ref,
    dq_ref,
    dkv_ref,
    dkv_sibling_ref,
    dgain_ref,
    keys,
    keys_t,
    vals,
    q_n,
    q_t,
    do_n,
    do_t,
    delta,
    dq_acc,
    dk_acc,
    dv_acc,
):
    seq = pl.program_id(0)
    rows = run_rows
    heads = q_ref.shape[2] // rows
    blocks = keys.shape[0] // rows
    scale = math.log2(math.e) / math.sqrt(rows)
    plain_scale = 1.0 / math.sqrt(rows)
    for p in range(blocks):
        at = source_ref[seq * blocks + p]
        block = kv_ref[at // 2, 0, pl.ds(pl.multiple_of((at % 2) * rows, rows), rows), :]
        keys[p * rows : (p + 1) * rows, :] = block[:, :rows]
        keys_t[:, p * rows : (p + 1) * rows] = block[:, :rows].T
        vals[p * rows : (p + 1) * rows, :] = block[:, rows:]
    dk_acc[...] = jnp.zeros_like(dk_acc)
    dv_acc[...] = jnp.zeros_like(dv_acc)

    @pl.when(seq == 0)
    def _():
        dgain_ref[...] = jnp.zeros_like(dgain_ref)

    key_iota = lax.broadcasted_iota(jnp.int32, (2 * rows, 2 * rows), 0)
    query_iota = lax.broadcasted_iota(jnp.int32, (2 * rows, 2 * rows), 1) % rows
    for run in range(2):
        place = place_ref[seq * 2 + run]
        here = slice(run * rows, (run + 1) * rows)
        for h in range(heads):
            cols = slice(h * rows, (h + 1) * rows)
            q_h = q_ref[0, here, cols]
            q_n[cols, :] = q_h
            q_t[:, cols] = q_h.T
            do_h = do_ref[0, here, cols]
            do_n[cols, :] = do_h
            do_ht = do_h.T
            do_t[:, cols] = do_ht
            o_ht = o_ref[0, here, cols].T
            delta[:, cols] = jnp.sum(do_ht.astype(f32) * o_ht.astype(f32), axis=0, keepdims=True)
        dq_acc[...] = jnp.zeros_like(dq_acc)

        def step(j, masked):
            start = pl.multiple_of(j * 2 * rows, 2 * rows)
            key_blk = keys[pl.ds(start, 2 * rows), :]
            key_t_blk = keys_t[:, pl.ds(start, 2 * rows)]
            val_blk = vals[pl.ds(start, 2 * rows), :]
            dk_sum = jnp.zeros((2 * rows, rows), f32)
            dv_sum = jnp.zeros((2 * rows, rows), f32)
            for pair in range(heads // 2):
                cols = slice(pair * 2 * rows, (pair + 1) * 2 * rows)
                scores = jnp.dot(key_blk, q_t[:, cols], preferred_element_type=f32)
                probs = jnp.exp2(scores * scale - lse_ref[0, run : run + 1, cols])
                if masked:
                    seen = start + key_iota <= place * rows + query_iota
                    probs = jnp.where(seen, probs, 0.0)
                prob_grad = jnp.dot(val_blk, do_t[:, cols], preferred_element_type=f32)
                score_grad = (probs * (prob_grad - delta[:, cols])).astype(bf16)
                dv_sum += jnp.dot(probs.astype(bf16), do_n[cols, :], preferred_element_type=f32)
                dk_sum += jnp.dot(score_grad, q_n[cols, :], preferred_element_type=f32)
                dq_acc[:, cols] += jnp.dot(key_t_blk, score_grad, preferred_element_type=f32)
            dk_acc[pl.ds(start, 2 * rows), :] += dk_sum
            dv_acc[pl.ds(start, 2 * rows), :] += dv_sum

        lax.fori_loop(0, place // 2, lambda j, c: (step(j, False), c)[1], 0)
        step(place // 2, True)
        for h in range(heads):
            cols = slice(h * rows, (h + 1) * rows)
            turned = dq_acc[:, cols].T * plain_scale
            back, share = head_back(
                turned, proj_ref[0, here, cols], cos_ref[0, here, :], sin_ref[0, here, :], gain_ref[...]
            )
            dq_ref[0, here, cols] = back.astype(bf16)
            dgain_ref[...] += jnp.sum(share.reshape(rows // 8, 8, rows), axis=0)
    for p in range(blocks):
        at = source_ref[seq * blocks + p]
        span = slice(p * rows, (p + 1) * rows)
        there = pl.ds(pl.multiple_of((at % 2) * rows, rows), rows)
        slot = at // 2

        def put(ref):
            ref[slot // 2, 0, there, :rows] = (dk_acc[span, :] * plain_scale).astype(bf16)
            ref[slot // 2, 0, there, rows:] = dv_acc[span, :].astype(bf16)

        pl.when(slot % 2 == 0)(functools.partial(put, dkv_ref))
        pl.when(slot % 2 == 1)(functools.partial(put, dkv_sibling_ref))


def attend(places, sources, queries, kv):
    seqs, rows, width = queries.shape
    slots, _, _, pair_width = kv.shape
    head_dim = pair_width // 2
    seq_len = slots * rows
    return pl.pallas_call(
        attend_kernel,
        out_shape=(
            jax.ShapeDtypeStruct(queries.shape, bf16),
            jax.ShapeDtypeStruct((seqs, 2, width), f32),
        ),
        grid_spec=pltpu.PrefetchScalarGridSpec(
            num_scalar_prefetch=2,
            grid=(seqs,),
            in_specs=[
                pl.BlockSpec((1, rows, width), lambda s, *_: (s, 0, 0)),
                pl.BlockSpec((slots, 1, rows, pair_width), lambda s, *_: (0, s, 0, 0)),
            ],
            out_specs=[
                pl.BlockSpec((1, rows, width), lambda s, *_: (s, 0, 0)),
                pl.BlockSpec((1, 2, width), lambda s, *_: (s, 0, 0)),
            ],
            scratch_shapes=[
                pltpu.VMEM((seq_len, head_dim), bf16),
                pltpu.VMEM((head_dim, seq_len), bf16),
                pltpu.VMEM((head_dim, width), bf16),
                pltpu.VMEM((head_dim, width), f32),
                pltpu.VMEM((8, width), f32),
            ],
        ),
        compiler_params=pltpu.CompilerParams(vmem_limit_bytes=32 * 2**20),
        cost_estimate=pl.CostEstimate(flops=1000, bytes_accessed=1000, transcendentals=0),
        name="attend",
    )(places, sources, queries, kv)


def attend_back(places, sources, queries, kv, mixed, mixed_grad, lse, projected, cosine, sine, gain):
    seqs, rows, width = queries.shape
    slots, _, _, pair_width = kv.shape
    head_dim = pair_width // 2
    seq_len = slots * rows
    block = pl.BlockSpec((1, rows, width), lambda s, *_: (s, 0, 0))
    angle_block = pl.BlockSpec((1, rows, head_dim), lambda s, *_: (s, 0, 0))
    kv_block = pl.BlockSpec((slots, 1, rows, pair_width), lambda s, *_: (0, s, 0, 0))
    half_kv_block = pl.BlockSpec((slots // 2, 1, rows, pair_width), lambda s, *_: (0, s, 0, 0))
    return pl.pallas_call(
        attend_back_kernel,
        out_shape=(
            jax.ShapeDtypeStruct(queries.shape, bf16),
            jax.ShapeDtypeStruct((slots // 2,) + kv.shape[1:], bf16),
            jax.ShapeDtypeStruct((slots // 2,) + kv.shape[1:], bf16),
            jax.ShapeDtypeStruct((8, head_dim), f32),
        ),
        grid_spec=pltpu.PrefetchScalarGridSpec(
            num_scalar_prefetch=2,
            grid=(seqs,),
            in_specs=[
                block,
                kv_block,
                block,
                block,
                pl.BlockSpec((1, 2, width), lambda s, *_: (s, 0, 0)),
                block,
                angle_block,
                angle_block,
                pl.BlockSpec((1, head_dim), lambda s, *_: (0, 0)),
            ],
            out_specs=[
                block,
                half_kv_block,
                half_kv_block,
                pl.BlockSpec((8, head_dim), lambda s, *_: (0, 0)),
            ],
            scratch_shapes=[
                pltpu.VMEM((seq_len, head_dim), bf16),
                pltpu.VMEM((head_dim, seq_len), bf16),
                pltpu.VMEM((seq_len, head_dim), bf16),
                pltpu.VMEM((width, head_dim), bf16),
                pltpu.VMEM((head_dim, width), bf16),
                pltpu.VMEM((width, head_dim), bf16),
                pltpu.VMEM((head_dim, width), bf16),
                pltpu.VMEM((1, width), f32),
                pltpu.VMEM((head_dim, width), f32),
                pltpu.VMEM((seq_len, head_dim), f32),
                pltpu.VMEM((seq_len, head_dim), f32),
            ],
        ),
        compiler_params=pltpu.CompilerParams(vmem_limit_bytes=40 * 2**20),
        cost_estimate=pl.CostEstimate(flops=1000, bytes_accessed=1000, transcendentals=0),
        name="attend_back",
    )(places, sources, queries, kv, mixed, mixed_grad, lse, projected, cosine, sine, gain)


def project(acts, weight, cosine, sine, gain_q, gain_k, heads):
    seqs, rows, depth = acts.shape
    head_dim = cosine.shape[2]
    width = weight.shape[1]
    angle_block = pl.BlockSpec((1, rows, head_dim), lambda s: (s, 0, 0))
    gain_block = pl.BlockSpec((1, head_dim), lambda s: (0, 0))

    def block(columns):
        return pl.BlockSpec((1, rows, columns), lambda s: (s, 0, 0))

    return pl.pallas_call(
        functools.partial(project_kernel, heads),
        out_shape=(
            jax.ShapeDtypeStruct((seqs, rows, width), f32),
            jax.ShapeDtypeStruct((seqs, rows, heads * head_dim), bf16),
            jax.ShapeDtypeStruct((seqs, rows, 2 * head_dim), bf16),
        ),
        grid=(seqs,),
        in_specs=[
            block(depth),
            pl.BlockSpec((depth, width), lambda s: (0, 0)),
            angle_block,
            angle_block,
            gain_block,
            gain_block,
        ],
        out_specs=[block(width), block(heads * head_dim), block(2 * head_dim)],
        compiler_params=pltpu.CompilerParams(vmem_limit_bytes=40 * 2**20),
        cost_estimate=pl.CostEstimate(flops=1000, bytes_accessed=1000, transcendentals=0),
        name="project",
    )(acts, weight, cosine, sine, gain_q, gain_k)


def key_back(held, projected, cosine, sine, gain):
    seqs, rows, pair_width = held[0].shape
    head_dim = pair_width // 2
    pairs_before = projected.shape[2] // pair_width - 1
    block = pl.BlockSpec((1, rows, pair_width), lambda s: (s, 0, 0))
    angle_block = pl.BlockSpec((1, rows, head_dim), lambda s: (s, 0, 0))
    return pl.pallas_call(
        key_back_kernel,
        out_shape=(
            jax.ShapeDtypeStruct(held[0].shape, bf16),
            jax.ShapeDtypeStruct((8, head_dim), f32),
        ),
        grid=(seqs,),
        in_specs=[
            block,
            block,
            block,
            block,
            pl.BlockSpec((1, rows, pair_width), lambda s: (s, 0, pairs_before)),
            angle_block,
            angle_block,
            pl.BlockSpec((1, head_dim), lambda s: (0, 0)),
        ],
        out_specs=[block, pl.BlockSpec((8, head_dim), lambda s: (0, 0))],
        name="key_back",
    )(*held, projected, cosine, sine, gain)


def hot_rows(slot_row, capacity):
    count = slot_row.shape[1]
    return slot_row == lax.broadcasted_iota(jnp.int32, (capacity, count), 0).astype(f32)


def hot_columns(slot_column, capacity):
    count = slot_column.shape[0]
    return (slot_column == lax.broadcasted_iota(jnp.int32, (count, capacity), 1).astype(f32)).astype(bf16)


def select_rows(capacity, slot_ref, s, pieces, store):
    for core in range(2):
        near = pieces[5 * core : 5 * core + 3]
        low, high = pieces[5 * core + 3], pieces[5 * core + 4]
        for k in range(4):
            source = 4 * core + k
            hot = hot_rows(slot_ref[s, source : source + 1, :], capacity).astype(bf16)
            if k < 3:
                rows = jnp.dot(hot, near[k][...], preferred_element_type=f32)
            else:
                half = low.shape[0]
                rows = jnp.dot(hot[:, :half], low[...], preferred_element_type=f32)
                rows += jnp.dot(hot[:, half:], high[...], preferred_element_type=f32)
            store(source, rows.astype(bf16))


def combine_kernel(capacity, column_ref, kept_ref, got_ref, own_ref, x_ref, y_ref, low_ref, high_ref):
    for k in range(4):
        span = slice(k * capacity, (k + 1) * capacity)
        own_hot = hot_columns(column_ref[0, :, k : k + 1], capacity)
        sibling_hot = hot_columns(column_ref[0, :, 4 + k : 5 + k], capacity)
        total = jnp.dot(own_hot, kept_ref[0, span, :], preferred_element_type=f32)
        total += jnp.dot(sibling_hot, got_ref[0, span, :], preferred_element_type=f32)
        total = total.astype(bf16)
        if k < 3:
            (own_ref, x_ref, y_ref)[k][0] = total
        else:
            half = total.shape[0] // 2
            low_ref[0] = total[:half]
            high_ref[0] = total[half:]


def combine_rows(columns, kept, got, capacity):
    chunks, rows, sources = columns.shape
    width = kept.shape[2]
    tile = width // 4
    at = lambda k, d: (k, 0, d)
    whole = pl.BlockSpec((1, rows, tile), at)
    half = pl.BlockSpec((1, rows // 2, tile), at)
    return pl.pallas_call(
        functools.partial(combine_kernel, capacity),
        out_shape=[jax.ShapeDtypeStruct((chunks, rows, width), bf16)] * 3
        + [jax.ShapeDtypeStruct((chunks, rows // 2, width), bf16)] * 2,
        grid=(chunks, 4),
        in_specs=[
            pl.BlockSpec((1, rows, sources), lambda k, d: (k, 0, 0)),
            pl.BlockSpec((1, 4 * capacity, tile), at),
            pl.BlockSpec((1, 4 * capacity, tile), at),
        ],
        out_specs=[whole] * 3 + [half] * 2,
        cost_estimate=pl.CostEstimate(flops=1000, bytes_accessed=1000, transcendentals=0),
        name="combine_rows",
    )(columns, kept, got)


def flip(index, bit):
    return index + bit - 2 * bit * ((index // bit) % 2)


def neighbours():
    ctx, fsdp = lax.axis_index("ctx"), lax.axis_index("fsdp")
    return dict(
        core=(flip(ctx, 1), fsdp),
        x=(ctx, flip(fsdp, 1)),
        y=(ctx, flip(fsdp, 2)),
        z=[None, (flip(ctx, 2), fsdp), (flip(ctx, 4), fsdp), (flip(flip(ctx, 2), 4), fsdp)],
    )


def greet(partners):
    barrier = pltpu.get_barrier_semaphore()
    for partner in partners:
        pl.semaphore_signal(barrier, inc=1, device_id=partner, device_id_type=pl.DeviceIdType.MESH)
    pl.semaphore_wait(barrier, len(partners))


def send(source, target, sent, received, partner):
    return pltpu.make_async_remote_copy(
        src_ref=source,
        dst_ref=target,
        send_sem=sent,
        recv_sem=received,
        device_id=partner,
        device_id_type=pl.DeviceIdType.MESH,
    )


class Exchange:
    def __init__(self, near, table, outgoing, landing, sent, got):
        self.partners = [near["x"], near["y"], near["core"], near["z"][1], near["z"][2]]
        self.table, self.outgoing, self.landing = table, outgoing, landing
        self.sent, self.got = sent, got
        self.rows = [[r for r in range(32) if (r >> bit) % 2] for bit in range(5)]

    def copy(self, bit):
        return send(
            self.outgoing.at[bit],
            self.landing.at[bit],
            self.sent.at[bit],
            self.got.at[bit],
            self.partners[bit],
        )

    def start(self, bit):
        for i, r in enumerate(self.rows[bit]):
            self.outgoing[bit, i] = self.table[r]
        self.copy(bit).start()

    def end(self, bit):
        self.copy(bit).wait_recv()
        for i, r in enumerate(self.rows[bit]):
            self.table[r] = self.landing[bit, i]

    def finish(self):
        for bit in range(5):
            self.copy(bit).wait_send()


def exchange_scratch(width):
    return [
        pltpu.VMEM((5, 16, 1, width), f32),
        pltpu.VMEM((5, 16, 1, width), f32),
        pltpu.SemaphoreType.DMA((5,)),
        pltpu.SemaphoreType.DMA((5,)),
    ]


class Chain:
    def __init__(self, near, own, place, sent, got):
        self.near, self.own, self.place, self.sent, self.got = near, own, place, sent, got
        z = lax.axis_index("ctx") // 2
        self.inner = (z == 1) | (z == 2)
        self.outer = (z == 0) | (z == 3)

    def copy(self, source, slot, number, partner):
        return send(
            source, self.place(slot), self.sent.at[number], self.got.at[slot - 1], self.near["z"][partner]
        )

    def first(self):
        return self.copy(self.own, 1, 0, 1)

    def inner_copies(self, stage):
        if stage == 0:
            return [(self.own, 3, 1, 3)]
        if stage == 1:
            return [(self.place(1), 2, 2, 3), (self.place(3), 2, 3, 1)]
        return [(self.place(2), 3, 4, 1)]

    def start(self):
        self.first().start()
        self.start_inner(0)

    def start_inner(self, stage):
        @pl.when(self.inner)
        def _():
            for copy in self.inner_copies(stage):
                self.copy(*copy).start()

    def wait(self, slot):
        if slot < 3:
            self.copy(self.own, slot, 0, 1).wait_recv()
        else:
            @pl.when(self.outer)
            def _():
                self.copy(self.own, 3, 0, 1).wait_recv()

    def wait_inner_last(self):
        @pl.when(self.inner)
        def _():
            self.copy(self.own, 3, 0, 1).wait_recv()

    def step(self, slot):
        if slot == 1:
            self.wait(1)
            self.wait_inner_last()
            self.start_inner(1)
        elif slot == 2:
            self.wait(2)
            self.start_inner(2)
        else:
            self.wait(3)

    def finish(self):
        self.first().wait_send()

        @pl.when(self.inner)
        def _():
            for stage in range(3):
                for copy in self.inner_copies(stage):
                    self.copy(*copy).wait_send()


def gather_experts_kernel(
    capacity,
    steps,
    acts_ref,
    slot_ref,
    sibling_ref,
    gates_ref,
    gate_ref,
    up_ref,
    down_ref,
    grad_ref,
    grad_x_ref,
    grad_y_ref,
    rows_ref,
    grad_rows_ref,
    hidden_ref,
    gate_low_ref,
    up_low_ref,
    kept_ref,
    got_ref,
    given_ref,
    out_kept_ref,
    out_got_ref,
    out_given_ref,
    scalar_ref,
    buffer_ref,
    grad_far_ref,
    sent_ref,
    grad_sent_ref,
    gate_acc,
    up_acc,
    back_acc,
    hidden_now,
    gate_low_now,
    up_low_now,
    gate_all,
    up_all,
    down_all,
    gate_table,
    z_sent,
    z_got,
    grad_z_sent,
    grad_z_got,
    near_sent,
    near_got,
    far_sent,
    far_got,
    grad_far_sent,
    grad_far_got,
    rows_sent,
    rows_got,
    given_sent,
    given_got,
    weight_sem,
    local,
    *exchange_refs,
):
    near = neighbours()
    chunks = slot_ref.shape[0]
    half = acts_ref.shape[0] // 2
    width = acts_ref.shape[1]
    tile = width // steps
    part = 4 * capacity
    group = 2 * part
    greet([near["core"], near["x"], near["y"]] + near["z"][1:])
    chain = Chain(near, acts_ref, lambda s: buffer_ref.at[s, 0], z_sent, z_got)
    grad_chain = Chain(
        near, grad_far_ref.at[0], lambda s: grad_far_ref.at[s], grad_z_sent, grad_z_got
    )
    exchange = Exchange(near, gate_table, *exchange_refs)

    def to_near(s, k):
        source = acts_ref if s == 0 else buffer_ref.at[s, 0]
        return send(
            source, buffer_ref.at[s, 1 + k], near_sent.at[s, k], near_got.at[s, k], near["xy"[k]]
        )

    def to_far(s, k):
        span = pl.ds(k * half, half)
        return send(
            buffer_ref.at[s, 1 + k, span],
            buffer_ref.at[s, 3, span],
            far_sent.at[s, k],
            far_got.at[s, k],
            near["yx"[k]],
        )

    def grad_to_far(k):
        span = pl.ds(k * half, half)
        return send(
            (grad_x_ref, grad_y_ref)[k].at[0, span],
            grad_far_ref.at[0, span],
            grad_far_sent.at[k],
            grad_far_got.at[k],
            near["yx"[k]],
        )

    def to_sibling_rows(s, i):
        source, target = ((grad_sent_ref, grad_rows_ref), (sent_ref, rows_ref))[i]
        return send(
            source.at[s],
            target.at[s, pl.ds(part, part)],
            rows_sent.at[s, i],
            rows_got.at[s, i],
            near["core"],
        )

    def to_sibling(s, i):
        source, target = ((given_ref, got_ref), (out_given_ref, out_got_ref))[i]
        return send(
            source.at[s], target.at[s], given_sent.at[s, i], given_got.at[s, i], near["core"]
        )

    def fetch_weight(i):
        source, target = ((down_ref, down_all), (gate_ref, gate_all), (up_ref, up_all))[i]
        return pltpu.make_async_copy(source, target, weight_sem.at[i])

    def span_of(d):
        return pl.ds(pl.multiple_of(d * tile, tile), tile)

    def select_step(s, *blocks):
        tokens, (own_blk, sibling_blk) = blocks[:-2], blocks[-2:]
        for k in range(4):
            hot = jnp.concatenate(
                [
                    hot_rows(slot_ref[s, k : k + 1, :], capacity).astype(bf16),
                    hot_rows(sibling_ref[s, k : k + 1, :], capacity).astype(bf16),
                ],
                axis=0,
            )
            block = tokens[0][k] if len(tokens) == 1 else tokens[k][...]
            rows = jnp.dot(hot, block, preferred_element_type=f32).astype(bf16)
            own_blk[k * capacity : (k + 1) * capacity, :] = rows[:capacity]
            sibling_blk[k * capacity : (k + 1) * capacity, :] = rows[capacity:]

    def select(s, i):
        out = pl.BlockSpec((part, tile), lambda d: (0, d))
        if i:
            in_specs = [pl.BlockSpec((4, 2 * half, tile), lambda d: (0, 0, d))]
            tokens = [buffer_ref.at[s]]
        else:
            in_specs = [pl.BlockSpec((2 * half, tile), lambda d: (0, d))] * 4
            tokens = [ref.at[s] for ref in (grad_ref, grad_x_ref, grad_y_ref, grad_far_ref)]
        target, sent = ((grad_rows_ref, grad_sent_ref), (rows_ref, sent_ref))[i]
        pltpu.emit_pipeline(
            functools.partial(select_step, s),
            grid=(steps,),
            in_specs=in_specs,
            out_specs=[out, out],
        )(*tokens, target.at[s, pl.ds(0, part)], sent.at[s])
        to_sibling_rows(s, i).start()

    def grad_step(rows_blk):
        d = pl.program_id(0)

        @pl.when(d == 0)
        def _():
            back_acc[...] = jnp.zeros_like(back_acc)

        back_acc[...] += lax.dot_general(
            rows_blk[...],
            down_all[:, span_of(d)],
            (((1,), (1,)), ((), ())),
            preferred_element_type=f32,
        )

    def compute_grad(s):
        pltpu.emit_pipeline(
            grad_step,
            grid=(steps,),
            in_specs=[pl.BlockSpec((group, tile), lambda d: (0, d))],
        )(grad_rows_ref.at[s])

    def experts_step(s, rows_blk, given_blk, kept_blk, out_given_blk, out_kept_blk):
        step = pl.program_id(0)
        span_now = span_of(step % steps)

        @pl.when(step == 0)
        def _():
            gate_acc[...] = jnp.zeros_like(gate_acc)
            up_acc[...] = jnp.zeros_like(up_acc)

        @pl.when(step < steps)
        def _():
            gate_acc[...] += jnp.dot(
                rows_blk[...], gate_all[span_now, :], preferred_element_type=f32
            )
            up_acc[...] += jnp.dot(
                rows_blk[...], up_all[span_now, :], preferred_element_type=f32
            )

        @pl.when(step == steps - 1)
        def _():
            for source in range(8):
                span = slice(source * capacity, (source + 1) * capacity)
                hot = hot_rows(slot_ref[s, source : source + 1, :], capacity)
                weighted = jnp.where(hot, gate_table[8 * s + source], 0.0)
                gate_val = jnp.sum(weighted, axis=1, keepdims=True)
                gate_pre, up_pre, back = gate_acc[span, :], up_acc[span, :], back_acc[span, :]
                sig = 1.0 / (1.0 + jnp.exp(-gate_pre))
                silu = gate_pre * sig
                hidden = (silu * up_pre).astype(bf16).astype(f32)
                hidden_now[span, :] = (hidden * gate_val).astype(bf16)
                scalar = jnp.sum(hidden * back, axis=1, keepdims=True)
                scalar_ref[s, source : source + 1, :] = jnp.sum(
                    jnp.where(hot, scalar, 0.0), axis=0, keepdims=True
                )
                hidden_grad = gate_val * back
                gate_low_now[span, :] = (
                    hidden_grad * up_pre * sig * (1.0 + gate_pre * (1.0 - sig))
                ).astype(bf16)
                up_low_now[span, :] = (hidden_grad * silu).astype(bf16)

        if s + 1 < chunks:

            @pl.when(step == steps)
            def _():
                near_done(s + 1)
                if s + 2 < chunks:
                    next_slot(s + 2)

        @pl.when(step >= steps)
        def _():
            last = (((1,), (1,)), ((), ()))
            row_grad = lax.dot_general(
                gate_low_now[...], gate_all[span_now, :], last, preferred_element_type=f32
            )
            row_grad += lax.dot_general(
                up_low_now[...], up_all[span_now, :], last, preferred_element_type=f32
            )
            row_grad = row_grad.astype(bf16)
            kept_blk[...] = row_grad[:part]
            given_blk[...] = row_grad[part:]
            weighted = jnp.dot(
                hidden_now[...], down_all[:, span_now], preferred_element_type=f32
            ).astype(bf16)
            out_kept_blk[...] = weighted[:part]
            out_given_blk[...] = weighted[part:]

    def store(s, i):
        now, whole = (
            (hidden_now, hidden_ref),
            (gate_low_now, gate_low_ref),
            (up_low_now, up_low_ref),
        )[i]
        return pltpu.make_async_copy(now, whole.at[s], local.at[1 + i])

    def compute(s):
        if s:
            for i in range(3):
                store(s - 1, i).wait()
        late = pl.BlockSpec((part, tile), lambda d: (0, jnp.maximum(d - steps, 0)))
        pltpu.emit_pipeline(
            functools.partial(experts_step, s),
            grid=(2 * steps,),
            in_specs=[pl.BlockSpec((group, tile), lambda d: (0, jnp.minimum(d, steps - 1)))],
            out_specs=[late] * 4,
        )(
            rows_ref.at[s],
            given_ref.at[s],
            kept_ref.at[s],
            out_given_ref.at[s],
            out_kept_ref.at[s],
        )
        for i in range(3):
            store(s, i).start()

    def near_done(s):
        for k in range(2):
            to_near(s, k).wait_recv()
            to_far(s, k).start()

    def next_slot(s):
        chain.step(s)
        to_near(s, 0).start()
        to_near(s, 1).start()

    for i in range(3):
        fetch_weight(i).start()
    gate_table[...] = gates_ref[...]
    exchange.start(0)
    chain.start()
    to_near(0, 0).start()
    exchange.end(0)
    exchange.start(1)
    to_near(0, 1).start()
    exchange.end(1)
    keep = pltpu.make_async_copy(acts_ref, buffer_ref.at[0, 0], local.at[0])
    keep.start()
    for k in range(2):
        grad_to_far(k).start()
    for bit in range(2, 5):
        exchange.start(bit)
        exchange.end(bit)
    keep.wait()
    near_done(0)
    next_slot(1)
    for s in range(chunks):
        if s == 0:
            for k in range(2):
                grad_to_far(k).wait_recv()
            grad_chain.start()
        else:
            grad_chain.step(s)
        select(s, 0)
        for k in range(2):
            to_far(s, k).wait_recv()
        select(s, 1)
        if s == 0:
            for i in range(3):
                fetch_weight(i).wait()
        to_sibling_rows(s, 0).wait_recv()
        compute_grad(s)
        to_sibling_rows(s, 1).wait_recv()
        compute(s)
        if s + 1 < chunks:
            to_sibling(s, 0).start()
            to_sibling(s, 1).start()
    for i in range(3):
        store(chunks - 1, i).wait()
    chain.finish()
    grad_chain.finish()
    exchange.finish()
    for k in range(2):
        grad_to_far(k).wait_send()
    for s in range(chunks):
        for k in range(2):
            to_near(s, k).wait_send()
            to_far(s, k).wait_send()
            to_sibling_rows(s, k).wait_send()
        if s + 1 < chunks:
            to_sibling(s, 0).wait()
            to_sibling(s, 1).wait()


def gather_experts(acts, slots, sibling_slots, gates, gate_w, up_w, down_w, grads, capacity):
    chunks, sources, rows = slots.shape
    width, hidden = gate_w.shape
    group = sources * capacity
    steps = 4
    anywhere = pl.BlockSpec(memory_space=pl.ANY)
    held = pl.BlockSpec(memory_space=pltpu.VMEM)
    dma = pltpu.SemaphoreType.DMA

    def low(*shape):
        return jax.ShapeDtypeStruct((chunks,) + shape, bf16)

    return pl.pallas_call(
        functools.partial(gather_experts_kernel, capacity, steps),
        out_shape=[low(group, width)] * 2
        + [low(group, hidden)] * 3
        + [low(group // 2, width)] * 6
        + [jax.ShapeDtypeStruct((chunks, sources, rows), f32)]
        + [low(4, rows, width), low(rows, width)]
        + [low(group // 2, width)] * 2,
        in_specs=[held] * 4 + [anywhere] * 6,
        out_specs=[anywhere] * 11 + [held] + [anywhere] * 4,
        scratch_shapes=[pltpu.VMEM((group, hidden), f32)] * 3
        + [pltpu.VMEM((group, hidden), bf16)] * 3
        + [
            pltpu.VMEM(gate_w.shape, bf16),
            pltpu.VMEM(up_w.shape, bf16),
            pltpu.VMEM(down_w.shape, bf16),
            pltpu.VMEM(gates.shape, f32),
            dma((5,)),
            dma((3,)),
            dma((5,)),
            dma((3,)),
        ]
        + [dma((chunks, 2))] * 4
        + [dma((2,))] * 2
        + [dma((chunks, 2))] * 4
        + [dma((3,)), dma((4,))]
        + exchange_scratch(rows),
        compiler_params=pltpu.CompilerParams(
            collective_id=1, has_side_effects=True, vmem_limit_bytes=60 * 2**20
        ),
        cost_estimate=pl.CostEstimate(flops=1000, bytes_accessed=1000, transcendentals=0),
        name="gather_experts",
    )(acts, slots, sibling_slots, gates, gate_w, up_w, down_w, *grads)


def return_rows_kernel(
    capacity,
    column_ref,
    kept_ref,
    got_ref,
    given_ref,
    out_given_ref,
    out_got_in_ref,
    scalar_ref,
    out_ref,
    out_got_ref,
    table_ref,
    kept_now,
    got_now,
    sums,
    relay,
    from_x,
    from_y,
    own,
    from_z,
    kept_sem,
    got_sem,
    first_sent,
    first_got,
    second_sent,
    second_got,
    z_sent,
    z_got,
    core_sent,
    core_got,
    *exchange_refs,
):
    near = neighbours()
    exchange = Exchange(near, table_ref, *exchange_refs)
    chunks, rows = sums.shape[0], sums.shape[2]
    final = chunks - 1
    half = rows // 2
    low, high = pl.ds(0, half), pl.ds(half, half)
    greet([near["core"], near["x"], near["y"]] + near["z"][1:])
    order = [2, 3, 1, 0]

    def fetch_kept(s):
        return pltpu.make_async_copy(kept_ref.at[s], kept_now.at[s], kept_sem.at[s])

    def fetch_got(s):
        if s == final:
            return send(
                given_ref.at[s], got_now.at[s], core_sent.at[0], core_got.at[0], near["core"]
            )
        return pltpu.make_async_copy(got_ref.at[s], got_now.at[s], got_sem.at[s])

    def to_sibling():
        return send(
            out_given_ref.at[final], out_got_ref.at[final], core_sent.at[1], core_got.at[1], near["core"]
        )

    def first(s, i):
        source, target, partner = (
            (sums.at[s, 3, low], relay.at[s, 0], near["x"]),
            (sums.at[s, 3, high], relay.at[s, 1], near["y"]),
            (sums.at[s, 1, low], from_x.at[s, low], near["x"]),
            (sums.at[s, 2, high], from_y.at[s, high], near["y"]),
        )[i]
        return send(source, target, first_sent.at[s, i], first_got.at[s, i], partner)

    def second(s, i):
        source, target, partner = (
            (sums.at[s, 2, low], from_y.at[s, low], near["y"]),
            (sums.at[s, 1, high], from_x.at[s, high], near["x"]),
        )[i]
        return send(source, target, second_sent.at[s, i], second_got.at[s, i], partner)

    def along_z(s):
        return send(own.at[s], from_z.at[s - 1], z_sent.at[s - 1], z_got.at[s - 1], near["z"][s])

    tile = 256

    def combine(s):
        fetch_kept(s).wait()
        if s == final:
            fetch_got(s).wait_recv()
        else:
            fetch_got(s).wait()

        def columns_step(d, carry):
            cols = pl.ds(pl.multiple_of(d * tile, tile), tile)
            for k in range(4):
                span = slice(k * capacity, (k + 1) * capacity)
                own_hot = hot_columns(column_ref[s, :, k : k + 1], capacity)
                sibling_hot = hot_columns(column_ref[s, :, 4 + k : 5 + k], capacity)
                total = jnp.dot(own_hot, kept_now[s, span, cols], preferred_element_type=f32)
                total += jnp.dot(sibling_hot, got_now[s, span, cols], preferred_element_type=f32)
                sums[s, k, :, cols] = total.astype(bf16)
            return carry

        lax.fori_loop(0, sums.shape[3] // tile, columns_step, 0)
        for i in range(4):
            first(s, i).start()

    def pass_on(s):
        for i in range(2):
            first(s, i).wait_recv()
        sums[s, 2, :half] = (sums[s, 2, :half].astype(f32) + relay[s, 0].astype(f32)).astype(bf16)
        sums[s, 1, half:] = (sums[s, 1, half:].astype(f32) + relay[s, 1].astype(f32)).astype(bf16)
        for i in range(2):
            second(s, i).start()

    def finish(s):
        for i in range(2):
            first(s, 2 + i).wait_recv()
            second(s, i).wait_recv()
        total = sums[s, 0].astype(f32) + from_x[s].astype(f32) + from_y[s].astype(f32)
        if s:
            own[s] = total.astype(bf16)
            along_z(s).start()
        else:
            out_ref[...] = total

    fetch_got(final).start()
    for s in order:
        fetch_kept(s).start()
        if s != final:
            fetch_got(s).start()
    table_ref[...] = scalar_ref[...]
    for bit in range(2):
        exchange.start(bit)
        exchange.end(bit)
    for i, s in enumerate(order):
        combine(s)
        if i < 3:
            exchange.start(2 + i)
            exchange.end(2 + i)
        if i == 0:
            to_sibling().start()
        if i >= 1:
            pass_on(order[i - 1])
        if i >= 2:
            finish(order[i - 2])
    pass_on(order[-1])
    finish(order[-2])
    finish(order[-1])
    for s in order[:-1]:
        along_z(s).wait_recv()
        out_ref[...] += from_z[s - 1].astype(f32)
    to_sibling().wait()
    exchange.finish()
    fetch_got(final).wait_send()
    for s in order:
        for i in range(4):
            first(s, i).wait_send()
        for i in range(2):
            second(s, i).wait_send()
        if s:
            along_z(s).wait_send()


def return_rows(columns, kept, got, given, out_given, out_got, scalars, capacity):
    chunks, rows, _ = columns.shape
    width = kept.shape[2]
    held = pl.BlockSpec(memory_space=pltpu.VMEM)
    anywhere = pl.BlockSpec(memory_space=pl.ANY)
    dma = pltpu.SemaphoreType.DMA
    return pl.pallas_call(
        functools.partial(return_rows_kernel, capacity),
        out_shape=(
            jax.ShapeDtypeStruct((rows, width), f32),
            jax.ShapeDtypeStruct(out_got.shape, out_got.dtype),
            jax.ShapeDtypeStruct(scalars.shape, f32),
        ),
        in_specs=[held] + [anywhere] * 5 + [held],
        out_specs=[held, anywhere, held],
        input_output_aliases={5: 1},
        scratch_shapes=[
            pltpu.VMEM((chunks, 4 * capacity, width), bf16),
            pltpu.VMEM((chunks, 4 * capacity, width), bf16),
            pltpu.VMEM((chunks, 4, rows, width), bf16),
            pltpu.VMEM((chunks, 2, rows // 2, width), bf16),
            pltpu.VMEM((chunks, rows, width), bf16),
            pltpu.VMEM((chunks, rows, width), bf16),
            pltpu.VMEM((chunks, rows, width), bf16),
            pltpu.VMEM((chunks - 1, rows, width), bf16),
            dma((chunks,)),
            dma((chunks,)),
            dma((chunks, 4)),
            dma((chunks, 4)),
            dma((chunks, 2)),
            dma((chunks, 2)),
            dma((chunks - 1,)),
            dma((chunks - 1,)),
            dma((2,)),
            dma((2,)),
        ]
        + exchange_scratch(scalars.shape[2]),
        compiler_params=pltpu.CompilerParams(
            collective_id=2, has_side_effects=True, vmem_limit_bytes=60 * 2**20
        ),
        cost_estimate=pl.CostEstimate(flops=1000, bytes_accessed=1000, transcendentals=0),
        name="return_rows",
    )(columns, kept, got, given, out_given, out_got, scalars)


def gather_first_kernel(
    q_width,
    kv_heads,
    acts_ref,
    grad_ref,
    weight_ref,
    named_ref,
    acts_out,
    grad_out,
    weight_out,
    table_ref,
    own_weight,
    near_sent,
    near_got,
    far_sent,
    far_got,
    weight_sent,
    weight_got,
    core_sent,
    core_got,
    z_sent,
    z_got,
    local,
    *exchange_refs,
):
    near = neighbours()
    exchange = Exchange(near, table_ref, *exchange_refs)
    ctx, fsdp = lax.axis_index("ctx"), lax.axis_index("fsdp")
    far = (ctx, flip(flip(fsdp, 1), 2))
    partners = [near["x"], near["y"], far]
    groups = [flip(fsdp, 1), flip(fsdp, 2), flip(flip(fsdp, 1), 2)]
    greet([near["core"]] + partners + near["z"][1:])
    rows = acts_ref.shape[0]
    half = rows // 2
    shard_rows = weight_ref.shape[0]
    half_shard = shard_rows // 2
    own_width = weight_out.shape[1]
    head_dim = (own_width - q_width) // 2
    all_q = weight_ref.shape[1] - 2 * kv_heads * head_dim
    core = lax.rem(ctx, 2)
    chain = Chain(near, grad_ref, lambda s: grad_out.at[s], z_sent, z_got)

    def to_near(k):
        return send(acts_ref, acts_out.at[1 + k], near_sent.at[k], near_got.at[k], partners[k])

    def to_far(k):
        span = pl.ds(k * half, half)
        return send(
            acts_out.at[1 + k, span], acts_out.at[3, span], far_sent.at[k], far_got.at[k], partners[1 - k]
        )

    def spans(group):
        return (
            (pl.ds(pl.multiple_of(group * q_width, 128), q_width), pl.ds(0, q_width)),
            (pl.ds(pl.multiple_of(all_q + group * head_dim, 128), head_dim), pl.ds(q_width, head_dim)),
            (
                pl.ds(pl.multiple_of(all_q + (kv_heads + group) * head_dim, 128), head_dim),
                pl.ds(q_width + head_dim, head_dim),
            ),
        )

    def weight_to(k, i):
        there, here = spans(groups[k])[i]
        from_row = pl.multiple_of(core * half_shard, 16)
        to_row = pl.multiple_of(fsdp * shard_rows + core * half_shard, 16)
        return send(
            weight_ref.at[pl.ds(from_row, half_shard), there],
            weight_out.at[pl.ds(to_row, half_shard), here],
            weight_sent.at[k, i],
            weight_got.at[k, i],
            partners[k],
        )

    def weight_on(k):
        row = pl.multiple_of(groups[k] * shard_rows + core * half_shard, 16)
        part = weight_out.at[pl.ds(row, half_shard)]
        return send(part, part, core_sent.at[k], core_got.at[k], near["core"])

    table_ref[...] = named_ref[...]
    exchange.start(0)
    to_near(0).start()
    chain.start()
    exchange.end(0)
    exchange.start(1)
    to_near(1).start()
    exchange.end(1)
    for k in (2, 0, 1):
        for i in range(3):
            weight_to(k, i).start()
    exchange.start(2)
    exchange.end(2)
    own_parts = [
        pltpu.make_async_copy(weight_ref.at[:, there], own_weight.at[:, here], local.at[i])
        for i, (there, here) in enumerate(spans(fsdp))
    ]
    keeps = [
        pltpu.make_async_copy(acts_ref, acts_out.at[0], local.at[3]),
        pltpu.make_async_copy(grad_ref, grad_out.at[0], local.at[4]),
    ]
    for copy in own_parts + keeps:
        copy.start()
    for copy in own_parts:
        copy.wait()
    place = pltpu.make_async_copy(
        own_weight,
        weight_out.at[pl.ds(pl.multiple_of(fsdp * shard_rows, 16), shard_rows)],
        local.at[5],
    )
    place.start()
    for k in range(2):
        to_near(k).wait_recv()
        to_far(k).start()
    chain.step(1)
    exchange.start(3)
    exchange.end(3)
    exchange.start(4)
    chain.step(2)
    for k in (2, 0, 1):
        for i in range(3):
            weight_to(k, i).wait_recv()
        weight_on(k).start()
    exchange.end(4)
    for k in range(2):
        to_far(k).wait_recv()
    for k in range(3):
        weight_on(k).wait_recv()
    chain.step(3)
    for copy in keeps + [place]:
        copy.wait()
    chain.finish()
    exchange.finish()
    for k in range(2):
        to_near(k).wait_send()
        to_far(k).wait_send()
    for k in range(3):
        for i in range(3):
            weight_to(k, i).wait_send()
        weight_on(k).wait_send()


def gather_first(acts, grad, weight, named, n_fsdp, z_count, q_width, kv_heads, head_dim):
    rows, width = acts.shape
    own_width = q_width + 2 * head_dim
    held = pl.BlockSpec(memory_space=pltpu.VMEM)
    anywhere = pl.BlockSpec(memory_space=pl.ANY)
    dma = pltpu.SemaphoreType.DMA
    return pl.pallas_call(
        functools.partial(gather_first_kernel, q_width, kv_heads),
        out_shape=(
            jax.ShapeDtypeStruct((n_fsdp, rows, width), bf16),
            jax.ShapeDtypeStruct((z_count, rows, width), bf16),
            jax.ShapeDtypeStruct((n_fsdp * weight.shape[0], own_width), bf16),
            jax.ShapeDtypeStruct(named.shape, f32),
        ),
        in_specs=[held, held, anywhere, held],
        out_specs=[anywhere] * 3 + [held],
        scratch_shapes=[
            pltpu.VMEM((weight.shape[0], own_width), bf16),
            dma((2,)),
            dma((2,)),
            dma((2,)),
            dma((2,)),
            dma((3, 3)),
            dma((3, 3)),
            dma((3,)),
            dma((3,)),
            dma((5,)),
            dma((3,)),
            dma((6,)),
        ]
        + exchange_scratch(named.shape[2]),
        compiler_params=pltpu.CompilerParams(
            collective_id=3, has_side_effects=True, vmem_limit_bytes=32 * 2**20
        ),
        cost_estimate=pl.CostEstimate(flops=1000, bytes_accessed=1000, transcendentals=0),
        name="gather_first",
    )(acts, grad, weight, named)


def finish_kernel(
    kv_heads,
    parts_ref,
    tokens_ref,
    resid_grad_ref,
    gain_ref,
    shares_ref,
    q_ref,
    kv_ref,
    router_ref,
    later_ref,
    got_ref,
    own_ref,
    for_x_ref,
    for_y_ref,
    resid_ref,
    out_weight_ref,
    grad_ref,
    gains_ref,
    weight_ref,
    router_out_ref,
    output_ref,
    out_weight_out,
    out_weight_got,
    owner_sent,
    owner_got,
    parts_now,
    resid_grad_now,
    resid_now,
    own_now,
    q_now,
    kv_now,
    router_now,
    fetched,
    stream_fetched,
    rows_x,
    rows_y,
    rows_z,
    rows_own,
    relay,
    from_x,
    from_y,
    q_core,
    kv_core,
    router_core,
    q_sum,
    kv_sum,
    router_sum,
    q_z,
    kv_z,
    router_z,
    q_total,
    kv_total,
    router_total,
    router_got,
    gain_got,
    first_sent,
    first_got,
    second_sent,
    second_got,
    core_sent,
    core_got,
    z_sent,
    z_got,
    row_sent,
    row_got,
    gain_sent,
    gain_in,
    rows_sent,
    rows_got,
    local,
):
    near = neighbours()
    ctx, fsdp = lax.axis_index("ctx"), lax.axis_index("fsdp")
    groups = [fsdp, flip(fsdp, 1), flip(fsdp, 2), flip(flip(fsdp, 1), 2)]
    partners = [None] + [(ctx, group) for group in groups[1:]]
    moves = fsdp != 0
    stays = fsdp == 0
    owner = (
        ctx
        + 2 * (fsdp % 2) * (1 - 2 * ((ctx // 2) % 2))
        + 4 * (fsdp // 2) * (1 - 2 * ((ctx // 4) % 2)),
        fsdp,
    )
    greet([near["core"]] + partners[1:] + near["z"][1:])
    to_owner = lambda: send(out_weight_ref, out_weight_got, owner_sent, owner_got, owner)
    keep_owned = lambda: pltpu.make_async_copy(out_weight_ref, out_weight_got, owner_got)

    @pl.when(moves)
    def _():
        to_owner().start()

    @pl.when(stays)
    def _():
        keep_owned().start()

    rows = tokens_ref.shape[0]
    half = rows // 2
    low, high = pl.ds(0, half), pl.ds(half, half)
    own_ctx = [ctx] + [partner[0] for partner in near["z"][1:]]
    chunks = len(own_ctx)
    streams = (
        (q_ref, q_core, q_sum, q_z, q_total, q_now),
        (kv_ref, kv_core, kv_sum, kv_z, kv_total, kv_now),
        (router_ref, router_core, router_sum, router_z, router_total, router_now),
    )
    out_rows = weight_ref.shape[0]
    q_width = q_ref.shape[2]
    head_dim = kv_ref.shape[2] // 2
    all_q = weight_ref.shape[1] - 2 * kv_heads * head_dim

    def first(i):
        source, target, partner = (
            (parts_ref.at[3, low], relay.at[0], near["x"]),
            (parts_ref.at[3, high], relay.at[1], near["y"]),
            (parts_ref.at[1, low], from_x.at[low], near["x"]),
            (parts_ref.at[2, high], from_y.at[high], near["y"]),
        )[i]
        return send(source, target, first_sent.at[i], first_got.at[i], partner)

    def second(i):
        source, target, partner = (
            (relay.at[0], from_y.at[low], near["y"]),
            (relay.at[1], from_x.at[high], near["x"]),
        )[i]
        return send(source, target, second_sent.at[i], second_got.at[i], partner)

    def to_core(i, s):
        source, landing = streams[i][:2]
        return send(
            source.at[flip(own_ctx[s], 1)],
            landing.at[s],
            core_sent.at[i, s],
            core_got.at[i, s],
            near["core"],
        )

    def along_z(i, s):
        return send(
            streams[i][2].at[s],
            streams[i][3].at[s - 1],
            z_sent.at[i, s - 1],
            z_got.at[i, s - 1],
            near["z"][1 + (s == 2)],
        )

    def row_parts(k):
        span = pl.ds(pl.multiple_of(groups[k] * out_rows, 8), out_rows)

        def at(start, width):
            return pl.ds(pl.multiple_of(start, 128), width)

        return (
            (q_total.at[span], weight_ref.at[:, at(fsdp * q_width, q_width)]),
            (
                kv_total.at[span, pl.ds(0, head_dim)],
                weight_ref.at[:, at(all_q + fsdp * head_dim, head_dim)],
            ),
            (
                kv_total.at[span, pl.ds(head_dim, head_dim)],
                weight_ref.at[:, at(all_q + (kv_heads + fsdp) * head_dim, head_dim)],
            ),
            (router_total.at[span], router_got.at[k]),
        )

    def to_row(k, i):
        source, target = row_parts(k)[i]
        return send(source, target, row_sent.at[k - 1, i], row_got.at[k - 1, i], partners[k])

    def keep_row(i):
        source, target = row_parts(0)[i]
        return pltpu.make_async_copy(source, target, local.at[i])

    gain_partners = [near["core"], near["x"], near["y"], near["z"][1], near["z"][2]]

    def share(i):
        return send(
            gains_ref, gain_got.at[i], gain_sent.at[i], gain_in.at[i], gain_partners[i]
        )

    def fetch(i):
        source, target = (
            (parts_ref.at[0], parts_now.at[pl.ds(0, rows)]),
            (parts_ref.at[2, low], parts_now.at[pl.ds(rows, half)]),
            (parts_ref.at[1, high], parts_now.at[pl.ds(rows + half, half)]),
            (resid_grad_ref, resid_grad_now),
            (resid_ref, resid_now),
            (own_ref.at[pl.ds(0, 2)], own_now),
        )[i]
        return pltpu.make_async_copy(source, target, fetched.at[i])

    def fetch_stream(i, s):
        return pltpu.make_async_copy(
            streams[i][0].at[own_ctx[s]], streams[i][5].at[s], stream_fetched.at[i, s]
        )

    def rows_copy(i):
        source, target, partner = (
            (rows_own.at[0], rows_z.at[0], near["z"][2]),
            (for_x_ref.at[1], rows_x.at[1], near["x"]),
            (for_y_ref.at[1], rows_y.at[1], near["y"]),
            (for_x_ref.at[0], rows_x.at[0], near["x"]),
            (for_y_ref.at[0], rows_y.at[0], near["y"]),
            (rows_own.at[1], rows_z.at[1], near["z"][1]),
        )[i]
        return send(source, target, rows_sent.at[i], rows_got.at[i], partner)

    for i in range(4):
        first(i).start()
    for s in (3, 1, 2, 0):
        for i in range(3):
            to_core(i, s).start()
            fetch_stream(i, s).start()
    for i in range(6):
        fetch(i).start()
    rows_own[0] = (later_ref[...].astype(f32) + got_ref[...].astype(f32)).astype(bf16)
    rows_copy(0).start()
    for s in (3, 1, 2, 0):
        for i in range(3):
            _, landing, total, _, _, now = streams[i]
            fetch_stream(i, s).wait()
            to_core(i, s).wait_recv()
            total[s] = (now[s].astype(f32) + landing[s].astype(f32)).astype(bf16)
            if s % 2:
                along_z(i, s).start()
    for i in range(2):
        first(i).wait_recv()
    for i in range(3):
        fetch(i).wait()
    relay[0] = (relay[0].astype(f32) + parts_now[rows : rows + half].astype(f32)).astype(bf16)
    relay[1] = (relay[1].astype(f32) + parts_now[rows + half :].astype(f32)).astype(bf16)
    for i in range(2):
        second(i).start()
    for i in range(1, 5):
        rows_copy(i).start()
    for i in range(2):
        first(2 + i).wait_recv()
        second(i).wait_recv()
    gains_ref[...] = shares_ref[...]
    block = 32
    for i in range(3, 6):
        fetch(i).wait()

    def back_step(b, carry):
        span = pl.ds(pl.multiple_of(b * block, block), block)
        grad = (
            parts_now[span, :].astype(f32)
            + from_x[span, :].astype(f32)
            + from_y[span, :].astype(f32)
        )
        values = tokens_ref[span, :].astype(f32)
        scale = lax.rsqrt(jnp.mean(values * values, axis=-1, keepdims=True) + eps_norm)
        unit = values * scale
        scaled = grad * gain_ref[...]
        back = scale * (scaled - unit * jnp.mean(scaled * unit, axis=-1, keepdims=True))
        grad_ref[span, :] = resid_grad_now[span, :] + back
        gains_ref[0] += jnp.sum(grad * unit, axis=0, keepdims=True)
        return carry

    lax.fori_loop(0, rows // block, back_step, 0)
    share(0).start()
    for i in range(3):
        _, _, held, landing, _, _ = streams[i]
        along_z(i, 3).wait_recv()
        held[2] = (held[2].astype(f32) + landing[2].astype(f32)).astype(bf16)
        along_z(i, 2).start()
    for i in range(1, 3):
        rows_copy(i).wait_recv()
    rows_own[1] = (own_now[1].astype(f32) + rows_x[1].astype(f32) + rows_y[1].astype(f32)).astype(bf16)
    rows_copy(5).start()

    def add_share(i):
        if i:
            share(i).start()
        share(i).wait()
        gains_ref[...] += gain_got[i]

    for i in range(3):
        add_share(i)
    for i in range(3):
        _, _, held, landing, total, _ = streams[i]
        for s in range(1, 3):
            along_z(i, s).wait_recv()
        total[...] = held[0].astype(f32) + landing[0].astype(f32) + landing[1].astype(f32)
    for k in range(1, 4):
        for i in range(4):
            to_row(k, i).start()
    for i in range(3):
        keep_row(i).start()
    for i in range(3, len(gain_partners)):
        add_share(i)
    own = pl.ds(pl.multiple_of(fsdp * out_rows, 8), out_rows)
    router_all = router_total[own, :]
    for k in range(1, 4):
        for i in range(4):
            to_row(k, i).wait()
        router_all += router_got[k]
    router_out_ref[...] = router_all
    for i in range(3):
        keep_row(i).wait()
    for i in (0, 3, 4, 5):
        rows_copy(i).wait_recv()

    @pl.when(moves)
    def _():
        to_owner().wait()

    @pl.when(stays)
    def _():
        keep_owned().wait()

    out_weight_out[...] = out_weight_got[...].astype(f32)

    def output_step(b, carry):
        span = pl.ds(pl.multiple_of(b * block, block), block)
        total = resid_now[span, :] + own_now[0, span, :].astype(f32)
        for part in (rows_x[0, span, :], rows_y[0, span, :], rows_z[0, span, :], rows_z[1, span, :]):
            total += part.astype(f32)
        output_ref[span, :] = total.astype(bf16)
        return carry

    lax.fori_loop(0, rows // block, output_step, 0)
    for i in range(6):
        rows_copy(i).wait_send()
    for i in range(4):
        first(i).wait_send()
    for i in range(2):
        second(i).wait_send()
    for i in range(3):
        for s in range(chunks):
            to_core(i, s).wait_send()
            if s:
                along_z(i, s).wait_send()


def finish(parts, tokens, resid_grad, gain, shares, grad_q, grad_kv, grad_router, expert_rows, resid, out_weight, kv_heads):
    rows, width = tokens.shape
    n_ctx, share_rows, q_width = grad_q.shape
    pair_width, router_width = grad_kv.shape[2], grad_router.shape[2]
    chunks = n_ctx // 2
    out_rows = share_rows // 4
    all_width = 4 * q_width + kv_heads * pair_width
    held = pl.BlockSpec(memory_space=pltpu.VMEM)
    anywhere = pl.BlockSpec(memory_space=pl.ANY)
    dma = pltpu.SemaphoreType.DMA
    widths = (q_width, pair_width, router_width)
    return pl.pallas_call(
        functools.partial(finish_kernel, kv_heads),
        out_shape=(
            jax.ShapeDtypeStruct((rows, width), f32),
            jax.ShapeDtypeStruct(shares.shape, f32),
            jax.ShapeDtypeStruct((out_rows, all_width), f32),
            jax.ShapeDtypeStruct((out_rows, router_width), f32),
            jax.ShapeDtypeStruct((rows, width), bf16),
            jax.ShapeDtypeStruct(out_weight.shape, f32),
        ),
        in_specs=[anywhere, held, anywhere, held, held]
        + [anywhere] * 3
        + [held, held]
        + [anywhere] * 5,
        out_specs=[held] * 6,
        scratch_shapes=[
            pltpu.VMEM(out_weight.shape, bf16),
            dma,
            dma,
            pltpu.VMEM((2 * rows, width), bf16),
            pltpu.VMEM((rows, width), f32),
            pltpu.VMEM((rows, width), f32),
            pltpu.VMEM((2, rows, width), bf16),
        ]
        + [pltpu.VMEM((chunks, share_rows, columns), bf16) for columns in widths]
        + [
            dma((6,)),
            dma((3, chunks)),
            pltpu.VMEM((2, rows, width), bf16),
            pltpu.VMEM((2, rows, width), bf16),
            pltpu.VMEM((2, rows, width), bf16),
            pltpu.VMEM((2, rows, width), bf16),
            pltpu.VMEM((2, rows // 2, width), bf16),
            pltpu.VMEM((rows, width), bf16),
            pltpu.VMEM((rows, width), bf16),
        ]
        + [pltpu.VMEM((chunks, share_rows, columns), bf16) for columns in widths]
        + [pltpu.VMEM((chunks, share_rows, columns), bf16) for columns in widths]
        + [pltpu.VMEM((chunks - 1, share_rows, columns), bf16) for columns in widths]
        + [pltpu.VMEM((share_rows, columns), f32) for columns in widths]
        + [
            pltpu.VMEM((4, out_rows, router_width), f32),
            pltpu.VMEM((5,) + shares.shape, f32),
            dma((4,)),
            dma((4,)),
            dma((2,)),
            dma((2,)),
            dma((3, chunks)),
            dma((3, chunks)),
            dma((3, chunks - 1)),
            dma((3, chunks - 1)),
            dma((3, 4)),
            dma((3, 4)),
            dma((5,)),
            dma((5,)),
            dma((7,)),
            dma((7,)),
            dma((3,)),
        ],
        compiler_params=pltpu.CompilerParams(
            collective_id=4, has_side_effects=True, vmem_limit_bytes=62 * 2**20
        ),
        cost_estimate=pl.CostEstimate(flops=1000, bytes_accessed=1000, transcendentals=0),
        name="finish",
    )(parts, tokens, resid_grad, gain, shares, grad_q, grad_kv, grad_router, *expert_rows, resid, out_weight)


def fast_body(
    n_ctx,
    tokens,
    positions,
    expert_ids,
    attn_gain,
    query_key_value_weight,
    q_gain,
    k_gain,
    output_weight,
    ffn_gain,
    router_weight,
    w_gate,
    w_up,
    w_down,
    cotangent,
):
    n_fsdp = 4
    n_all = n_ctx * n_fsdp
    ctx_at = lax.axis_index("ctx")
    fsdp_at = lax.axis_index("fsdp")
    core_at = ctx_at % 2
    own_at = ctx_at * n_fsdp + fsdp_at
    row_count = tokens.shape[1]
    model_width = tokens.shape[2]
    head_dim = q_gain.shape[0]
    shard_rows = query_key_value_weight.shape[0]
    heads = output_weight.shape[0] // head_dim
    q_width = heads * head_dim
    all_q = q_width * n_fsdp
    kv_heads = (query_key_value_weight.shape[1] - all_q) // (2 * head_dim)
    own_width = q_width + 2 * head_dim
    expert_count = n_all
    top_count = expert_ids.shape[2]
    capacity = row_count * top_count * 3 // (2 * expert_count)
    z_count = n_ctx // 2
    chunk_rows = 2 * n_fsdp * capacity

    inputs = tokens.reshape(row_count, model_width).astype(f32)
    places = positions.reshape(row_count)
    chosen = expert_ids.reshape(row_count, top_count)
    grad_res_low = cotangent.reshape(row_count, model_width)
    grad_res = grad_res_low.astype(f32)

    relative = jnp.bitwise_xor(own_at, jnp.arange(n_all, dtype=jnp.int32))
    chosen_rel = (chosen[:, :, None] == relative[None, None, :]).astype(f32)
    named = jnp.sum(chosen_rel, axis=1).T
    first_block = jnp.broadcast_to((places[0] // run_rows).astype(f32), (n_all, 128))
    named = jnp.concatenate([named, first_block], axis=1)[:, None, :]

    rms_one = lax.rsqrt(jnp.mean(inputs * inputs, axis=-1, keepdims=True) + eps_norm)
    acts = (inputs * rms_one * attn_gain).astype(bf16)
    acts_group, grad_slots, weight_qkv, small = gather_first(
        acts, grad_res_low, query_key_value_weight, named, n_fsdp, z_count, q_width, kv_heads, head_dim
    )
    named_here = small[:, 0, :row_count]
    block_table = small[:, 0, row_count].astype(jnp.int32).reshape(n_ctx, n_fsdp)
    acts_group = acts_group.reshape(n_fsdp * row_count, model_width)

    group_rows = n_fsdp * row_count
    blocks_total = 2 * n_ctx
    own_blocks = block_table[0]
    run_blocks = jnp.stack([own_blocks, blocks_total - 1 - own_blocks], axis=1)
    row_places = (
        run_blocks[:, :, None] * run_rows + jnp.arange(run_rows, dtype=jnp.int32)[None, None, :]
    ).reshape(n_fsdp, row_count, 1)
    angles = row_places.astype(f32) * frequencies(head_dim)
    cosine, sine = jnp.cos(angles), jnp.sin(angles)
    cosine = jnp.concatenate([cosine, cosine], axis=-1)
    sine = jnp.concatenate([-sine, sine], axis=-1)
    block_index = jnp.arange(blocks_total, dtype=jnp.int32)
    slot_index = jnp.arange(n_ctx, dtype=jnp.int32)[:, None, None]
    source_table = jnp.sum(
        jnp.where(block_table[:, :, None] == block_index, 2 * slot_index, 0)
        + jnp.where(blocks_total - 1 - block_table[:, :, None] == block_index, 2 * slot_index + 1, 0),
        axis=0,
    )
    place_list = run_blocks.reshape(-1)
    source_list = source_table.reshape(-1)

    projected, query_low, kv_own = project(
        acts_group.reshape(n_fsdp, row_count, model_width),
        weight_qkv,
        cosine,
        sine,
        q_gain[None],
        k_gain[None],
        heads,
    )

    grad_x = swap(grad_slots, "fsdp", n_fsdp, 1)
    grad_y = swap(grad_slots, "fsdp", n_fsdp, 2)

    kv_slots = [kv_own] + [swap(kv_own, "ctx", n_ctx, 2 * k) for k in range(1, z_count)]
    kv_slots = jnp.stack(kv_slots)
    kv_all = jnp.stack([kv_slots, swap(kv_slots, "ctx", n_ctx, 1)], axis=1)
    kv_all = kv_all.reshape(n_ctx, n_fsdp, row_count, 2 * head_dim)

    mixed, lse = attend(place_list, source_list, query_low, kv_all)
    heads_low = mixed.reshape(group_rows, q_width)
    heads_low = after(heads_low, (grad_x, grad_y))

    resid_parts = jnp.dot(heads_low, output_weight, preferred_element_type=f32).astype(bf16)
    resid = inputs + scatter_parts(resid_parts.reshape(n_fsdp, row_count, model_width))
    rms_two = lax.rsqrt(jnp.mean(resid * resid, axis=-1, keepdims=True) + eps_norm)
    acts_two = (resid * rms_two * ffn_gain).astype(bf16)

    full_router = by_fsdp(
        [router_weight] + [swap(router_weight, "fsdp", n_fsdp, k) for k in range(1, n_fsdp)], fsdp_at
    ).reshape(n_fsdp * shard_rows, expert_count)
    logits = jnp.dot(acts_two, full_router, preferred_element_type=f32)
    pick_table = (chosen[:, :, None] == jnp.arange(expert_count)[None, None, :]).astype(f32)
    picked = jnp.sum(logits[:, None, :] * pick_table, axis=-1)
    gate_vals, gate_back = jax.vjp(lambda values: jax.nn.softmax(values, axis=-1), picked)
    gates_rel = jnp.sum(chosen_rel * gate_vals[:, :, None], axis=1).T

    upper = jnp.triu(jnp.ones((row_count, row_count), bf16), 1)
    rank = jnp.dot(named_here.astype(bf16), upper, preferred_element_type=f32)
    slots = jnp.where(named_here > 0.5, rank, -1.0).reshape(z_count, 2 * n_fsdp, row_count)
    sibling_slots = swap(slots[:, n_fsdp:], "ctx", n_ctx, 1)
    columns = jnp.swapaxes(jnp.concatenate([slots[:, :n_fsdp], sibling_slots], axis=1), 1, 2)
    gates = gates_rel[:, None, :]
    gate_w = w_gate[0]
    up_w = w_up[0]
    down_w = w_down[0]


    (
        act_rows,
        grad_rows,
        hidden_rows,
        gate_lows,
        up_lows,
        kept,
        got,
        given,
        out_kept,
        out_got,
        out_given,
        scalars,
        *_,
    ) = gather_experts(
        acts_two,
        slots,
        sibling_slots,
        gates,
        gate_w,
        up_w,
        down_w,
        [grad_slots, grad_x, grad_y],
        capacity,
    )
    acts_two_grad, out_got, gate_grad_rel = return_rows(
        columns, kept, got, given, out_given, out_got, scalars.reshape(n_all, 1, row_count), capacity
    )
    gate_grad = jnp.sum(chosen_rel * gate_grad_rel[:, 0].T[:, None, :], axis=-1)
    (picked_grad,) = gate_back(gate_grad)
    logit_grad = jnp.sum(picked_grad[:, :, None] * pick_table, axis=1).astype(bf16)
    acts_two_grad = acts_two_grad + jnp.dot(
        logit_grad, full_router.T, preferred_element_type=f32
    )

    scaled = ffn_gain * acts_two_grad
    grad_ffn_gain = jnp.sum(acts_two_grad * resid * rms_two, axis=0)
    resid_grad = (
        grad_res
        + rms_two * scaled
        - resid * (rms_two**3 * jnp.mean(scaled * resid, axis=-1, keepdims=True))
    )
    attn_grad = resid_grad.astype(bf16)
    row_total = z_count * chunk_rows

    def weight_grad(left, right, earlier):
        left = after(left, earlier)
        return jnp.einsum(
            "rd,rf->df",
            left.reshape(row_total, -1),
            right.reshape(row_total, -1),
            preferred_element_type=f32,
        )[None]

    grad_w_down = weight_grad(hidden_rows, grad_rows, attn_grad)
    combined = combine_rows(after(columns, attn_grad), out_kept, out_got, capacity)
    half_rows = row_count // 2
    near_x = swap(attn_grad, "fsdp", n_fsdp, 1)
    near_y = swap(attn_grad, "fsdp", n_fsdp, 2)
    near_x, near_y, *combined = after((near_x, near_y), combined, True)
    out_own, out_x, out_y, out_low, out_high = combined
    far_low = swap(near_x[:half_rows], "fsdp", n_fsdp, 2)
    far_high = swap(near_y[half_rows:], "fsdp", n_fsdp, 1)
    far_low, far_high, grad_w_down = after((far_low, far_high), (grad_w_down,), True)
    attn_grad_group = jnp.concatenate([attn_grad, near_x, near_y, far_low, far_high], axis=0)
    heads_grad = jnp.einsum(
        "td,cd->tc", attn_grad_group, output_weight, preferred_element_type=f32
    ).astype(bf16)
    grad_w_out = jnp.einsum(
        "tc,td->cd", heads_low, attn_grad_group, preferred_element_type=f32
    ).astype(bf16)
    heads_grad = heads_grad.reshape(n_fsdp, row_count, q_width)
    per_ctx = grad_w_out.shape[0] // n_ctx
    out_split = grad_w_out.reshape(2, z_count, per_ctx, model_width)
    out_keep = pick(out_split, core_at)
    out_away = pick(out_split, 1 - core_at)
    out_keep = after(out_keep, heads_grad)
    out_sum = (out_keep.astype(f32) + swap(out_away, "ctx", n_ctx, 1).astype(f32)).astype(bf16)
    piece_at = (ctx_at // 2) ^ fsdp_at
    heads_grad = after(heads_grad, out_sum)
    out_terms = [
        swap(pick(out_sum, piece_at ^ k), "ctx", n_ctx, 2 * k) for k in range(1, z_count)
    ]
    dq, dkv, dkv_away, dq_gain = attend_back(
        place_list,
        source_list,
        query_low,
        kv_all,
        mixed,
        heads_grad,
        lse,
        projected,
        cosine,
        sine,
        q_gain[None],
    )

    half_slots = z_count // 2
    out_low, out_high = after((out_low, out_high), attn_grad_group)
    from_x = swap(out_low, "fsdp", n_fsdp, 1)
    from_y = swap(out_high, "fsdp", n_fsdp, 2)
    dkv_got = swap(dkv_away, "ctx", n_ctx, 1)
    dq, dkv, dq_gain, from_x, from_y, *out_terms = after(
        (dq, dkv, dq_gain), (from_x, from_y, *out_terms), True
    )

    def added(parts, term, low, span):
        term = term[span].astype(f32)
        parts = parts[span].astype(f32)
        pad = ((0, 0), (0, half_rows), (0, 0)) if low else ((0, 0), (half_rows, 0), (0, 0))
        return (parts + jnp.pad(term, pad)).astype(bf16)

    near_span, far_span = slice(0, half_slots), slice(half_slots, z_count)
    later_x = swap(added(out_x, from_y, False, far_span), "fsdp", n_fsdp, 1)
    later_y = swap(added(out_y, from_x, True, far_span), "fsdp", n_fsdp, 2)
    sooner_x = added(out_x, from_y, False, near_span)
    sooner_y = added(out_y, from_x, True, near_span)
    proj_low_q = dq.reshape(group_rows, q_width)

    held = (dkv.astype(f32) + dkv_got.astype(f32)).astype(bf16)
    held_core = held
    held = [held[0]] + [swap(held[k], "ctx", n_ctx, 2 * k) for k in range(1, z_count)]
    out_later = (
        out_own[far_span].astype(f32) + later_x.astype(f32) + later_y.astype(f32)
    ).astype(bf16)
    held = after(held, out_later)
    dkv_own, dk_gain = key_back(held, projected, cosine, sine, k_gain[None])
    proj_low_kv = dkv_own.reshape(group_rows, 2 * head_dim)
    acts_parts = (
        jnp.einsum("tc,dc->td", proj_low_q, weight_qkv[:, :q_width], preferred_element_type=f32)
        + jnp.einsum("tc,dc->td", proj_low_kv, weight_qkv[:, q_width:], preferred_element_type=f32)
    ).astype(bf16)

    def token_sum(left, right):
        return jnp.einsum("td,tc->dc", left, right, preferred_element_type=f32).astype(bf16)

    share_rows = model_width // n_ctx
    grad_q = token_sum(after(acts_group, held_core), proj_low_q).reshape(n_ctx, share_rows, q_width)
    out_got = swap(out_later[1], "ctx", n_ctx, 2)
    grad_kv = token_sum(acts_group, after(proj_low_kv, out_got)).reshape(n_ctx, share_rows, 2 * head_dim)
    padded = jnp.pad(logit_grad, ((0, 0), (0, -expert_count % 128)))
    grad_router = token_sum(after(acts_two, attn_grad_group), padded)
    grad_router = grad_router.reshape(n_ctx, share_rows, -1)
    small_gains = jnp.concatenate([jnp.sum(dq_gain, axis=0), jnp.sum(dk_gain, axis=0)])
    shares = jnp.stack(
        [
            jnp.zeros_like(grad_ffn_gain),
            grad_ffn_gain,
            jnp.pad(small_gains, (0, model_width - small_gains.shape[0])),
        ]
    )[:, None, :]
    grad_w_out = pick(after(out_sum, held_core), piece_at).astype(f32)
    for term in out_terms:
        grad_w_out = grad_w_out + term.astype(f32)
    grad_w_out = lax.ppermute(
        after(grad_w_out.astype(bf16), out_later),
        ("ctx", "fsdp"),
        [
            (c * n_fsdp + f, c * n_fsdp + (f ^ (c // 2)))
            for c in range(n_ctx)
            for f in range(n_fsdp)
        ],
    )
    grad_tokens, gains, grad_w_qkv, grad_w_router, output, grad_w_out = finish(
        acts_parts.reshape(n_fsdp, row_count, model_width),
        tokens.reshape(row_count, model_width),
        resid_grad,
        attn_gain[None],
        shares,
        grad_q,
        grad_kv,
        grad_router,
        (out_later[0], out_got, out_own, sooner_x, sooner_y),
        resid,
        grad_w_out,
        kv_heads,
    )
    output = output.reshape(tokens.shape)
    grad_tokens = grad_tokens.reshape(tokens.shape)
    grad_w_router = grad_w_router[:, :expert_count]
    grad_attn_gain = gains[0, 0]
    grad_ffn_gain = gains[1, 0]
    grad_q_gain = gains[2, 0, :head_dim]
    grad_k_gain = gains[2, 0, head_dim : 2 * head_dim]

    grad_w_gate = weight_grad(act_rows, gate_lows, held_core)
    grad_w_up = weight_grad(act_rows, up_lows, grad_q)

    return (
        output,
        grad_tokens,
        grad_attn_gain,
        grad_w_qkv,
        grad_q_gain,
        grad_k_gain,
        grad_w_out,
        grad_ffn_gain,
        grad_w_router,
        grad_w_gate,
        grad_w_up,
        grad_w_down,
    )


def solution(mesh):
    n_ctx, n_fsdp = mesh.shape["ctx"], mesh.shape["fsdp"]

    def body(*arrays):
        heads_kv = (arrays[4].shape[1] - arrays[7].shape[0] * n_fsdp) // (2 * arrays[5].shape[0])
        if n_fsdp == 4 and heads_kv == n_fsdp and n_ctx == 8:
            return fast_body(n_ctx, *arrays)
        return general_body(*arrays)

    whole = P(("ctx", "fsdp"), None, None)
    rows = P(("ctx", "fsdp"), None)
    split = P("fsdp", "ctx", None)
    return jax.shard_map(
        body,
        mesh=mesh,
        in_specs=(
            split,
            P("fsdp", "ctx"),
            split,
            P(),
            P("fsdp", None),
            P(),
            P(),
            P("fsdp", None),
            P(),
            P("fsdp", None),
            whole,
            whole,
            whole,
            split,
        ),
        out_specs=(split, split, P(), rows, P(), P(), rows, P(), rows, whole, whole, whole),
        check_vma=False,
    )
```
